32 devices in a mesh: section: 2 (over x), group: 4 (over y, core), dp: 4 (over z).
Axes of the slice: x: 2, y: 2, z: 4, core: 2. Of those that a mesh axis runs over, the one named last changes fastest.
Arguments:
- byte_states: bfloat16 [64, 1024, 1024], P(('group', 'dp')), may hold values from -6 to 6
- patch_lengths: int32 [64, 256], P(('group', 'dp')), may hold values from 1 to 8, 1024 in all within a row
- patch_docs: int32 [64, 256], P(('group', 'dp')), may hold values from 0 to 7, never falling along the last dimension, each value on 1 to 64 neighbouring positions
- attn_qkv: bfloat16 [2, 3, 1024, 1024], P('section', None, 'dp'), may hold values from -0.1875 to 0.1875
- attn_out: bfloat16 [2, 1024, 1024], P('section', 'dp'), may hold values from -0.75 to 0.75
- norm_gains: float32 [2, 2, 1024], P('section'), may hold values from 0.25 to 1.75
- ffn_in: bfloat16 [1024, 5632], P(('section', 'dp')), may hold values from -0.1875 to 0.1875
- ffn_down: bfloat16 [2816, 1024], P(('section', 'dp')), may hold values from -0.109375 to 0.109375
- cotangent: bfloat16 [64, 256, 1024], P(('group', 'dp')), may hold values from -6 to 6
Outputs:
- latents: bfloat16 [64, 256, 1024], P(('group', 'dp'), None, 'section')
- byte_grads: bfloat16 [64, 1024, 1024], P(('group', 'dp'), None, 'section')
- grad_attn_qkv: float32 [2, 3, 1024, 1024], P('section', None, 'dp')
- grad_attn_out: float32 [2, 1024, 1024], P('section', 'dp')
- grad_norm_gains: float32 [2, 2, 1024], P('section', None, 'dp')
- grad_ffn_in: float32 [1024, 5632], P(('section', 'dp'))
- grad_ffn_down: float32 [2816, 1024], P(('section', 'dp'))
The draws below stay inside these ranges and needn't reach their ends.
Inputs may be any that keep to these rules, and one draw needn't show every extreme that they name: `patch_lengths`: each row's 256 patch lengths sum to 1024; in every row the longest patch has exactly 8 bytes. `patch_docs`: document numbers never fall along a row; each of the 8 documents of a row has 1 to 64 patches, and one has exactly that many.
All inputs are finite; a program needn't handle non-finite values.
Results may differ from the reference program's by a relative error of at most 0.023.
Values may be sent and summed in bfloat16 or wider, within the bound.
No kernel may reach another device: no remote copies, remote signals or barrier semaphores. Data moves between devices by JAX's collectives and lax.ppermute only.
A program may use at most 320 MiB of HBM per device.

```python
import math
import jax
import jax.numpy as jnp
import numpy as np
from jax import lax

D = 1024
HEADS = 16
HEAD_DIM = 64
FF = 2816
ROW_BYTES = 1024
DOCS = 8
PATCHES = 256
ROWS = 64


def shard_levels(key, shape, split, smallest, largest):
    loudness = 1.0
    for dim, parts in split:
        draws = jax.random.uniform(jax.random.fold_in(jax.random.fold_in(key, 6), dim), (parts,), jnp.float32, smallest / len(split), largest / len(split))
        loudness = loudness * jnp.repeat(jnp.exp(draws), shape[dim] // parts).reshape((-1,) + (1,) * (len(shape) - 1 - dim))
    return loudness


def length_profile(amount, total, bound, skew):
    loads = [(1 << 20) // math.isqrt(grade ** skew) + 1 for grade in range(2, amount + 1)]
    spare, given = total - bound - (amount - 1), [1] * (amount - 1)
    while spare > 0:
        candidates = [i for i in range(amount - 1) if given[i] < bound]
        mass, left = sum([loads[i] for i in candidates]), spare
        for i in candidates:
            addition = min(bound - given[i], max(1, left * loads[i] // mass), spare)
            given[i] = given[i] + addition
            spare = spare - addition
    return np.array([bound] + given)


def ragged(stream_key, amount, total, limit, skew):
    if amount == 2:
        one = jax.random.randint(stream_key, (), max(1, total - limit), min(limit, total - 1) + 1)
        return jnp.stack([one, total - one])
    tallies = jnp.asarray(length_profile(amount, total, limit, skew), jnp.int32)
    pairs = (amount - 1) // 2
    source_of, taker = tallies[1:1 + 2 * pairs:2], tallies[2:2 + 2 * pairs:2]
    margin = jnp.minimum(source_of - 1, limit - taker)
    passed = jax.random.randint(jax.random.fold_in(stream_key, 1), (pairs,), 0, 1 << 20) % (margin + 1)
    tallies = tallies.at[1:1 + 2 * pairs:2].set(source_of - passed).at[2:2 + 2 * pairs:2].set(taker + passed)
    return tallies[jax.random.permutation(jax.random.fold_in(stream_key, 2), amount)]


def bell_draw(rng, dims, scale, limit, split=(), kind=jnp.bfloat16):
    drawn = scale * jax.random.normal(rng, dims, jnp.float32)
    if split:
        drawn = drawn * shard_levels(rng, dims, split, -0.22, 0.18)
    return jnp.clip(drawn, -limit, limit).astype(kind)


def setup_inputs(seed: int = 0) -> dict:
    seeds = jax.random.split(jax.random.key(seed), 10)
    return {
        "byte_states": bell_draw(seeds[0], (ROWS, ROW_BYTES, D), 1.0, 6.0, ((0, 16),)),
        "patch_lengths": jax.vmap(lambda own: ragged(own, PATCHES, ROW_BYTES, 8, 1))(jax.random.split(seeds[1], ROWS)).reshape((ROWS, PATCHES)).astype(jnp.int32),
        "patch_docs": jax.vmap(lambda own: jnp.searchsorted(jnp.cumsum(ragged(own, DOCS, PATCHES, PATCHES // 4, 1)), jnp.arange(PATCHES), side="right"))(jax.random.split(seeds[2], ROWS)).reshape((ROWS, PATCHES)).astype(jnp.int32),
        "attn_qkv": bell_draw(seeds[3], (2, 3, D, D), D ** -0.5, 0.1875, ((0, 2), (2, 4))),
        "attn_out": bell_draw(seeds[4], (2, D, D), (D // 16) ** -0.5, 0.75, ((0, 2), (1, 4))),
        "norm_gains": jnp.clip(1.0 + 0.15 * jax.random.normal(seeds[5], (2, 2, D), jnp.float32), 0.25, 1.75),
        "ffn_in": bell_draw(seeds[6], (D, 2 * FF), D ** -0.5, 0.1875, ((0, 8),)),
        "ffn_down": bell_draw(seeds[7], (FF, D), FF ** -0.5, 0.109375, ((0, 8),)),
        "cotangent": bell_draw(seeds[8], (ROWS, PATCHES, D), 1.0, 6.0, ((0, 16),)),
    }


@jax.custom_vjp
def low(v):
    return lax.optimization_barrier(v.astype(jnp.bfloat16)).astype(jnp.float32)

@jax.custom_vjp
def low_back(v):
    return v

def low_keep(v):
    return (low(v), None)

def low_pass(kept, grad):
    return (grad,)

def back_keep(v):
    return (v, None)

def back_low(kept, grad):
    return (low(grad),)
low.defvjp(low_keep, low_pass)
low_back.defvjp(back_keep, back_low)
EPS = 1e-05
HIGHEST = lax.Precision.HIGHEST

def product(left, right):
    return jnp.dot(left, right, precision=HIGHEST)

def rms_rows(values, gain_row):
    return values * lax.rsqrt(lax.optimization_barrier(jnp.mean(values * values, axis=-1, keepdims=True)) + EPS) * gain_row

def attention(queries, key_rows, value_rows, allowed, out_weight):
    rows_query = queries.shape[0]
    rows_key = key_rows.shape[0]
    query_heads = queries.reshape(rows_query, HEADS, HEAD_DIM)
    key_heads = key_rows.reshape(rows_key, HEADS, HEAD_DIM)
    value_heads = value_rows.reshape(rows_key, HEADS, HEAD_DIM)
    scores = low_back(jnp.einsum('qhd,khd->hqk', query_heads, key_heads, precision=HIGHEST) * HEAD_DIM ** (-0.5))
    scores = jnp.where(allowed[None], scores, -1e+30)
    probabilities = low(jax.nn.softmax(scores, axis=-1))
    context = jnp.einsum('hqk,khd->qhd', probabilities, value_heads, precision=HIGHEST).reshape(rows_query, D)
    context = low_back(low(context))
    return low_back(product(context, out_weight))

def row_tables(lengths, doc_ids):
    patch_ends = jnp.cumsum(lengths).astype(jnp.int32)
    positions = jnp.arange(ROW_BYTES, dtype=jnp.int32)
    patch_ids = jnp.arange(PATCHES, dtype=jnp.int32)
    owning_patch = lax.optimization_barrier(jnp.sum((patch_ends[None, :] <= positions[:, None]).astype(jnp.int32), axis=1)).astype(jnp.int32)
    byte_docs = doc_ids[owning_patch]
    cross_mask = (byte_docs[None, :] == doc_ids[:, None]) & (positions[None, :] < patch_ends[:, None])
    causal_mask = (doc_ids[None, :] == doc_ids[:, None]) & (patch_ids[None, :] <= patch_ids[:, None])
    member = (owning_patch[None, :] == patch_ids[:, None]).astype(jnp.float32)
    return (member, cross_mask, causal_mask)

def layer_one(byte_row, lengths, member, cross_mask, qkv_weight, out_weight, gain_rows):
    pooled = product(member, byte_row) / lengths.astype(jnp.float32)[:, None]
    query_in = low(rms_rows(pooled, gain_rows[0, 0]))
    key_in = low(rms_rows(byte_row, gain_rows[0, 1]))
    queries = low_back(low(product(query_in, qkv_weight[0, 0])))
    key_rows = low_back(low(product(key_in, qkv_weight[0, 1])))
    value_rows = low_back(low(product(key_in, qkv_weight[0, 2])))
    carried = pooled + attention(queries, key_rows, value_rows, cross_mask, out_weight[0])
    return low_back(low(carried))

def layer_two(carried, causal_mask, qkv_weight, out_weight, gain_rows, in_weight, down_weight):
    normed = low(rms_rows(carried, gain_rows[1, 0]))
    queries = low_back(low(product(normed, qkv_weight[1, 0])))
    key_rows = low_back(low(product(normed, qkv_weight[1, 1])))
    value_rows = low_back(low(product(normed, qkv_weight[1, 2])))
    residual = carried + attention(queries, key_rows, value_rows, causal_mask, out_weight[1])
    mix_in = low(rms_rows(residual, gain_rows[1, 1]))
    gate_up = low_back(product(mix_in, in_weight))
    hidden = low(jax.nn.silu(gate_up[:, :FF]) * gate_up[:, FF:])
    return residual + low_back(product(hidden, down_weight))

def reference(byte_states, patch_lengths, patch_docs, attn_qkv, attn_out, norm_gains, ffn_in, ffn_down, cotangent):
    weights = (attn_qkv.astype(jnp.float32), attn_out.astype(jnp.float32), norm_gains, ffn_in.astype(jnp.float32), ffn_down.astype(jnp.float32))

    def one_row(totals, inputs):
        byte_row, lengths, doc_ids, cot_row = inputs
        member, cross_mask, causal_mask = row_tables(lengths, doc_ids)

        def forward(params, byte_wide):
            qkv_weight, out_weight, gain_rows, in_weight, down_weight = params
            carried = layer_one(byte_wide, lengths, member, cross_mask, qkv_weight, out_weight, gain_rows)
            return layer_two(carried, causal_mask, qkv_weight, out_weight, gain_rows, in_weight, down_weight)
        latent, pullback = jax.vjp(forward, weights, byte_row.astype(jnp.float32))
        gradients, byte_grad = pullback(cot_row.astype(jnp.float32))
        totals = jax.tree.map(lambda left, right: left + right, totals, gradients)
        return (totals, (latent.astype(jnp.bfloat16), byte_grad.astype(jnp.bfloat16)))
    initial = jax.tree.map(jnp.zeros_like, weights)
    totals, (latents, byte_grads) = lax.scan(one_row, initial, (byte_states, patch_lengths, patch_docs, cotangent))
    return (latents, byte_grads, totals[0], totals[1], totals[2], totals[3], totals[4])
```

```python
import functools

import jax
import jax.numpy as jnp
from jax import lax
from jax.experimental import pallas as pl
from jax.experimental.pallas import tpu as pltpu
from jax.sharding import PartitionSpec as P

D = 1024
HEADS = 16
HEAD_DIM = 64
PAIRS = HEADS // 2
FF = 2816
ROW_BYTES = 1024
PATCHES = 256
QT = 128
TILES = PATCHES // QT

EPS = 1e-05
SCALE = HEAD_DIM ** (-0.5)
EXCLUDED = -1e30

BF = jnp.bfloat16
F32 = jnp.float32


def nn(left, right):
    return jnp.dot(left, right, preferred_element_type=F32)


def tn(left, right):
    return lax.dot_general(left, right, (((0,), (0,)), ((), ())), preferred_element_type=F32)


def nt(left, right):
    return lax.dot_general(left, right, (((1,), (1,)), ((), ())), preferred_element_type=F32)


def two_heads(block):
    lane = lax.broadcasted_iota(jnp.int32, block.shape, 1)
    zero = jnp.zeros_like(block)
    first = lane < HEAD_DIM
    return jnp.concatenate([jnp.where(first, block, zero), jnp.where(first, zero, block)], axis=0)


def own_lanes(both):
    picked = jnp.concatenate([both[:HEAD_DIM, :QT], both[HEAD_DIM:, QT:]], axis=0)
    return picked.T


def twice(row):
    return jnp.concatenate([row, row], axis=1)


def attend_kernel(chunk, first_ref, stop_ref, lo_ref, hi_ref, q_ref, k_ref, v_ref, c_ref, l_ref, s_ref):
    row = pl.program_id(0)
    for tile in range(TILES):
        own = pl.ds(tile * QT, QT)
        queries = two_heads(q_ref[own, :].astype(F32) * SCALE).astype(BF)
        lo = twice(lo_ref[0, :, own])
        hi = twice(hi_ref[0, :, own])
        first = first_ref[row, tile]
        stop = stop_ref[row, tile]

        def scores(j, top):
            start = pl.multiple_of(j * chunk, chunk)
            part = nt(k_ref[pl.ds(start, chunk), :], queries)
            at = lax.broadcasted_iota(jnp.int32, part.shape, 0) + start
            part = jnp.where((at >= lo) & (at < hi), part, EXCLUDED)
            s_ref[pl.ds(start, chunk), :] = part
            return jnp.maximum(top, jnp.max(part, axis=0, keepdims=True))

        top = lax.fori_loop(first, stop, scores, jnp.full((1, 2 * QT), EXCLUDED, F32))

        def context(j, carry):
            total, acc = carry
            start = pl.multiple_of(j * chunk, chunk)
            weight = jnp.exp(s_ref[pl.ds(start, chunk), :] - top)
            total = total + jnp.sum(weight, axis=0, keepdims=True)
            acc = acc + tn(v_ref[pl.ds(start, chunk), :], weight.astype(BF))
            return (total, acc)

        total, acc = lax.fori_loop(
            first, stop, context, (jnp.zeros((1, 2 * QT), F32), jnp.zeros((2 * HEAD_DIM, 2 * QT), F32))
        )
        c_ref[own, :] = own_lanes(acc / total).astype(BF)
        l_ref[0, 0, tile : tile + 1, :] = top + jnp.log(total)


def attend_back_kernel(
    chunk, first_ref, stop_ref, lo_ref, hi_ref, q_ref, k_ref, v_ref, l_ref, c_ref, dc_ref,
    dq_ref, dk_ref, dv_ref, dk_acc, dv_acc,
):
    row = pl.program_id(0)
    dk_acc[...] = jnp.zeros_like(dk_acc)
    dv_acc[...] = jnp.zeros_like(dv_acc)
    for tile in range(TILES):
        own = pl.ds(tile * QT, QT)
        queries = two_heads(q_ref[own, :].astype(F32) * SCALE).astype(BF)
        grads = dc_ref[own, :].astype(F32)
        inner = (grads * c_ref[own, :].astype(F32)).T
        delta = jnp.concatenate(
            [
                jnp.sum(inner[:HEAD_DIM], axis=0, keepdims=True),
                jnp.sum(inner[HEAD_DIM:], axis=0, keepdims=True),
            ],
            axis=1,
        )
        grads = two_heads(grads).astype(BF)
        lo = twice(lo_ref[0, :, own])
        hi = twice(hi_ref[0, :, own])
        logsum = l_ref[0, 0, tile : tile + 1, :]

        def step(j, acc):
            start = pl.multiple_of(j * chunk, chunk)
            here = pl.ds(start, chunk)
            keys = k_ref[here, :]
            part = nt(keys, queries)
            at = lax.broadcasted_iota(jnp.int32, part.shape, 0) + start
            part = jnp.where((at >= lo) & (at < hi), part, EXCLUDED)
            prob = jnp.exp(part - logsum)
            slope = prob * (nt(v_ref[here, :], grads) - delta)
            slope = slope.astype(BF)
            dv_acc[here, :] += nn(prob.astype(BF), grads)
            dk_acc[here, :] += nn(slope, queries)
            return acc + tn(keys, slope)

        acc = lax.fori_loop(
            first_ref[row, tile], stop_ref[row, tile], step, jnp.zeros((2 * HEAD_DIM, 2 * QT), F32)
        )
        dq_ref[own, :] = (own_lanes(acc) * SCALE).astype(BF)
    dk_ref[...] = dk_acc[...].astype(BF)
    dv_ref[...] = dv_acc[...].astype(BF)


def attention_specs(keys):
    per_query = pl.BlockSpec((PATCHES, 2 * HEAD_DIM), lambda r, h, *_: (r, h))
    per_key = pl.BlockSpec((keys, 2 * HEAD_DIM), lambda r, h, *_: (r, h))
    bound = pl.BlockSpec((1, 1, PATCHES), lambda r, h, *_: (r, 0, 0))
    logs = pl.BlockSpec((1, 1, TILES, 2 * QT), lambda r, h, *_: (r, h, 0, 0))
    return per_query, per_key, bound, logs


def attend(bounds, q, k, v):
    first, stop, lo, hi, chunk = bounds
    rows = lo.shape[0]
    keys = k.shape[0] // rows
    per_query, per_key, bound, logs = attention_specs(keys)
    return pl.pallas_call(
        functools.partial(attend_kernel, chunk),
        grid_spec=pltpu.PrefetchScalarGridSpec(
            num_scalar_prefetch=2,
            grid=(rows, PAIRS),
            in_specs=[bound, bound, per_query, per_key, per_key],
            out_specs=[per_query, logs],
            scratch_shapes=[pltpu.VMEM((keys, 2 * QT), F32)],
        ),
        out_shape=[
            jax.ShapeDtypeStruct(q.shape, BF),
            jax.ShapeDtypeStruct((rows, PAIRS, TILES, 2 * QT), F32),
        ],
        compiler_params=pltpu.CompilerParams(vmem_limit_bytes=32 << 20),
        name="attend",
    )(first, stop, lo, hi, q, k, v)


def attend_back(bounds, q, k, v, logsum, context, grads):
    first, stop, lo, hi, chunk = bounds
    rows = lo.shape[0]
    keys = k.shape[0] // rows
    per_query, per_key, bound, logs = attention_specs(keys)
    return pl.pallas_call(
        functools.partial(attend_back_kernel, chunk),
        grid_spec=pltpu.PrefetchScalarGridSpec(
            num_scalar_prefetch=2,
            grid=(rows, PAIRS),
            in_specs=[bound, bound, per_query, per_key, per_key, logs, per_query, per_query],
            out_specs=[per_query, per_key, per_key],
            scratch_shapes=[pltpu.VMEM((keys, 2 * HEAD_DIM), F32)] * 2,
        ),
        out_shape=[
            jax.ShapeDtypeStruct(q.shape, BF),
            jax.ShapeDtypeStruct(k.shape, BF),
            jax.ShapeDtypeStruct(k.shape, BF),
        ],
        compiler_params=pltpu.CompilerParams(vmem_limit_bytes=32 << 20),
        name="attend_back",
    )(first, stop, lo, hi, q, k, v, logsum, context, grads)


def scale_of(values):
    return lax.rsqrt(jnp.mean(values * values, axis=-1, keepdims=True) + EPS)


def norm_backward(values, row_scale, gain_row, incoming):
    weighted = incoming * gain_row
    projection = jnp.mean(weighted * values, axis=-1, keepdims=True)
    grad_values = row_scale * weighted - values * (row_scale * row_scale * row_scale) * projection
    grad_gain = jnp.sum(incoming * values * row_scale, axis=0)
    return grad_values, grad_gain


def chunk_bounds(lo, hi, chunk):
    first = lo[:, ::QT] // chunk
    stop = (hi[:, QT - 1 :: QT] + chunk - 1) // chunk
    return first, stop, lo[:, None, :], hi[:, None, :], chunk


def shards(
    byte_states, patch_lengths, patch_docs, attn_qkv, attn_out, norm_gains, ffn_in, ffn_down, cotangent
):
    section = lax.axis_index("section")
    group = lax.axis_index("group")
    sections = lax.axis_size("section")
    groups = lax.axis_size("group")
    everyone = ("section", "dp", "group")

    def share(shard):
        rows = shard.shape[0] // groups
        return lax.dynamic_slice_in_dim(shard, group * rows, rows, 0)

    def whole(shard):
        return lax.all_gather(share(shard), everyone, axis=0, tiled=True)

    wq, wk, wv, wo = [
        whole(shard) for shard in (attn_qkv[0, 0], attn_qkv[0, 1], attn_qkv[0, 2], attn_out[0])
    ]
    w_in, w_down = whole(ffn_in), whole(ffn_down)
    gains = lax.all_gather(norm_gains, "section", axis=0, tiled=True)

    rows = byte_states.shape[0] // sections
    mine = lambda a: lax.dynamic_slice_in_dim(a, section * rows, rows, 0)
    states, lengths, docs, cot = [mine(a) for a in (byte_states, patch_lengths, patch_docs, cotangent)]
    cot = cot.reshape(rows * PATCHES, D)

    ends = jnp.cumsum(lengths, axis=1)
    earlier = docs[:, None, :] < docs[:, :, None]
    doc_start = jnp.sum(jnp.where(earlier, lengths[:, None, :], 0), axis=2)
    doc_first = jnp.sum(earlier.astype(jnp.int32), axis=2)
    cross = chunk_bounds(doc_start, ends, 256)
    ids = jnp.broadcast_to(lax.iota(jnp.int32, PATCHES) + 1, doc_first.shape)
    causal = chunk_bounds(doc_first, ids, 128)
    positions = lax.iota(jnp.int32, ROW_BYTES)
    member = (positions < ends[:, :, None]) & (positions >= (ends - lengths)[:, :, None])
    member = member.astype(BF)
    count = lengths.astype(F32).reshape(rows * PATCHES, 1)

    pooled = jnp.einsum("rpb,rbd->rpd", member, states, preferred_element_type=F32)
    pooled = pooled.reshape(rows * PATCHES, D) / count
    wide = states.reshape(rows * ROW_BYTES, D).astype(F32)
    query_scale, key_scale = scale_of(pooled), scale_of(wide)
    query_in = (pooled * query_scale * gains[0, 0]).astype(BF)
    key_in = (wide * key_scale * gains[0, 1]).astype(BF)
    q1 = nn(query_in, wq[:D]).astype(BF)
    k1 = nn(key_in, wk[:D]).astype(BF)
    v1 = nn(key_in, wv[:D]).astype(BF)
    c1, l1 = attend(cross, q1, k1, v1)
    carried = (pooled + nn(c1, wo[:D])).astype(BF)

    carried_wide = carried.astype(F32)
    first_scale = scale_of(carried_wide)
    normed_in = (carried_wide * first_scale * gains[1, 0]).astype(BF)
    q2 = nn(normed_in, wq[D:]).astype(BF)
    k2 = nn(normed_in, wk[D:]).astype(BF)
    v2 = nn(normed_in, wv[D:]).astype(BF)
    c2, l2 = attend(causal, q2, k2, v2)
    residual = carried_wide + nn(c2, wo[D:])
    second_scale = scale_of(residual)
    mix_in = (residual * second_scale * gains[1, 1]).astype(BF)
    gate_up = nn(mix_in, w_in)
    gate, up = gate_up[:, :FF], gate_up[:, FF:]
    sig = jax.nn.sigmoid(gate)
    hidden = (gate * sig * up).astype(BF)
    latents = (residual + nn(hidden, w_down)).astype(BF)

    grad_down = tn(hidden, cot).astype(BF)
    grad_hidden = nt(cot, w_down)
    grad_gate = grad_hidden * up * sig * (1.0 + gate * (1.0 - sig))
    grad_up = grad_hidden * gate * sig
    dgu = jnp.concatenate([grad_gate, grad_up], axis=1).astype(BF)
    grad_in = tn(mix_in, dgu).astype(BF)

    def summed(grad, axes):
        return lax.psum_scatter(grad, axes, scatter_dimension=0, tiled=True)

    sum_down = summed(grad_down, everyone)
    sum_in = summed(grad_in, everyone)

    grad_mix, gain_mix = norm_backward(residual, second_scale, gains[1, 1], nt(dgu, w_in))
    grad_residual = grad_mix + cot.astype(F32)
    branch = grad_residual.astype(BF)

    dc2 = nt(branch, wo[D:]).astype(BF)
    dq2, dk2, dv2 = attend_back(causal, q2, k2, v2, l2, c2, dc2)
    grads_two = [tn(normed_in, dq2), tn(normed_in, dk2), tn(normed_in, dv2), tn(c2, branch)]
    grad_normed = nt(dq2, wq[D:]) + nt(dk2, wk[D:]) + nt(dv2, wv[D:])
    grad_carried, gain_normed = norm_backward(carried_wide, first_scale, gains[1, 0], grad_normed)
    d_carried = (grad_residual + grad_carried).astype(BF)
    spread = ("dp", "group", "section")
    sums_two = [summed(g.astype(BF), spread) for g in grads_two]

    dc1 = nt(d_carried, wo[:D]).astype(BF)
    dq1, dk1, dv1 = attend_back(cross, q1, k1, v1, l1, c1, dc1)
    grads_one = [tn(query_in, dq1), tn(key_in, dk1), tn(key_in, dv1), tn(c1, d_carried)]
    sums_one = [summed(g.astype(BF), spread) for g in grads_one]
    grad_pooled, gain_query = norm_backward(pooled, query_scale, gains[0, 0], nt(dq1, wq[:D]))
    grad_wide, gain_key = norm_backward(
        wide, key_scale, gains[0, 1], nt(dk1, wk[:D]) + nt(dv1, wv[:D])
    )
    per_patch = (grad_pooled + d_carried.astype(F32)) / count
    spread_back = jnp.einsum(
        "rpb,rpd->rbd", member, per_patch.astype(BF).reshape(rows, PATCHES, D), preferred_element_type=F32
    )
    byte_grads = (grad_wide + spread_back.reshape(rows * ROW_BYTES, D)).astype(BF)

    half = D // sections
    swap = [(0, 1), (1, 0)]

    def halves(values, length):
        values = values.reshape(rows, length, D)
        other = lax.dynamic_slice_in_dim(values, (1 - section) * half, half, 2)
        own = lax.dynamic_slice_in_dim(values, section * half, half, 2)
        got = lax.ppermute(other, "section", swap)
        return jnp.where(
            section == 0, jnp.concatenate([own, got], axis=0), jnp.concatenate([got, own], axis=0)
        )

    latents_out = halves(latents, PATCHES)
    bytes_out = halves(byte_grads, ROW_BYTES)

    def to_group(part):
        return lax.all_gather(part, "group", axis=0, tiled=True)

    ffn_gin, ffn_gdown = to_group(sum_in).astype(F32), to_group(sum_down).astype(F32)
    ones, twos = jnp.stack(sums_one), jnp.stack(sums_two)
    kept = jnp.where(section == 0, ones, twos)
    sent = jnp.where(section == 0, twos, ones)
    got = lax.ppermute(sent, "section", swap)
    pieces = jnp.where(section == 0, jnp.stack([kept, got], axis=1), jnp.stack([got, kept], axis=1))
    quarter = pieces.reshape(4, -1, D)
    attn = lax.all_gather(quarter, "group", axis=1, tiled=True).astype(F32)
    gain_grads = jnp.stack([gain_query, gain_key, gain_normed, gain_mix])
    gain_grads = lax.psum(gain_grads, everyone).reshape(2, 2, D)
    gain_grads = lax.dynamic_slice_in_dim(gain_grads, section, 1, 0)
    width = D // lax.axis_size("dp")
    gain_out = lax.dynamic_slice_in_dim(gain_grads, lax.axis_index("dp") * width, width, 2)
    return (latents_out, bytes_out, attn[None, :3], attn[3][None], gain_out, ffn_gin, ffn_gdown)


def solution(mesh):
    in_specs = (
        P(("group", "dp"), None, None),
        P(("group", "dp"), None),
        P(("group", "dp"), None),
        P("section", None, "dp", None),
        P("section", "dp", None),
        P("section", None, None),
        P(("section", "dp"), None),
        P(("section", "dp"), None),
        P(("group", "dp"), None, None),
    )
    out_specs = (
        P(("group", "dp"), None, "section"),
        P(("group", "dp"), None, "section"),
        P("section", None, "dp", None),
        P("section", "dp", None),
        P("section", None, "dp"),
        P(("section", "dp"), None),
        P(("section", "dp"), None),
    )
    return jax.shard_map(shards, mesh=mesh, in_specs=in_specs, out_specs=out_specs, check_vma=False)
```

```python
import functools

import jax
import jax.numpy as jnp
from jax import lax
from jax.experimental import pallas as pl
from jax.experimental.pallas import tpu as pltpu
from jax.sharding import PartitionSpec as P

D = 1024
HEADS = 16
HEAD_DIM = 64
PAIRS = HEADS // 2
FF = 2816
ROW_BYTES = 1024
PATCHES = 256
QT = 128
TILES = PATCHES // QT

EPS = 1e-05
SCALE = HEAD_DIM ** (-0.5)
EXCLUDED = -1e30

BF = jnp.bfloat16
F32 = jnp.float32


def nn(left, right):
    return jnp.dot(left, right, preferred_element_type=F32)


def tn(left, right):
    return lax.dot_general(left, right, (((0,), (0,)), ((), ())), preferred_element_type=F32)


def nt(left, right):
    return lax.dot_general(left, right, (((1,), (1,)), ((), ())), preferred_element_type=F32)


def two_heads(block):
    lane = lax.broadcasted_iota(jnp.int32, block.shape, 1)
    zero = jnp.zeros_like(block)
    first = lane < HEAD_DIM
    return jnp.concatenate([jnp.where(first, block, zero), jnp.where(first, zero, block)], axis=0)


def own_lanes(both):
    picked = jnp.concatenate([both[:HEAD_DIM, :QT], both[HEAD_DIM:, QT:]], axis=0)
    return picked.T


def twice(row):
    return jnp.concatenate([row, row], axis=1)


def attend_kernel(chunk, first_ref, stop_ref, lo_ref, hi_ref, q_ref, k_ref, v_ref, c_ref, l_ref, s_ref):
    row = pl.program_id(0)
    for tile in range(TILES):
        own = pl.ds(tile * QT, QT)
        queries = two_heads(q_ref[own, :].astype(F32) * SCALE).astype(BF)
        lo = twice(lo_ref[0, :, own])
        hi = twice(hi_ref[0, :, own])
        first = first_ref[row, tile]
        stop = stop_ref[row, tile]

        def scores(j, top):
            start = pl.multiple_of(j * chunk, chunk)
            part = nt(k_ref[pl.ds(start, chunk), :], queries)
            at = lax.broadcasted_iota(jnp.int32, part.shape, 0) + start
            part = jnp.where((at >= lo) & (at < hi), part, EXCLUDED)
            s_ref[pl.ds(start, chunk), :] = part
            return jnp.maximum(top, jnp.max(part, axis=0, keepdims=True))

        top = lax.fori_loop(first, stop, scores, jnp.full((1, 2 * QT), EXCLUDED, F32))

        def context(j, carry):
            total, acc = carry
            start = pl.multiple_of(j * chunk, chunk)
            weight = jnp.exp(s_ref[pl.ds(start, chunk), :] - top)
            total = total + jnp.sum(weight, axis=0, keepdims=True)
            acc = acc + tn(v_ref[pl.ds(start, chunk), :], weight.astype(BF))
            return (total, acc)

        total, acc = lax.fori_loop(
            first, stop, context, (jnp.zeros((1, 2 * QT), F32), jnp.zeros((2 * HEAD_DIM, 2 * QT), F32))
        )
        c_ref[own, :] = own_lanes(acc / total).astype(BF)
        l_ref[0, 0, tile : tile + 1, :] = top + jnp.log(total)


def attend_back_kernel(
    chunk, first_ref, stop_ref, lo_ref, hi_ref, q_ref, k_ref, v_ref, l_ref, c_ref, dc_ref,
    dq_ref, dk_ref, dv_ref, dk_acc, dv_acc,
):
    row = pl.program_id(0)
    dk_acc[...] = jnp.zeros_like(dk_acc)
    dv_acc[...] = jnp.zeros_like(dv_acc)
    for tile in range(TILES):
        own = pl.ds(tile * QT, QT)
        queries = two_heads(q_ref[own, :].astype(F32) * SCALE).astype(BF)
        grads = dc_ref[own, :].astype(F32)
        inner = (grads * c_ref[own, :].astype(F32)).T
        delta = jnp.concatenate(
            [
                jnp.sum(inner[:HEAD_DIM], axis=0, keepdims=True),
                jnp.sum(inner[HEAD_DIM:], axis=0, keepdims=True),
            ],
            axis=1,
        )
        grads = two_heads(grads).astype(BF)
        lo = twice(lo_ref[0, :, own])
        hi = twice(hi_ref[0, :, own])
        logsum = l_ref[0, 0, tile : tile + 1, :]

        def step(j, acc):
            start = pl.multiple_of(j * chunk, chunk)
            here = pl.ds(start, chunk)
            keys = k_ref[here, :]
            part = nt(keys, queries)
            at = lax.broadcasted_iota(jnp.int32, part.shape, 0) + start
            part = jnp.where((at >= lo) & (at < hi), part, EXCLUDED)
            prob = jnp.exp(part - logsum)
            slope = prob * (nt(v_ref[here, :], grads) - delta)
            slope = slope.astype(BF)
            dv_acc[here, :] += nn(prob.astype(BF), grads)
            dk_acc[here, :] += nn(slope, queries)
            return acc + tn(keys, slope)

        acc = lax.fori_loop(
            first_ref[row, tile], stop_ref[row, tile], step, jnp.zeros((2 * HEAD_DIM, 2 * QT), F32)
        )
        dq_ref[own, :] = (own_lanes(acc) * SCALE).astype(BF)
    dk_ref[...] = dk_acc[...].astype(BF)
    dv_ref[...] = dv_acc[...].astype(BF)


def attention_specs(keys):
    per_query = pl.BlockSpec((PATCHES, 2 * HEAD_DIM), lambda r, h, *_: (r, h))
    per_key = pl.BlockSpec((keys, 2 * HEAD_DIM), lambda r, h, *_: (r, h))
    bound = pl.BlockSpec((1, 1, PATCHES), lambda r, h, *_: (r, 0, 0))
    logs = pl.BlockSpec((1, 1, TILES, 2 * QT), lambda r, h, *_: (r, h, 0, 0))
    return per_query, per_key, bound, logs


def attend(bounds, q, k, v):
    first, stop, lo, hi, chunk = bounds
    rows = lo.shape[0]
    keys = k.shape[0] // rows
    per_query, per_key, bound, logs = attention_specs(keys)
    return pl.pallas_call(
        functools.partial(attend_kernel, chunk),
        grid_spec=pltpu.PrefetchScalarGridSpec(
            num_scalar_prefetch=2,
            grid=(rows, PAIRS),
            in_specs=[bound, bound, per_query, per_key, per_key],
            out_specs=[per_query, logs],
            scratch_shapes=[pltpu.VMEM((keys, 2 * QT), F32)],
        ),
        out_shape=[
            jax.ShapeDtypeStruct(q.shape, BF),
            jax.ShapeDtypeStruct((rows, PAIRS, TILES, 2 * QT), F32),
        ],
        compiler_params=pltpu.CompilerParams(vmem_limit_bytes=32 << 20),
        name="attend",
    )(first, stop, lo, hi, q, k, v)


def attend_back(bounds, q, k, v, logsum, context, grads):
    first, stop, lo, hi, chunk = bounds
    rows = lo.shape[0]
    keys = k.shape[0] // rows
    per_query, per_key, bound, logs = attention_specs(keys)
    return pl.pallas_call(
        functools.partial(attend_back_kernel, chunk),
        grid_spec=pltpu.PrefetchScalarGridSpec(
            num_scalar_prefetch=2,
            grid=(rows, PAIRS),
            in_specs=[bound, bound, per_query, per_key, per_key, logs, per_query, per_query],
            out_specs=[per_query, per_key, per_key],
            scratch_shapes=[pltpu.VMEM((keys, 2 * HEAD_DIM), F32)] * 2,
        ),
        out_shape=[
            jax.ShapeDtypeStruct(q.shape, BF),
            jax.ShapeDtypeStruct(k.shape, BF),
            jax.ShapeDtypeStruct(k.shape, BF),
        ],
        compiler_params=pltpu.CompilerParams(vmem_limit_bytes=32 << 20),
        name="attend_back",
    )(first, stop, lo, hi, q, k, v, logsum, context, grads)


def scale_of(values):
    return lax.rsqrt(jnp.mean(values * values, axis=-1, keepdims=True) + EPS)


def norm_backward(values, row_scale, gain_row, incoming):
    weighted = incoming * gain_row
    projection = jnp.mean(weighted * values, axis=-1, keepdims=True)
    grad_values = row_scale * weighted - values * (row_scale * row_scale * row_scale) * projection
    grad_gain = jnp.sum(incoming * values * row_scale, axis=0)
    return grad_values, grad_gain


def chunk_bounds(lo, hi, chunk):
    first = lo[:, ::QT] // chunk
    stop = (hi[:, QT - 1 :: QT] + chunk - 1) // chunk
    return first, stop, lo[:, None, :], hi[:, None, :], chunk


def shards(
    byte_states, patch_lengths, patch_docs, attn_qkv, attn_out, norm_gains, ffn_in, ffn_down, cotangent
):
    section = lax.axis_index("section")
    group = lax.axis_index("group")
    sections = lax.axis_size("section")
    groups = lax.axis_size("group")
    core, side = group % 2, group // 2

    def whole(shard):
        rows = shard.shape[0] // groups
        part = lax.dynamic_slice_in_dim(shard, group * rows, rows, 0)
        return lax.all_gather(part, ("section", "dp", "group"), axis=0, tiled=True)

    four = jnp.concatenate([attn_qkv[0], attn_out], axis=0)
    matrix = lax.dynamic_index_in_dim(four, group, 0, keepdims=False)
    matrices = lax.all_gather(matrix, ("section", "group", "dp"), axis=0, tiled=True)
    matrices = matrices.reshape(sections, groups, D, D)
    wq, wk, wv, wo = [matrices[:, index] for index in range(4)]
    w_in, w_down = whole(ffn_in), whole(ffn_down)
    gains = lax.all_gather(norm_gains, "section", axis=0, tiled=True)

    rows = byte_states.shape[0] // sections
    mine = lambda a: lax.dynamic_slice_in_dim(a, section * rows, rows, 0)
    states, lengths, docs, cot = [mine(a) for a in (byte_states, patch_lengths, patch_docs, cotangent)]
    cot = cot.reshape(rows * PATCHES, D)

    ends = jnp.cumsum(lengths, axis=1)
    earlier = docs[:, None, :] < docs[:, :, None]
    doc_start = jnp.sum(jnp.where(earlier, lengths[:, None, :], 0), axis=2)
    doc_first = jnp.sum(earlier.astype(jnp.int32), axis=2)
    cross = chunk_bounds(doc_start, ends, 256)
    ids = jnp.broadcast_to(lax.iota(jnp.int32, PATCHES) + 1, doc_first.shape)
    causal = chunk_bounds(doc_first, ids, 128)
    positions = lax.iota(jnp.int32, ROW_BYTES)
    member = (positions < ends[:, :, None]) & (positions >= (ends - lengths)[:, :, None])
    member = member.astype(BF)
    count = lengths.astype(F32).reshape(rows * PATCHES, 1)

    pooled = jnp.einsum("rpb,rbd->rpd", member, states, preferred_element_type=F32)
    pooled = pooled.reshape(rows * PATCHES, D) / count
    wide = states.reshape(rows * ROW_BYTES, D).astype(F32)
    query_scale, key_scale = scale_of(pooled), scale_of(wide)
    query_in = (pooled * query_scale * gains[0, 0]).astype(BF)
    key_in = (wide * key_scale * gains[0, 1]).astype(BF)
    q1 = nn(query_in, wq[0]).astype(BF)
    k1 = nn(key_in, wk[0]).astype(BF)
    v1 = nn(key_in, wv[0]).astype(BF)
    c1, l1 = attend(cross, q1, k1, v1)
    carried = (pooled + nn(c1, wo[0])).astype(BF)

    carried_wide = carried.astype(F32)
    first_scale = scale_of(carried_wide)
    normed_in = (carried_wide * first_scale * gains[1, 0]).astype(BF)
    q2 = nn(normed_in, wq[1]).astype(BF)
    k2 = nn(normed_in, wk[1]).astype(BF)
    v2 = nn(normed_in, wv[1]).astype(BF)
    c2, l2 = attend(causal, q2, k2, v2)
    residual = carried_wide + nn(c2, wo[1])
    second_scale = scale_of(residual)
    mix_in = (residual * second_scale * gains[1, 1]).astype(BF)
    gate_up = nn(mix_in, w_in)
    gate, up = gate_up[:, :FF], gate_up[:, FF:]
    sig = jax.nn.sigmoid(gate)
    hidden = (gate * sig * up).astype(BF)
    latents = (residual + nn(hidden, w_down)).astype(BF)

    grad_hidden = nt(cot, w_down)
    grad_gate = grad_hidden * up * sig * (1.0 + gate * (1.0 - sig))
    grad_up = grad_hidden * gate * sig
    dgu = jnp.concatenate([grad_gate, grad_up], axis=1).astype(BF)

    def exchanged(values, axis, part, pairs, where):
        size = values.shape[where] // 2
        other = lax.dynamic_slice_in_dim(values, (1 - part) * size, size, where)
        own = lax.dynamic_slice_in_dim(values, part * size, size, where)
        return (own.astype(F32) + lax.ppermute(other, axis, pairs).astype(F32)).astype(BF)

    def over_section(values, where):
        return exchanged(values, "section", section, [(0, 1), (1, 0)], where)

    def over_side(values, where):
        return exchanged(values, "group", side, [(0, 2), (1, 3), (2, 0), (3, 1)], where)

    def chip_sum(half_of):
        got = lax.ppermute(half_of(1 - core).astype(BF), "group", [(0, 1), (1, 0), (2, 3), (3, 2)])
        return (half_of(core) + got.astype(F32)).astype(BF)

    def columns(values, part):
        size = values.shape[-1] // 2
        return lax.dynamic_slice_in_dim(values, part * size, size, values.ndim - 1)

    def line_sum(values, where):
        return lax.psum_scatter(values, "dp", scatter_dimension=where, tiled=True)

    sum_in = chip_sum(lambda part: tn(mix_in, columns(dgu, part)))
    sum_in = line_sum(over_side(over_section(sum_in, 0), 1), 0)
    sum_down = chip_sum(lambda part: tn(hidden, columns(cot, part)))
    sum_down = line_sum(over_section(over_side(sum_down, 1), 0), 0)

    grad_mix, gain_mix = norm_backward(residual, second_scale, gains[1, 1], nt(dgu, w_in))
    grad_residual = grad_mix + cot.astype(F32)
    branch = grad_residual.astype(BF)

    dc2 = nt(branch, wo[1]).astype(BF)
    dq2, dk2, dv2 = attend_back(causal, q2, k2, v2, l2, c2, dc2)

    def four_sums(pairs):
        def half_of(part):
            return jnp.stack([tn(left, columns(right, part)) for left, right in pairs])

        return chip_sum(half_of)

    sums_two = four_sums([(normed_in, dq2), (normed_in, dk2), (normed_in, dv2), (c2, branch)])
    sums_two = line_sum(over_section(over_side(sums_two, 2), 2), 1)
    grad_normed = nt(dq2, wq[1]) + nt(dk2, wk[1]) + nt(dv2, wv[1])
    grad_carried, gain_normed = norm_backward(carried_wide, first_scale, gains[1, 0], grad_normed)
    d_carried = (grad_residual + grad_carried).astype(BF)

    dc1 = nt(d_carried, wo[0]).astype(BF)
    dq1, dk1, dv1 = attend_back(cross, q1, k1, v1, l1, c1, dc1)
    sums_one = four_sums([(query_in, dq1), (key_in, dk1), (key_in, dv1), (c1, d_carried)])
    sums_one = line_sum(over_section(over_side(sums_one, 2), 2), 1)
    grad_pooled, gain_query = norm_backward(pooled, query_scale, gains[0, 0], nt(dq1, wq[0]))
    grad_wide, gain_key = norm_backward(
        wide, key_scale, gains[0, 1], nt(dk1, wk[0]) + nt(dv1, wv[0])
    )
    per_patch = (grad_pooled + d_carried.astype(F32)) / count
    spread_back = jnp.einsum(
        "rpb,rpd->rbd", member, per_patch.astype(BF).reshape(rows, PATCHES, D), preferred_element_type=F32
    )
    byte_grads = (grad_wide + spread_back.reshape(rows * ROW_BYTES, D)).astype(BF)

    half = D // sections
    swap = [(0, 1), (1, 0)]

    def halves(values, length):
        values = values.reshape(rows, length, D)
        other = lax.dynamic_slice_in_dim(values, (1 - section) * half, half, 2)
        own = lax.dynamic_slice_in_dim(values, section * half, half, 2)
        got = lax.ppermute(other, "section", swap)
        return jnp.where(
            section == 0, jnp.concatenate([own, got], axis=0), jnp.concatenate([got, own], axis=0)
        )

    latents_out = halves(latents, PATCHES)
    bytes_out = halves(byte_grads, ROW_BYTES)

    def to_group(part):
        every = lax.all_gather(part, "group", axis=0, tiled=False)
        every = every.reshape((2, 2) + part.shape)
        every = jnp.moveaxis(every, (1, 0), (-3, -2))
        return every.reshape(part.shape[:-1] + (-1,)).astype(F32)

    ffn_gin, ffn_gdown = to_group(sum_in), to_group(sum_down)
    kept = jnp.where(section == 0, sums_one, sums_two)
    sent = jnp.where(section == 0, sums_two, sums_one)
    got = lax.ppermute(sent, "section", swap)
    quarter = jnp.where(
        section == 0, jnp.concatenate([kept, got], axis=2), jnp.concatenate([got, kept], axis=2)
    )
    attn = to_group(quarter)
    gain_grads = jnp.stack([gain_query, gain_key, gain_normed, gain_mix])
    gain_grads = lax.psum(gain_grads, ("section", "group", "dp")).reshape(2, 2, D)
    gain_grads = lax.dynamic_slice_in_dim(gain_grads, section, 1, 0)
    width = D // lax.axis_size("dp")
    gain_out = lax.dynamic_slice_in_dim(gain_grads, lax.axis_index("dp") * width, width, 2)
    return (latents_out, bytes_out, attn[None, :3], attn[3][None], gain_out, ffn_gin, ffn_gdown)


def solution(mesh):
    in_specs = (
        P(("group", "dp"), None, None),
        P(("group", "dp"), None),
        P(("group", "dp"), None),
        P("section", None, "dp", None),
        P("section", "dp", None),
        P("section", None, None),
        P(("section", "dp"), None),
        P(("section", "dp"), None),
        P(("group", "dp"), None, None),
    )
    out_specs = (
        P(("group", "dp"), None, "section"),
        P(("group", "dp"), None, "section"),
        P("section", None, "dp", None),
        P("section", "dp", None),
        P("section", None, "dp"),
        P(("section", "dp"), None),
        P(("section", "dp"), None),
    )
    return jax.shard_map(shards, mesh=mesh, in_specs=in_specs, out_specs=out_specs, check_vma=False)
```

```python
import functools

import jax
import jax.numpy as jnp
from jax import lax
from jax.experimental import pallas as pl
from jax.experimental.pallas import tpu as pltpu
from jax.sharding import PartitionSpec as P

D = 1024
HEADS = 16
HEAD_DIM = 64
PAIRS = HEADS // 2
BLOCK = 512
FF = 2816
ROW_BYTES = 1024
PATCHES = 256
QT = 128
TILES = PATCHES // QT

EPS = 1e-05
SCALE = HEAD_DIM ** (-0.5)
EXCLUDED = -1e30

BF = jnp.bfloat16
F32 = jnp.float32


def nn(left, right):
    return jnp.dot(left, right, preferred_element_type=F32)


def tn(left, right):
    return lax.dot_general(left, right, (((0,), (0,)), ((), ())), preferred_element_type=F32)


def nt(left, right):
    return lax.dot_general(left, right, (((1,), (1,)), ((), ())), preferred_element_type=F32)


def two_heads(block):
    lane = lax.broadcasted_iota(jnp.int32, block.shape, 1)
    zero = jnp.zeros_like(block)
    first = lane < HEAD_DIM
    return jnp.concatenate([jnp.where(first, block, zero), jnp.where(first, zero, block)], axis=0)


def own_lanes(both):
    picked = jnp.concatenate([both[:HEAD_DIM, :QT], both[HEAD_DIM:, QT:]], axis=0)
    return picked.T


def twice(row):
    return jnp.concatenate([row, row], axis=1)


def attend_kernel(chunk, first_ref, stop_ref, lo_ref, hi_ref, q_ref, k_ref, v_ref, c_ref, l_ref, s_ref):
    row = pl.program_id(0)
    for tile in range(TILES):
        own = pl.ds(tile * QT, QT)
        queries = two_heads(q_ref[own, :].astype(F32) * SCALE).astype(BF)
        lo = twice(lo_ref[0, :, own])
        hi = twice(hi_ref[0, :, own])
        first = first_ref[row, tile]
        stop = stop_ref[row, tile]

        def scores(j, top):
            start = pl.multiple_of(j * chunk, chunk)
            part = nt(k_ref[pl.ds(start, chunk), :], queries)
            at = lax.broadcasted_iota(jnp.int32, part.shape, 0) + start
            part = jnp.where((at >= lo) & (at < hi), part, EXCLUDED)
            s_ref[pl.ds(start, chunk), :] = part
            return jnp.maximum(top, jnp.max(part, axis=0, keepdims=True))

        top = lax.fori_loop(first, stop, scores, jnp.full((1, 2 * QT), EXCLUDED, F32))

        def context(j, carry):
            total, acc = carry
            start = pl.multiple_of(j * chunk, chunk)
            weight = jnp.exp(s_ref[pl.ds(start, chunk), :] - top)
            total = total + jnp.sum(weight, axis=0, keepdims=True)
            acc = acc + tn(v_ref[pl.ds(start, chunk), :], weight.astype(BF))
            return (total, acc)

        total, acc = lax.fori_loop(
            first, stop, context, (jnp.zeros((1, 2 * QT), F32), jnp.zeros((2 * HEAD_DIM, 2 * QT), F32))
        )
        c_ref[own, :] = own_lanes(acc / total).astype(BF)
        l_ref[0, 0, tile : tile + 1, :] = top + jnp.log(total)


def attend_back_kernel(
    chunk, first_ref, stop_ref, lo_ref, hi_ref, q_ref, k_ref, v_ref, l_ref, c_ref, dc_ref,
    dq_ref, dk_ref, dv_ref, dk_acc, dv_acc,
):
    row = pl.program_id(0)
    dk_acc[...] = jnp.zeros_like(dk_acc)
    dv_acc[...] = jnp.zeros_like(dv_acc)
    for tile in range(TILES):
        own = pl.ds(tile * QT, QT)
        queries = two_heads(q_ref[own, :].astype(F32) * SCALE).astype(BF)
        grads = dc_ref[own, :].astype(F32)
        inner = (grads * c_ref[own, :].astype(F32)).T
        delta = jnp.concatenate(
            [
                jnp.sum(inner[:HEAD_DIM], axis=0, keepdims=True),
                jnp.sum(inner[HEAD_DIM:], axis=0, keepdims=True),
            ],
            axis=1,
        )
        grads = two_heads(grads).astype(BF)
        lo = twice(lo_ref[0, :, own])
        hi = twice(hi_ref[0, :, own])
        logsum = l_ref[0, 0, tile : tile + 1, :]

        def step(j, acc):
            start = pl.multiple_of(j * chunk, chunk)
            here = pl.ds(start, chunk)
            keys = k_ref[here, :]
            part = nt(keys, queries)
            at = lax.broadcasted_iota(jnp.int32, part.shape, 0) + start
            part = jnp.where((at >= lo) & (at < hi), part, EXCLUDED)
            prob = jnp.exp(part - logsum)
            slope = prob * (nt(v_ref[here, :], grads) - delta)
            slope = slope.astype(BF)
            dv_acc[here, :] += nn(prob.astype(BF), grads)
            dk_acc[here, :] += nn(slope, queries)
            return acc + tn(keys, slope)

        acc = lax.fori_loop(
            first_ref[row, tile], stop_ref[row, tile], step, jnp.zeros((2 * HEAD_DIM, 2 * QT), F32)
        )
        dq_ref[own, :] = (own_lanes(acc) * SCALE).astype(BF)
    dk_ref[...] = dk_acc[...].astype(BF)
    dv_ref[...] = dv_acc[...].astype(BF)


def attention_specs(keys):
    per_query = pl.BlockSpec((PATCHES, 2 * HEAD_DIM), lambda r, h, *_: (r, h))
    per_key = pl.BlockSpec((keys, 2 * HEAD_DIM), lambda r, h, *_: (r, h))
    bound = pl.BlockSpec((1, 1, PATCHES), lambda r, h, *_: (r, 0, 0))
    logs = pl.BlockSpec((1, 1, TILES, 2 * QT), lambda r, h, *_: (r, h, 0, 0))
    return per_query, per_key, bound, logs


def kernel_cost(q, k, products):
    scores = q.shape[0] * k.shape[0] // (q.shape[0] // PATCHES) * HEADS
    return pl.CostEstimate(
        flops=products * 2 * scores * 256, bytes_accessed=2 * q.nbytes + 4 * k.nbytes, transcendentals=scores
    )


def attend(bounds, q, k, v):
    first, stop, lo, hi, chunk = bounds
    rows = lo.shape[0]
    keys = k.shape[0] // rows
    per_query, per_key, bound, logs = attention_specs(keys)
    return pl.pallas_call(
        functools.partial(attend_kernel, chunk),
        grid_spec=pltpu.PrefetchScalarGridSpec(
            num_scalar_prefetch=2,
            grid=(rows, PAIRS),
            in_specs=[bound, bound, per_query, per_key, per_key],
            out_specs=[per_query, logs],
            scratch_shapes=[pltpu.VMEM((keys, 2 * QT), F32)],
        ),
        out_shape=[
            jax.ShapeDtypeStruct(q.shape, BF),
            jax.ShapeDtypeStruct((rows, PAIRS, TILES, 2 * QT), F32),
        ],
        compiler_params=pltpu.CompilerParams(vmem_limit_bytes=32 << 20),
        cost_estimate=kernel_cost(q, k, 2),
        name="attend",
    )(first, stop, lo, hi, q, k, v)


def attend_back(bounds, q, k, v, logsum, context, grads):
    first, stop, lo, hi, chunk = bounds
    rows = lo.shape[0]
    keys = k.shape[0] // rows
    per_query, per_key, bound, logs = attention_specs(keys)
    return pl.pallas_call(
        functools.partial(attend_back_kernel, chunk),
        grid_spec=pltpu.PrefetchScalarGridSpec(
            num_scalar_prefetch=2,
            grid=(rows, PAIRS),
            in_specs=[bound, bound, per_query, per_key, per_key, logs, per_query, per_query],
            out_specs=[per_query, per_key, per_key],
            scratch_shapes=[pltpu.VMEM((keys, 2 * HEAD_DIM), F32)] * 2,
        ),
        out_shape=[
            jax.ShapeDtypeStruct(q.shape, BF),
            jax.ShapeDtypeStruct(k.shape, BF),
            jax.ShapeDtypeStruct(k.shape, BF),
        ],
        compiler_params=pltpu.CompilerParams(vmem_limit_bytes=32 << 20),
        cost_estimate=kernel_cost(q, k, 5),
        name="attend_back",
    )(first, stop, lo, hi, q, k, v, logsum, context, grads)


def scale_of(values):
    return lax.rsqrt(jnp.mean(values * values, axis=-1, keepdims=True) + EPS)


def norm_backward(values, row_scale, gain_row, incoming):
    weighted = incoming * gain_row
    projection = jnp.mean(weighted * values, axis=-1, keepdims=True)
    grad_values = row_scale * weighted - values * (row_scale * row_scale * row_scale) * projection
    grad_gain = jnp.sum(incoming * values * row_scale, axis=0)
    return grad_values, grad_gain


def chunk_bounds(lo, hi, chunk):
    first = lo[:, ::QT] // chunk
    stop = (hi[:, QT - 1 :: QT] + chunk - 1) // chunk
    return first, stop, lo[:, None, :], hi[:, None, :], chunk


def shards(
    byte_states, patch_lengths, patch_docs, attn_qkv, attn_out, norm_gains, ffn_in, ffn_down, cotangent
):
    section = lax.axis_index("section")
    group = lax.axis_index("group")
    sections = lax.axis_size("section")
    groups = lax.axis_size("group")
    core, side = group % 2, group // 2

    four = jnp.concatenate([attn_qkv[0], attn_out], axis=0)
    matrix = lax.dynamic_index_in_dim(four, group, 0, keepdims=False)
    matrices = lax.all_gather(matrix, ("section", "group", "dp"), axis=0, tiled=True)
    matrices = matrices.reshape(sections, groups, D, D)
    wq, wk, wv, wo = [matrices[:, index] for index in range(4)]
    blocks = []
    for shard in (ffn_in, ffn_down):
        height = shard.shape[0] // groups
        part = lax.dynamic_slice_in_dim(shard, group * height, height, 0)
        blocks += [part[:, at : at + BLOCK] for at in range(0, part.shape[1], BLOCK)]
    ffn = lax.all_gather(jnp.concatenate(blocks, axis=0), ("section", "dp", "group"), axis=0, tiled=False)
    in_rows = ffn_in.size // groups // BLOCK
    w_in, w_down = [
        part.reshape(part.shape[0], width // BLOCK, -1, BLOCK).swapaxes(1, 2).reshape(-1, width)
        for part, width in ((ffn[:, :in_rows], 2 * FF), (ffn[:, in_rows:], D))
    ]
    gains = lax.all_gather(norm_gains, "section", axis=0, tiled=True)

    rows = byte_states.shape[0] // sections
    mine = lambda a: lax.dynamic_slice_in_dim(a, section * rows, rows, 0)
    states, lengths, docs, cot = [mine(a) for a in (byte_states, patch_lengths, patch_docs, cotangent)]
    cot = cot.reshape(rows * PATCHES, D)

    ends = jnp.cumsum(lengths, axis=1)
    earlier = docs[:, None, :] < docs[:, :, None]
    doc_start = jnp.sum(jnp.where(earlier, lengths[:, None, :], 0), axis=2)
    doc_first = jnp.sum(earlier.astype(jnp.int32), axis=2)
    cross = chunk_bounds(doc_start, ends, 256)
    ids = jnp.broadcast_to(lax.iota(jnp.int32, PATCHES) + 1, doc_first.shape)
    causal = chunk_bounds(doc_first, ids, 128)
    positions = lax.iota(jnp.int32, ROW_BYTES)
    member = (positions < ends[:, :, None]) & (positions >= (ends - lengths)[:, :, None])
    member = member.astype(BF)
    count = lengths.astype(F32).reshape(rows * PATCHES, 1)

    pooled = jnp.einsum("rpb,rbd->rpd", member, states, preferred_element_type=F32)
    pooled = pooled.reshape(rows * PATCHES, D) / count
    wide = states.reshape(rows * ROW_BYTES, D).astype(F32)
    query_scale, key_scale = scale_of(pooled), scale_of(wide)
    query_in = (pooled * query_scale * gains[0, 0]).astype(BF)
    key_in = (wide * key_scale * gains[0, 1]).astype(BF)
    q1 = nn(query_in, wq[0]).astype(BF)
    k1 = nn(key_in, wk[0]).astype(BF)
    v1 = nn(key_in, wv[0]).astype(BF)
    c1, l1 = attend(cross, q1, k1, v1)
    carried = (pooled + nn(c1, wo[0])).astype(BF)

    carried_wide = carried.astype(F32)
    first_scale = scale_of(carried_wide)
    normed_in = (carried_wide * first_scale * gains[1, 0]).astype(BF)
    q2 = nn(normed_in, wq[1]).astype(BF)
    k2 = nn(normed_in, wk[1]).astype(BF)
    v2 = nn(normed_in, wv[1]).astype(BF)
    c2, l2 = attend(causal, q2, k2, v2)
    residual = carried_wide + nn(c2, wo[1])
    second_scale = scale_of(residual)
    mix_in = (residual * second_scale * gains[1, 1]).astype(BF)
    gate_up = nn(mix_in, w_in)
    gate, up = gate_up[:, :FF], gate_up[:, FF:]
    sig = jax.nn.sigmoid(gate)
    hidden = (gate * sig * up).astype(BF)
    latents = (residual + nn(hidden, w_down)).astype(BF)

    grad_hidden = nt(cot, w_down)
    grad_gate = grad_hidden * up * sig * (1.0 + gate * (1.0 - sig))
    grad_up = grad_hidden * gate * sig
    dgu = jnp.concatenate([grad_gate, grad_up], axis=1).astype(BF)

    core_pairs = [(0, 1), (1, 0), (2, 3), (3, 2)]
    side_pairs = [(0, 2), (1, 3), (2, 0), (3, 1)]
    swap = [(0, 1), (1, 0)]

    def exchanged(values, axis, part, pairs, where):
        size = values.shape[where] // 2
        other = lax.dynamic_slice_in_dim(values, (1 - part) * size, size, where)
        own = lax.dynamic_slice_in_dim(values, part * size, size, where)
        return (own.astype(F32) + lax.ppermute(other, axis, pairs).astype(F32)).astype(BF)

    def over_section(values, where):
        return exchanged(values, "section", section, swap, where)

    def over_side(values, where):
        return exchanged(values, "group", side, side_pairs, where)

    def columns(values, part):
        size = values.shape[-1] // 2
        return lax.dynamic_slice_in_dim(values, part * size, size, values.ndim - 1)

    def line_sum(values, where):
        return lax.psum_scatter(values, "dp", scatter_dimension=where, tiled=True)

    def products(pairs, part):
        out = [tn(left, columns(right, part)) for left, right in pairs]
        return out[0] if len(out) == 1 else jnp.stack(out)

    def to_core(pairs):
        return products(pairs, 1 - core).astype(BF)

    def of_chip(pairs, sent):
        got = lax.ppermute(sent, "group", core_pairs)
        return (products(pairs, core) + got.astype(F32)).astype(BF)

    together = lax.optimization_barrier

    in_pairs, down_pairs = [(mix_in, dgu)], [(hidden, cot)]
    send_in, send_down = to_core(in_pairs), to_core(down_pairs)
    dgu_next, send_in, send_down = together((dgu, send_in, send_down))
    grad_mix, gain_mix = norm_backward(residual, second_scale, gains[1, 1], nt(dgu_next, w_in))
    grad_residual = grad_mix + cot.astype(F32)
    branch = grad_residual.astype(BF)
    dc2 = nt(branch, wo[1]).astype(BF)
    half_in, half_down = of_chip(in_pairs, send_in), of_chip(down_pairs, send_down)
    dc2, half_in, half_down = together((dc2, half_in, half_down))

    dq2, dk2, dv2 = attend_back(causal, q2, k2, v2, l2, c2, dc2)
    two_pairs = [(normed_in, dq2), (normed_in, dk2), (normed_in, dv2), (c2, branch)]
    send_two = to_core(two_pairs)
    dq2, dk2, dv2, send_two = together((dq2, dk2, dv2, send_two))
    grad_normed = nt(dq2, wq[1]) + nt(dk2, wk[1]) + nt(dv2, wv[1])
    grad_carried, gain_normed = norm_backward(carried_wide, first_scale, gains[1, 0], grad_normed)
    d_carried = (grad_residual + grad_carried).astype(BF)
    dc1 = nt(d_carried, wo[0]).astype(BF)
    half_in = over_section(half_in, 0)
    half_two = of_chip(two_pairs, send_two)
    dc1, half_in, half_two = together((dc1, half_in, half_two))
    sum_down = over_side(over_section(line_sum(half_down.reshape(sections, -1, D // 2), 1), 0), 2)
    sum_down = sum_down[0]

    dq1, dk1, dv1 = attend_back(cross, q1, k1, v1, l1, c1, dc1)
    half_in = over_side(half_in, 1)
    half_two = over_side(half_two, 2)
    one_pairs = [(query_in, dq1), (key_in, dk1)], [(key_in, dv1), (c1, d_carried)]
    send_one = [to_core(pairs) for pairs in one_pairs]
    dq1, dk1, dv1, send_one, half_in, half_two = together((dq1, dk1, dv1, send_one, half_in, half_two))
    sum_in = line_sum(half_in, 0)
    sum_two = line_sum(over_section(half_two, 2), 1)
    half_one = [of_chip(pairs, sent) for pairs, sent in zip(one_pairs, send_one)]
    dq1, dk1, dv1, half_one = together((dq1, dk1, dv1, half_one))
    half_one = jnp.concatenate(
        [over_side(over_section(half_one[0], 2), 2), over_section(over_side(half_one[1], 2), 2)], axis=0
    )
    sum_one = line_sum(half_one, 1)
    grad_pooled, gain_query = norm_backward(pooled, query_scale, gains[0, 0], nt(dq1, wq[0]))
    grad_wide, gain_key = norm_backward(
        wide, key_scale, gains[0, 1], nt(dk1, wk[0]) + nt(dv1, wv[0])
    )
    per_patch = (grad_pooled + d_carried.astype(F32)) / count
    spread_back = jnp.einsum(
        "rpb,rpd->rbd", member, per_patch.astype(BF).reshape(rows, PATCHES, D), preferred_element_type=F32
    )
    byte_grads = (grad_wide + spread_back.reshape(rows * ROW_BYTES, D)).astype(BF)

    half = D // sections

    def halves(values, length):
        values = values.reshape(rows, length, D)
        other = lax.dynamic_slice_in_dim(values, (1 - section) * half, half, 2)
        own = lax.dynamic_slice_in_dim(values, section * half, half, 2)
        got = lax.ppermute(other, "section", swap)
        return jnp.where(
            section == 0, jnp.concatenate([own, got], axis=0), jnp.concatenate([got, own], axis=0)
        )

    latents_out = halves(latents, PATCHES)
    bytes_out = halves(byte_grads, ROW_BYTES)

    def of_group(part):
        every = lax.all_gather(part, "group", axis=0, tiled=False)
        return [every[index] for index in range(groups)]

    def laid_out(parts, order):
        return jnp.concatenate([parts[index] for index in order], axis=-1).astype(F32)

    ffn_gin, ffn_gdown = [laid_out(of_group(part), (0, 2, 1, 3)) for part in (sum_in, sum_down)]

    kept = jnp.where(section == 0, sum_one, sum_two)
    sent = jnp.where(section == 0, sum_two, sum_one)
    got = lax.ppermute(sent, "section", swap)
    eighths = jnp.where(
        section == 0, jnp.concatenate([kept, got], axis=2), jnp.concatenate([got, kept], axis=2)
    )
    width = eighths.shape[2] // 2
    parts = [piece for every in of_group(eighths) for piece in (every[..., :width], every[..., width:])]
    side_first = laid_out(parts, (0, 1, 4, 5, 2, 3, 6, 7))
    section_first = laid_out([part[:2] for part in parts], (0, 4, 1, 5, 2, 6, 3, 7))
    leading = jnp.where(section == 0, section_first, side_first[:2])
    grad_qkv = jnp.concatenate([leading, side_first[2:3]], axis=0)[None]

    gain_grads = jnp.stack([gain_query, gain_key, gain_normed, gain_mix])
    for axis, pairs in (("group", core_pairs), ("group", side_pairs), ("section", swap)):
        gain_grads = gain_grads + lax.ppermute(gain_grads, axis, pairs)
    gain_grads = jnp.sum(lax.all_gather(gain_grads, "dp", axis=0, tiled=False), axis=0)
    gain_grads = lax.dynamic_slice_in_dim(gain_grads.reshape(2, 2, D), section, 1, 0)
    width = D // lax.axis_size("dp")
    gain_out = lax.dynamic_slice_in_dim(gain_grads, lax.axis_index("dp") * width, width, 2)
    return (latents_out, bytes_out, grad_qkv, side_first[3:], gain_out, ffn_gin, ffn_gdown)


def solution(mesh):
    in_specs = (
        P(("group", "dp"), None, None),
        P(("group", "dp"), None),
        P(("group", "dp"), None),
        P("section", None, "dp", None),
        P("section", "dp", None),
        P("section", None, None),
        P(("section", "dp"), None),
        P(("section", "dp"), None),
        P(("group", "dp"), None, None),
    )
    out_specs = (
        P(("group", "dp"), None, "section"),
        P(("group", "dp"), None, "section"),
        P("section", None, "dp", None),
        P("section", "dp", None),
        P("section", None, "dp"),
        P(("section", "dp"), None),
        P(("section", "dp"), None),
    )
    return jax.shard_map(shards, mesh=mesh, in_specs=in_specs, out_specs=out_specs, check_vma=False)
```

```python
import functools

import jax
import jax.numpy as jnp
from jax import lax
from jax.experimental import pallas as pl
from jax.experimental.pallas import tpu as pltpu
from jax.sharding import PartitionSpec as P

D = 1024
HEADS = 16
HEAD_DIM = 64
PAIR = 2 * HEAD_DIM
PAIRS = HEADS // 2
FF = 2816
ROW_BYTES = 1024
PATCHES = 256
QT = 128
TILES = PATCHES // QT
CAUSAL_SPANS = ((0, 1), (0, 2))

EPS = 1e-05
SCALE = HEAD_DIM ** (-0.5)
EXCLUDED = -1e30

BF = jnp.bfloat16
F32 = jnp.float32


def nn(left, right):
    return jnp.dot(left, right, preferred_element_type=F32)


def tn(left, right):
    return lax.dot_general(left, right, (((0,), (0,)), ((), ())), preferred_element_type=F32)


def nt(left, right):
    return lax.dot_general(left, right, (((1,), (1,)), ((), ())), preferred_element_type=F32)


def two_heads(block):
    lane = lax.broadcasted_iota(jnp.int32, block.shape, 1)
    zero = jnp.zeros_like(block)
    first = lane < HEAD_DIM
    return jnp.concatenate([jnp.where(first, block, zero), jnp.where(first, zero, block)], axis=0)


def own_lanes(both):
    picked = jnp.concatenate([both[:HEAD_DIM, :QT], both[HEAD_DIM:, QT:]], axis=0)
    return picked.T


def twice(row):
    return jnp.concatenate([row, row], axis=1)


def fill_bias(keys, lo_ref, hi_ref, bias_ref):
    at = lax.broadcasted_iota(jnp.int32, (keys, QT), 0)
    for tile in range(TILES):
        own = pl.ds(tile * QT, QT)
        inside = (at >= lo_ref[0, :, own]) & (at < hi_ref[0, :, own])
        bias_ref[tile] = jnp.where(inside, 0.0, EXCLUDED)


def over_chunks(spans, tile, bounds, body, init):
    if spans is None:
        return lax.fori_loop(*bounds, body, init)
    for j in range(*spans[tile]):
        init = body(j, init)
    return init


def chunk_at(spans, chunk, j):
    return pl.ds(j * chunk if spans is not None else pl.multiple_of(j * chunk, chunk), chunk)


def attend_kernel(
    chunk, spans, first_ref, stop_ref, lo_ref, hi_ref, q_ref, k_ref, v_ref, c_ref, l_ref, bias_ref, s_ref
):
    row = pl.program_id(0)
    pairs = range(q_ref.shape[1] // PAIR)
    lanes = [pl.ds(pair * PAIR, PAIR) for pair in pairs]
    pl.when(pl.program_id(1) == 0)(lambda: fill_bias(k_ref.shape[0], lo_ref, hi_ref, bias_ref))
    for tile in range(TILES):
        own = pl.ds(tile * QT, QT)
        queries = [two_heads(q_ref[own, at].astype(F32) * SCALE).astype(BF) for at in lanes]
        bounds = (first_ref[row, tile], stop_ref[row, tile])

        def scores(j, tops):
            here = chunk_at(spans, chunk, j)
            bias = twice(bias_ref[tile, here, :])
            out = []
            for pair in pairs:
                part = nt(k_ref[here, lanes[pair]], queries[pair]) + bias
                s_ref[pair, here, :] = part
                out.append(jnp.maximum(tops[pair], jnp.max(part, axis=0, keepdims=True)))
            return tuple(out)

        tops = (jnp.full((1, 2 * QT), EXCLUDED, F32),) * len(pairs)
        tops = over_chunks(spans, tile, bounds, scores, tops)

        def context(j, sums):
            here = chunk_at(spans, chunk, j)
            out = []
            for pair in pairs:
                total, acc = sums[pair]
                weight = jnp.exp(s_ref[pair, here, :] - tops[pair])
                total = total + jnp.sum(weight, axis=0, keepdims=True)
                out.append((total, acc + tn(v_ref[here, lanes[pair]], weight.astype(BF))))
            return tuple(out)

        sums = ((jnp.zeros((1, 2 * QT), F32), jnp.zeros((PAIR, 2 * QT), F32)),) * len(pairs)
        sums = over_chunks(spans, tile, bounds, context, sums)
        for pair in pairs:
            total, acc = sums[pair]
            c_ref[own, lanes[pair]] = own_lanes(acc / total).astype(BF)
            l_ref[0, pair, tile : tile + 1, :] = tops[pair] + jnp.log(total)


def attend_back_kernel(
    chunk, spans, first_ref, stop_ref, lo_ref, hi_ref, q_ref, k_ref, v_ref, l_ref, c_ref, dc_ref,
    dq_ref, dk_ref, dv_ref, bias_ref, dk_acc, dv_acc,
):
    row = pl.program_id(0)
    pairs = range(q_ref.shape[1] // PAIR)
    lanes = [pl.ds(pair * PAIR, PAIR) for pair in pairs]
    pl.when(pl.program_id(1) == 0)(lambda: fill_bias(k_ref.shape[0], lo_ref, hi_ref, bias_ref))
    dk_acc[...] = jnp.zeros_like(dk_acc)
    dv_acc[...] = jnp.zeros_like(dv_acc)
    for tile in range(TILES):
        own = pl.ds(tile * QT, QT)
        queries, grads, deltas, logs = [], [], [], []
        for pair in pairs:
            queries.append(two_heads(q_ref[own, lanes[pair]].astype(F32) * SCALE).astype(BF))
            grad = dc_ref[own, lanes[pair]].astype(F32)
            inner = (grad * c_ref[own, lanes[pair]].astype(F32)).T
            heads = [jnp.sum(part, axis=0, keepdims=True) for part in (inner[:HEAD_DIM], inner[HEAD_DIM:])]
            deltas.append(jnp.concatenate(heads, axis=1))
            grads.append(two_heads(grad).astype(BF))
            logs.append(l_ref[0, pair, tile : tile + 1, :])

        def step(j, accs):
            here = chunk_at(spans, chunk, j)
            bias = twice(bias_ref[tile, here, :])
            out = []
            for pair in pairs:
                keys = k_ref[here, lanes[pair]]
                prob = jnp.exp(nt(keys, queries[pair]) + bias - logs[pair])
                slope = prob * (nt(v_ref[here, lanes[pair]], grads[pair]) - deltas[pair])
                slope = slope.astype(BF)
                dv_acc[here, lanes[pair]] += nn(prob.astype(BF), grads[pair])
                dk_acc[here, lanes[pair]] += nn(slope, queries[pair])
                out.append(accs[pair] + tn(keys, slope))
            return tuple(out)

        bounds = (first_ref[row, tile], stop_ref[row, tile])
        accs = (jnp.zeros((PAIR, 2 * QT), F32),) * len(pairs)
        accs = over_chunks(spans, tile, bounds, step, accs)
        for pair in pairs:
            dq_ref[own, lanes[pair]] = (own_lanes(accs[pair]) * SCALE).astype(BF)
    dk_ref[...] = dk_acc[...].astype(BF)
    dv_ref[...] = dv_acc[...].astype(BF)


def attention_specs(keys, wide):
    per_query = pl.BlockSpec((PATCHES, wide * PAIR), lambda r, h, *_: (r, h))
    per_key = pl.BlockSpec((keys, wide * PAIR), lambda r, h, *_: (r, h))
    bound = pl.BlockSpec((1, 1, PATCHES), lambda r, h, *_: (r, 0, 0))
    logs = pl.BlockSpec((1, wide, TILES, 2 * QT), lambda r, h, *_: (r, h, 0, 0))
    return per_query, per_key, bound, logs


def kernel_cost(q, k, products):
    scores = q.shape[0] * k.shape[0] // (q.shape[0] // PATCHES) * HEADS
    return pl.CostEstimate(
        flops=products * 2 * scores * 256, bytes_accessed=2 * q.nbytes + 4 * k.nbytes, transcendentals=scores
    )


def attend(bounds, q, k, v, wide, spans=None):
    first, stop, lo, hi, chunk = bounds
    rows = lo.shape[0]
    keys = k.shape[0] // rows
    per_query, per_key, bound, logs = attention_specs(keys, wide)
    return pl.pallas_call(
        functools.partial(attend_kernel, chunk, spans),
        grid_spec=pltpu.PrefetchScalarGridSpec(
            num_scalar_prefetch=2,
            grid=(rows, PAIRS // wide),
            in_specs=[bound, bound, per_query, per_key, per_key],
            out_specs=[per_query, logs],
            scratch_shapes=[pltpu.VMEM((TILES, keys, QT), F32), pltpu.VMEM((wide, keys, 2 * QT), F32)],
        ),
        out_shape=[
            jax.ShapeDtypeStruct(q.shape, BF),
            jax.ShapeDtypeStruct((rows, PAIRS, TILES, 2 * QT), F32),
        ],
        compiler_params=pltpu.CompilerParams(vmem_limit_bytes=48 << 20),
        cost_estimate=kernel_cost(q, k, 2),
        name="attend",
    )(first, stop, lo, hi, q, k, v)


def attend_back(bounds, q, k, v, logsum, context, grads, wide, spans=None):
    first, stop, lo, hi, chunk = bounds
    rows = lo.shape[0]
    keys = k.shape[0] // rows
    per_query, per_key, bound, logs = attention_specs(keys, wide)
    return pl.pallas_call(
        functools.partial(attend_back_kernel, chunk, spans),
        grid_spec=pltpu.PrefetchScalarGridSpec(
            num_scalar_prefetch=2,
            grid=(rows, PAIRS // wide),
            in_specs=[bound, bound, per_query, per_key, per_key, logs, per_query, per_query],
            out_specs=[per_query, per_key, per_key],
            scratch_shapes=[pltpu.VMEM((TILES, keys, QT), F32)] + [pltpu.VMEM((keys, wide * PAIR), F32)] * 2,
        ),
        out_shape=[
            jax.ShapeDtypeStruct(q.shape, BF),
            jax.ShapeDtypeStruct(k.shape, BF),
            jax.ShapeDtypeStruct(k.shape, BF),
        ],
        compiler_params=pltpu.CompilerParams(vmem_limit_bytes=48 << 20),
        cost_estimate=kernel_cost(q, k, 5),
        name="attend_back",
    )(first, stop, lo, hi, q, k, v, logsum, context, grads)


def scale_of(values):
    return lax.rsqrt(jnp.mean(values * values, axis=-1, keepdims=True) + EPS)


def norm_backward(values, row_scale, gain_row, incoming):
    weighted = incoming * gain_row
    projection = jnp.mean(weighted * values, axis=-1, keepdims=True)
    grad_values = row_scale * weighted - values * (row_scale * row_scale * row_scale) * projection
    grad_gain = jnp.sum(incoming * values * row_scale, axis=0)
    return grad_values, grad_gain


def chunk_bounds(lo, hi, chunk):
    first = lo[:, ::QT] // chunk
    stop = (hi[:, QT - 1 :: QT] + chunk - 1) // chunk
    return first, stop, lo[:, None, :], hi[:, None, :], chunk


def shards(
    byte_states, patch_lengths, patch_docs, attn_qkv, attn_out, norm_gains, ffn_in, ffn_down, cotangent
):
    section = lax.axis_index("section")
    group = lax.axis_index("group")
    sections = lax.axis_size("section")
    groups = lax.axis_size("group")
    core, side = group % 2, group // 2

    core_pairs = [(0, 1), (1, 0), (2, 3), (3, 2)]
    side_pairs = [(0, 2), (1, 3), (2, 0), (3, 1)]
    swap = [(0, 1), (1, 0)]
    together = lax.optimization_barrier

    four = jnp.concatenate([attn_qkv[0], attn_out], axis=0)
    matrix = lax.dynamic_index_in_dim(four, group, 0, keepdims=False)
    matrices = lax.all_gather(matrix, ("section", "group", "dp"), axis=0, tiled=True)

    def quarter_of(shard):
        height = shard.shape[0] // groups
        return lax.dynamic_slice_in_dim(shard, group * height, height, 0)

    w_in = lax.all_gather(quarter_of(ffn_in), ("section", "dp", "group"), axis=0, tiled=True)
    gains = lax.all_gather(norm_gains, "section", axis=0, tiled=True)

    def both(values, part, axis, pairs):
        got = lax.ppermute(values, axis, pairs)
        return jnp.where(part == 0, jnp.stack([values, got]), jnp.stack([got, values]))

    line, place = lax.axis_size("dp"), lax.axis_index("dp")
    quarter = quarter_of(ffn_down)
    down = jnp.zeros((line,) + quarter.shape, BF)
    for step in range(line):
        moved = lax.ppermute(quarter, "dp", [(i, (i + step) % line) for i in range(line)]) if step else quarter
        down = lax.dynamic_update_slice_in_dim(down, moved[None], (place - step) % line, 0)
    matrices, down = together((matrices, down))
    matrices = matrices.reshape(sections, groups, D, D)
    wq, wk, wv, wo = [matrices[:, index] for index in range(4)]
    down = both(down, section, "section", swap)

    rows = byte_states.shape[0] // sections
    mine = lambda a: lax.dynamic_slice_in_dim(a, section * rows, rows, 0)
    states, lengths, docs, cot = [mine(a) for a in (byte_states, patch_lengths, patch_docs, cotangent)]
    cot = cot.reshape(rows * PATCHES, D)

    ends = jnp.cumsum(lengths, axis=1)
    earlier = docs[:, None, :] < docs[:, :, None]
    doc_start = jnp.sum(jnp.where(earlier, lengths[:, None, :], 0), axis=2)
    doc_first = jnp.sum(earlier.astype(jnp.int32), axis=2)
    cross, cross_back = chunk_bounds(doc_start, ends, 256), chunk_bounds(doc_start, ends, 512)
    ids = jnp.broadcast_to(lax.iota(jnp.int32, PATCHES) + 1, doc_first.shape)
    causal = chunk_bounds(doc_first, ids, 128)
    positions = lax.iota(jnp.int32, ROW_BYTES)
    member = (positions < ends[:, :, None]) & (positions >= (ends - lengths)[:, :, None])
    member = member.astype(BF)
    count = lengths.astype(F32).reshape(rows * PATCHES, 1)

    pooled = jnp.einsum("rpb,rbd->rpd", member, states, preferred_element_type=F32)
    pooled = pooled.reshape(rows * PATCHES, D) / count
    wide = states.reshape(rows * ROW_BYTES, D).astype(F32)
    query_scale, key_scale = scale_of(pooled), scale_of(wide)
    query_in = (pooled * query_scale * gains[0, 0]).astype(BF)
    key_in = (wide * key_scale * gains[0, 1]).astype(BF)
    q1 = nn(query_in, wq[0]).astype(BF)
    k1 = nn(key_in, wk[0]).astype(BF)
    v1 = nn(key_in, wv[0]).astype(BF)
    v1, down = together((v1, down))
    down = both(down, side, "group", side_pairs)
    c1, l1 = attend(cross, q1, k1, v1, 8)
    c1, down = together((c1, down))
    down = both(down, core, "group", core_pairs)
    w_down = down.transpose(2, 3, 1, 0, 4, 5).reshape(FF, D)
    carried = (pooled + nn(c1, wo[0])).astype(BF)

    carried_wide = carried.astype(F32)
    first_scale = scale_of(carried_wide)
    normed_in = (carried_wide * first_scale * gains[1, 0]).astype(BF)
    q2 = nn(normed_in, wq[1]).astype(BF)
    k2 = nn(normed_in, wk[1]).astype(BF)
    v2 = nn(normed_in, wv[1]).astype(BF)
    c2, l2 = attend(causal, q2, k2, v2, 8, CAUSAL_SPANS)
    residual = carried_wide + nn(c2, wo[1])
    second_scale = scale_of(residual)
    mix_in = (residual * second_scale * gains[1, 1]).astype(BF)
    gate_up = nn(mix_in, w_in)
    gate, up = gate_up[:, :FF], gate_up[:, FF:]
    sig = jax.nn.sigmoid(gate)
    hidden = (gate * sig * up).astype(BF)
    latents = (residual + nn(hidden, w_down)).astype(BF)

    grad_hidden = nt(cot, w_down)
    grad_gate = grad_hidden * up * sig * (1.0 + gate * (1.0 - sig))
    grad_up = grad_hidden * gate * sig
    dgu = jnp.concatenate([grad_gate, grad_up], axis=1).astype(BF)

    def exchanged(values, axis, part, pairs, where):
        size = values.shape[where] // 2
        other = lax.dynamic_slice_in_dim(values, (1 - part) * size, size, where)
        own = lax.dynamic_slice_in_dim(values, part * size, size, where)
        return (own.astype(F32) + lax.ppermute(other, axis, pairs).astype(F32)).astype(BF)

    def over_section(values, where):
        return exchanged(values, "section", section, swap, where)

    def over_side(values, where):
        return exchanged(values, "group", side, side_pairs, where)

    def columns(values, part):
        size = values.shape[-1] // 2
        return lax.dynamic_slice_in_dim(values, part * size, size, values.ndim - 1)

    def line_sum(values, where):
        return lax.psum_scatter(values, "dp", scatter_dimension=where, tiled=True)

    def products(pairs, part):
        out = [tn(left, columns(right, part)) for left, right in pairs]
        return out[0] if len(out) == 1 else jnp.stack(out)

    def to_core(pairs):
        return products(pairs, 1 - core).astype(BF)

    def of_chip(pairs, sent):
        got = lax.ppermute(sent, "group", core_pairs)
        return (products(pairs, core) + got.astype(F32)).astype(BF)

    in_pairs, down_pairs = [(mix_in, dgu)], [(hidden, cot)]
    send_in, send_down = to_core(in_pairs), to_core(down_pairs)
    dgu_next, send_in, send_down = together((dgu, send_in, send_down))
    grad_mix, gain_mix = norm_backward(residual, second_scale, gains[1, 1], nt(dgu_next, w_in))
    grad_residual = grad_mix + cot.astype(F32)
    branch = grad_residual.astype(BF)
    dc2 = nt(branch, wo[1]).astype(BF)
    half_in, half_down = of_chip(in_pairs, send_in), of_chip(down_pairs, send_down)
    dc2, half_in, half_down = together((dc2, half_in, half_down))

    dq2, dk2, dv2 = attend_back(causal, q2, k2, v2, l2, c2, dc2, 8, CAUSAL_SPANS)
    two_pairs = [(normed_in, dq2), (normed_in, dk2), (normed_in, dv2), (c2, branch)]
    send_two = to_core(two_pairs)
    dq2, dk2, dv2, send_two = together((dq2, dk2, dv2, send_two))
    grad_normed = nt(dq2, wq[1]) + nt(dk2, wk[1]) + nt(dv2, wv[1])
    grad_carried, gain_normed = norm_backward(carried_wide, first_scale, gains[1, 0], grad_normed)
    d_carried = (grad_residual + grad_carried).astype(BF)
    dc1 = nt(d_carried, wo[0]).astype(BF)
    half_in = over_section(half_in, 0)
    half_two = of_chip(two_pairs, send_two)
    dc1, half_in, half_two = together((dc1, half_in, half_two))
    sum_down = over_side(over_section(line_sum(half_down.reshape(sections, -1, D // 2), 1), 0), 2)
    sum_down = sum_down[0]

    dq1, dk1, dv1 = attend_back(cross_back, q1, k1, v1, l1, c1, dc1, 4)
    half_in = over_side(half_in, 1)
    half_two = over_side(half_two, 2)
    one_pairs = [(query_in, dq1), (key_in, dk1)], [(key_in, dv1), (c1, d_carried)]
    send_one = [to_core(pairs) for pairs in one_pairs]
    dq1, dk1, dv1, send_one, half_in, half_two = together((dq1, dk1, dv1, send_one, half_in, half_two))
    sum_in = line_sum(half_in, 0)
    sum_two = line_sum(over_section(half_two, 2), 1)
    half_one = [of_chip(pairs, sent) for pairs, sent in zip(one_pairs, send_one)]
    dq1, dk1, dv1, half_one = together((dq1, dk1, dv1, half_one))
    half_one = jnp.concatenate(
        [over_side(over_section(half_one[0], 2), 2), over_section(over_side(half_one[1], 2), 2)], axis=0
    )
    sum_one = line_sum(half_one, 1)
    grad_pooled, gain_query = norm_backward(pooled, query_scale, gains[0, 0], nt(dq1, wq[0]))
    grad_wide, gain_key = norm_backward(
        wide, key_scale, gains[0, 1], nt(dk1, wk[0]) + nt(dv1, wv[0])
    )
    per_patch = (grad_pooled + d_carried.astype(F32)) / count
    spread_back = jnp.einsum(
        "rpb,rpd->rbd", member, per_patch.astype(BF).reshape(rows, PATCHES, D), preferred_element_type=F32
    )
    byte_grads = (grad_wide + spread_back.reshape(rows * ROW_BYTES, D)).astype(BF)

    half = D // sections

    def halves(values, length):
        values = values.reshape(rows, length, D)
        other = lax.dynamic_slice_in_dim(values, (1 - section) * half, half, 2)
        own = lax.dynamic_slice_in_dim(values, section * half, half, 2)
        got = lax.ppermute(other, "section", swap)
        return jnp.where(
            section == 0, jnp.concatenate([own, got], axis=0), jnp.concatenate([got, own], axis=0)
        )

    latents_out = halves(latents, PATCHES)
    bytes_out = halves(byte_grads, ROW_BYTES)

    def of_group(part):
        every = lax.all_gather(part, "group", axis=0, tiled=False)
        return [every[index] for index in range(groups)]

    def laid_out(parts, order):
        return jnp.concatenate([parts[index] for index in order], axis=-1).astype(F32)

    ffn_gin, ffn_gdown = [laid_out(of_group(part), (0, 2, 1, 3)) for part in (sum_in, sum_down)]

    kept = jnp.where(section == 0, sum_one, sum_two)
    sent = jnp.where(section == 0, sum_two, sum_one)
    got = lax.ppermute(sent, "section", swap)
    eighths = jnp.where(
        section == 0, jnp.concatenate([kept, got], axis=2), jnp.concatenate([got, kept], axis=2)
    )
    width = eighths.shape[2] // 2
    parts = [piece for every in of_group(eighths) for piece in (every[..., :width], every[..., width:])]
    side_first = laid_out(parts, (0, 1, 4, 5, 2, 3, 6, 7))
    section_first = laid_out([part[:2] for part in parts], (0, 4, 1, 5, 2, 6, 3, 7))
    leading = jnp.where(section == 0, section_first, side_first[:2])
    grad_qkv = jnp.concatenate([leading, side_first[2:3]], axis=0)[None]

    gain_grads = jnp.stack([gain_query, gain_key, gain_normed, gain_mix])
    for axis, pairs in (("group", core_pairs), ("group", side_pairs), ("section", swap)):
        gain_grads = gain_grads + lax.ppermute(gain_grads, axis, pairs)
    gain_grads = jnp.sum(lax.all_gather(gain_grads, "dp", axis=0, tiled=False), axis=0)
    gain_grads = lax.dynamic_slice_in_dim(gain_grads.reshape(2, 2, D), section, 1, 0)
    width = D // lax.axis_size("dp")
    gain_out = lax.dynamic_slice_in_dim(gain_grads, lax.axis_index("dp") * width, width, 2)
    return (latents_out, bytes_out, grad_qkv, side_first[3:], gain_out, ffn_gin, ffn_gdown)


def solution(mesh):
    in_specs = (
        P(("group", "dp"), None, None),
        P(("group", "dp"), None),
        P(("group", "dp"), None),
        P("section", None, "dp", None),
        P("section", "dp", None),
        P("section", None, None),
        P(("section", "dp"), None),
        P(("section", "dp"), None),
        P(("group", "dp"), None, None),
    )
    out_specs = (
        P(("group", "dp"), None, "section"),
        P(("group", "dp"), None, "section"),
        P("section", None, "dp", None),
        P("section", "dp", None),
        P("section", None, "dp"),
        P(("section", "dp"), None),
        P(("section", "dp"), None),
    )
    return jax.shard_map(shards, mesh=mesh, in_specs=in_specs, out_specs=out_specs, check_vma=False)
```

```python
import functools

import jax
import jax.numpy as jnp
from jax import lax
from jax.experimental import pallas as pl
from jax.experimental.pallas import tpu as pltpu
from jax.sharding import PartitionSpec as P

D = 1024
HEADS = 16
HEAD_DIM = 64
PAIR = 2 * HEAD_DIM
PAIRS = HEADS // 2
FF = 2816
ROW_BYTES = 1024
PATCHES = 256
QT = 128
TILES = PATCHES // QT
CAUSAL_SPANS = ((0, 1), (0, 2))

EPS = 1e-05
SCALE = HEAD_DIM ** (-0.5)
EXCLUDED = -1e30

BF = jnp.bfloat16
F32 = jnp.float32


def nn(left, right):
    return jnp.dot(left, right, preferred_element_type=F32)


def tn(left, right):
    return lax.dot_general(left, right, (((0,), (0,)), ((), ())), preferred_element_type=F32)


def nt(left, right):
    return lax.dot_general(left, right, (((1,), (1,)), ((), ())), preferred_element_type=F32)


def two_heads(block):
    lane = lax.broadcasted_iota(jnp.int32, block.shape, 1)
    zero = jnp.zeros_like(block)
    first = lane < HEAD_DIM
    return jnp.concatenate([jnp.where(first, block, zero), jnp.where(first, zero, block)], axis=0)


def own_lanes(both):
    picked = jnp.concatenate([both[:HEAD_DIM, :QT], both[HEAD_DIM:, QT:]], axis=0)
    return picked.T


def twice(row):
    return jnp.concatenate([row, row], axis=1)


def fill_bias(keys, lo_ref, hi_ref, bias_ref):
    at = lax.broadcasted_iota(jnp.int32, (keys, QT), 0)
    for tile in range(TILES):
        own = pl.ds(tile * QT, QT)
        inside = (at >= lo_ref[0, :, own]) & (at < hi_ref[0, :, own])
        bias_ref[tile] = jnp.where(inside, 0.0, EXCLUDED)


def over_chunks(spans, tile, bounds, body, init):
    if spans is None:
        return lax.fori_loop(*bounds, body, init)
    for j in range(*spans[tile]):
        init = body(j, init)
    return init


def chunk_at(spans, chunk, j):
    return pl.ds(j * chunk if spans is not None else pl.multiple_of(j * chunk, chunk), chunk)


def attend_kernel(
    chunk, spans, first_ref, stop_ref, lo_ref, hi_ref, q_ref, k_ref, v_ref, c_ref, l_ref, bias_ref, s_ref
):
    row = pl.program_id(0)
    pairs = range(q_ref.shape[1] // PAIR)
    lanes = [pl.ds(pair * PAIR, PAIR) for pair in pairs]
    pl.when(pl.program_id(1) == 0)(lambda: fill_bias(k_ref.shape[0], lo_ref, hi_ref, bias_ref))
    for tile in range(TILES):
        own = pl.ds(tile * QT, QT)
        queries = [two_heads(q_ref[own, at].astype(F32) * SCALE).astype(BF) for at in lanes]
        bounds = (first_ref[row, tile], stop_ref[row, tile])

        def scores(j, tops):
            here = chunk_at(spans, chunk, j)
            bias = twice(bias_ref[tile, here, :])
            out = []
            for pair in pairs:
                part = nt(k_ref[here, lanes[pair]], queries[pair]) + bias
                s_ref[pair, here, :] = part
                out.append(jnp.maximum(tops[pair], jnp.max(part, axis=0, keepdims=True)))
            return tuple(out)

        tops = (jnp.full((1, 2 * QT), EXCLUDED, F32),) * len(pairs)
        tops = over_chunks(spans, tile, bounds, scores, tops)

        def context(j, sums):
            here = chunk_at(spans, chunk, j)
            out = []
            for pair in pairs:
                total, acc = sums[pair]
                weight = jnp.exp(s_ref[pair, here, :] - tops[pair])
                total = total + jnp.sum(weight, axis=0, keepdims=True)
                out.append((total, acc + tn(v_ref[here, lanes[pair]], weight.astype(BF))))
            return tuple(out)

        sums = ((jnp.zeros((1, 2 * QT), F32), jnp.zeros((PAIR, 2 * QT), F32)),) * len(pairs)
        sums = over_chunks(spans, tile, bounds, context, sums)
        for pair in pairs:
            total, acc = sums[pair]
            c_ref[own, lanes[pair]] = own_lanes(acc / total).astype(BF)
            l_ref[0, pair, tile : tile + 1, :] = tops[pair] + jnp.log(total)


def attend_back_kernel(
    chunk, spans, first_ref, stop_ref, lo_ref, hi_ref, q_ref, k_ref, v_ref, l_ref, c_ref, dc_ref,
    dq_ref, dk_ref, dv_ref, bias_ref, dk_acc, dv_acc,
):
    row = pl.program_id(0)
    pairs = range(q_ref.shape[1] // PAIR)
    lanes = [pl.ds(pair * PAIR, PAIR) for pair in pairs]
    pl.when(pl.program_id(1) == 0)(lambda: fill_bias(k_ref.shape[0], lo_ref, hi_ref, bias_ref))
    dk_acc[...] = jnp.zeros_like(dk_acc)
    dv_acc[...] = jnp.zeros_like(dv_acc)
    for tile in range(TILES):
        own = pl.ds(tile * QT, QT)
        queries, grads, deltas, logs = [], [], [], []
        for pair in pairs:
            queries.append(two_heads(q_ref[own, lanes[pair]].astype(F32) * SCALE).astype(BF))
            grad = dc_ref[own, lanes[pair]].astype(F32)
            inner = (grad * c_ref[own, lanes[pair]].astype(F32)).T
            heads = [jnp.sum(part, axis=0, keepdims=True) for part in (inner[:HEAD_DIM], inner[HEAD_DIM:])]
            deltas.append(jnp.concatenate(heads, axis=1))
            grads.append(two_heads(grad).astype(BF))
            logs.append(l_ref[0, pair, tile : tile + 1, :])

        def step(j, accs):
            here = chunk_at(spans, chunk, j)
            bias = twice(bias_ref[tile, here, :])
            out = []
            for pair in pairs:
                keys = k_ref[here, lanes[pair]]
                prob = jnp.exp(nt(keys, queries[pair]) + bias - logs[pair])
                slope = prob * (nt(v_ref[here, lanes[pair]], grads[pair]) - deltas[pair])
                slope = slope.astype(BF)
                dv_acc[here, lanes[pair]] += nn(prob.astype(BF), grads[pair])
                dk_acc[here, lanes[pair]] += nn(slope, queries[pair])
                out.append(accs[pair] + tn(keys, slope))
            return tuple(out)

        bounds = (first_ref[row, tile], stop_ref[row, tile])
        accs = (jnp.zeros((PAIR, 2 * QT), F32),) * len(pairs)
        accs = over_chunks(spans, tile, bounds, step, accs)
        for pair in pairs:
            dq_ref[own, lanes[pair]] = (own_lanes(accs[pair]) * SCALE).astype(BF)
    dk_ref[...] = dk_acc[...].astype(BF)
    dv_ref[...] = dv_acc[...].astype(BF)


def attention_specs(keys, wide):
    per_query = pl.BlockSpec((PATCHES, wide * PAIR), lambda r, h, *_: (r, h))
    per_key = pl.BlockSpec((keys, wide * PAIR), lambda r, h, *_: (r, h))
    bound = pl.BlockSpec((1, 1, PATCHES), lambda r, h, *_: (r, 0, 0))
    logs = pl.BlockSpec((1, wide, TILES, 2 * QT), lambda r, h, *_: (r, h, 0, 0))
    return per_query, per_key, bound, logs


def kernel_cost(q, k, products):
    scores = q.shape[0] * k.shape[0] // (q.shape[0] // PATCHES) * HEADS
    return pl.CostEstimate(
        flops=products * 2 * scores * 256, bytes_accessed=2 * q.nbytes + 4 * k.nbytes, transcendentals=scores
    )


def attend(bounds, q, k, v, wide, spans=None):
    first, stop, lo, hi, chunk = bounds
    rows = lo.shape[0]
    keys = k.shape[0] // rows
    per_query, per_key, bound, logs = attention_specs(keys, wide)
    return pl.pallas_call(
        functools.partial(attend_kernel, chunk, spans),
        grid_spec=pltpu.PrefetchScalarGridSpec(
            num_scalar_prefetch=2,
            grid=(rows, PAIRS // wide),
            in_specs=[bound, bound, per_query, per_key, per_key],
            out_specs=[per_query, logs],
            scratch_shapes=[pltpu.VMEM((TILES, keys, QT), F32), pltpu.VMEM((wide, keys, 2 * QT), F32)],
        ),
        out_shape=[
            jax.ShapeDtypeStruct(q.shape, BF),
            jax.ShapeDtypeStruct((rows, PAIRS, TILES, 2 * QT), F32),
        ],
        compiler_params=pltpu.CompilerParams(vmem_limit_bytes=48 << 20),
        cost_estimate=kernel_cost(q, k, 2),
        name="attend",
    )(first, stop, lo, hi, q, k, v)


def attend_back(bounds, q, k, v, logsum, context, grads, wide, spans=None):
    first, stop, lo, hi, chunk = bounds
    rows = lo.shape[0]
    keys = k.shape[0] // rows
    per_query, per_key, bound, logs = attention_specs(keys, wide)
    return pl.pallas_call(
        functools.partial(attend_back_kernel, chunk, spans),
        grid_spec=pltpu.PrefetchScalarGridSpec(
            num_scalar_prefetch=2,
            grid=(rows, PAIRS // wide),
            in_specs=[bound, bound, per_query, per_key, per_key, logs, per_query, per_query],
            out_specs=[per_query, per_key, per_key],
            scratch_shapes=[pltpu.VMEM((TILES, keys, QT), F32)] + [pltpu.VMEM((keys, wide * PAIR), F32)] * 2,
        ),
        out_shape=[
            jax.ShapeDtypeStruct(q.shape, BF),
            jax.ShapeDtypeStruct(k.shape, BF),
            jax.ShapeDtypeStruct(k.shape, BF),
        ],
        compiler_params=pltpu.CompilerParams(vmem_limit_bytes=48 << 20),
        cost_estimate=kernel_cost(q, k, 5),
        name="attend_back",
    )(first, stop, lo, hi, q, k, v, logsum, context, grads)


def scale_of(values):
    return lax.rsqrt(jnp.mean(values * values, axis=-1, keepdims=True) + EPS)


def norm_backward(values, row_scale, gain_row, incoming):
    weighted = incoming * gain_row
    projection = jnp.mean(weighted * values, axis=-1, keepdims=True)
    grad_values = row_scale * weighted - values * (row_scale * row_scale * row_scale) * projection
    grad_gain = jnp.sum(incoming * values * row_scale, axis=0)
    return grad_values, grad_gain


def chunk_bounds(lo, hi, chunk):
    first = lo[:, ::QT] // chunk
    stop = (hi[:, QT - 1 :: QT] + chunk - 1) // chunk
    return first, stop, lo[:, None, :], hi[:, None, :], chunk


def shards(
    byte_states, patch_lengths, patch_docs, attn_qkv, attn_out, norm_gains, ffn_in, ffn_down, cotangent
):
    section = lax.axis_index("section")
    group = lax.axis_index("group")
    sections = lax.axis_size("section")
    groups = lax.axis_size("group")
    core, side = group % 2, group // 2

    core_pairs = [(0, 1), (1, 0), (2, 3), (3, 2)]
    side_pairs = [(0, 2), (1, 3), (2, 0), (3, 1)]
    swap = [(0, 1), (1, 0)]
    together = lax.optimization_barrier

    four = jnp.concatenate([attn_qkv[0], attn_out], axis=0)
    matrix = lax.dynamic_index_in_dim(four, group, 0, keepdims=False)
    matrices = lax.all_gather(matrix, ("section", "group", "dp"), axis=0, tiled=True)

    gains = lax.all_gather(norm_gains, "section", axis=0, tiled=True)

    def quarter_of(shard):
        height = shard.shape[0] // groups
        return lax.dynamic_slice_in_dim(shard, group * height, height, 0)

    def in_order(part, own, got):
        return jnp.where(part == 0, jnp.stack([own, got]), jnp.stack([got, own]))

    def both(values, part, axis, pairs):
        return in_order(part, values, lax.ppermute(values, axis, pairs))

    units = FF // sections

    def of_units(values, part):
        halves = [lax.dynamic_slice_in_dim(values, at + part * units, units, 1) for at in (0, FF)]
        return jnp.concatenate(halves, axis=1)

    quarter = quarter_of(ffn_in)
    got = lax.ppermute(of_units(quarter, 1 - section), "section", swap)
    w_in = in_order(section, of_units(quarter, section), got)
    w_in = lax.all_gather(w_in, ("dp", "group"), axis=1, tiled=True).reshape(D, 2 * units)

    line, place = lax.axis_size("dp"), lax.axis_index("dp")
    quarter = quarter_of(ffn_down)
    down = jnp.zeros((line,) + quarter.shape, BF)
    for step in range(line):
        moved = lax.ppermute(quarter, "dp", [(i, (i + step) % line) for i in range(line)]) if step else quarter
        down = lax.dynamic_update_slice_in_dim(down, moved[None], (place - step) % line, 0)
    matrices, down = together((matrices, down))
    matrices = matrices.reshape(sections, groups, D, D)
    wq, wk, wv, wo = [matrices[:, index] for index in range(4)]
    down = both(down, side, "group", side_pairs)

    rows = byte_states.shape[0] // sections
    mine = lambda a: lax.dynamic_slice_in_dim(a, section * rows, rows, 0)
    states, lengths, docs, cot = [mine(a) for a in (byte_states, patch_lengths, patch_docs, cotangent)]
    tokens = rows * PATCHES
    cot = cot.reshape(tokens, D)
    other_cot = lax.dynamic_slice_in_dim(cotangent, (1 - section) * rows, rows, 0).reshape(tokens, D)
    cots = jnp.concatenate([cot, other_cot], axis=0)

    ends = jnp.cumsum(lengths, axis=1)
    earlier = docs[:, None, :] < docs[:, :, None]
    doc_start = jnp.sum(jnp.where(earlier, lengths[:, None, :], 0), axis=2)
    doc_first = jnp.sum(earlier.astype(jnp.int32), axis=2)
    cross, cross_back = chunk_bounds(doc_start, ends, 256), chunk_bounds(doc_start, ends, 512)
    ids = jnp.broadcast_to(lax.iota(jnp.int32, PATCHES) + 1, doc_first.shape)
    causal = chunk_bounds(doc_first, ids, 128)
    positions = lax.iota(jnp.int32, ROW_BYTES)
    member = (positions < ends[:, :, None]) & (positions >= (ends - lengths)[:, :, None])
    member = member.astype(BF)
    count = lengths.astype(F32).reshape(rows * PATCHES, 1)

    pooled = jnp.einsum("rpb,rbd->rpd", member, states, preferred_element_type=F32)
    pooled = pooled.reshape(rows * PATCHES, D) / count
    wide = states.reshape(rows * ROW_BYTES, D).astype(F32)
    query_scale, key_scale = scale_of(pooled), scale_of(wide)
    query_in = (pooled * query_scale * gains[0, 0]).astype(BF)
    key_in = (wide * key_scale * gains[0, 1]).astype(BF)
    q1 = nn(query_in, wq[0]).astype(BF)
    k1 = nn(key_in, wk[0]).astype(BF)
    v1 = nn(key_in, wv[0]).astype(BF)
    v1, down = together((v1, down))
    down = both(down, core, "group", core_pairs)
    c1, l1 = attend(cross, q1, k1, v1, 8)
    c1, down = together((c1, down))
    w_down = down.transpose(2, 1, 0, 3, 4).reshape(units, D)
    carried = (pooled + nn(c1, wo[0])).astype(BF)

    carried_wide = carried.astype(F32)
    first_scale = scale_of(carried_wide)
    normed_in = (carried_wide * first_scale * gains[1, 0]).astype(BF)
    q2 = nn(normed_in, wq[1]).astype(BF)
    k2 = nn(normed_in, wk[1]).astype(BF)
    v2 = nn(normed_in, wv[1]).astype(BF)
    c2, l2 = attend(causal, q2, k2, v2, 8, CAUSAL_SPANS)
    residual = carried_wide + nn(c2, wo[1])
    second_scale = scale_of(residual)
    mix_in = (residual * second_scale * gains[1, 1]).astype(BF)
    mixed = jnp.concatenate([mix_in, lax.ppermute(mix_in, "section", swap)], axis=0)
    gate_up = nn(mixed, w_in)
    gate, up = gate_up[:, :units], gate_up[:, units:]
    sig = jax.nn.sigmoid(gate)
    hidden = (gate * sig * up).astype(BF)

    grad_hidden = nt(cots, w_down)
    grad_gate = grad_hidden * up * sig * (1.0 + gate * (1.0 - sig))
    grad_up = grad_hidden * gate * sig
    dgu = jnp.concatenate([grad_gate, grad_up], axis=1).astype(BF)

    def exchanged(values, axis, part, pairs, where):
        size = values.shape[where] // 2
        other = lax.dynamic_slice_in_dim(values, (1 - part) * size, size, where)
        own = lax.dynamic_slice_in_dim(values, part * size, size, where)
        return (own.astype(F32) + lax.ppermute(other, axis, pairs).astype(F32)).astype(BF)

    def over_section(values, where):
        return exchanged(values, "section", section, swap, where)

    def over_side(values, where):
        return exchanged(values, "group", side, side_pairs, where)

    def columns(values, part):
        size = values.shape[-1] // 2
        return lax.dynamic_slice_in_dim(values, part * size, size, values.ndim - 1)

    def line_sum(values, where):
        return lax.psum_scatter(values, "dp", scatter_dimension=where, tiled=True)

    def products(pairs, part):
        out = [tn(left, columns(right, part)) for left, right in pairs]
        return out[0] if len(out) == 1 else jnp.stack(out)

    def to_core(pairs):
        return products(pairs, 1 - core).astype(BF)

    def of_chip(pairs, sent):
        got = lax.ppermute(sent, "group", core_pairs)
        return (products(pairs, core) + got.astype(F32)).astype(BF)

    in_pairs, down_pairs = [(mixed, dgu)], [(hidden, cots)]
    mix_other = nt(dgu[tokens:], w_in).astype(BF)
    send_in, send_down = to_core(in_pairs), to_core(down_pairs)
    dgu_own, mix_other, send_in, send_down = together((dgu[:tokens], mix_other, send_in, send_down))
    mix_got = lax.ppermute(mix_other, "section", swap)

    half = D // sections
    parts = nn(hidden, w_down)
    parts = jnp.concatenate([residual + parts[:tokens], parts[tokens:]], axis=0)
    sent = lax.dynamic_slice_in_dim(parts, (1 - section) * half, half, 1).astype(BF)
    kept = lax.dynamic_slice_in_dim(parts, section * half, half, 1)
    dgu_own, sent = together((dgu_own, sent))
    got = lax.ppermute(sent, "section", swap).astype(F32)
    latents = in_order(section, kept[:tokens] + got[tokens:], kept[tokens:] + got[:tokens])
    latents_out = latents.astype(BF).reshape(sections * rows, PATCHES, half)

    grad_mixed = nt(dgu_own, w_in) + mix_got.astype(F32)
    grad_mix, gain_mix = norm_backward(residual, second_scale, gains[1, 1], grad_mixed)
    grad_residual = grad_mix + cot.astype(F32)
    branch = grad_residual.astype(BF)
    dc2 = nt(branch, wo[1]).astype(BF)
    half_in, half_down = of_chip(in_pairs, send_in), of_chip(down_pairs, send_down)
    dc2, half_in, half_down = together((dc2, half_in, half_down))

    dq2, dk2, dv2 = attend_back(causal, q2, k2, v2, l2, c2, dc2, 8, CAUSAL_SPANS)
    two_pairs = [(normed_in, dq2), (normed_in, dk2), (normed_in, dv2), (c2, branch)]
    send_two = to_core(two_pairs)
    dq2, dk2, dv2, send_two = together((dq2, dk2, dv2, send_two))
    grad_normed = nt(dq2, wq[1]) + nt(dk2, wk[1]) + nt(dv2, wv[1])
    grad_carried, gain_normed = norm_backward(carried_wide, first_scale, gains[1, 0], grad_normed)
    d_carried = (grad_residual + grad_carried).astype(BF)
    dc1 = nt(d_carried, wo[0]).astype(BF)
    half_in = over_side(half_in.reshape(sections, line, 2, -1, units), 2)
    half_two = of_chip(two_pairs, send_two)
    dc1, half_in, half_two = together((dc1, half_in, half_two))
    sum_down = over_side(line_sum(half_down, 0), 1)
    sum_in = line_sum(half_in, 1).reshape(sections, -1, units)
    sum_in = jnp.stack([lax.dynamic_index_in_dim(sum_in, section, 0, False),
                        lax.ppermute(lax.dynamic_index_in_dim(sum_in, 1 - section, 0, False), "section", swap)])
    sum_in = jnp.where(section == 0, sum_in, sum_in[::-1])

    dq1, dk1, dv1 = attend_back(cross_back, q1, k1, v1, l1, c1, dc1, 4)
    half_two = over_section(half_two, 2)
    one_pairs = [(query_in, dq1), (key_in, dk1)], [(key_in, dv1), (c1, d_carried)]
    send_one = [to_core(pairs) for pairs in one_pairs]
    dq1, dk1, dv1, send_one, half_two = together((dq1, dk1, dv1, send_one, half_two))
    sum_two = line_sum(over_side(half_two, 2), 1)
    half_one = [of_chip(pairs, sent) for pairs, sent in zip(one_pairs, send_one)]
    dq1, dk1, dv1, half_one = together((dq1, dk1, dv1, half_one))
    half_one = jnp.concatenate(
        [over_side(over_section(half_one[0], 2), 2), over_section(over_side(half_one[1], 2), 2)], axis=0
    )
    sum_one = line_sum(half_one, 1)
    grad_pooled, gain_query = norm_backward(pooled, query_scale, gains[0, 0], nt(dq1, wq[0]))
    grad_wide, gain_key = norm_backward(
        wide, key_scale, gains[0, 1], nt(dk1, wk[0]) + nt(dv1, wv[0])
    )
    per_patch = (grad_pooled + d_carried.astype(F32)) / count
    spread_back = jnp.einsum(
        "rpb,rpd->rbd", member, per_patch.astype(BF).reshape(rows, PATCHES, D), preferred_element_type=F32
    )
    byte_grads = (grad_wide + spread_back.reshape(rows * ROW_BYTES, D)).astype(BF)

    byte_grads = byte_grads.reshape(rows, ROW_BYTES, D)
    other = lax.dynamic_slice_in_dim(byte_grads, (1 - section) * half, half, 2)
    own = lax.dynamic_slice_in_dim(byte_grads, section * half, half, 2)
    bytes_out = in_order(section, own, lax.ppermute(other, "section", swap))
    bytes_out = bytes_out.reshape(sections * rows, ROW_BYTES, half)

    def of_group(part):
        every = lax.all_gather(part, "group", axis=0, tiled=False)
        return [every[index] for index in range(groups)]

    def laid_out(parts, order):
        return jnp.concatenate([parts[index] for index in order], axis=-1).astype(F32)

    ffn_gdown = laid_out(of_group(sum_down), (0, 2, 1, 3))
    every = of_group(sum_in)
    ffn_gin = jnp.concatenate(
        [laid_out([every[at][t] for at in (2 * y, 2 * y + 1) for t in range(sections)], range(4)) for y in (0, 1)],
        axis=0,
    )

    kept = jnp.where(section == 0, sum_one, sum_two)
    sent = jnp.where(section == 0, sum_two, sum_one)
    got = lax.ppermute(sent, "section", swap)
    eighths = jnp.where(
        section == 0, jnp.concatenate([kept, got], axis=2), jnp.concatenate([got, kept], axis=2)
    )
    width = eighths.shape[2] // 2
    parts = [piece for every in of_group(eighths) for piece in (every[..., :width], every[..., width:])]
    section_first = laid_out(parts, (0, 4, 1, 5, 2, 6, 3, 7))
    side_first = laid_out([part[2:] for part in parts], (0, 1, 4, 5, 2, 3, 6, 7))
    last = jnp.where(section == 0, side_first, section_first[2:])
    grad_qkv = jnp.concatenate([section_first[:2], last[:1]], axis=0)[None]

    gain_grads = jnp.stack([gain_query, gain_key, gain_normed, gain_mix])
    for axis, pairs in (("group", core_pairs), ("group", side_pairs), ("section", swap)):
        gain_grads = gain_grads + lax.ppermute(gain_grads, axis, pairs)
    gain_grads = jnp.sum(lax.all_gather(gain_grads, "dp", axis=0, tiled=False), axis=0)
    gain_grads = lax.dynamic_slice_in_dim(gain_grads.reshape(2, 2, D), section, 1, 0)
    width = D // lax.axis_size("dp")
    gain_out = lax.dynamic_slice_in_dim(gain_grads, lax.axis_index("dp") * width, width, 2)
    return (latents_out, bytes_out, grad_qkv, last[1:], gain_out, ffn_gin, ffn_gdown)


def solution(mesh):
    in_specs = (
        P(("group", "dp"), None, None),
        P(("group", "dp"), None),
        P(("group", "dp"), None),
        P("section", None, "dp", None),
        P("section", "dp", None),
        P("section", None, None),
        P(("section", "dp"), None),
        P(("section", "dp"), None),
        P(("group", "dp"), None, None),
    )
    out_specs = (
        P(("group", "dp"), None, "section"),
        P(("group", "dp"), None, "section"),
        P("section", None, "dp", None),
        P("section", "dp", None),
        P("section", None, "dp"),
        P(("section", "dp"), None),
        P(("section", "dp"), None),
    )
    return jax.shard_map(shards, mesh=mesh, in_specs=in_specs, out_specs=out_specs, check_vma=False)
```

```python
import functools

import jax
import jax.numpy as jnp
from jax import lax
from jax.experimental import pallas as pl
from jax.experimental.pallas import tpu as pltpu
from jax.sharding import PartitionSpec as P

D = 1024
HEADS = 16
HEAD_DIM = 64
PAIR = 2 * HEAD_DIM
PAIRS = HEADS // 2
FF = 2816
ROW_BYTES = 1024
PATCHES = 256
QT = 128
TILES = PATCHES // QT
CAUSAL_SPANS = ((0, 1), (0, 2))

EPS = 1e-05
SCALE = HEAD_DIM ** (-0.5)
EXCLUDED = -1e30

BF = jnp.bfloat16
F32 = jnp.float32


def nn(left, right):
    return jnp.dot(left, right, preferred_element_type=F32)


def tn(left, right):
    return lax.dot_general(left, right, (((0,), (0,)), ((), ())), preferred_element_type=F32)


def nt(left, right):
    return lax.dot_general(left, right, (((1,), (1,)), ((), ())), preferred_element_type=F32)


def two_heads(block):
    lane = lax.broadcasted_iota(jnp.int32, block.shape, 1)
    zero = jnp.zeros_like(block)
    first = lane < HEAD_DIM
    return jnp.concatenate([jnp.where(first, block, zero), jnp.where(first, zero, block)], axis=0)


def own_lanes(both):
    picked = jnp.concatenate([both[:HEAD_DIM, :QT], both[HEAD_DIM:, QT:]], axis=0)
    return picked.T


def twice(row):
    return jnp.concatenate([row, row], axis=1)


def fill_bias(keys, lo_ref, hi_ref, bias_ref):
    at = lax.broadcasted_iota(jnp.int32, (keys, QT), 0)
    for tile in range(TILES):
        own = pl.ds(tile * QT, QT)
        inside = (at >= lo_ref[0, :, own]) & (at < hi_ref[0, :, own])
        bias_ref[tile] = jnp.where(inside, 0.0, EXCLUDED)


def over_chunks(spans, tile, bounds, body, init):
    if spans is None:
        return lax.fori_loop(*bounds, body, init)
    for j in range(*spans[tile]):
        init = body(j, init)
    return init


def chunk_at(spans, chunk, j):
    return pl.ds(j * chunk if spans is not None else pl.multiple_of(j * chunk, chunk), chunk)


def attend_kernel(
    chunk, spans, first_ref, stop_ref, lo_ref, hi_ref, q_ref, k_ref, v_ref, c_ref, l_ref, bias_ref, s_ref
):
    row = pl.program_id(0)
    pairs = range(q_ref.shape[1] // PAIR)
    lanes = [pl.ds(pair * PAIR, PAIR) for pair in pairs]
    pl.when(pl.program_id(1) == 0)(lambda: fill_bias(k_ref.shape[0], lo_ref, hi_ref, bias_ref))
    for tile in range(TILES):
        own = pl.ds(tile * QT, QT)
        queries = [two_heads(q_ref[own, at].astype(F32) * SCALE).astype(BF) for at in lanes]
        bounds = (first_ref[row, tile], stop_ref[row, tile])

        def scores(j, tops):
            here = chunk_at(spans, chunk, j)
            bias = twice(bias_ref[tile, here, :])
            out = []
            for pair in pairs:
                part = nt(k_ref[here, lanes[pair]], queries[pair]) + bias
                s_ref[pair, here, :] = part
                out.append(jnp.maximum(tops[pair], jnp.max(part, axis=0, keepdims=True)))
            return tuple(out)

        tops = (jnp.full((1, 2 * QT), EXCLUDED, F32),) * len(pairs)
        tops = over_chunks(spans, tile, bounds, scores, tops)

        def context(j, sums):
            here = chunk_at(spans, chunk, j)
            out = []
            for pair in pairs:
                total, acc = sums[pair]
                weight = jnp.exp(s_ref[pair, here, :] - tops[pair])
                total = total + jnp.sum(weight, axis=0, keepdims=True)
                out.append((total, acc + tn(v_ref[here, lanes[pair]], weight.astype(BF))))
            return tuple(out)

        sums = ((jnp.zeros((1, 2 * QT), F32), jnp.zeros((PAIR, 2 * QT), F32)),) * len(pairs)
        sums = over_chunks(spans, tile, bounds, context, sums)
        for pair in pairs:
            total, acc = sums[pair]
            c_ref[own, lanes[pair]] = own_lanes(acc / total).astype(BF)
            l_ref[0, pair, tile : tile + 1, :] = tops[pair] + jnp.log(total)


def attend_back_kernel(
    chunk, spans, first_ref, stop_ref, lo_ref, hi_ref, q_ref, k_ref, v_ref, l_ref, c_ref, dc_ref,
    dq_ref, dk_ref, dv_ref, bias_ref, dk_acc, dv_acc,
):
    row = pl.program_id(0)
    pairs = range(q_ref.shape[1] // PAIR)
    lanes = [pl.ds(pair * PAIR, PAIR) for pair in pairs]
    pl.when(pl.program_id(1) == 0)(lambda: fill_bias(k_ref.shape[0], lo_ref, hi_ref, bias_ref))
    dk_acc[...] = jnp.zeros_like(dk_acc)
    dv_acc[...] = jnp.zeros_like(dv_acc)
    for tile in range(TILES):
        own = pl.ds(tile * QT, QT)
        queries, grads, deltas, logs = [], [], [], []
        for pair in pairs:
            queries.append(two_heads(q_ref[own, lanes[pair]].astype(F32) * SCALE).astype(BF))
            grad = dc_ref[own, lanes[pair]].astype(F32)
            inner = (grad * c_ref[own, lanes[pair]].astype(F32)).T
            heads = [jnp.sum(part, axis=0, keepdims=True) for part in (inner[:HEAD_DIM], inner[HEAD_DIM:])]
            deltas.append(jnp.concatenate(heads, axis=1))
            grads.append(two_heads(grad).astype(BF))
            logs.append(l_ref[0, pair, tile : tile + 1, :])

        def step(j, accs):
            here = chunk_at(spans, chunk, j)
            bias = twice(bias_ref[tile, here, :])
            out = []
            for pair in pairs:
                keys = k_ref[here, lanes[pair]]
                prob = jnp.exp(nt(keys, queries[pair]) + bias - logs[pair])
                slope = prob * (nt(v_ref[here, lanes[pair]], grads[pair]) - deltas[pair])
                slope = slope.astype(BF)
                dv_acc[here, lanes[pair]] += nn(prob.astype(BF), grads[pair])
                dk_acc[here, lanes[pair]] += nn(slope, queries[pair])
                out.append(accs[pair] + tn(keys, slope))
            return tuple(out)

        bounds = (first_ref[row, tile], stop_ref[row, tile])
        accs = (jnp.zeros((PAIR, 2 * QT), F32),) * len(pairs)
        accs = over_chunks(spans, tile, bounds, step, accs)
        for pair in pairs:
            dq_ref[own, lanes[pair]] = (own_lanes(accs[pair]) * SCALE).astype(BF)
    dk_ref[...] = dk_acc[...].astype(BF)
    dv_ref[...] = dv_acc[...].astype(BF)


def attention_specs(keys, wide):
    per_query = pl.BlockSpec((PATCHES, wide * PAIR), lambda r, h, *_: (r, h))
    per_key = pl.BlockSpec((keys, wide * PAIR), lambda r, h, *_: (r, h))
    bound = pl.BlockSpec((1, 1, PATCHES), lambda r, h, *_: (r, 0, 0))
    logs = pl.BlockSpec((1, wide, TILES, 2 * QT), lambda r, h, *_: (r, h, 0, 0))
    return per_query, per_key, bound, logs


def kernel_cost(q, k, products):
    scores = q.shape[0] * k.shape[0] // (q.shape[0] // PATCHES) * HEADS
    return pl.CostEstimate(
        flops=products * 2 * scores * 256, bytes_accessed=2 * q.nbytes + 4 * k.nbytes, transcendentals=scores
    )


def attend(bounds, q, k, v, wide, spans=None):
    first, stop, lo, hi, chunk = bounds
    rows = lo.shape[0]
    keys = k.shape[0] // rows
    per_query, per_key, bound, logs = attention_specs(keys, wide)
    return pl.pallas_call(
        functools.partial(attend_kernel, chunk, spans),
        grid_spec=pltpu.PrefetchScalarGridSpec(
            num_scalar_prefetch=2,
            grid=(rows, PAIRS // wide),
            in_specs=[bound, bound, per_query, per_key, per_key],
            out_specs=[per_query, logs],
            scratch_shapes=[pltpu.VMEM((TILES, keys, QT), F32), pltpu.VMEM((wide, keys, 2 * QT), F32)],
        ),
        out_shape=[
            jax.ShapeDtypeStruct(q.shape, BF),
            jax.ShapeDtypeStruct((rows, PAIRS, TILES, 2 * QT), F32),
        ],
        compiler_params=pltpu.CompilerParams(vmem_limit_bytes=48 << 20),
        cost_estimate=kernel_cost(q, k, 2),
        name="attend",
    )(first, stop, lo, hi, q, k, v)


def attend_back(bounds, q, k, v, logsum, context, grads, wide, spans=None):
    first, stop, lo, hi, chunk = bounds
    rows = lo.shape[0]
    keys = k.shape[0] // rows
    per_query, per_key, bound, logs = attention_specs(keys, wide)
    return pl.pallas_call(
        functools.partial(attend_back_kernel, chunk, spans),
        grid_spec=pltpu.PrefetchScalarGridSpec(
            num_scalar_prefetch=2,
            grid=(rows, PAIRS // wide),
            in_specs=[bound, bound, per_query, per_key, per_key, logs, per_query, per_query],
            out_specs=[per_query, per_key, per_key],
            scratch_shapes=[pltpu.VMEM((TILES, keys, QT), F32)] + [pltpu.VMEM((keys, wide * PAIR), F32)] * 2,
        ),
        out_shape=[
            jax.ShapeDtypeStruct(q.shape, BF),
            jax.ShapeDtypeStruct(k.shape, BF),
            jax.ShapeDtypeStruct(k.shape, BF),
        ],
        compiler_params=pltpu.CompilerParams(vmem_limit_bytes=48 << 20),
        cost_estimate=kernel_cost(q, k, 5),
        name="attend_back",
    )(first, stop, lo, hi, q, k, v, logsum, context, grads)


def scale_of(values):
    return lax.rsqrt(jnp.mean(values * values, axis=-1, keepdims=True) + EPS)


def norm_backward(values, row_scale, gain_row, incoming):
    weighted = incoming * gain_row
    projection = jnp.mean(weighted * values, axis=-1, keepdims=True)
    grad_values = row_scale * weighted - values * (row_scale * row_scale * row_scale) * projection
    grad_gain = jnp.sum(incoming * values * row_scale, axis=0)
    return grad_values, grad_gain


def chunk_bounds(lo, hi, chunk):
    first = lo[:, ::QT] // chunk
    stop = (hi[:, QT - 1 :: QT] + chunk - 1) // chunk
    return first, stop, lo[:, None, :], hi[:, None, :], chunk


def shards(
    byte_states, patch_lengths, patch_docs, attn_qkv, attn_out, norm_gains, ffn_in, ffn_down, cotangent
):
    section = lax.axis_index("section")
    group = lax.axis_index("group")
    sections = lax.axis_size("section")
    groups = lax.axis_size("group")
    core, side = group % 2, group // 2

    core_pairs = [(0, 1), (1, 0), (2, 3), (3, 2)]
    side_pairs = [(0, 2), (1, 3), (2, 0), (3, 1)]
    swap = [(0, 1), (1, 0)]
    together = lax.optimization_barrier

    gains = lax.all_gather(norm_gains, "section", axis=0, tiled=True)

    def quarter_of(shard):
        height = shard.shape[0] // groups
        return lax.dynamic_slice_in_dim(shard, group * height, height, 0)

    def in_order(part, own, got):
        return jnp.where(part == 0, jnp.stack([own, got]), jnp.stack([got, own]))

    def both(values, part, axis, pairs):
        return in_order(part, values, lax.ppermute(values, axis, pairs))

    units = FF // sections

    def of_units(values, part):
        halves = [lax.dynamic_slice_in_dim(values, at + part * units, units, 1) for at in (0, FF)]
        return jnp.concatenate(halves, axis=1)

    quarter = quarter_of(ffn_in)
    got = lax.ppermute(of_units(quarter, 1 - section), "section", swap)
    w_in = in_order(section, of_units(quarter, section), got)
    w_in = lax.all_gather(w_in, ("dp", "group"), axis=1, tiled=True).reshape(D, 2 * units)

    height = attn_qkv.shape[2] // groups
    quarter = lax.dynamic_slice_in_dim(attn_qkv[0], group * height, height, 1)
    qkv = lax.all_gather(quarter, ("section", "dp", "group"), axis=1, tiled=True)

    line, place = lax.axis_size("dp"), lax.axis_index("dp")
    wo = both(quarter_of(attn_out[0]), section, "section", swap)
    chain = jnp.concatenate([wo.reshape(-1, D), quarter_of(ffn_down)], axis=0)
    moved = [chain if step == 0 else lax.ppermute(chain, "dp", [(i, (i + step) % line) for i in range(line)])
             for step in range(line)]
    chain = jnp.zeros((line,) + chain.shape, BF)
    for step in range(line):
        chain = lax.dynamic_update_slice_in_dim(chain, moved[step][None], (place - step) % line, 0)
    chain = both(chain, side, "group", side_pairs)
    qkv, chain = together((qkv, chain))
    wq, wk, wv = [matrix.reshape(sections, D, D) for matrix in qkv]

    rows = byte_states.shape[0] // sections
    mine = lambda a: lax.dynamic_slice_in_dim(a, section * rows, rows, 0)
    states, lengths, docs, cot = [mine(a) for a in (byte_states, patch_lengths, patch_docs, cotangent)]
    tokens = rows * PATCHES
    cot = cot.reshape(tokens, D)
    other_cot = lax.dynamic_slice_in_dim(cotangent, (1 - section) * rows, rows, 0).reshape(tokens, D)
    cots = jnp.concatenate([cot, other_cot], axis=0)

    ends = jnp.cumsum(lengths, axis=1)
    earlier = docs[:, None, :] < docs[:, :, None]
    doc_start = jnp.sum(jnp.where(earlier, lengths[:, None, :], 0), axis=2)
    doc_first = jnp.sum(earlier.astype(jnp.int32), axis=2)
    cross, cross_back = chunk_bounds(doc_start, ends, 256), chunk_bounds(doc_start, ends, 512)
    ids = jnp.broadcast_to(lax.iota(jnp.int32, PATCHES) + 1, doc_first.shape)
    causal = chunk_bounds(doc_first, ids, 128)
    positions = lax.iota(jnp.int32, ROW_BYTES)
    member = (positions < ends[:, :, None]) & (positions >= (ends - lengths)[:, :, None])
    member = member.astype(BF)
    count = lengths.astype(F32).reshape(rows * PATCHES, 1)

    pooled = jnp.einsum("rpb,rbd->rpd", member, states, preferred_element_type=F32)
    pooled = pooled.reshape(rows * PATCHES, D) / count
    wide = states.reshape(rows * ROW_BYTES, D).astype(F32)
    query_scale, key_scale = scale_of(pooled), scale_of(wide)
    query_in = (pooled * query_scale * gains[0, 0]).astype(BF)
    key_in = (wide * key_scale * gains[0, 1]).astype(BF)
    q1 = nn(query_in, wq[0]).astype(BF)
    k1 = nn(key_in, wk[0]).astype(BF)
    v1 = nn(key_in, wv[0]).astype(BF)
    v1, chain = together((v1, chain))
    chain = both(chain, core, "group", core_pairs)
    c1, l1 = attend(cross, q1, k1, v1, 8)
    c1, chain = together((c1, chain))
    chain = chain.transpose(2, 1, 0, 3, 4)
    at = sections * height
    wo = chain[:, :, :, :at].reshape(line, 2, 2, sections, height, D).transpose(3, 0, 1, 2, 4, 5)
    wo = wo.reshape(sections, D, D)
    w_down = chain[:, :, :, at:].reshape(units, D)
    carried = (pooled + nn(c1, wo[0])).astype(BF)

    carried_wide = carried.astype(F32)
    first_scale = scale_of(carried_wide)
    normed_in = (carried_wide * first_scale * gains[1, 0]).astype(BF)
    q2 = nn(normed_in, wq[1]).astype(BF)
    k2 = nn(normed_in, wk[1]).astype(BF)
    v2 = nn(normed_in, wv[1]).astype(BF)
    c2, l2 = attend(causal, q2, k2, v2, 8, CAUSAL_SPANS)
    residual = carried_wide + nn(c2, wo[1])
    second_scale = scale_of(residual)
    mix_in = (residual * second_scale * gains[1, 1]).astype(BF)
    mixed = jnp.concatenate([mix_in, lax.ppermute(mix_in, "section", swap)], axis=0)
    gate_up = nn(mixed, w_in)
    gate, up = gate_up[:, :units], gate_up[:, units:]
    sig = jax.nn.sigmoid(gate)
    hidden = (gate * sig * up).astype(BF)

    grad_hidden = nt(cots, w_down)
    grad_gate = grad_hidden * up * sig * (1.0 + gate * (1.0 - sig))
    grad_up = grad_hidden * gate * sig
    dgu = jnp.concatenate([grad_gate, grad_up], axis=1).astype(BF)

    def exchanged(values, axis, part, pairs, where):
        size = values.shape[where] // 2
        other = lax.dynamic_slice_in_dim(values, (1 - part) * size, size, where)
        own = lax.dynamic_slice_in_dim(values, part * size, size, where)
        return (own.astype(F32) + lax.ppermute(other, axis, pairs).astype(F32)).astype(BF)

    def over_section(values, where):
        return exchanged(values, "section", section, swap, where)

    def over_side(values, where):
        return exchanged(values, "group", side, side_pairs, where)

    def columns(values, part):
        size = values.shape[-1] // 2
        return lax.dynamic_slice_in_dim(values, part * size, size, values.ndim - 1)

    def line_sum(values, where):
        return lax.psum_scatter(values, "dp", scatter_dimension=where, tiled=True)

    def products(pairs, part):
        out = [tn(left, columns(right, part)) for left, right in pairs]
        return out[0] if len(out) == 1 else jnp.stack(out)

    def to_core(pairs):
        return products(pairs, 1 - core).astype(BF)

    def of_chip(pairs, sent):
        got = lax.ppermute(sent, "group", core_pairs)
        return (products(pairs, core) + got.astype(F32)).astype(BF)

    mix_other = nt(dgu[tokens:], w_in).astype(BF)
    dgu, mix_other = together((dgu, mix_other))
    in_pairs, down_pairs = [(mixed, dgu)], [(hidden, cots)]
    send_in, send_down = to_core(in_pairs), to_core(down_pairs)
    dgu_own, send_in, send_down = together((dgu[:tokens], send_in, send_down))
    mix_got = lax.ppermute(mix_other, "section", swap)

    half = D // sections
    parts = nn(hidden, w_down)
    parts = jnp.concatenate([residual + parts[:tokens], parts[tokens:]], axis=0)
    sent = lax.dynamic_slice_in_dim(parts, (1 - section) * half, half, 1).astype(BF)
    kept = lax.dynamic_slice_in_dim(parts, section * half, half, 1)
    dgu_own, sent = together((dgu_own, sent))
    got = lax.ppermute(sent, "section", swap).astype(F32)
    half_in, half_down = of_chip(in_pairs, send_in), of_chip(down_pairs, send_down)
    mix_got, half_in, half_down = together((mix_got, half_in, half_down))
    grad_mixed = nt(dgu_own, w_in) + mix_got.astype(F32)
    grad_mix, gain_mix = norm_backward(residual, second_scale, gains[1, 1], grad_mixed)
    grad_residual = grad_mix + cot.astype(F32)
    branch = grad_residual.astype(BF)
    dc2 = nt(branch, wo[1]).astype(BF)

    dc2, got = together((dc2, got))
    latents = in_order(section, kept[:tokens] + got[tokens:], kept[tokens:] + got[:tokens])
    latents_out = latents.astype(BF).reshape(sections * rows, PATCHES, half)

    dq2, dk2, dv2 = attend_back(causal, q2, k2, v2, l2, c2, dc2, 8, CAUSAL_SPANS)
    two_pairs = [(normed_in, dq2), (normed_in, dk2), (normed_in, dv2), (c2, branch)]
    send_two = to_core(two_pairs)
    dq2, dk2, dv2, send_two = together((dq2, dk2, dv2, send_two))
    grad_normed = nt(dq2, wq[1]) + nt(dk2, wk[1]) + nt(dv2, wv[1])
    grad_carried, gain_normed = norm_backward(carried_wide, first_scale, gains[1, 0], grad_normed)
    d_carried = (grad_residual + grad_carried).astype(BF)
    dc1 = nt(d_carried, wo[0]).astype(BF)
    half_in = over_side(half_in.reshape(sections, line, 2, -1, units), 2)
    half_two = of_chip(two_pairs, send_two)
    dc1, half_in, half_two = together((dc1, half_in, half_two))
    sum_down = over_side(line_sum(half_down, 0), 1)
    sum_in = line_sum(half_in.reshape(sections, -1, units), 1)
    sum_in = jnp.stack([lax.dynamic_index_in_dim(sum_in, section, 0, False),
                        lax.ppermute(lax.dynamic_index_in_dim(sum_in, 1 - section, 0, False), "section", swap)])
    sum_in = jnp.where(section == 0, sum_in, sum_in[::-1])

    dq1, dk1, dv1 = attend_back(cross_back, q1, k1, v1, l1, c1, dc1, 4)
    half_two = over_section(half_two, 2)
    one_pairs = [(query_in, dq1), (key_in, dk1)], [(key_in, dv1), (c1, d_carried)]
    send_one = [to_core(pairs) for pairs in one_pairs]
    dq1, dk1, dv1, send_one = together((dq1, dk1, dv1, send_one))
    grad_query_in = nt(dq1, wq[0])
    grad_key_in = nt(dk1, wk[0]) + nt(dv1, wv[0])
    dq1, dk1, dv1, grad_query_in, grad_key_in = together((dq1, dk1, dv1, grad_query_in, grad_key_in))
    one_pairs = [(query_in, dq1), (key_in, dk1)], [(key_in, dv1), (c1, d_carried)]
    half_one = [of_chip(pairs, sent) for pairs, sent in zip(one_pairs, send_one)]
    grad_query_in, grad_key_in, half_one, half_two = together((grad_query_in, grad_key_in, half_one, half_two))
    half_two = over_side(half_two, 2)
    grad_pooled, gain_query = norm_backward(pooled, query_scale, gains[0, 0], grad_query_in)
    per_patch = (grad_pooled + d_carried.astype(F32)) / count
    per_patch = per_patch.astype(BF).reshape(rows, PATCHES, D)
    first_one = over_section(half_one[0], 2), over_side(half_one[1], 2)

    gain_key, kept_bytes, sent_bytes = 0.0, [], []
    for row in range(rows):
        here = slice(row * ROW_BYTES, (row + 1) * ROW_BYTES)
        grad_wide, gain = norm_backward(wide[here], key_scale[here], gains[0, 1], grad_key_in[here])
        grad_bytes = (grad_wide + tn(member[row], per_patch[row])).astype(BF)
        gain_key = gain_key + gain
        kept_bytes.append(lax.dynamic_slice_in_dim(grad_bytes, section * half, half, 1))
        sent_bytes.append(lax.dynamic_slice_in_dim(grad_bytes, (1 - section) * half, half, 1))
    sent_bytes[-1], first_one, half_two = together((sent_bytes[-1], first_one, half_two))
    sum_two = line_sum(half_two, 1)
    got_bytes = [lax.ppermute(sent, "section", swap) for sent in sent_bytes]
    half_one = jnp.concatenate([over_side(first_one[0], 2), over_section(first_one[1], 2)], axis=0)
    half_one, sum_two, got_bytes[:-1] = together((half_one, sum_two, got_bytes[:-1]))
    sum_one = line_sum(half_one, 1)

    def of_group(part):
        every = lax.all_gather(part, "group", axis=0, tiled=False)
        return [every[index] for index in range(groups)]

    def laid_out(parts, order):
        return jnp.concatenate([parts[index] for index in order], axis=-1).astype(F32)

    ffn_gdown = laid_out(of_group(sum_down), (0, 2, 1, 3))
    every = of_group(sum_in)
    ffn_gin = jnp.concatenate(
        [laid_out([every[at][t] for at in (2 * y, 2 * y + 1) for t in range(sections)], range(4)) for y in (0, 1)],
        axis=0,
    )

    gain_grads = jnp.stack([gain_query, gain_key, gain_normed, gain_mix])
    for axis, pairs in (("group", core_pairs), ("group", side_pairs), ("section", swap)):
        gain_grads = gain_grads + lax.ppermute(gain_grads, axis, pairs)
        gain_grads, got_bytes = together((gain_grads, got_bytes))
    gain_grads = jnp.sum(lax.all_gather(gain_grads, "dp", axis=0, tiled=False), axis=0)
    sum_one, gain_grads, got_bytes, ffn_gin, ffn_gdown = together(
        (sum_one, gain_grads, got_bytes, ffn_gin, ffn_gdown)
    )
    bytes_out = in_order(section, jnp.stack(kept_bytes), jnp.stack(got_bytes))
    bytes_out = bytes_out.reshape(sections * rows, ROW_BYTES, half)

    kept = jnp.where(section == 0, sum_one, sum_two)
    sent = jnp.where(section == 0, sum_two, sum_one)
    got = lax.ppermute(sent, "section", swap)
    eighths = jnp.where(
        section == 0, jnp.concatenate([kept, got], axis=2), jnp.concatenate([got, kept], axis=2)
    )
    width = eighths.shape[2] // 2
    parts = [piece for every in of_group(eighths) for piece in (every[..., :width], every[..., width:])]
    section_first = laid_out(parts, (0, 4, 1, 5, 2, 6, 3, 7))
    side_first = laid_out([part[2:] for part in parts], (0, 1, 4, 5, 2, 3, 6, 7))
    last = jnp.where(section == 0, side_first, section_first[2:])
    grad_qkv = jnp.concatenate([section_first[:2], last[:1]], axis=0)[None]

    gain_grads = lax.dynamic_slice_in_dim(gain_grads.reshape(2, 2, D), section, 1, 0)
    width = D // lax.axis_size("dp")
    gain_out = lax.dynamic_slice_in_dim(gain_grads, lax.axis_index("dp") * width, width, 2)
    return (latents_out, bytes_out, grad_qkv, last[1:], gain_out, ffn_gin, ffn_gdown)


def solution(mesh):
    in_specs = (
        P(("group", "dp"), None, None),
        P(("group", "dp"), None),
        P(("group", "dp"), None),
        P("section", None, "dp", None),
        P("section", "dp", None),
        P("section", None, None),
        P(("section", "dp"), None),
        P(("section", "dp"), None),
        P(("group", "dp"), None, None),
    )
    out_specs = (
        P(("group", "dp"), None, "section"),
        P(("group", "dp"), None, "section"),
        P("section", None, "dp", None),
        P("section", "dp", None),
        P("section", None, "dp"),
        P(("section", "dp"), None),
        P(("section", "dp"), None),
    )
    return jax.shard_map(shards, mesh=mesh, in_specs=in_specs, out_specs=out_specs, check_vma=False)
```

```python
import functools

import jax
import jax.numpy as jnp
from jax import lax
from jax.experimental import pallas as pl
from jax.experimental.pallas import tpu as pltpu
from jax.sharding import PartitionSpec as P

D = 1024
HEADS = 16
HEAD_DIM = 64
PAIR = 2 * HEAD_DIM
PAIRS = HEADS // 2
FF = 2816
ROW_BYTES = 1024
PATCHES = 256
QT = 128
TILES = PATCHES // QT
CAUSAL_SPANS = ((0, 1), (0, 2))

EPS = 1e-05
SCALE = HEAD_DIM ** (-0.5)
EXCLUDED = -1e30

BF = jnp.bfloat16
F32 = jnp.float32


def nn(left, right):
    return jnp.dot(left, right, preferred_element_type=F32)


def tn(left, right):
    return lax.dot_general(left, right, (((0,), (0,)), ((), ())), preferred_element_type=F32)


def nt(left, right):
    return lax.dot_general(left, right, (((1,), (1,)), ((), ())), preferred_element_type=F32)


def two_heads(block):
    lane = lax.broadcasted_iota(jnp.int32, block.shape, 1)
    zero = jnp.zeros_like(block)
    first = lane < HEAD_DIM
    return jnp.concatenate([jnp.where(first, block, zero), jnp.where(first, zero, block)], axis=0)


def own_lanes(both):
    picked = jnp.concatenate([both[:HEAD_DIM, :QT], both[HEAD_DIM:, QT:]], axis=0)
    return picked.T


def twice(row):
    return jnp.concatenate([row, row], axis=1)


def fill_bias(keys, lo_ref, hi_ref, bias_ref):
    at = lax.broadcasted_iota(jnp.int32, (keys, QT), 0)
    for tile in range(TILES):
        own = pl.ds(tile * QT, QT)
        inside = (at >= lo_ref[0, :, own]) & (at < hi_ref[0, :, own])
        bias_ref[tile] = jnp.where(inside, 0.0, EXCLUDED)


def over_chunks(spans, tile, bounds, body, init):
    if spans is None:
        return lax.fori_loop(*bounds, body, init)
    for j in range(*spans[tile]):
        init = body(j, init)
    return init


def chunk_at(spans, chunk, j):
    return pl.ds(j * chunk if spans is not None else pl.multiple_of(j * chunk, chunk), chunk)


def attend_kernel(
    chunk, spans, first_ref, stop_ref, lo_ref, hi_ref, q_ref, k_ref, v_ref, c_ref, l_ref, bias_ref, s_ref
):
    row = pl.program_id(0)
    pairs = range(q_ref.shape[1] // PAIR)
    lanes = [pl.ds(pair * PAIR, PAIR) for pair in pairs]
    pl.when(pl.program_id(1) == 0)(lambda: fill_bias(k_ref.shape[0], lo_ref, hi_ref, bias_ref))
    for tile in range(TILES):
        own = pl.ds(tile * QT, QT)
        queries = [two_heads(q_ref[own, at].astype(F32) * SCALE).astype(BF) for at in lanes]
        bounds = (first_ref[row, tile], stop_ref[row, tile])

        def scores(j, tops):
            here = chunk_at(spans, chunk, j)
            bias = twice(bias_ref[tile, here, :])
            out = []
            for pair in pairs:
                part = nt(k_ref[here, lanes[pair]], queries[pair]) + bias
                s_ref[pair, here, :] = part
                out.append(jnp.maximum(tops[pair], jnp.max(part, axis=0, keepdims=True)))
            return tuple(out)

        tops = (jnp.full((1, 2 * QT), EXCLUDED, F32),) * len(pairs)
        tops = over_chunks(spans, tile, bounds, scores, tops)

        def context(j, sums):
            here = chunk_at(spans, chunk, j)
            out = []
            for pair in pairs:
                total, acc = sums[pair]
                weight = jnp.exp(s_ref[pair, here, :] - tops[pair])
                total = total + jnp.sum(weight, axis=0, keepdims=True)
                out.append((total, acc + tn(v_ref[here, lanes[pair]], weight.astype(BF))))
            return tuple(out)

        sums = ((jnp.zeros((1, 2 * QT), F32), jnp.zeros((PAIR, 2 * QT), F32)),) * len(pairs)
        sums = over_chunks(spans, tile, bounds, context, sums)
        for pair in pairs:
            total, acc = sums[pair]
            c_ref[own, lanes[pair]] = own_lanes(acc / total).astype(BF)
            l_ref[0, pair, tile : tile + 1, :] = tops[pair] + jnp.log(total)


def attend_back_kernel(
    chunk, spans, first_ref, stop_ref, lo_ref, hi_ref, q_ref, k_ref, v_ref, l_ref, c_ref, dc_ref,
    dq_ref, dk_ref, dv_ref, bias_ref, dk_acc, dv_acc,
):
    row = pl.program_id(0)
    pairs = range(q_ref.shape[1] // PAIR)
    lanes = [pl.ds(pair * PAIR, PAIR) for pair in pairs]
    pl.when(pl.program_id(1) == 0)(lambda: fill_bias(k_ref.shape[0], lo_ref, hi_ref, bias_ref))
    dk_acc[...] = jnp.zeros_like(dk_acc)
    dv_acc[...] = jnp.zeros_like(dv_acc)
    for tile in range(TILES):
        own = pl.ds(tile * QT, QT)
        queries, grads, deltas, logs = [], [], [], []
        for pair in pairs:
            queries.append(two_heads(q_ref[own, lanes[pair]].astype(F32) * SCALE).astype(BF))
            grad = dc_ref[own, lanes[pair]].astype(F32)
            inner = (grad * c_ref[own, lanes[pair]].astype(F32)).T
            heads = [jnp.sum(part, axis=0, keepdims=True) for part in (inner[:HEAD_DIM], inner[HEAD_DIM:])]
            deltas.append(jnp.concatenate(heads, axis=1))
            grads.append(two_heads(grad).astype(BF))
            logs.append(l_ref[0, pair, tile : tile + 1, :])

        def step(j, accs):
            here = chunk_at(spans, chunk, j)
            bias = twice(bias_ref[tile, here, :])
            out = []
            for pair in pairs:
                keys = k_ref[here, lanes[pair]]
                prob = jnp.exp(nt(keys, queries[pair]) + bias - logs[pair])
                slope = prob * (nt(v_ref[here, lanes[pair]], grads[pair]) - deltas[pair])
                slope = slope.astype(BF)
                dv_acc[here, lanes[pair]] += nn(prob.astype(BF), grads[pair])
                dk_acc[here, lanes[pair]] += nn(slope, queries[pair])
                out.append(accs[pair] + tn(keys, slope))
            return tuple(out)

        bounds = (first_ref[row, tile], stop_ref[row, tile])
        accs = (jnp.zeros((PAIR, 2 * QT), F32),) * len(pairs)
        accs = over_chunks(spans, tile, bounds, step, accs)
        for pair in pairs:
            dq_ref[own, lanes[pair]] = (own_lanes(accs[pair]) * SCALE).astype(BF)
    dk_ref[...] = dk_acc[...].astype(BF)
    dv_ref[...] = dv_acc[...].astype(BF)


def attention_specs(keys, wide):
    per_query = pl.BlockSpec((PATCHES, wide * PAIR), lambda r, h, *_: (r, h))
    per_key = pl.BlockSpec((keys, wide * PAIR), lambda r, h, *_: (r, h))
    bound = pl.BlockSpec((1, 1, PATCHES), lambda r, h, *_: (r, 0, 0))
    logs = pl.BlockSpec((1, wide, TILES, 2 * QT), lambda r, h, *_: (r, h, 0, 0))
    return per_query, per_key, bound, logs


def kernel_cost(q, k, products):
    scores = q.shape[0] * k.shape[0] // (q.shape[0] // PATCHES) * HEADS
    return pl.CostEstimate(
        flops=products * 2 * scores * 256, bytes_accessed=2 * q.nbytes + 4 * k.nbytes, transcendentals=scores
    )


def attend(bounds, q, k, v, wide, spans=None):
    first, stop, lo, hi, chunk = bounds
    rows = lo.shape[0]
    keys = k.shape[0] // rows
    per_query, per_key, bound, logs = attention_specs(keys, wide)
    return pl.pallas_call(
        functools.partial(attend_kernel, chunk, spans),
        grid_spec=pltpu.PrefetchScalarGridSpec(
            num_scalar_prefetch=2,
            grid=(rows, PAIRS // wide),
            in_specs=[bound, bound, per_query, per_key, per_key],
            out_specs=[per_query, logs],
            scratch_shapes=[pltpu.VMEM((TILES, keys, QT), F32), pltpu.VMEM((wide, keys, 2 * QT), F32)],
        ),
        out_shape=[
            jax.ShapeDtypeStruct(q.shape, BF),
            jax.ShapeDtypeStruct((rows, PAIRS, TILES, 2 * QT), F32),
        ],
        compiler_params=pltpu.CompilerParams(vmem_limit_bytes=48 << 20),
        cost_estimate=kernel_cost(q, k, 2),
        name="attend",
    )(first, stop, lo, hi, q, k, v)


def attend_back(bounds, q, k, v, logsum, context, grads, wide, spans=None):
    first, stop, lo, hi, chunk = bounds
    rows = lo.shape[0]
    keys = k.shape[0] // rows
    per_query, per_key, bound, logs = attention_specs(keys, wide)
    return pl.pallas_call(
        functools.partial(attend_back_kernel, chunk, spans),
        grid_spec=pltpu.PrefetchScalarGridSpec(
            num_scalar_prefetch=2,
            grid=(rows, PAIRS // wide),
            in_specs=[bound, bound, per_query, per_key, per_key, logs, per_query, per_query],
            out_specs=[per_query, per_key, per_key],
            scratch_shapes=[pltpu.VMEM((TILES, keys, QT), F32)] + [pltpu.VMEM((keys, wide * PAIR), F32)] * 2,
        ),
        out_shape=[
            jax.ShapeDtypeStruct(q.shape, BF),
            jax.ShapeDtypeStruct(k.shape, BF),
            jax.ShapeDtypeStruct(k.shape, BF),
        ],
        compiler_params=pltpu.CompilerParams(vmem_limit_bytes=48 << 20),
        cost_estimate=kernel_cost(q, k, 5),
        name="attend_back",
    )(first, stop, lo, hi, q, k, v, logsum, context, grads)


def scale_of(values):
    return lax.rsqrt(jnp.mean(values * values, axis=-1, keepdims=True) + EPS)


def norm_backward(values, row_scale, gain_row, incoming):
    weighted = incoming * gain_row
    projection = jnp.mean(weighted * values, axis=-1, keepdims=True)
    grad_values = row_scale * weighted - values * (row_scale * row_scale * row_scale) * projection
    grad_gain = jnp.sum(incoming * values * row_scale, axis=0)
    return grad_values, grad_gain


def chunk_bounds(lo, hi, chunk):
    first = lo[:, ::QT] // chunk
    stop = (hi[:, QT - 1 :: QT] + chunk - 1) // chunk
    return first, stop, lo[:, None, :], hi[:, None, :], chunk


def shards(
    byte_states, patch_lengths, patch_docs, attn_qkv, attn_out, norm_gains, ffn_in, ffn_down, cotangent
):
    section = lax.axis_index("section")
    group = lax.axis_index("group")
    sections = lax.axis_size("section")
    groups = lax.axis_size("group")
    core, side = group % 2, group // 2

    core_pairs = [(0, 1), (1, 0), (2, 3), (3, 2)]
    side_pairs = [(0, 2), (1, 3), (2, 0), (3, 1)]
    swap = [(0, 1), (1, 0)]
    together = lax.optimization_barrier

    four = jnp.concatenate([attn_qkv[0], attn_out], axis=0)
    matrix = lax.dynamic_index_in_dim(four, group, 0, keepdims=False)
    matrices = lax.all_gather(matrix, ("section", "group", "dp"), axis=0, tiled=True)

    gains = lax.all_gather(norm_gains, "section", axis=0, tiled=True)

    def quarter_of(shard):
        height = shard.shape[0] // groups
        return lax.dynamic_slice_in_dim(shard, group * height, height, 0)

    def in_order(part, own, got):
        return jnp.where(part == 0, jnp.stack([own, got]), jnp.stack([got, own]))

    def both(values, part, axis, pairs):
        return in_order(part, values, lax.ppermute(values, axis, pairs))

    units = FF // sections

    def of_units(values, part):
        halves = [lax.dynamic_slice_in_dim(values, at + part * units, units, 1) for at in (0, FF)]
        return jnp.concatenate(halves, axis=1)

    quarter = quarter_of(ffn_in)
    got = lax.ppermute(of_units(quarter, 1 - section), "section", swap)
    w_in = in_order(section, of_units(quarter, section), got)
    w_in = lax.all_gather(w_in, ("dp", "group"), axis=1, tiled=True).reshape(D, 2 * units)

    line, place = lax.axis_size("dp"), lax.axis_index("dp")
    quarter = quarter_of(ffn_down)
    down = jnp.zeros((line,) + quarter.shape, BF)
    for step in range(line):
        moved = lax.ppermute(quarter, "dp", [(i, (i + step) % line) for i in range(line)]) if step else quarter
        down = lax.dynamic_update_slice_in_dim(down, moved[None], (place - step) % line, 0)
    matrices = matrices.reshape(sections, groups, D, D)
    wq, wk, wv, wo = [matrices[:, index] for index in range(4)]

    rows = byte_states.shape[0] // sections
    mine = lambda a: lax.dynamic_slice_in_dim(a, section * rows, rows, 0)
    states, lengths, docs, cot = [mine(a) for a in (byte_states, patch_lengths, patch_docs, cotangent)]
    tokens = rows * PATCHES
    cot = cot.reshape(tokens, D)
    other_cot = lax.dynamic_slice_in_dim(cotangent, (1 - section) * rows, rows, 0).reshape(tokens, D)
    cots = jnp.concatenate([cot, other_cot], axis=0)

    ends = jnp.cumsum(lengths, axis=1)
    earlier = docs[:, None, :] < docs[:, :, None]
    doc_start = jnp.sum(jnp.where(earlier, lengths[:, None, :], 0), axis=2)
    doc_first = jnp.sum(earlier.astype(jnp.int32), axis=2)
    cross, cross_back = chunk_bounds(doc_start, ends, 256), chunk_bounds(doc_start, ends, 512)
    ids = jnp.broadcast_to(lax.iota(jnp.int32, PATCHES) + 1, doc_first.shape)
    causal = chunk_bounds(doc_first, ids, 128)
    positions = lax.iota(jnp.int32, ROW_BYTES)
    member = (positions < ends[:, :, None]) & (positions >= (ends - lengths)[:, :, None])
    member = member.astype(BF)
    count = lengths.astype(F32).reshape(rows * PATCHES, 1)

    pooled = jnp.einsum("rpb,rbd->rpd", member, states, preferred_element_type=F32)
    pooled = pooled.reshape(rows * PATCHES, D) / count
    wide = states.reshape(rows * ROW_BYTES, D).astype(F32)
    query_scale, key_scale = scale_of(pooled), scale_of(wide)
    query_in = (pooled * query_scale * gains[0, 0]).astype(BF)
    key_in = (wide * key_scale * gains[0, 1]).astype(BF)
    q1 = nn(query_in, wq[0]).astype(BF)
    k1 = nn(key_in, wk[0]).astype(BF)
    v1 = nn(key_in, wv[0]).astype(BF)
    v1, down = together((v1, down))
    down = both(down, side, "group", side_pairs)
    c1, l1 = attend(cross, q1, k1, v1, 8)
    carried = (pooled + nn(c1, wo[0])).astype(BF)

    carried_wide = carried.astype(F32)
    first_scale = scale_of(carried_wide)
    normed_in = (carried_wide * first_scale * gains[1, 0]).astype(BF)
    q2 = nn(normed_in, wq[1]).astype(BF)
    k2 = nn(normed_in, wk[1]).astype(BF)
    v2 = nn(normed_in, wv[1]).astype(BF)
    c2, l2 = attend(causal, q2, k2, v2, 8, CAUSAL_SPANS)
    c2, down = together((c2, down))
    down = both(down, core, "group", core_pairs)
    w_down = down.transpose(2, 1, 0, 3, 4).reshape(units, D)
    residual = carried_wide + nn(c2, wo[1])
    second_scale = scale_of(residual)
    mix_in = (residual * second_scale * gains[1, 1]).astype(BF)
    mixed = jnp.concatenate([mix_in, lax.ppermute(mix_in, "section", swap)], axis=0)
    gate_up = nn(mixed, w_in)
    gate, up = gate_up[:, :units], gate_up[:, units:]
    sig = jax.nn.sigmoid(gate)
    hidden = (gate * sig * up).astype(BF)

    grad_hidden = nt(cots, w_down)
    grad_gate = grad_hidden * up * sig * (1.0 + gate * (1.0 - sig))
    grad_up = grad_hidden * gate * sig
    dgu = jnp.concatenate([grad_gate, grad_up], axis=1).astype(BF)

    def exchanged(values, axis, part, pairs, where):
        size = values.shape[where] // 2
        other = lax.dynamic_slice_in_dim(values, (1 - part) * size, size, where)
        own = lax.dynamic_slice_in_dim(values, part * size, size, where)
        return (own.astype(F32) + lax.ppermute(other, axis, pairs).astype(F32)).astype(BF)

    def over_section(values, where):
        return exchanged(values, "section", section, swap, where)

    def over_side(values, where):
        return exchanged(values, "group", side, side_pairs, where)

    def columns(values, part):
        size = values.shape[-1] // 2
        return lax.dynamic_slice_in_dim(values, part * size, size, values.ndim - 1)

    def line_sum(values, where):
        return lax.psum_scatter(values, "dp", scatter_dimension=where, tiled=True)

    def products(pairs, part):
        out = [tn(left, columns(right, part)) for left, right in pairs]
        return out[0] if len(out) == 1 else jnp.stack(out)

    def to_core(pairs):
        return products(pairs, 1 - core).astype(BF)

    def of_chip(pairs, sent):
        got = lax.ppermute(sent, "group", core_pairs)
        return (products(pairs, core) + got.astype(F32)).astype(BF)

    in_pairs, down_pairs = [(mixed, dgu)], [(hidden, cots)]
    mix_other = nt(dgu[tokens:], w_in).astype(BF)
    send_in, send_down = to_core(in_pairs), to_core(down_pairs)
    dgu_own, mix_other, send_in, send_down = together((dgu[:tokens], mix_other, send_in, send_down))
    mix_got = lax.ppermute(mix_other, "section", swap)

    half = D // sections
    parts = nn(hidden, w_down)
    parts = jnp.concatenate([residual + parts[:tokens], parts[tokens:]], axis=0)
    sent = lax.dynamic_slice_in_dim(parts, (1 - section) * half, half, 1).astype(BF)
    kept = lax.dynamic_slice_in_dim(parts, section * half, half, 1)
    dgu_own, sent = together((dgu_own, sent))
    got = lax.ppermute(sent, "section", swap)

    half_in, half_down = of_chip(in_pairs, send_in), of_chip(down_pairs, send_down)
    mix_got, half_in, half_down = together((mix_got, half_in, half_down))
    grad_mixed = nt(dgu_own, w_in) + mix_got.astype(F32)
    grad_mix, gain_mix = norm_backward(residual, second_scale, gains[1, 1], grad_mixed)
    grad_residual = grad_mix + cot.astype(F32)
    branch = grad_residual.astype(BF)
    dc2 = nt(branch, wo[1]).astype(BF)

    dq2, dk2, dv2 = attend_back(causal, q2, k2, v2, l2, c2, dc2, 8, CAUSAL_SPANS)
    two_pairs = [(normed_in, dq2), (normed_in, dk2), (normed_in, dv2), (c2, branch)]
    send_two = to_core(two_pairs)
    dq2, dk2, dv2, send_two = together((dq2, dk2, dv2, send_two))
    grad_normed = nt(dq2, wq[1]) + nt(dk2, wk[1]) + nt(dv2, wv[1])
    grad_carried, gain_normed = norm_backward(carried_wide, first_scale, gains[1, 0], grad_normed)
    d_carried = (grad_residual + grad_carried).astype(BF)
    dc1 = nt(d_carried, wo[0]).astype(BF)
    half_in = over_side(half_in.reshape(sections, line, 2, -1, units), 2)
    half_two = of_chip(two_pairs, send_two)
    dc1, half_in, half_two, got = together((dc1, half_in, half_two, got))
    got = got.astype(F32)
    latents = in_order(section, kept[:tokens] + got[tokens:], kept[tokens:] + got[:tokens])
    latents_out = latents.astype(BF).reshape(sections * rows, PATCHES, half)
    sum_down = over_side(line_sum(half_down, 0), 1)
    sum_in = line_sum(half_in.reshape(sections, -1, units), 1)
    sum_in = jnp.stack([lax.dynamic_index_in_dim(sum_in, section, 0, False),
                        lax.ppermute(lax.dynamic_index_in_dim(sum_in, 1 - section, 0, False), "section", swap)])
    sum_in = jnp.where(section == 0, sum_in, sum_in[::-1])

    dq1, dk1, dv1 = attend_back(cross_back, q1, k1, v1, l1, c1, dc1, 4)
    half_two = over_section(half_two, 2)
    one_pairs = [(query_in, dq1), (key_in, dk1)], [(key_in, dv1), (c1, d_carried)]
    send_one = [to_core(pairs) for pairs in one_pairs]
    dq1, dk1, dv1, send_one, half_two = together((dq1, dk1, dv1, send_one, half_two))
    half_two = over_side(half_two, 2)
    grad_query_in = nt(dq1, wq[0])
    grad_key_in = nt(dk1, wk[0]) + nt(dv1, wv[0])
    dq1, dk1, dv1, grad_query_in, grad_key_in = together((dq1, dk1, dv1, grad_query_in, grad_key_in))
    one_pairs = [(query_in, dq1), (key_in, dk1)], [(key_in, dv1), (c1, d_carried)]
    half_one = [of_chip(pairs, sent) for pairs, sent in zip(one_pairs, send_one)]
    grad_query_in, grad_key_in, half_one, half_two = together((grad_query_in, grad_key_in, half_one, half_two))
    sum_two = line_sum(half_two, 1)
    half_one = over_section(half_one[0], 2), over_side(half_one[1], 2)
    grad_pooled, gain_query = norm_backward(pooled, query_scale, gains[0, 0], grad_query_in)
    grad_wide, gain_key = norm_backward(wide, key_scale, gains[0, 1], grad_key_in)
    per_patch = (grad_pooled + d_carried.astype(F32)) / count
    spread_back = jnp.einsum(
        "rpb,rpd->rbd", member, per_patch.astype(BF).reshape(rows, PATCHES, D), preferred_element_type=F32
    )
    byte_grads = (grad_wide + spread_back.reshape(rows * ROW_BYTES, D)).astype(BF)
    byte_grads, half_one, sum_two = together((byte_grads, half_one, sum_two))
    byte_grads = byte_grads.reshape(rows, ROW_BYTES, D)
    other = lax.dynamic_slice_in_dim(byte_grads, (1 - section) * half, half, 2)
    own = lax.dynamic_slice_in_dim(byte_grads, section * half, half, 2)
    got = lax.ppermute(other, "section", swap)
    half_one = jnp.concatenate([over_side(half_one[0], 2), over_section(half_one[1], 2)], axis=0)
    sum_one = line_sum(half_one, 1)
    sum_one, got = together((sum_one, got))
    bytes_out = in_order(section, own, got).reshape(sections * rows, ROW_BYTES, half)

    def of_group(part):
        every = lax.all_gather(part, "group", axis=0, tiled=False)
        return [every[index] for index in range(groups)]

    def laid_out(parts, order):
        return jnp.concatenate([parts[index] for index in order], axis=-1).astype(F32)

    ffn_gdown = laid_out(of_group(sum_down), (0, 2, 1, 3))
    every = of_group(sum_in)
    ffn_gin = jnp.concatenate(
        [laid_out([every[at][t] for at in (2 * y, 2 * y + 1) for t in range(sections)], range(4)) for y in (0, 1)],
        axis=0,
    )

    kept = jnp.where(section == 0, sum_one, sum_two)
    sent = jnp.where(section == 0, sum_two, sum_one)
    got = lax.ppermute(sent, "section", swap)
    eighths = jnp.where(
        section == 0, jnp.concatenate([kept, got], axis=2), jnp.concatenate([got, kept], axis=2)
    )
    width = eighths.shape[2] // 2
    parts = [piece for every in of_group(eighths) for piece in (every[..., :width], every[..., width:])]
    section_first = laid_out(parts, (0, 4, 1, 5, 2, 6, 3, 7))
    side_first = laid_out([part[2:] for part in parts], (0, 1, 4, 5, 2, 3, 6, 7))
    last = jnp.where(section == 0, side_first, section_first[2:])
    grad_qkv = jnp.concatenate([section_first[:2], last[:1]], axis=0)[None]

    gain_grads = jnp.stack([gain_query, gain_key, gain_normed, gain_mix])
    for axis, pairs in (("group", core_pairs), ("group", side_pairs), ("section", swap)):
        gain_grads = gain_grads + lax.ppermute(gain_grads, axis, pairs)
    gain_grads = jnp.sum(lax.all_gather(gain_grads, "dp", axis=0, tiled=False), axis=0)
    gain_grads = lax.dynamic_slice_in_dim(gain_grads.reshape(2, 2, D), section, 1, 0)
    width = D // lax.axis_size("dp")
    gain_out = lax.dynamic_slice_in_dim(gain_grads, lax.axis_index("dp") * width, width, 2)
    return (latents_out, bytes_out, grad_qkv, last[1:], gain_out, ffn_gin, ffn_gdown)


def solution(mesh):
    in_specs = (
        P(("group", "dp"), None, None),
        P(("group", "dp"), None),
        P(("group", "dp"), None),
        P("section", None, "dp", None),
        P("section", "dp", None),
        P("section", None, None),
        P(("section", "dp"), None),
        P(("section", "dp"), None),
        P(("group", "dp"), None, None),
    )
    out_specs = (
        P(("group", "dp"), None, "section"),
        P(("group", "dp"), None, "section"),
        P("section", None, "dp", None),
        P("section", "dp", None),
        P("section", None, "dp"),
        P(("section", "dp"), None),
        P(("section", "dp"), None),
    )
    return jax.shard_map(shards, mesh=mesh, in_specs=in_specs, out_specs=out_specs, check_vma=False)
```

```python
import functools

import jax
import jax.numpy as jnp
from jax import lax
from jax.experimental import pallas as pl
from jax.experimental.pallas import tpu as pltpu
from jax.sharding import PartitionSpec as P

D = 1024
HEADS = 16
HEAD_DIM = 64
PAIR = 2 * HEAD_DIM
PAIRS = HEADS // 2
FF = 2816
ROW_BYTES = 1024
PATCHES = 256
QT = 128
TILES = PATCHES // QT
CAUSAL_SPANS = ((0, 1), (0, 2))

EPS = 1e-05
SCALE = HEAD_DIM ** (-0.5)
EXCLUDED = -1e30

BF = jnp.bfloat16
F32 = jnp.float32


def nn(left, right):
    return jnp.dot(left, right, preferred_element_type=F32)


def tn(left, right):
    return lax.dot_general(left, right, (((0,), (0,)), ((), ())), preferred_element_type=F32)


def nt(left, right):
    return lax.dot_general(left, right, (((1,), (1,)), ((), ())), preferred_element_type=F32)


def two_heads(block):
    lane = lax.broadcasted_iota(jnp.int32, block.shape, 1)
    zero = jnp.zeros_like(block)
    first = lane < HEAD_DIM
    return jnp.concatenate([jnp.where(first, block, zero), jnp.where(first, zero, block)], axis=0)


def own_lanes(both):
    picked = jnp.concatenate([both[:HEAD_DIM, :QT], both[HEAD_DIM:, QT:]], axis=0)
    return picked.T


def twice(row):
    return jnp.concatenate([row, row], axis=1)


def fill_bias(keys, lo_ref, hi_ref, bias_ref):
    at = lax.broadcasted_iota(jnp.int32, (keys, QT), 0)
    for tile in range(TILES):
        own = pl.ds(tile * QT, QT)
        inside = (at >= lo_ref[0, :, own]) & (at < hi_ref[0, :, own])
        bias_ref[tile] = jnp.where(inside, 0.0, EXCLUDED)


def over_chunks(spans, tile, bounds, body, init):
    if spans is None:
        return lax.fori_loop(*bounds, body, init)
    for j in range(*spans[tile]):
        init = body(j, init)
    return init


def chunk_at(spans, chunk, j):
    return pl.ds(j * chunk if spans is not None else pl.multiple_of(j * chunk, chunk), chunk)


def attend_kernel(
    chunk, spans, first_ref, stop_ref, lo_ref, hi_ref, q_ref, k_ref, v_ref, c_ref, l_ref, bias_ref, s_ref
):
    row = pl.program_id(0)
    pairs = range(q_ref.shape[1] // PAIR)
    lanes = [pl.ds(pair * PAIR, PAIR) for pair in pairs]
    pl.when(pl.program_id(1) == 0)(lambda: fill_bias(k_ref.shape[0], lo_ref, hi_ref, bias_ref))
    for tile in range(TILES):
        own = pl.ds(tile * QT, QT)
        queries = [two_heads(q_ref[own, at].astype(F32) * SCALE).astype(BF) for at in lanes]
        bounds = (first_ref[row, tile], stop_ref[row, tile])

        def scores(j, tops):
            here = chunk_at(spans, chunk, j)
            bias = twice(bias_ref[tile, here, :])
            out = []
            for pair in pairs:
                part = nt(k_ref[here, lanes[pair]], queries[pair]) + bias
                s_ref[pair, here, :] = part
                out.append(jnp.maximum(tops[pair], jnp.max(part, axis=0, keepdims=True)))
            return tuple(out)

        tops = (jnp.full((1, 2 * QT), EXCLUDED, F32),) * len(pairs)
        tops = over_chunks(spans, tile, bounds, scores, tops)

        def context(j, sums):
            here = chunk_at(spans, chunk, j)
            out = []
            for pair in pairs:
                total, acc = sums[pair]
                weight = jnp.exp(s_ref[pair, here, :] - tops[pair])
                total = total + jnp.sum(weight, axis=0, keepdims=True)
                out.append((total, acc + tn(v_ref[here, lanes[pair]], weight.astype(BF))))
            return tuple(out)

        sums = ((jnp.zeros((1, 2 * QT), F32), jnp.zeros((PAIR, 2 * QT), F32)),) * len(pairs)
        sums = over_chunks(spans, tile, bounds, context, sums)
        for pair in pairs:
            total, acc = sums[pair]
            c_ref[own, lanes[pair]] = own_lanes(acc / total).astype(BF)
            l_ref[0, pair, tile : tile + 1, :] = tops[pair] + jnp.log(total)


def attend_back_kernel(
    chunk, spans, first_ref, stop_ref, lo_ref, hi_ref, q_ref, k_ref, v_ref, l_ref, c_ref, dc_ref,
    dq_ref, dk_ref, dv_ref, bias_ref, dk_acc, dv_acc,
):
    row = pl.program_id(0)
    pairs = range(q_ref.shape[1] // PAIR)
    lanes = [pl.ds(pair * PAIR, PAIR) for pair in pairs]
    pl.when(pl.program_id(1) == 0)(lambda: fill_bias(k_ref.shape[0], lo_ref, hi_ref, bias_ref))
    dk_acc[...] = jnp.zeros_like(dk_acc)
    dv_acc[...] = jnp.zeros_like(dv_acc)
    for tile in range(TILES):
        own = pl.ds(tile * QT, QT)
        queries, grads, deltas, logs = [], [], [], []
        for pair in pairs:
            queries.append(two_heads(q_ref[own, lanes[pair]].astype(F32) * SCALE).astype(BF))
            grad = dc_ref[own, lanes[pair]].astype(F32)
            inner = (grad * c_ref[own, lanes[pair]].astype(F32)).T
            heads = [jnp.sum(part, axis=0, keepdims=True) for part in (inner[:HEAD_DIM], inner[HEAD_DIM:])]
            deltas.append(jnp.concatenate(heads, axis=1))
            grads.append(two_heads(grad).astype(BF))
            logs.append(l_ref[0, pair, tile : tile + 1, :])

        def step(j, accs):
            here = chunk_at(spans, chunk, j)
            bias = twice(bias_ref[tile, here, :])
            out = []
            for pair in pairs:
                keys = k_ref[here, lanes[pair]]
                prob = jnp.exp(nt(keys, queries[pair]) + bias - logs[pair])
                slope = prob * (nt(v_ref[here, lanes[pair]], grads[pair]) - deltas[pair])
                slope = slope.astype(BF)
                dv_acc[here, lanes[pair]] += nn(prob.astype(BF), grads[pair])
                dk_acc[here, lanes[pair]] += nn(slope, queries[pair])
                out.append(accs[pair] + tn(keys, slope))
            return tuple(out)

        bounds = (first_ref[row, tile], stop_ref[row, tile])
        accs = (jnp.zeros((PAIR, 2 * QT), F32),) * len(pairs)
        accs = over_chunks(spans, tile, bounds, step, accs)
        for pair in pairs:
            dq_ref[own, lanes[pair]] = (own_lanes(accs[pair]) * SCALE).astype(BF)
    dk_ref[...] = dk_acc[...].astype(BF)
    dv_ref[...] = dv_acc[...].astype(BF)


def attention_specs(keys, wide):
    per_query = pl.BlockSpec((PATCHES, wide * PAIR), lambda r, h, *_: (r, h))
    per_key = pl.BlockSpec((keys, wide * PAIR), lambda r, h, *_: (r, h))
    bound = pl.BlockSpec((1, 1, PATCHES), lambda r, h, *_: (r, 0, 0))
    logs = pl.BlockSpec((1, wide, TILES, 2 * QT), lambda r, h, *_: (r, h, 0, 0))
    return per_query, per_key, bound, logs


def kernel_cost(q, k, products):
    scores = q.shape[0] * k.shape[0] // (q.shape[0] // PATCHES) * HEADS
    return pl.CostEstimate(
        flops=products * 2 * scores * 256, bytes_accessed=2 * q.nbytes + 4 * k.nbytes, transcendentals=scores
    )


def attend(bounds, q, k, v, wide, spans=None):
    first, stop, lo, hi, chunk = bounds
    rows = lo.shape[0]
    keys = k.shape[0] // rows
    per_query, per_key, bound, logs = attention_specs(keys, wide)
    return pl.pallas_call(
        functools.partial(attend_kernel, chunk, spans),
        grid_spec=pltpu.PrefetchScalarGridSpec(
            num_scalar_prefetch=2,
            grid=(rows, PAIRS // wide),
            in_specs=[bound, bound, per_query, per_key, per_key],
            out_specs=[per_query, logs],
            scratch_shapes=[pltpu.VMEM((TILES, keys, QT), F32), pltpu.VMEM((wide, keys, 2 * QT), F32)],
        ),
        out_shape=[
            jax.ShapeDtypeStruct(q.shape, BF),
            jax.ShapeDtypeStruct((rows, PAIRS, TILES, 2 * QT), F32),
        ],
        compiler_params=pltpu.CompilerParams(vmem_limit_bytes=48 << 20),
        cost_estimate=kernel_cost(q, k, 2),
        name="attend",
    )(first, stop, lo, hi, q, k, v)


def attend_back(bounds, q, k, v, logsum, context, grads, wide, spans=None):
    first, stop, lo, hi, chunk = bounds
    rows = lo.shape[0]
    keys = k.shape[0] // rows
    per_query, per_key, bound, logs = attention_specs(keys, wide)
    return pl.pallas_call(
        functools.partial(attend_back_kernel, chunk, spans),
        grid_spec=pltpu.PrefetchScalarGridSpec(
            num_scalar_prefetch=2,
            grid=(rows, PAIRS // wide),
            in_specs=[bound, bound, per_query, per_key, per_key, logs, per_query, per_query],
            out_specs=[per_query, per_key, per_key],
            scratch_shapes=[pltpu.VMEM((TILES, keys, QT), F32)] + [pltpu.VMEM((keys, wide * PAIR), F32)] * 2,
        ),
        out_shape=[
            jax.ShapeDtypeStruct(q.shape, BF),
            jax.ShapeDtypeStruct(k.shape, BF),
            jax.ShapeDtypeStruct(k.shape, BF),
        ],
        compiler_params=pltpu.CompilerParams(vmem_limit_bytes=48 << 20),
        cost_estimate=kernel_cost(q, k, 5),
        name="attend_back",
    )(first, stop, lo, hi, q, k, v, logsum, context, grads)


def scale_of(values):
    return lax.rsqrt(jnp.mean(values * values, axis=-1, keepdims=True) + EPS)


def norm_backward(values, row_scale, gain_row, incoming):
    weighted = incoming * gain_row
    projection = jnp.mean(weighted * values, axis=-1, keepdims=True)
    grad_values = row_scale * weighted - values * (row_scale * row_scale * row_scale) * projection
    grad_gain = jnp.sum(incoming * values * row_scale, axis=0)
    return grad_values, grad_gain


def chunk_bounds(lo, hi, chunk):
    first = lo[:, ::QT] // chunk
    stop = (hi[:, QT - 1 :: QT] + chunk - 1) // chunk
    return first, stop, lo[:, None, :], hi[:, None, :], chunk


def shards(
    byte_states, patch_lengths, patch_docs, attn_qkv, attn_out, norm_gains, ffn_in, ffn_down, cotangent
):
    section = lax.axis_index("section")
    group = lax.axis_index("group")
    sections = lax.axis_size("section")
    groups = lax.axis_size("group")
    core, side = group % 2, group // 2

    core_pairs = [(0, 1), (1, 0), (2, 3), (3, 2)]
    side_pairs = [(0, 2), (1, 3), (2, 0), (3, 1)]
    swap = [(0, 1), (1, 0)]
    together = lax.optimization_barrier

    four = jnp.concatenate([attn_qkv[0], attn_out], axis=0)
    matrix = lax.dynamic_index_in_dim(four, group, 0, keepdims=False)
    matrices = lax.all_gather(matrix, ("section", "group", "dp"), axis=0, tiled=True)

    gains = lax.all_gather(norm_gains, "section", axis=0, tiled=True)

    def quarter_of(shard):
        height = shard.shape[0] // groups
        return lax.dynamic_slice_in_dim(shard, group * height, height, 0)

    def in_order(part, own, got):
        return jnp.where(part == 0, jnp.stack([own, got]), jnp.stack([got, own]))

    def both(values, part, axis, pairs):
        return in_order(part, values, lax.ppermute(values, axis, pairs))

    units = FF // sections

    def of_units(values, part):
        halves = [lax.dynamic_slice_in_dim(values, at + part * units, units, 1) for at in (0, FF)]
        return jnp.concatenate(halves, axis=1)

    quarter = quarter_of(ffn_in)
    got = lax.ppermute(of_units(quarter, 1 - section), "section", swap)
    w_in = in_order(section, of_units(quarter, section), got)
    w_in = lax.all_gather(w_in, ("dp", "group"), axis=1, tiled=True).reshape(D, 2 * units)

    line, place = lax.axis_size("dp"), lax.axis_index("dp")
    quarter = quarter_of(ffn_down)
    down = jnp.zeros((line,) + quarter.shape, BF)
    for step in range(line):
        moved = lax.ppermute(quarter, "dp", [(i, (i + step) % line) for i in range(line)]) if step else quarter
        down = lax.dynamic_update_slice_in_dim(down, moved[None], (place - step) % line, 0)
    matrices = matrices.reshape(sections, groups, D, D)
    wq, wk, wv, wo = [matrices[:, index] for index in range(4)]

    rows = byte_states.shape[0] // sections
    mine = lambda a: lax.dynamic_slice_in_dim(a, section * rows, rows, 0)
    states, lengths, docs, cot = [mine(a) for a in (byte_states, patch_lengths, patch_docs, cotangent)]
    tokens = rows * PATCHES
    cot = cot.reshape(tokens, D)
    other_cot = lax.dynamic_slice_in_dim(cotangent, (1 - section) * rows, rows, 0).reshape(tokens, D)
    cots = jnp.concatenate([cot, other_cot], axis=0)

    ends = jnp.cumsum(lengths, axis=1)
    earlier = docs[:, None, :] < docs[:, :, None]
    doc_start = jnp.sum(jnp.where(earlier, lengths[:, None, :], 0), axis=2)
    doc_first = jnp.sum(earlier.astype(jnp.int32), axis=2)
    cross, cross_back = chunk_bounds(doc_start, ends, 256), chunk_bounds(doc_start, ends, 512)
    ids = jnp.broadcast_to(lax.iota(jnp.int32, PATCHES) + 1, doc_first.shape)
    causal = chunk_bounds(doc_first, ids, 128)
    positions = lax.iota(jnp.int32, ROW_BYTES)
    member = (positions < ends[:, :, None]) & (positions >= (ends - lengths)[:, :, None])
    member = member.astype(BF)
    count = lengths.astype(F32).reshape(rows * PATCHES, 1)

    pooled = jnp.einsum("rpb,rbd->rpd", member, states, preferred_element_type=F32)
    pooled = pooled.reshape(rows * PATCHES, D) / count
    wide = states.reshape(rows * ROW_BYTES, D).astype(F32)
    query_scale, key_scale = scale_of(pooled), scale_of(wide)
    query_in = (pooled * query_scale * gains[0, 0]).astype(BF)
    key_in = (wide * key_scale * gains[0, 1]).astype(BF)
    q1 = nn(query_in, wq[0]).astype(BF)
    k1 = nn(key_in, wk[0]).astype(BF)
    v1 = nn(key_in, wv[0]).astype(BF)
    v1, down = together((v1, down))
    down = both(down, side, "group", side_pairs)
    c1, l1 = attend(cross, q1, k1, v1, 8)
    carried = (pooled + nn(c1, wo[0])).astype(BF)

    carried_wide = carried.astype(F32)
    first_scale = scale_of(carried_wide)
    normed_in = (carried_wide * first_scale * gains[1, 0]).astype(BF)
    q2 = nn(normed_in, wq[1]).astype(BF)
    k2 = nn(normed_in, wk[1]).astype(BF)
    v2 = nn(normed_in, wv[1]).astype(BF)
    c2, l2 = attend(causal, q2, k2, v2, 8, CAUSAL_SPANS)
    c2, down = together((c2, down))
    down = both(down, core, "group", core_pairs)
    w_down = down.transpose(2, 1, 0, 3, 4).reshape(units, D)
    residual = carried_wide + nn(c2, wo[1])
    second_scale = scale_of(residual)
    mix_in = (residual * second_scale * gains[1, 1]).astype(BF)
    mixed = jnp.concatenate([mix_in, lax.ppermute(mix_in, "section", swap)], axis=0)
    gate_up = nn(mixed, w_in)
    gate, up = gate_up[:, :units], gate_up[:, units:]
    sig = jax.nn.sigmoid(gate)
    hidden = (gate * sig * up).astype(BF)

    grad_hidden = nt(cots, w_down)
    grad_gate = grad_hidden * up * sig * (1.0 + gate * (1.0 - sig))
    grad_up = grad_hidden * gate * sig
    dgu = jnp.concatenate([grad_gate, grad_up], axis=1).astype(BF)

    def exchanged(values, axis, part, pairs, where):
        size = values.shape[where] // 2
        other = lax.dynamic_slice_in_dim(values, (1 - part) * size, size, where)
        own = lax.dynamic_slice_in_dim(values, part * size, size, where)
        return (own.astype(F32) + lax.ppermute(other, axis, pairs).astype(F32)).astype(BF)

    def over_section(values, where):
        return exchanged(values, "section", section, swap, where)

    def over_side(values, where):
        return exchanged(values, "group", side, side_pairs, where)

    def columns(values, part):
        size = values.shape[-1] // 2
        return lax.dynamic_slice_in_dim(values, part * size, size, values.ndim - 1)

    def line_sum(values, where):
        return lax.psum_scatter(values, "dp", scatter_dimension=where, tiled=True)

    def products(pairs, part):
        out = [tn(left, columns(right, part)) for left, right in pairs]
        return out[0] if len(out) == 1 else jnp.stack(out)

    def to_core(pairs):
        return products(pairs, 1 - core).astype(BF)

    def of_chip(pairs, sent):
        got = lax.ppermute(sent, "group", core_pairs)
        return (products(pairs, core) + got.astype(F32)).astype(BF)

    in_pairs, down_pairs = [(mixed, dgu)], [(hidden, cots)]
    mix_other = nt(dgu[tokens:], w_in).astype(BF)
    send_in, send_down = to_core(in_pairs), to_core(down_pairs)
    dgu_own, mix_other, send_in, send_down = together((dgu[:tokens], mix_other, send_in, send_down))
    mix_got = lax.ppermute(mix_other, "section", swap)

    half = D // sections
    parts = nn(hidden, w_down)
    parts = jnp.concatenate([residual + parts[:tokens], parts[tokens:]], axis=0)
    sent = lax.dynamic_slice_in_dim(parts, (1 - section) * half, half, 1).astype(BF)
    kept = lax.dynamic_slice_in_dim(parts, section * half, half, 1)
    dgu_own, sent = together((dgu_own, sent))
    got = lax.ppermute(sent, "section", swap)

    half_in, half_down = of_chip(in_pairs, send_in), of_chip(down_pairs, send_down)
    mix_got, half_in, half_down = together((mix_got, half_in, half_down))
    grad_mixed = nt(dgu_own, w_in) + mix_got.astype(F32)
    grad_mix, gain_mix = norm_backward(residual, second_scale, gains[1, 1], grad_mixed)
    grad_residual = grad_mix + cot.astype(F32)
    branch = grad_residual.astype(BF)
    dc2 = nt(branch, wo[1]).astype(BF)

    dq2, dk2, dv2 = attend_back(causal, q2, k2, v2, l2, c2, dc2, 8, CAUSAL_SPANS)
    two_pairs = [(normed_in, dq2), (normed_in, dk2), (normed_in, dv2), (c2, branch)]
    send_two = to_core(two_pairs)
    half_in = over_side(half_in.reshape(sections, line, 2, -1, units), 2)
    sum_down = line_sum(half_down, 0)
    dq2, dk2, dv2, send_two, half_in, sum_down = together((dq2, dk2, dv2, send_two, half_in, sum_down))
    sum_in = line_sum(half_in.reshape(sections, -1, units), 1)
    grad_normed = nt(dq2, wq[1]) + nt(dk2, wk[1]) + nt(dv2, wv[1])
    grad_carried, gain_normed = norm_backward(carried_wide, first_scale, gains[1, 0], grad_normed)
    d_carried = (grad_residual + grad_carried).astype(BF)
    dc1 = nt(d_carried, wo[0]).astype(BF)
    half_two = of_chip(two_pairs, send_two)
    dc1, half_two, got = together((dc1, half_two, got))
    got = got.astype(F32)
    latents = in_order(section, kept[:tokens] + got[tokens:], kept[tokens:] + got[:tokens])
    latents_out = latents.astype(BF).reshape(sections * rows, PATCHES, half)
    dq1, dk1, dv1 = attend_back(cross_back, q1, k1, v1, l1, c1, dc1, 4)
    half_two = over_section(half_two, 2)
    one_pairs = [(query_in, dq1), (key_in, dk1)], [(key_in, dv1), (c1, d_carried)]
    send_one = [to_core(pairs) for pairs in one_pairs]
    dq1, dk1, dv1, send_one, half_two, sum_in, sum_down = together(
        (dq1, dk1, dv1, send_one, half_two, sum_in, sum_down)
    )
    half_two = over_side(half_two, 2)
    sum_in = jnp.stack([lax.dynamic_index_in_dim(sum_in, section, 0, False),
                        lax.ppermute(lax.dynamic_index_in_dim(sum_in, 1 - section, 0, False), "section", swap)])
    sum_in = jnp.where(section == 0, sum_in, sum_in[::-1])

    def gathered(part):
        return lax.all_gather(part, "group", axis=0, tiled=False)

    def laid_out(parts, order):
        return jnp.concatenate([parts[index] for index in order], axis=-1).astype(F32)

    sum_in = gathered(sum_in)
    half_one = [of_chip(pairs, sent) for pairs, sent in zip(one_pairs, send_one)]
    dq1, dk1, dv1, half_one = together((dq1, dk1, dv1, half_one))
    grad_query_in = nt(dq1, wq[0])
    grad_key_in = nt(dk1, wk[0]) + nt(dv1, wv[0])
    half_one = over_section(half_one[0], 2), over_side(half_one[1], 2)
    grad_query_in, grad_key_in, half_one, half_two, sum_in = together(
        (grad_query_in, grad_key_in, half_one, half_two, sum_in)
    )
    sum_two = line_sum(half_two, 1)
    half_one = jnp.concatenate([over_side(half_one[0], 2), over_section(half_one[1], 2)], axis=0)
    half_one, sum_two, sum_down = together((half_one, sum_two, sum_down))
    sum_down = over_side(sum_down, 1)
    sum_one = line_sum(half_one, 1)

    grad_pooled, gain_query = norm_backward(pooled, query_scale, gains[0, 0], grad_query_in)
    grad_wide, gain_key = norm_backward(wide, key_scale, gains[0, 1], grad_key_in)
    per_patch = (grad_pooled + d_carried.astype(F32)) / count
    spread_back = jnp.einsum(
        "rpb,rpd->rbd", member, per_patch.astype(BF).reshape(rows, PATCHES, D), preferred_element_type=F32
    )
    byte_grads = (grad_wide + spread_back.reshape(rows * ROW_BYTES, D)).astype(BF)
    byte_grads = byte_grads.reshape(rows, ROW_BYTES, D)
    other = lax.dynamic_slice_in_dim(byte_grads, (1 - section) * half, half, 2)
    own = lax.dynamic_slice_in_dim(byte_grads, section * half, half, 2)

    gain_grads = jnp.stack([gain_query, gain_key, gain_normed, gain_mix])
    gain_grads = gain_grads + lax.ppermute(gain_grads, "section", swap)
    other, gain_grads = together((other, gain_grads))
    got = [lax.ppermute(other[row], "section", swap) for row in range(rows)]
    for pairs in (core_pairs, side_pairs):
        gain_grads = gain_grads + lax.ppermute(gain_grads, "group", pairs)
    gain_grads = jnp.sum(lax.all_gather(gain_grads, "dp", axis=0, tiled=False), axis=0)

    ffn_gdown = laid_out(gathered(sum_down), (0, 2, 1, 3))
    ffn_gin = jnp.concatenate(
        [laid_out([sum_in[at, t] for at in (2 * y, 2 * y + 1) for t in range(sections)], range(4)) for y in (0, 1)],
        axis=0,
    )
    sum_one, got[0], gain_grads, ffn_gdown = together((sum_one, got[0], gain_grads, ffn_gdown))
    bytes_out = in_order(section, own, jnp.stack(got)).reshape(sections * rows, ROW_BYTES, half)

    kept = jnp.where(section == 0, sum_one, sum_two)
    sent = jnp.where(section == 0, sum_two, sum_one)
    got = lax.ppermute(sent, "section", swap)
    eighths = jnp.where(
        section == 0, jnp.concatenate([kept, got], axis=2), jnp.concatenate([got, kept], axis=2)
    )
    width = eighths.shape[2] // 2
    parts = [piece for every in gathered(eighths) for piece in (every[..., :width], every[..., width:])]
    section_first = laid_out(parts, (0, 4, 1, 5, 2, 6, 3, 7))
    side_first = laid_out([part[2:] for part in parts], (0, 1, 4, 5, 2, 3, 6, 7))
    last = jnp.where(section == 0, side_first, section_first[2:])
    grad_qkv = jnp.concatenate([section_first[:2], last[:1]], axis=0)[None]

    gain_grads = lax.dynamic_slice_in_dim(gain_grads.reshape(2, 2, D), section, 1, 0)
    width = D // lax.axis_size("dp")
    gain_out = lax.dynamic_slice_in_dim(gain_grads, lax.axis_index("dp") * width, width, 2)
    return (latents_out, bytes_out, grad_qkv, last[1:], gain_out, ffn_gin, ffn_gdown)


def solution(mesh):
    in_specs = (
        P(("group", "dp"), None, None),
        P(("group", "dp"), None),
        P(("group", "dp"), None),
        P("section", None, "dp", None),
        P("section", "dp", None),
        P("section", None, None),
        P(("section", "dp"), None),
        P(("section", "dp"), None),
        P(("group", "dp"), None, None),
    )
    out_specs = (
        P(("group", "dp"), None, "section"),
        P(("group", "dp"), None, "section"),
        P("section", None, "dp", None),
        P("section", "dp", None),
        P("section", None, "dp"),
        P(("section", "dp"), None),
        P(("section", "dp"), None),
    )
    return jax.shard_map(shards, mesh=mesh, in_specs=in_specs, out_specs=out_specs, check_vma=False)
```

```python
import functools

import jax
import jax.numpy as jnp
from jax import lax
from jax.experimental import pallas as pl
from jax.experimental.pallas import tpu as pltpu
from jax.sharding import PartitionSpec as P

D = 1024
HEADS = 16
HEAD_DIM = 64
PAIR = 2 * HEAD_DIM
PAIRS = HEADS // 2
FF = 2816
ROW_BYTES = 1024
PATCHES = 256
QT = 128
TILES = PATCHES // QT
CAUSAL_SPANS = ((0, 1), (0, 2))

EPS = 1e-05
SCALE = HEAD_DIM ** (-0.5)
EXCLUDED = -1e30

BF = jnp.bfloat16
F32 = jnp.float32


def nn(left, right):
    return jnp.dot(left, right, preferred_element_type=F32)


def tn(left, right):
    return lax.dot_general(left, right, (((0,), (0,)), ((), ())), preferred_element_type=F32)


def nt(left, right):
    return lax.dot_general(left, right, (((1,), (1,)), ((), ())), preferred_element_type=F32)


def two_heads(block):
    lane = lax.broadcasted_iota(jnp.int32, block.shape, 1)
    zero = jnp.zeros_like(block)
    first = lane < HEAD_DIM
    return jnp.concatenate([jnp.where(first, block, zero), jnp.where(first, zero, block)], axis=0)


def own_lanes(both):
    picked = jnp.concatenate([both[:HEAD_DIM, :QT], both[HEAD_DIM:, QT:]], axis=0)
    return picked.T


def twice(row):
    return jnp.concatenate([row, row], axis=1)


def fill_bias(keys, lo_ref, hi_ref, bias_ref):
    at = lax.broadcasted_iota(jnp.int32, (keys, QT), 0)
    for tile in range(TILES):
        own = pl.ds(tile * QT, QT)
        inside = (at >= lo_ref[0, :, own]) & (at < hi_ref[0, :, own])
        bias_ref[tile] = jnp.where(inside, 0.0, EXCLUDED)


def over_chunks(spans, tile, bounds, body, init):
    if spans is None:
        return lax.fori_loop(*bounds, body, init)
    for j in range(*spans[tile]):
        init = body(j, init)
    return init


def chunk_at(spans, chunk, j):
    return pl.ds(j * chunk if spans is not None else pl.multiple_of(j * chunk, chunk), chunk)


def attend_kernel(
    chunk, spans, first_ref, stop_ref, lo_ref, hi_ref, q_ref, k_ref, v_ref, c_ref, l_ref, bias_ref, s_ref
):
    row = pl.program_id(0)
    pairs = range(q_ref.shape[1] // PAIR)
    lanes = [pl.ds(pair * PAIR, PAIR) for pair in pairs]
    pl.when(pl.program_id(1) == 0)(lambda: fill_bias(k_ref.shape[0], lo_ref, hi_ref, bias_ref))
    for tile in range(TILES):
        own = pl.ds(tile * QT, QT)
        queries = [two_heads(q_ref[own, at].astype(F32) * SCALE).astype(BF) for at in lanes]
        bounds = (first_ref[row, tile], stop_ref[row, tile])

        def scores(j, tops):
            here = chunk_at(spans, chunk, j)
            bias = twice(bias_ref[tile, here, :])
            out = []
            for pair in pairs:
                part = nt(k_ref[here, lanes[pair]], queries[pair]) + bias
                s_ref[pair, here, :] = part
                out.append(jnp.maximum(tops[pair], jnp.max(part, axis=0, keepdims=True)))
            return tuple(out)

        tops = (jnp.full((1, 2 * QT), EXCLUDED, F32),) * len(pairs)
        tops = over_chunks(spans, tile, bounds, scores, tops)

        def context(j, sums):
            here = chunk_at(spans, chunk, j)
            out = []
            for pair in pairs:
                total, acc = sums[pair]
                weight = jnp.exp(s_ref[pair, here, :] - tops[pair])
                total = total + jnp.sum(weight, axis=0, keepdims=True)
                out.append((total, acc + tn(v_ref[here, lanes[pair]], weight.astype(BF))))
            return tuple(out)

        sums = ((jnp.zeros((1, 2 * QT), F32), jnp.zeros((PAIR, 2 * QT), F32)),) * len(pairs)
        sums = over_chunks(spans, tile, bounds, context, sums)
        for pair in pairs:
            total, acc = sums[pair]
            c_ref[own, lanes[pair]] = own_lanes(acc / total).astype(BF)
            l_ref[0, pair, tile : tile + 1, :] = tops[pair] + jnp.log(total)


def attend_back_kernel(
    chunk, spans, first_ref, stop_ref, lo_ref, hi_ref, q_ref, k_ref, v_ref, l_ref, c_ref, dc_ref,
    dq_ref, dk_ref, dv_ref, bias_ref, dk_acc, dv_acc,
):
    row = pl.program_id(0)
    pairs = range(q_ref.shape[1] // PAIR)
    lanes = [pl.ds(pair * PAIR, PAIR) for pair in pairs]
    pl.when(pl.program_id(1) == 0)(lambda: fill_bias(k_ref.shape[0], lo_ref, hi_ref, bias_ref))
    dk_acc[...] = jnp.zeros_like(dk_acc)
    dv_acc[...] = jnp.zeros_like(dv_acc)
    for tile in range(TILES):
        own = pl.ds(tile * QT, QT)
        queries, grads, deltas, logs = [], [], [], []
        for pair in pairs:
            queries.append(two_heads(q_ref[own, lanes[pair]].astype(F32) * SCALE).astype(BF))
            grad = dc_ref[own, lanes[pair]].astype(F32)
            inner = (grad * c_ref[own, lanes[pair]].astype(F32)).T
            heads = [jnp.sum(part, axis=0, keepdims=True) for part in (inner[:HEAD_DIM], inner[HEAD_DIM:])]
            deltas.append(jnp.concatenate(heads, axis=1))
            grads.append(two_heads(grad).astype(BF))
            logs.append(l_ref[0, pair, tile : tile + 1, :])

        def step(j, accs):
            here = chunk_at(spans, chunk, j)
            bias = twice(bias_ref[tile, here, :])
            out = []
            for pair in pairs:
                keys = k_ref[here, lanes[pair]]
                prob = jnp.exp(nt(keys, queries[pair]) + bias - logs[pair])
                slope = prob * (nt(v_ref[here, lanes[pair]], grads[pair]) - deltas[pair])
                slope = slope.astype(BF)
                dv_acc[here, lanes[pair]] += nn(prob.astype(BF), grads[pair])
                dk_acc[here, lanes[pair]] += nn(slope, queries[pair])
                out.append(accs[pair] + tn(keys, slope))
            return tuple(out)

        bounds = (first_ref[row, tile], stop_ref[row, tile])
        accs = (jnp.zeros((PAIR, 2 * QT), F32),) * len(pairs)
        accs = over_chunks(spans, tile, bounds, step, accs)
        for pair in pairs:
            dq_ref[own, lanes[pair]] = (own_lanes(accs[pair]) * SCALE).astype(BF)
    dk_ref[...] = dk_acc[...].astype(BF)
    dv_ref[...] = dv_acc[...].astype(BF)


def attention_specs(keys, wide):
    per_query = pl.BlockSpec((PATCHES, wide * PAIR), lambda r, h, *_: (r, h))
    per_key = pl.BlockSpec((keys, wide * PAIR), lambda r, h, *_: (r, h))
    bound = pl.BlockSpec((1, 1, PATCHES), lambda r, h, *_: (r, 0, 0))
    logs = pl.BlockSpec((1, wide, TILES, 2 * QT), lambda r, h, *_: (r, h, 0, 0))
    return per_query, per_key, bound, logs


def kernel_cost(q, k, products):
    scores = q.shape[0] * k.shape[0] // (q.shape[0] // PATCHES) * HEADS
    return pl.CostEstimate(
        flops=products * 2 * scores * 256, bytes_accessed=2 * q.nbytes + 4 * k.nbytes, transcendentals=scores
    )


def attend(bounds, q, k, v, wide, spans=None):
    first, stop, lo, hi, chunk = bounds
    rows = lo.shape[0]
    keys = k.shape[0] // rows
    per_query, per_key, bound, logs = attention_specs(keys, wide)
    return pl.pallas_call(
        functools.partial(attend_kernel, chunk, spans),
        grid_spec=pltpu.PrefetchScalarGridSpec(
            num_scalar_prefetch=2,
            grid=(rows, PAIRS // wide),
            in_specs=[bound, bound, per_query, per_key, per_key],
            out_specs=[per_query, logs],
            scratch_shapes=[pltpu.VMEM((TILES, keys, QT), F32), pltpu.VMEM((wide, keys, 2 * QT), F32)],
        ),
        out_shape=[
            jax.ShapeDtypeStruct(q.shape, BF),
            jax.ShapeDtypeStruct((rows, PAIRS, TILES, 2 * QT), F32),
        ],
        compiler_params=pltpu.CompilerParams(vmem_limit_bytes=48 << 20),
        cost_estimate=kernel_cost(q, k, 2),
        name="attend",
    )(first, stop, lo, hi, q, k, v)


def attend_back(bounds, q, k, v, logsum, context, grads, wide, spans=None):
    first, stop, lo, hi, chunk = bounds
    rows = lo.shape[0]
    keys = k.shape[0] // rows
    per_query, per_key, bound, logs = attention_specs(keys, wide)
    return pl.pallas_call(
        functools.partial(attend_back_kernel, chunk, spans),
        grid_spec=pltpu.PrefetchScalarGridSpec(
            num_scalar_prefetch=2,
            grid=(rows, PAIRS // wide),
            in_specs=[bound, bound, per_query, per_key, per_key, logs, per_query, per_query],
            out_specs=[per_query, per_key, per_key],
            scratch_shapes=[pltpu.VMEM((TILES, keys, QT), F32)] + [pltpu.VMEM((keys, wide * PAIR), F32)] * 2,
        ),
        out_shape=[
            jax.ShapeDtypeStruct(q.shape, BF),
            jax.ShapeDtypeStruct(k.shape, BF),
            jax.ShapeDtypeStruct(k.shape, BF),
        ],
        compiler_params=pltpu.CompilerParams(vmem_limit_bytes=48 << 20),
        cost_estimate=kernel_cost(q, k, 5),
        name="attend_back",
    )(first, stop, lo, hi, q, k, v, logsum, context, grads)


def scale_of(values):
    return lax.rsqrt(jnp.mean(values * values, axis=-1, keepdims=True) + EPS)


def norm_backward(values, row_scale, gain_row, incoming):
    weighted = incoming * gain_row
    projection = jnp.mean(weighted * values, axis=-1, keepdims=True)
    grad_values = row_scale * weighted - values * (row_scale * row_scale * row_scale) * projection
    grad_gain = jnp.sum(incoming * values * row_scale, axis=0)
    return grad_values, grad_gain


def chunk_bounds(lo, hi, chunk):
    first = lo[:, ::QT] // chunk
    stop = (hi[:, QT - 1 :: QT] + chunk - 1) // chunk
    return first, stop, lo[:, None, :], hi[:, None, :], chunk


def shards(
    byte_states, patch_lengths, patch_docs, attn_qkv, attn_out, norm_gains, ffn_in, ffn_down, cotangent
):
    section = lax.axis_index("section")
    group = lax.axis_index("group")
    sections = lax.axis_size("section")
    groups = lax.axis_size("group")
    core, side = group % 2, group // 2

    core_pairs = [(0, 1), (1, 0), (2, 3), (3, 2)]
    side_pairs = [(0, 2), (1, 3), (2, 0), (3, 1)]
    swap = [(0, 1), (1, 0)]
    together = lax.optimization_barrier

    four = jnp.concatenate([attn_qkv[0], attn_out], axis=0)
    matrix = lax.dynamic_index_in_dim(four, group, 0, keepdims=False)
    matrices = lax.all_gather(matrix, ("section", "group", "dp"), axis=0, tiled=True)

    gains = lax.all_gather(norm_gains, "section", axis=0, tiled=True)

    def quarter_of(shard):
        height = shard.shape[0] // groups
        return lax.dynamic_slice_in_dim(shard, group * height, height, 0)

    def in_order(part, own, got):
        return jnp.where(part == 0, jnp.stack([own, got]), jnp.stack([got, own]))

    def both(values, part, axis, pairs):
        return in_order(part, values, lax.ppermute(values, axis, pairs))

    units = FF // sections

    def of_units(values, part):
        halves = [lax.dynamic_slice_in_dim(values, at + part * units, units, 1) for at in (0, FF)]
        return jnp.concatenate(halves, axis=1)

    quarter = quarter_of(ffn_in)
    got = lax.ppermute(of_units(quarter, 1 - section), "section", swap)
    w_in = in_order(section, of_units(quarter, section), got)
    w_in = lax.all_gather(w_in, ("dp", "group"), axis=1, tiled=True).reshape(D, 2 * units)

    line, place = lax.axis_size("dp"), lax.axis_index("dp")
    quarter = quarter_of(ffn_down)
    down = jnp.zeros((line,) + quarter.shape, BF)
    for step in range(line):
        moved = lax.ppermute(quarter, "dp", [(i, (i + step) % line) for i in range(line)]) if step else quarter
        down = lax.dynamic_update_slice_in_dim(down, moved[None], (place - step) % line, 0)
    matrices = matrices.reshape(sections, groups, D, D)
    wq, wk, wv, wo = [matrices[:, index] for index in range(4)]

    rows = byte_states.shape[0] // sections
    mine = lambda a: lax.dynamic_slice_in_dim(a, section * rows, rows, 0)
    states, lengths, docs, cot = [mine(a) for a in (byte_states, patch_lengths, patch_docs, cotangent)]
    tokens = rows * PATCHES
    cot = cot.reshape(tokens, D)
    other_cot = lax.dynamic_slice_in_dim(cotangent, (1 - section) * rows, rows, 0).reshape(tokens, D)
    cots = jnp.concatenate([cot, other_cot], axis=0)

    ends = jnp.cumsum(lengths, axis=1)
    earlier = docs[:, None, :] < docs[:, :, None]
    doc_start = jnp.sum(jnp.where(earlier, lengths[:, None, :], 0), axis=2)
    doc_first = jnp.sum(earlier.astype(jnp.int32), axis=2)
    cross, cross_back = chunk_bounds(doc_start, ends, 256), chunk_bounds(doc_start, ends, 512)
    ids = jnp.broadcast_to(lax.iota(jnp.int32, PATCHES) + 1, doc_first.shape)
    causal = chunk_bounds(doc_first, ids, 128)
    positions = lax.iota(jnp.int32, ROW_BYTES)
    member = (positions < ends[:, :, None]) & (positions >= (ends - lengths)[:, :, None])
    member = member.astype(BF)
    count = lengths.astype(F32).reshape(rows * PATCHES, 1)

    pooled = jnp.einsum("rpb,rbd->rpd", member, states, preferred_element_type=F32)
    pooled = pooled.reshape(rows * PATCHES, D) / count
    wide = states.reshape(rows * ROW_BYTES, D).astype(F32)
    query_scale, key_scale = scale_of(pooled), scale_of(wide)
    query_in = (pooled * query_scale * gains[0, 0]).astype(BF)
    key_in = (wide * key_scale * gains[0, 1]).astype(BF)
    q1 = nn(query_in, wq[0]).astype(BF)
    k1 = nn(key_in, wk[0]).astype(BF)
    v1 = nn(key_in, wv[0]).astype(BF)
    v1, down = together((v1, down))
    down = both(down, side, "group", side_pairs)
    c1, l1 = attend(cross, q1, k1, v1, 8)
    carried = (pooled + nn(c1, wo[0])).astype(BF)

    carried_wide = carried.astype(F32)
    first_scale = scale_of(carried_wide)
    normed_in = (carried_wide * first_scale * gains[1, 0]).astype(BF)
    q2 = nn(normed_in, wq[1]).astype(BF)
    k2 = nn(normed_in, wk[1]).astype(BF)
    v2 = nn(normed_in, wv[1]).astype(BF)
    c2, l2 = attend(causal, q2, k2, v2, 8, CAUSAL_SPANS)
    c2, down = together((c2, down))
    down = both(down, core, "group", core_pairs)
    w_down = down.transpose(2, 1, 0, 3, 4).reshape(units, D)
    residual = carried_wide + nn(c2, wo[1])
    second_scale = scale_of(residual)
    mix_in = (residual * second_scale * gains[1, 1]).astype(BF)
    mixed = jnp.concatenate([mix_in, lax.ppermute(mix_in, "section", swap)], axis=0)
    gate_up = nn(mixed, w_in)
    gate, up = gate_up[:, :units], gate_up[:, units:]
    sig = jax.nn.sigmoid(gate)
    hidden = (gate * sig * up).astype(BF)

    grad_hidden = nt(cots, w_down)
    grad_gate = grad_hidden * up * sig * (1.0 + gate * (1.0 - sig))
    grad_up = grad_hidden * gate * sig
    dgu = jnp.concatenate([grad_gate, grad_up], axis=1).astype(BF)

    def exchanged(values, axis, part, pairs, where):
        size = values.shape[where] // 2
        other = lax.dynamic_slice_in_dim(values, (1 - part) * size, size, where)
        own = lax.dynamic_slice_in_dim(values, part * size, size, where)
        return (own.astype(F32) + lax.ppermute(other, axis, pairs).astype(F32)).astype(BF)

    def over_section(values, where):
        return exchanged(values, "section", section, swap, where)

    def over_side(values, where):
        return exchanged(values, "group", side, side_pairs, where)

    def columns(values, part):
        size = values.shape[-1] // 2
        return lax.dynamic_slice_in_dim(values, part * size, size, values.ndim - 1)

    def line_sum(values, where):
        return lax.psum_scatter(values, "dp", scatter_dimension=where, tiled=True)

    def products(pairs, part):
        out = [tn(left, columns(right, part)) for left, right in pairs]
        return out[0] if len(out) == 1 else jnp.stack(out)

    def to_core(pairs):
        return products(pairs, 1 - core).astype(BF)

    def of_chip(pairs, sent):
        got = lax.ppermute(sent, "group", core_pairs)
        return (products(pairs, core) + got.astype(F32)).astype(BF)

    in_pairs, down_pairs = [(mixed, dgu)], [(hidden, cots)]
    mix_other = nt(dgu[tokens:], w_in).astype(BF)
    send_in, send_down = to_core(in_pairs), to_core(down_pairs)
    dgu_own, mix_other, send_in, send_down = together((dgu[:tokens], mix_other, send_in, send_down))
    mix_got = lax.ppermute(mix_other, "section", swap)

    half = D // sections
    parts = nn(hidden, w_down)
    parts = jnp.concatenate([residual + parts[:tokens], parts[tokens:]], axis=0)
    sent = lax.dynamic_slice_in_dim(parts, (1 - section) * half, half, 1).astype(BF)
    kept = lax.dynamic_slice_in_dim(parts, section * half, half, 1)
    dgu_own, sent = together((dgu_own, sent))
    got = lax.ppermute(sent, "section", swap)

    half_in, half_down = of_chip(in_pairs, send_in), of_chip(down_pairs, send_down)
    mix_got, half_in, half_down = together((mix_got, half_in, half_down))
    grad_mixed = nt(dgu_own, w_in) + mix_got.astype(F32)
    grad_mix, gain_mix = norm_backward(residual, second_scale, gains[1, 1], grad_mixed)
    grad_residual = grad_mix + cot.astype(F32)
    branch = grad_residual.astype(BF)
    dc2 = nt(branch, wo[1]).astype(BF)

    dq2, dk2, dv2 = attend_back(causal, q2, k2, v2, l2, c2, dc2, 8, CAUSAL_SPANS)
    two_pairs = [(normed_in, dq2), (normed_in, dk2), (normed_in, dv2), (c2, branch)]
    send_two = to_core(two_pairs)
    half_in = over_side(half_in.reshape(sections, line, 2, -1, units), 2)
    sum_down = line_sum(half_down, 0)
    dq2, dk2, dv2, send_two, half_in, sum_down = together((dq2, dk2, dv2, send_two, half_in, sum_down))
    sum_in = line_sum(half_in.reshape(sections, -1, units), 1)
    grad_normed = nt(dq2, wq[1]) + nt(dk2, wk[1]) + nt(dv2, wv[1])
    grad_carried, gain_normed = norm_backward(carried_wide, first_scale, gains[1, 0], grad_normed)
    d_carried = (grad_residual + grad_carried).astype(BF)
    dc1 = nt(d_carried, wo[0]).astype(BF)
    half_two = of_chip(two_pairs, send_two)
    dc1, half_two, got = together((dc1, half_two, got))
    got = got.astype(F32)
    latents = in_order(section, kept[:tokens] + got[tokens:], kept[tokens:] + got[:tokens])
    latents_out = latents.astype(BF).reshape(sections * rows, PATCHES, half)
    dq1, dk1, dv1 = attend_back(cross_back, q1, k1, v1, l1, c1, dc1, 4)
    half_two = over_section(half_two[:2], 2), over_side(half_two[2:], 2)
    dq1, half_two = together((dq1, half_two))
    half_two = jnp.concatenate([over_side(half_two[0], 2), over_section(half_two[1], 2)], axis=0)
    one_pairs = [(query_in, dq1), (key_in, dk1)], [(key_in, dv1), (c1, d_carried)]
    send_one = [to_core(pairs) for pairs in one_pairs]
    dq1, dk1, dv1, send_one, sum_in, sum_down = together((dq1, dk1, dv1, send_one, sum_in, sum_down))
    sum_in = jnp.stack([lax.dynamic_index_in_dim(sum_in, section, 0, False),
                        lax.ppermute(lax.dynamic_index_in_dim(sum_in, 1 - section, 0, False), "section", swap)])
    sum_in = jnp.where(section == 0, sum_in, sum_in[::-1])

    def gathered(part):
        return lax.all_gather(part, "group", axis=0, tiled=False)

    def laid_out(parts, order):
        return jnp.concatenate([parts[index] for index in order], axis=-1).astype(F32)

    sum_in = gathered(sum_in)
    half_one = [of_chip(pairs, sent) for pairs, sent in zip(one_pairs, send_one)]
    dq1, dk1, dv1, half_one, half_two = together((dq1, dk1, dv1, half_one, half_two))
    sum_two = line_sum(half_two, 1)
    grad_query_in = nt(dq1, wq[0])
    grad_key_in = nt(dk1, wk[0]) + nt(dv1, wv[0])
    half_one = over_section(half_one[0], 2), over_side(half_one[1], 2)
    grad_query_in, grad_key_in, half_one, sum_in = together((grad_query_in, grad_key_in, half_one, sum_in))
    half_one = jnp.concatenate([over_side(half_one[0], 2), over_section(half_one[1], 2)], axis=0)
    grad_query_in, grad_key_in, half_one, sum_two, sum_down = together(
        (grad_query_in, grad_key_in, half_one, sum_two, sum_down)
    )
    sum_down = over_side(sum_down, 1)
    sum_one = line_sum(half_one, 1)

    grad_pooled, gain_query = norm_backward(pooled, query_scale, gains[0, 0], grad_query_in)
    grad_wide, gain_key = norm_backward(wide, key_scale, gains[0, 1], grad_key_in)
    per_patch = (grad_pooled + d_carried.astype(F32)) / count
    spread_back = jnp.einsum(
        "rpb,rpd->rbd", member, per_patch.astype(BF).reshape(rows, PATCHES, D), preferred_element_type=F32
    )
    byte_grads = (grad_wide + spread_back.reshape(rows * ROW_BYTES, D)).astype(BF)
    byte_grads = byte_grads.reshape(rows, ROW_BYTES, D)
    other = lax.dynamic_slice_in_dim(byte_grads, (1 - section) * half, half, 2)
    own = lax.dynamic_slice_in_dim(byte_grads, section * half, half, 2)

    gain_grads = jnp.stack([gain_query, gain_key, gain_normed, gain_mix])
    gain_grads = gain_grads + lax.ppermute(gain_grads, "section", swap)
    other, gain_grads, sum_one = together((other, gain_grads, sum_one))
    got = [lax.ppermute(other[row], "section", swap) for row in range(rows)]
    for pairs in (core_pairs, side_pairs):
        gain_grads = gain_grads + lax.ppermute(gain_grads, "group", pairs)
    gain_grads = jnp.sum(lax.all_gather(gain_grads, "dp", axis=0, tiled=False), axis=0)

    ffn_gin = jnp.concatenate(
        [laid_out([sum_in[at, t] for at in (2 * y, 2 * y + 1) for t in range(sections)], range(4)) for y in (0, 1)],
        axis=0,
    )
    bytes_got = got

    kept = jnp.where(section == 0, sum_one, sum_two)
    sent = jnp.where(section == 0, sum_two, sum_one)
    got = lax.ppermute(sent, "section", swap)
    got, sum_down = together((got, sum_down))
    ffn_gdown = laid_out(gathered(sum_down), (0, 2, 1, 3))
    eighths = jnp.where(
        section == 0, jnp.concatenate([kept, got], axis=2), jnp.concatenate([got, kept], axis=2)
    )
    width = eighths.shape[2] // 2
    eighths, bytes_got = together((gathered(eighths), bytes_got))
    bytes_out = in_order(section, own, jnp.stack(bytes_got)).reshape(sections * rows, ROW_BYTES, half)
    parts = [piece for every in eighths for piece in (every[..., :width], every[..., width:])]
    section_first = laid_out([part[:2] for part in parts], (0, 4, 1, 5, 2, 6, 3, 7))
    side_first = laid_out([part[2:] for part in parts], (0, 1, 4, 5, 2, 3, 6, 7))
    grad_qkv = jnp.concatenate([section_first, side_first[:1]], axis=0)[None]

    gain_grads = lax.dynamic_slice_in_dim(gain_grads.reshape(2, 2, D), section, 1, 0)
    width = D // lax.axis_size("dp")
    gain_out = lax.dynamic_slice_in_dim(gain_grads, lax.axis_index("dp") * width, width, 2)
    return (latents_out, bytes_out, grad_qkv, side_first[1:], gain_out, ffn_gin, ffn_gdown)


def solution(mesh):
    in_specs = (
        P(("group", "dp"), None, None),
        P(("group", "dp"), None),
        P(("group", "dp"), None),
        P("section", None, "dp", None),
        P("section", "dp", None),
        P("section", None, None),
        P(("section", "dp"), None),
        P(("section", "dp"), None),
        P(("group", "dp"), None, None),
    )
    out_specs = (
        P(("group", "dp"), None, "section"),
        P(("group", "dp"), None, "section"),
        P("section", None, "dp", None),
        P("section", "dp", None),
        P("section", None, "dp"),
        P(("section", "dp"), None),
        P(("section", "dp"), None),
    )
    return jax.shard_map(shards, mesh=mesh, in_specs=in_specs, out_specs=out_specs, check_vma=False)
```

```python
import functools

import jax
import jax.numpy as jnp
from jax import lax
from jax.experimental import pallas as pl
from jax.experimental.pallas import tpu as pltpu
from jax.sharding import PartitionSpec as P

D = 1024
HEADS = 16
HEAD_DIM = 64
PAIR = 2 * HEAD_DIM
PAIRS = HEADS // 2
FF = 2816
ROW_BYTES = 1024
PATCHES = 256
QT = 128
TILES = PATCHES // QT
CAUSAL_SPANS = ((0, 1), (0, 2))

EPS = 1e-05
SCALE = HEAD_DIM ** (-0.5)
EXCLUDED = -1e30

BF = jnp.bfloat16
F32 = jnp.float32


def nn(left, right):
    return jnp.dot(left, right, preferred_element_type=F32)


def tn(left, right):
    return lax.dot_general(left, right, (((0,), (0,)), ((), ())), preferred_element_type=F32)


def nt(left, right):
    return lax.dot_general(left, right, (((1,), (1,)), ((), ())), preferred_element_type=F32)


def two_heads(block):
    lane = lax.broadcasted_iota(jnp.int32, block.shape, 1)
    zero = jnp.zeros_like(block)
    first = lane < HEAD_DIM
    return jnp.concatenate([jnp.where(first, block, zero), jnp.where(first, zero, block)], axis=0)


def own_lanes(both):
    picked = jnp.concatenate([both[:HEAD_DIM, :QT], both[HEAD_DIM:, QT:]], axis=0)
    return picked.T


def twice(row):
    return jnp.concatenate([row, row], axis=1)


def fill_bias(keys, lo_ref, hi_ref, bias_ref):
    at = lax.broadcasted_iota(jnp.int32, (keys, QT), 0)
    for tile in range(TILES):
        own = pl.ds(tile * QT, QT)
        inside = (at >= lo_ref[0, :, own]) & (at < hi_ref[0, :, own])
        bias_ref[tile] = jnp.where(inside, 0.0, EXCLUDED)


def over_chunks(spans, tile, bounds, body, init):
    if spans is None:
        return lax.fori_loop(*bounds, body, init)
    for j in range(*spans[tile]):
        init = body(j, init)
    return init


def chunk_at(spans, chunk, j):
    return pl.ds(j * chunk if spans is not None else pl.multiple_of(j * chunk, chunk), chunk)


def attend_kernel(
    chunk, spans, first_ref, stop_ref, lo_ref, hi_ref, q_ref, k_ref, v_ref, c_ref, l_ref, bias_ref, s_ref
):
    row = pl.program_id(0)
    pairs = range(q_ref.shape[1] // PAIR)
    lanes = [pl.ds(pair * PAIR, PAIR) for pair in pairs]
    pl.when(pl.program_id(1) == 0)(lambda: fill_bias(k_ref.shape[0], lo_ref, hi_ref, bias_ref))
    for tile in range(TILES):
        own = pl.ds(tile * QT, QT)
        queries = [two_heads(q_ref[own, at].astype(F32) * SCALE).astype(BF) for at in lanes]
        bounds = (first_ref[row, tile], stop_ref[row, tile])

        def scores(j, tops):
            here = chunk_at(spans, chunk, j)
            bias = twice(bias_ref[tile, here, :])
            out = []
            for pair in pairs:
                part = nt(k_ref[here, lanes[pair]], queries[pair]) + bias
                s_ref[pair, here, :] = part
                out.append(jnp.maximum(tops[pair], jnp.max(part, axis=0, keepdims=True)))
            return tuple(out)

        tops = (jnp.full((1, 2 * QT), EXCLUDED, F32),) * len(pairs)
        tops = over_chunks(spans, tile, bounds, scores, tops)

        def context(j, sums):
            here = chunk_at(spans, chunk, j)
            out = []
            for pair in pairs:
                total, acc = sums[pair]
                weight = jnp.exp(s_ref[pair, here, :] - tops[pair])
                total = total + jnp.sum(weight, axis=0, keepdims=True)
                out.append((total, acc + tn(v_ref[here, lanes[pair]], weight.astype(BF))))
            return tuple(out)

        sums = ((jnp.zeros((1, 2 * QT), F32), jnp.zeros((PAIR, 2 * QT), F32)),) * len(pairs)
        sums = over_chunks(spans, tile, bounds, context, sums)
        for pair in pairs:
            total, acc = sums[pair]
            c_ref[own, lanes[pair]] = own_lanes(acc / total).astype(BF)
            l_ref[0, pair, tile : tile + 1, :] = tops[pair] + jnp.log(total)


def attend_back_kernel(
    chunk, spans, first_ref, stop_ref, lo_ref, hi_ref, q_ref, k_ref, v_ref, l_ref, c_ref, dc_ref,
    dq_ref, dk_ref, dv_ref, bias_ref, dk_acc, dv_acc,
):
    row = pl.program_id(0)
    pairs = range(q_ref.shape[1] // PAIR)
    lanes = [pl.ds(pair * PAIR, PAIR) for pair in pairs]
    pl.when(pl.program_id(1) == 0)(lambda: fill_bias(k_ref.shape[0], lo_ref, hi_ref, bias_ref))
    dk_acc[...] = jnp.zeros_like(dk_acc)
    dv_acc[...] = jnp.zeros_like(dv_acc)
    for tile in range(TILES):
        own = pl.ds(tile * QT, QT)
        queries, grads, deltas, logs = [], [], [], []
        for pair in pairs:
            queries.append(two_heads(q_ref[own, lanes[pair]].astype(F32) * SCALE).astype(BF))
            grad = dc_ref[own, lanes[pair]].astype(F32)
            inner = (grad * c_ref[own, lanes[pair]].astype(F32)).T
            heads = [jnp.sum(part, axis=0, keepdims=True) for part in (inner[:HEAD_DIM], inner[HEAD_DIM:])]
            deltas.append(jnp.concatenate(heads, axis=1))
            grads.append(two_heads(grad).astype(BF))
            logs.append(l_ref[0, pair, tile : tile + 1, :])

        def step(j, accs):
            here = chunk_at(spans, chunk, j)
            bias = twice(bias_ref[tile, here, :])
            out = []
            for pair in pairs:
                keys = k_ref[here, lanes[pair]]
                prob = jnp.exp(nt(keys, queries[pair]) + bias - logs[pair])
                slope = prob * (nt(v_ref[here, lanes[pair]], grads[pair]) - deltas[pair])
                slope = slope.astype(BF)
                dv_acc[here, lanes[pair]] += nn(prob.astype(BF), grads[pair])
                dk_acc[here, lanes[pair]] += nn(slope, queries[pair])
                out.append(accs[pair] + tn(keys, slope))
            return tuple(out)

        bounds = (first_ref[row, tile], stop_ref[row, tile])
        accs = (jnp.zeros((PAIR, 2 * QT), F32),) * len(pairs)
        accs = over_chunks(spans, tile, bounds, step, accs)
        for pair in pairs:
            dq_ref[own, lanes[pair]] = (own_lanes(accs[pair]) * SCALE).astype(BF)
    dk_ref[...] = dk_acc[...].astype(BF)
    dv_ref[...] = dv_acc[...].astype(BF)


def attention_specs(keys, wide):
    per_query = pl.BlockSpec((PATCHES, wide * PAIR), lambda r, h, *_: (r, h))
    per_key = pl.BlockSpec((keys, wide * PAIR), lambda r, h, *_: (r, h))
    bound = pl.BlockSpec((1, 1, PATCHES), lambda r, h, *_: (r, 0, 0))
    logs = pl.BlockSpec((1, wide, TILES, 2 * QT), lambda r, h, *_: (r, h, 0, 0))
    return per_query, per_key, bound, logs


def kernel_cost(q, k, products):
    scores = q.shape[0] * k.shape[0] // (q.shape[0] // PATCHES) * HEADS
    return pl.CostEstimate(
        flops=products * 2 * scores * 256, bytes_accessed=2 * q.nbytes + 4 * k.nbytes, transcendentals=scores
    )


def attend(bounds, q, k, v, wide, spans=None):
    first, stop, lo, hi, chunk = bounds
    rows = lo.shape[0]
    keys = k.shape[0] // rows
    per_query, per_key, bound, logs = attention_specs(keys, wide)
    return pl.pallas_call(
        functools.partial(attend_kernel, chunk, spans),
        grid_spec=pltpu.PrefetchScalarGridSpec(
            num_scalar_prefetch=2,
            grid=(rows, PAIRS // wide),
            in_specs=[bound, bound, per_query, per_key, per_key],
            out_specs=[per_query, logs],
            scratch_shapes=[pltpu.VMEM((TILES, keys, QT), F32), pltpu.VMEM((wide, keys, 2 * QT), F32)],
        ),
        out_shape=[
            jax.ShapeDtypeStruct(q.shape, BF),
            jax.ShapeDtypeStruct((rows, PAIRS, TILES, 2 * QT), F32),
        ],
        compiler_params=pltpu.CompilerParams(vmem_limit_bytes=48 << 20),
        cost_estimate=kernel_cost(q, k, 2),
        name="attend",
    )(first, stop, lo, hi, q, k, v)


def attend_back(bounds, q, k, v, logsum, context, grads, wide, spans=None):
    first, stop, lo, hi, chunk = bounds
    rows = lo.shape[0]
    keys = k.shape[0] // rows
    per_query, per_key, bound, logs = attention_specs(keys, wide)
    return pl.pallas_call(
        functools.partial(attend_back_kernel, chunk, spans),
        grid_spec=pltpu.PrefetchScalarGridSpec(
            num_scalar_prefetch=2,
            grid=(rows, PAIRS // wide),
            in_specs=[bound, bound, per_query, per_key, per_key, logs, per_query, per_query],
            out_specs=[per_query, per_key, per_key],
            scratch_shapes=[pltpu.VMEM((TILES, keys, QT), F32)] + [pltpu.VMEM((keys, wide * PAIR), F32)] * 2,
        ),
        out_shape=[
            jax.ShapeDtypeStruct(q.shape, BF),
            jax.ShapeDtypeStruct(k.shape, BF),
            jax.ShapeDtypeStruct(k.shape, BF),
        ],
        compiler_params=pltpu.CompilerParams(vmem_limit_bytes=48 << 20),
        cost_estimate=kernel_cost(q, k, 5),
        name="attend_back",
    )(first, stop, lo, hi, q, k, v, logsum, context, grads)


def scale_of(values):
    return lax.rsqrt(jnp.mean(values * values, axis=-1, keepdims=True) + EPS)


def norm_backward(values, row_scale, gain_row, incoming):
    weighted = incoming * gain_row
    projection = jnp.mean(weighted * values, axis=-1, keepdims=True)
    grad_values = row_scale * weighted - values * (row_scale * row_scale * row_scale) * projection
    grad_gain = jnp.sum(incoming * values * row_scale, axis=0)
    return grad_values, grad_gain


def chunk_bounds(lo, hi, chunk):
    first = lo[:, ::QT] // chunk
    stop = (hi[:, QT - 1 :: QT] + chunk - 1) // chunk
    return first, stop, lo[:, None, :], hi[:, None, :], chunk


def shards(
    byte_states, patch_lengths, patch_docs, attn_qkv, attn_out, norm_gains, ffn_in, ffn_down, cotangent
):
    section = lax.axis_index("section")
    group = lax.axis_index("group")
    sections = lax.axis_size("section")
    groups = lax.axis_size("group")
    core, side = group % 2, group // 2

    core_pairs = [(0, 1), (1, 0), (2, 3), (3, 2)]
    side_pairs = [(0, 2), (1, 3), (2, 0), (3, 1)]
    swap = [(0, 1), (1, 0)]
    together = lax.optimization_barrier

    four = jnp.concatenate([attn_qkv[0], attn_out], axis=0)
    matrix = lax.dynamic_index_in_dim(four, group, 0, keepdims=False)
    matrices = lax.all_gather(matrix, ("section", "group", "dp"), axis=0, tiled=True)

    gains = lax.all_gather(norm_gains, "section", axis=0, tiled=True)

    def quarter_of(shard):
        height = shard.shape[0] // groups
        return lax.dynamic_slice_in_dim(shard, group * height, height, 0)

    def in_order(part, own, got):
        return jnp.where(part == 0, jnp.stack([own, got]), jnp.stack([got, own]))

    def both(values, part, axis, pairs):
        return in_order(part, values, lax.ppermute(values, axis, pairs))

    units = FF // sections

    def of_units(values, part):
        halves = [lax.dynamic_slice_in_dim(values, at + part * units, units, 1) for at in (0, FF)]
        return jnp.concatenate(halves, axis=1)

    quarter = quarter_of(ffn_in)
    got = lax.ppermute(of_units(quarter, 1 - section), "section", swap)
    w_in = in_order(section, of_units(quarter, section), got)
    w_in = lax.all_gather(w_in, ("dp", "group"), axis=1, tiled=True).reshape(D, 2 * units)

    line, place = lax.axis_size("dp"), lax.axis_index("dp")
    quarter = quarter_of(ffn_down)
    down = jnp.zeros((line,) + quarter.shape, BF)
    for step in range(line):
        moved = lax.ppermute(quarter, "dp", [(i, (i + step) % line) for i in range(line)]) if step else quarter
        down = lax.dynamic_update_slice_in_dim(down, moved[None], (place - step) % line, 0)
    matrices = matrices.reshape(sections, groups, D, D)
    wq, wk, wv, wo = [matrices[:, index] for index in range(4)]

    rows = byte_states.shape[0] // sections
    mine = lambda a: lax.dynamic_slice_in_dim(a, section * rows, rows, 0)
    states, lengths, docs, cot = [mine(a) for a in (byte_states, patch_lengths, patch_docs, cotangent)]
    tokens = rows * PATCHES
    cot = cot.reshape(tokens, D)
    other_cot = lax.dynamic_slice_in_dim(cotangent, (1 - section) * rows, rows, 0).reshape(tokens, D)
    cots = jnp.concatenate([cot, other_cot], axis=0)

    ends = jnp.cumsum(lengths, axis=1)
    earlier = docs[:, None, :] < docs[:, :, None]
    doc_start = jnp.sum(jnp.where(earlier, lengths[:, None, :], 0), axis=2)
    doc_first = jnp.sum(earlier.astype(jnp.int32), axis=2)
    cross, cross_back = chunk_bounds(doc_start, ends, 256), chunk_bounds(doc_start, ends, 512)
    ids = jnp.broadcast_to(lax.iota(jnp.int32, PATCHES) + 1, doc_first.shape)
    causal = chunk_bounds(doc_first, ids, 128)
    positions = lax.iota(jnp.int32, ROW_BYTES)
    member = (positions < ends[:, :, None]) & (positions >= (ends - lengths)[:, :, None])
    member = member.astype(BF)
    count = lengths.astype(F32).reshape(rows * PATCHES, 1)

    pooled = jnp.einsum("rpb,rbd->rpd", member, states, preferred_element_type=F32)
    pooled = pooled.reshape(rows * PATCHES, D) / count
    wide = states.reshape(rows * ROW_BYTES, D).astype(F32)
    query_scale, key_scale = scale_of(pooled), scale_of(wide)
    query_in = (pooled * query_scale * gains[0, 0]).astype(BF)
    key_in = (wide * key_scale * gains[0, 1]).astype(BF)
    q1 = nn(query_in, wq[0]).astype(BF)
    k1 = nn(key_in, wk[0]).astype(BF)
    v1 = nn(key_in, wv[0]).astype(BF)
    v1, down = together((v1, down))
    down = both(down, side, "group", side_pairs)
    c1, l1 = attend(cross, q1, k1, v1, 8)
    carried = (pooled + nn(c1, wo[0])).astype(BF)

    carried_wide = carried.astype(F32)
    first_scale = scale_of(carried_wide)
    normed_in = (carried_wide * first_scale * gains[1, 0]).astype(BF)
    q2 = nn(normed_in, wq[1]).astype(BF)
    k2 = nn(normed_in, wk[1]).astype(BF)
    v2 = nn(normed_in, wv[1]).astype(BF)
    c2, l2 = attend(causal, q2, k2, v2, 8, CAUSAL_SPANS)
    c2, down = together((c2, down))
    down = both(down, core, "group", core_pairs)
    w_down = down.transpose(2, 1, 0, 3, 4).reshape(units, D)
    residual = carried_wide + nn(c2, wo[1])
    second_scale = scale_of(residual)
    mix_in = (residual * second_scale * gains[1, 1]).astype(BF)
    mix_got = lax.ppermute(mix_in, "section", swap)
    grad_hidden = nt(cots, w_down).astype(BF)
    mix_got, grad_hidden = together((mix_got, grad_hidden))
    mixed = jnp.concatenate([mix_in, mix_got], axis=0)
    gate_up = nn(mixed, w_in)
    gate, up = gate_up[:, :units], gate_up[:, units:]
    sig = jax.nn.sigmoid(gate)
    hidden = (gate * sig * up).astype(BF)

    grad_hidden = grad_hidden.astype(F32)
    grad_gate = grad_hidden * up * sig * (1.0 + gate * (1.0 - sig))
    grad_up = grad_hidden * gate * sig
    dgu = jnp.concatenate([grad_gate, grad_up], axis=1).astype(BF)

    def exchanged(values, axis, part, pairs, where):
        size = values.shape[where] // 2
        other = lax.dynamic_slice_in_dim(values, (1 - part) * size, size, where)
        own = lax.dynamic_slice_in_dim(values, part * size, size, where)
        return (own.astype(F32) + lax.ppermute(other, axis, pairs).astype(F32)).astype(BF)

    def over_section(values, where):
        return exchanged(values, "section", section, swap, where)

    def over_side(values, where):
        return exchanged(values, "group", side, side_pairs, where)

    def columns(values, part):
        size = values.shape[-1] // 2
        return lax.dynamic_slice_in_dim(values, part * size, size, values.ndim - 1)

    def line_sum(values, where):
        return lax.psum_scatter(values, "dp", scatter_dimension=where, tiled=True)

    def products(pairs, part):
        out = [tn(left, columns(right, part)) for left, right in pairs]
        return out[0] if len(out) == 1 else jnp.stack(out)

    def to_core(pairs):
        return products(pairs, 1 - core).astype(BF)

    def of_chip(pairs, sent):
        got = lax.ppermute(sent, "group", core_pairs)
        return (products(pairs, core) + got.astype(F32)).astype(BF)

    in_pairs, down_pairs = [(mixed, dgu)], [(hidden, cots)]
    mix_other = nt(dgu[tokens:], w_in).astype(BF)
    send_in, send_down = to_core(in_pairs), to_core(down_pairs)
    dgu_own, mix_other, send_in, send_down = together((dgu[:tokens], mix_other, send_in, send_down))
    mix_got = lax.ppermute(mix_other, "section", swap)

    half = D // sections
    parts = nn(hidden, w_down)
    parts = jnp.concatenate([residual + parts[:tokens], parts[tokens:]], axis=0)
    sent = lax.dynamic_slice_in_dim(parts, (1 - section) * half, half, 1).astype(BF)
    kept = lax.dynamic_slice_in_dim(parts, section * half, half, 1)
    dgu_own, sent = together((dgu_own, sent))
    got = lax.ppermute(sent, "section", swap)

    half_in, half_down = of_chip(in_pairs, send_in), of_chip(down_pairs, send_down)
    mix_got, half_in, half_down = together((mix_got, half_in, half_down))
    grad_mixed = nt(dgu_own, w_in) + mix_got.astype(F32)
    grad_mix, gain_mix = norm_backward(residual, second_scale, gains[1, 1], grad_mixed)
    grad_residual = grad_mix + cot.astype(F32)
    branch = grad_residual.astype(BF)
    dc2 = nt(branch, wo[1]).astype(BF)

    dq2, dk2, dv2 = attend_back(causal, q2, k2, v2, l2, c2, dc2, 8, CAUSAL_SPANS)
    two_pairs = [(normed_in, dq2), (normed_in, dk2), (normed_in, dv2), (c2, branch)]
    send_two = to_core(two_pairs)
    half_in = over_side(half_in.reshape(sections, line, 2, -1, units), 2)
    sum_down = line_sum(half_down, 0)
    dq2, dk2, dv2, send_two, half_in, sum_down = together((dq2, dk2, dv2, send_two, half_in, sum_down))
    sum_in = line_sum(half_in.reshape(sections, -1, units), 1)
    grad_normed = nt(dq2, wq[1]) + nt(dk2, wk[1]) + nt(dv2, wv[1])
    grad_carried, gain_normed = norm_backward(carried_wide, first_scale, gains[1, 0], grad_normed)
    d_carried = (grad_residual + grad_carried).astype(BF)
    dc1 = nt(d_carried, wo[0]).astype(BF)
    half_two = of_chip(two_pairs, send_two)
    dc1, half_two, got = together((dc1, half_two, got))
    got = got.astype(F32)
    latents = in_order(section, kept[:tokens] + got[tokens:], kept[tokens:] + got[:tokens])
    latents_out = latents.astype(BF).reshape(sections * rows, PATCHES, half)
    dq1, dk1, dv1 = attend_back(cross_back, q1, k1, v1, l1, c1, dc1, 4)
    half_two = over_section(half_two[:2], 2), over_side(half_two[2:], 2)
    dq1, half_two = together((dq1, half_two))
    half_two = jnp.concatenate([over_side(half_two[0], 2), over_section(half_two[1], 2)], axis=0)
    one_pairs = [(query_in, dq1), (key_in, dk1)], [(key_in, dv1), (c1, d_carried)]
    send_one = [to_core(pairs) for pairs in one_pairs]
    dq1, dk1, dv1, send_one, sum_down = together((dq1, dk1, dv1, send_one, sum_down))
    def gathered(part):
        return lax.all_gather(part, "group", axis=0, tiled=False)

    def laid_out(parts, order):
        return jnp.concatenate([parts[index] for index in order], axis=-1).astype(F32)

    half_one = [of_chip(pairs, sent) for pairs, sent in zip(one_pairs, send_one)]
    dq1, dk1, dv1, half_one, half_two, sum_in = together((dq1, dk1, dv1, half_one, half_two, sum_in))
    sum_two = line_sum(half_two, 1)
    sum_in = jnp.stack([lax.dynamic_index_in_dim(sum_in, section, 0, False),
                        lax.ppermute(lax.dynamic_index_in_dim(sum_in, 1 - section, 0, False), "section", swap)])
    sum_in = jnp.where(section == 0, sum_in, sum_in[::-1])
    sum_in = gathered(sum_in)
    grad_query_in = nt(dq1, wq[0])
    grad_key_in = nt(dk1, wk[0]) + nt(dv1, wv[0])
    half_one = over_section(half_one[0], 2), over_side(half_one[1], 2)
    grad_query_in, grad_key_in, half_one = together((grad_query_in, grad_key_in, half_one))
    half_one = jnp.concatenate([over_side(half_one[0], 2), over_section(half_one[1], 2)], axis=0)
    grad_query_in, grad_key_in, half_one, sum_two, sum_down, sum_in = together(
        (grad_query_in, grad_key_in, half_one, sum_two, sum_down, sum_in)
    )
    sum_down = over_side(sum_down, 1)
    sum_one = line_sum(half_one, 1)

    grad_pooled, gain_query = norm_backward(pooled, query_scale, gains[0, 0], grad_query_in)
    grad_wide, gain_key = norm_backward(wide, key_scale, gains[0, 1], grad_key_in)
    per_patch = (grad_pooled + d_carried.astype(F32)) / count
    spread_back = jnp.einsum(
        "rpb,rpd->rbd", member, per_patch.astype(BF).reshape(rows, PATCHES, D), preferred_element_type=F32
    )
    byte_grads = (grad_wide + spread_back.reshape(rows * ROW_BYTES, D)).astype(BF)
    byte_grads = byte_grads.reshape(rows, ROW_BYTES, D)
    other = lax.dynamic_slice_in_dim(byte_grads, (1 - section) * half, half, 2)
    own = lax.dynamic_slice_in_dim(byte_grads, section * half, half, 2)

    gain_grads = jnp.stack([gain_query, gain_key, gain_normed, gain_mix])
    gain_grads = gain_grads + lax.ppermute(gain_grads, "section", swap)
    ffn_gin = jnp.concatenate(
        [laid_out([sum_in[at, t] for at in (2 * y, 2 * y + 1) for t in range(sections)], range(4)) for y in (0, 1)],
        axis=0,
    )

    early, gain_grads = together(([other[row] for row in range(rows - 1)], gain_grads))
    bytes_got = [lax.ppermute(part, "section", swap) for part in early]
    late, gain_grads, sum_one, bytes_got, ffn_gin = together(
        (other[rows - 1], gain_grads, sum_one, bytes_got, ffn_gin)
    )
    bytes_got.append(lax.ppermute(late, "section", swap))
    for pairs in (core_pairs, side_pairs):
        gain_grads = gain_grads + lax.ppermute(gain_grads, "group", pairs)
    gain_grads = jnp.sum(lax.all_gather(gain_grads, "dp", axis=0, tiled=False), axis=0)

    kept = jnp.where(section == 0, sum_one, sum_two)
    sent = jnp.where(section == 0, sum_two, sum_one)
    got = lax.ppermute(sent, "section", swap)
    got, sum_down = together((got, sum_down))
    ffn_gdown = laid_out(gathered(sum_down), (0, 2, 1, 3))
    eighths = jnp.where(
        section == 0, jnp.concatenate([kept, got], axis=2), jnp.concatenate([got, kept], axis=2)
    )
    width = eighths.shape[2] // 2
    eighths, bytes_got = together((gathered(eighths), bytes_got))
    bytes_out = in_order(section, own, jnp.stack(bytes_got)).reshape(sections * rows, ROW_BYTES, half)
    parts = [piece for every in eighths for piece in (every[..., :width], every[..., width:])]
    section_first = laid_out([part[:2] for part in parts], (0, 4, 1, 5, 2, 6, 3, 7))
    side_first = laid_out([part[2:] for part in parts], (0, 1, 4, 5, 2, 3, 6, 7))
    grad_qkv = jnp.concatenate([section_first, side_first[:1]], axis=0)[None]

    gain_grads = lax.dynamic_slice_in_dim(gain_grads.reshape(2, 2, D), section, 1, 0)
    width = D // lax.axis_size("dp")
    gain_out = lax.dynamic_slice_in_dim(gain_grads, lax.axis_index("dp") * width, width, 2)
    return (latents_out, bytes_out, grad_qkv, side_first[1:], gain_out, ffn_gin, ffn_gdown)


def solution(mesh):
    in_specs = (
        P(("group", "dp"), None, None),
        P(("group", "dp"), None),
        P(("group", "dp"), None),
        P("section", None, "dp", None),
        P("section", "dp", None),
        P("section", None, None),
        P(("section", "dp"), None),
        P(("section", "dp"), None),
        P(("group", "dp"), None, None),
    )
    out_specs = (
        P(("group", "dp"), None, "section"),
        P(("group", "dp"), None, "section"),
        P("section", None, "dp", None),
        P("section", "dp", None),
        P("section", None, "dp"),
        P(("section", "dp"), None),
        P(("section", "dp"), None),
    )
    return jax.shard_map(shards, mesh=mesh, in_specs=in_specs, out_specs=out_specs, check_vma=False)
```

```python
import functools

import jax
import jax.numpy as jnp
from jax import lax
from jax.experimental import pallas as pl
from jax.experimental.pallas import tpu as pltpu
from jax.sharding import PartitionSpec as P

D = 1024
HEADS = 16
HEAD_DIM = 64
PAIR = 2 * HEAD_DIM
PAIRS = HEADS // 2
FF = 2816
ROW_BYTES = 1024
PATCHES = 256
QT = 128
TILES = PATCHES // QT
CAUSAL_SPANS = ((0, 1), (0, 2))

EPS = 1e-05
SCALE = HEAD_DIM ** (-0.5)
EXCLUDED = -1e30

BF = jnp.bfloat16
F32 = jnp.float32


def nn(left, right):
    return jnp.dot(left, right, preferred_element_type=F32)


def tn(left, right):
    return lax.dot_general(left, right, (((0,), (0,)), ((), ())), preferred_element_type=F32)


def nt(left, right):
    return lax.dot_general(left, right, (((1,), (1,)), ((), ())), preferred_element_type=F32)


def two_heads(block):
    lane = lax.broadcasted_iota(jnp.int32, block.shape, 1)
    zero = jnp.zeros_like(block)
    first = lane < HEAD_DIM
    return jnp.concatenate([jnp.where(first, block, zero), jnp.where(first, zero, block)], axis=0)


def own_lanes(both):
    picked = jnp.concatenate([both[:HEAD_DIM, :QT], both[HEAD_DIM:, QT:]], axis=0)
    return picked.T


def twice(row):
    return jnp.concatenate([row, row], axis=1)


def fill_bias(keys, lo_ref, hi_ref, bias_ref):
    at = lax.broadcasted_iota(jnp.int32, (keys, QT), 0)
    for tile in range(TILES):
        own = pl.ds(tile * QT, QT)
        inside = (at >= lo_ref[0, :, own]) & (at < hi_ref[0, :, own])
        bias_ref[tile] = jnp.where(inside, 0.0, EXCLUDED)


def over_chunks(spans, tile, bounds, body, init):
    if spans is None:
        return lax.fori_loop(*bounds, body, init)
    for j in range(*spans[tile]):
        init = body(j, init)
    return init


def chunk_at(spans, chunk, j):
    return pl.ds(j * chunk if spans is not None else pl.multiple_of(j * chunk, chunk), chunk)


def attend_kernel(
    chunk, spans, first_ref, stop_ref, lo_ref, hi_ref, q_ref, k_ref, v_ref, c_ref, l_ref, bias_ref, s_ref
):
    row = pl.program_id(0)
    pairs = range(q_ref.shape[1] // PAIR)
    lanes = [pl.ds(pair * PAIR, PAIR) for pair in pairs]
    pl.when(pl.program_id(1) == 0)(lambda: fill_bias(k_ref.shape[0], lo_ref, hi_ref, bias_ref))
    for tile in range(TILES):
        own = pl.ds(tile * QT, QT)
        queries = [two_heads(q_ref[own, at].astype(F32) * SCALE).astype(BF) for at in lanes]
        bounds = (first_ref[row, tile], stop_ref[row, tile])

        def scores(j, tops):
            here = chunk_at(spans, chunk, j)
            bias = twice(bias_ref[tile, here, :])
            out = []
            for pair in pairs:
                part = nt(k_ref[here, lanes[pair]], queries[pair]) + bias
                s_ref[pair, here, :] = part
                out.append(jnp.maximum(tops[pair], jnp.max(part, axis=0, keepdims=True)))
            return tuple(out)

        tops = (jnp.full((1, 2 * QT), EXCLUDED, F32),) * len(pairs)
        tops = over_chunks(spans, tile, bounds, scores, tops)

        def context(j, sums):
            here = chunk_at(spans, chunk, j)
            out = []
            for pair in pairs:
                total, acc = sums[pair]
                weight = jnp.exp(s_ref[pair, here, :] - tops[pair])
                total = total + jnp.sum(weight, axis=0, keepdims=True)
                out.append((total, acc + tn(v_ref[here, lanes[pair]], weight.astype(BF))))
            return tuple(out)

        sums = ((jnp.zeros((1, 2 * QT), F32), jnp.zeros((PAIR, 2 * QT), F32)),) * len(pairs)
        sums = over_chunks(spans, tile, bounds, context, sums)
        for pair in pairs:
            total, acc = sums[pair]
            c_ref[own, lanes[pair]] = own_lanes(acc / total).astype(BF)
            l_ref[0, pair, tile : tile + 1, :] = tops[pair] + jnp.log(total)


def attend_back_kernel(
    chunk, spans, first_ref, stop_ref, lo_ref, hi_ref, q_ref, k_ref, v_ref, l_ref, c_ref, dc_ref,
    dq_ref, dk_ref, dv_ref, bias_ref, dk_acc, dv_acc,
):
    row = pl.program_id(0)
    pairs = range(q_ref.shape[1] // PAIR)
    lanes = [pl.ds(pair * PAIR, PAIR) for pair in pairs]
    pl.when(pl.program_id(1) == 0)(lambda: fill_bias(k_ref.shape[0], lo_ref, hi_ref, bias_ref))
    dk_acc[...] = jnp.zeros_like(dk_acc)
    dv_acc[...] = jnp.zeros_like(dv_acc)
    for tile in range(TILES):
        own = pl.ds(tile * QT, QT)
        queries, grads, deltas, logs = [], [], [], []
        for pair in pairs:
            queries.append(two_heads(q_ref[own, lanes[pair]].astype(F32) * SCALE).astype(BF))
            grad = dc_ref[own, lanes[pair]].astype(F32)
            inner = (grad * c_ref[own, lanes[pair]].astype(F32)).T
            heads = [jnp.sum(part, axis=0, keepdims=True) for part in (inner[:HEAD_DIM], inner[HEAD_DIM:])]
            deltas.append(jnp.concatenate(heads, axis=1))
            grads.append(two_heads(grad).astype(BF))
            logs.append(l_ref[0, pair, tile : tile + 1, :])

        def step(j, accs):
            here = chunk_at(spans, chunk, j)
            bias = twice(bias_ref[tile, here, :])
            out = []
            for pair in pairs:
                keys = k_ref[here, lanes[pair]]
                prob = jnp.exp(nt(keys, queries[pair]) + bias - logs[pair])
                slope = prob * (nt(v_ref[here, lanes[pair]], grads[pair]) - deltas[pair])
                slope = slope.astype(BF)
                dv_acc[here, lanes[pair]] += nn(prob.astype(BF), grads[pair])
                dk_acc[here, lanes[pair]] += nn(slope, queries[pair])
                out.append(accs[pair] + tn(keys, slope))
            return tuple(out)

        bounds = (first_ref[row, tile], stop_ref[row, tile])
        accs = (jnp.zeros((PAIR, 2 * QT), F32),) * len(pairs)
        accs = over_chunks(spans, tile, bounds, step, accs)
        for pair in pairs:
            dq_ref[own, lanes[pair]] = (own_lanes(accs[pair]) * SCALE).astype(BF)
    dk_ref[...] = dk_acc[...].astype(BF)
    dv_ref[...] = dv_acc[...].astype(BF)


def attention_specs(keys, wide):
    per_query = pl.BlockSpec((PATCHES, wide * PAIR), lambda r, h, *_: (r, h))
    per_key = pl.BlockSpec((keys, wide * PAIR), lambda r, h, *_: (r, h))
    bound = pl.BlockSpec((1, 1, PATCHES), lambda r, h, *_: (r, 0, 0))
    logs = pl.BlockSpec((1, wide, TILES, 2 * QT), lambda r, h, *_: (r, h, 0, 0))
    return per_query, per_key, bound, logs


def kernel_cost(q, k, products):
    scores = q.shape[0] * k.shape[0] // (q.shape[0] // PATCHES) * HEADS
    return pl.CostEstimate(
        flops=products * 2 * scores * 256, bytes_accessed=2 * q.nbytes + 4 * k.nbytes, transcendentals=scores
    )


def attend(bounds, q, k, v, wide, spans=None):
    first, stop, lo, hi, chunk = bounds
    rows = lo.shape[0]
    keys = k.shape[0] // rows
    per_query, per_key, bound, logs = attention_specs(keys, wide)
    return pl.pallas_call(
        functools.partial(attend_kernel, chunk, spans),
        grid_spec=pltpu.PrefetchScalarGridSpec(
            num_scalar_prefetch=2,
            grid=(rows, PAIRS // wide),
            in_specs=[bound, bound, per_query, per_key, per_key],
            out_specs=[per_query, logs],
            scratch_shapes=[pltpu.VMEM((TILES, keys, QT), F32), pltpu.VMEM((wide, keys, 2 * QT), F32)],
        ),
        out_shape=[
            jax.ShapeDtypeStruct(q.shape, BF),
            jax.ShapeDtypeStruct((rows, PAIRS, TILES, 2 * QT), F32),
        ],
        compiler_params=pltpu.CompilerParams(vmem_limit_bytes=48 << 20),
        cost_estimate=kernel_cost(q, k, 2),
        name="attend",
    )(first, stop, lo, hi, q, k, v)


def attend_back(bounds, q, k, v, logsum, context, grads, wide, spans=None):
    first, stop, lo, hi, chunk = bounds
    rows = lo.shape[0]
    keys = k.shape[0] // rows
    per_query, per_key, bound, logs = attention_specs(keys, wide)
    return pl.pallas_call(
        functools.partial(attend_back_kernel, chunk, spans),
        grid_spec=pltpu.PrefetchScalarGridSpec(
            num_scalar_prefetch=2,
            grid=(rows, PAIRS // wide),
            in_specs=[bound, bound, per_query, per_key, per_key, logs, per_query, per_query],
            out_specs=[per_query, per_key, per_key],
            scratch_shapes=[pltpu.VMEM((TILES, keys, QT), F32)] + [pltpu.VMEM((keys, wide * PAIR), F32)] * 2,
        ),
        out_shape=[
            jax.ShapeDtypeStruct(q.shape, BF),
            jax.ShapeDtypeStruct(k.shape, BF),
            jax.ShapeDtypeStruct(k.shape, BF),
        ],
        compiler_params=pltpu.CompilerParams(vmem_limit_bytes=48 << 20),
        cost_estimate=kernel_cost(q, k, 5),
        name="attend_back",
    )(first, stop, lo, hi, q, k, v, logsum, context, grads)


def scale_of(values):
    return lax.rsqrt(jnp.mean(values * values, axis=-1, keepdims=True) + EPS)


def norm_backward(values, row_scale, gain_row, incoming):
    weighted = incoming * gain_row
    projection = jnp.mean(weighted * values, axis=-1, keepdims=True)
    grad_values = row_scale * weighted - values * (row_scale * row_scale * row_scale) * projection
    grad_gain = jnp.sum(incoming * values * row_scale, axis=0)
    return grad_values, grad_gain


def chunk_bounds(lo, hi, chunk):
    first = lo[:, ::QT] // chunk
    stop = (hi[:, QT - 1 :: QT] + chunk - 1) // chunk
    return first, stop, lo[:, None, :], hi[:, None, :], chunk


def shards(
    byte_states, patch_lengths, patch_docs, attn_qkv, attn_out, norm_gains, ffn_in, ffn_down, cotangent
):
    section = lax.axis_index("section")
    group = lax.axis_index("group")
    sections = lax.axis_size("section")
    groups = lax.axis_size("group")
    core, side = group % 2, group // 2

    core_pairs = [(0, 1), (1, 0), (2, 3), (3, 2)]
    side_pairs = [(0, 2), (1, 3), (2, 0), (3, 1)]
    swap = [(0, 1), (1, 0)]
    together = lax.optimization_barrier

    four = jnp.concatenate([attn_qkv[0], attn_out], axis=0)
    matrix = lax.dynamic_index_in_dim(four, group, 0, keepdims=False)
    matrices = lax.all_gather(matrix, ("section", "group", "dp"), axis=0, tiled=True)

    gains = lax.all_gather(norm_gains, "section", axis=0, tiled=True)

    def quarter_of(shard):
        height = shard.shape[0] // groups
        return lax.dynamic_slice_in_dim(shard, group * height, height, 0)

    def in_order(part, own, got):
        return jnp.where(part == 0, jnp.stack([own, got]), jnp.stack([got, own]))

    def both(values, part, axis, pairs):
        return in_order(part, values, lax.ppermute(values, axis, pairs))

    units = FF // sections

    def of_units(values, part):
        halves = [lax.dynamic_slice_in_dim(values, at + part * units, units, 1) for at in (0, FF)]
        return jnp.concatenate(halves, axis=1)

    quarter = quarter_of(ffn_in)
    got = lax.ppermute(of_units(quarter, 1 - section), "section", swap)
    w_in = in_order(section, of_units(quarter, section), got)
    w_in = lax.all_gather(w_in, ("dp", "group"), axis=1, tiled=True).reshape(D, 2 * units)

    line, place = lax.axis_size("dp"), lax.axis_index("dp")
    quarter = quarter_of(ffn_down)
    down = jnp.zeros((line,) + quarter.shape, BF)
    for step in range(line):
        moved = lax.ppermute(quarter, "dp", [(i, (i + step) % line) for i in range(line)]) if step else quarter
        down = lax.dynamic_update_slice_in_dim(down, moved[None], (place - step) % line, 0)
    matrices = matrices.reshape(sections, groups, D, D)
    wq, wk, wv, wo = [matrices[:, index] for index in range(4)]

    rows = byte_states.shape[0] // sections
    mine = lambda a: lax.dynamic_slice_in_dim(a, section * rows, rows, 0)
    states, lengths, docs, cot = [mine(a) for a in (byte_states, patch_lengths, patch_docs, cotangent)]
    tokens = rows * PATCHES
    cot = cot.reshape(tokens, D)
    other_cot = lax.dynamic_slice_in_dim(cotangent, (1 - section) * rows, rows, 0).reshape(tokens, D)
    cots = jnp.concatenate([cot, other_cot], axis=0)

    ends = jnp.cumsum(lengths, axis=1)
    earlier = docs[:, None, :] < docs[:, :, None]
    doc_start = jnp.sum(jnp.where(earlier, lengths[:, None, :], 0), axis=2)
    doc_first = jnp.sum(earlier.astype(jnp.int32), axis=2)
    cross, cross_back = chunk_bounds(doc_start, ends, 256), chunk_bounds(doc_start, ends, 512)
    ids = jnp.broadcast_to(lax.iota(jnp.int32, PATCHES) + 1, doc_first.shape)
    causal = chunk_bounds(doc_first, ids, 128)
    positions = lax.iota(jnp.int32, ROW_BYTES)
    member = (positions < ends[:, :, None]) & (positions >= (ends - lengths)[:, :, None])
    member = member.astype(BF)
    count = lengths.astype(F32).reshape(rows * PATCHES, 1)

    pooled = jnp.einsum("rpb,rbd->rpd", member, states, preferred_element_type=F32)
    pooled = pooled.reshape(rows * PATCHES, D) / count
    wide = states.reshape(rows * ROW_BYTES, D).astype(F32)
    query_scale, key_scale = scale_of(pooled), scale_of(wide)
    query_in = (pooled * query_scale * gains[0, 0]).astype(BF)
    key_in = (wide * key_scale * gains[0, 1]).astype(BF)
    q1 = nn(query_in, wq[0]).astype(BF)
    k1 = nn(key_in, wk[0]).astype(BF)
    v1 = nn(key_in, wv[0]).astype(BF)
    v1, down = together((v1, down))
    down = both(down, side, "group", side_pairs)
    c1, l1 = attend(cross, q1, k1, v1, 8)
    carried = (pooled + nn(c1, wo[0])).astype(BF)

    carried_wide = carried.astype(F32)
    first_scale = scale_of(carried_wide)
    normed_in = (carried_wide * first_scale * gains[1, 0]).astype(BF)
    q2 = nn(normed_in, wq[1]).astype(BF)
    k2 = nn(normed_in, wk[1]).astype(BF)
    v2 = nn(normed_in, wv[1]).astype(BF)
    c2, l2 = attend(causal, q2, k2, v2, 8, CAUSAL_SPANS)
    c2, down = together((c2, down))
    down = both(down, core, "group", core_pairs)
    w_down = down.transpose(2, 1, 0, 3, 4).reshape(units, D)
    residual = carried_wide + nn(c2, wo[1])
    second_scale = scale_of(residual)
    mix_in = (residual * second_scale * gains[1, 1]).astype(BF)
    mix_got = lax.ppermute(mix_in, "section", swap)
    grad_hidden = nt(cots, w_down).astype(BF)
    mix_got, grad_hidden = together((mix_got, grad_hidden))
    mixed = jnp.concatenate([mix_in, mix_got], axis=0)
    gate_up = nn(mixed, w_in)
    gate, up = gate_up[:, :units], gate_up[:, units:]
    sig = jax.nn.sigmoid(gate)
    hidden = (gate * sig * up).astype(BF)

    grad_hidden = grad_hidden.astype(F32)
    grad_gate = grad_hidden * up * sig * (1.0 + gate * (1.0 - sig))
    grad_up = grad_hidden * gate * sig
    dgu = together(jnp.concatenate([grad_gate, grad_up], axis=1).astype(BF))

    def exchanged(values, axis, part, pairs, where):
        size = values.shape[where] // 2
        other = lax.dynamic_slice_in_dim(values, (1 - part) * size, size, where)
        own = lax.dynamic_slice_in_dim(values, part * size, size, where)
        return (own.astype(F32) + lax.ppermute(other, axis, pairs).astype(F32)).astype(BF)

    def over_section(values, where):
        return exchanged(values, "section", section, swap, where)

    def over_side(values, where):
        return exchanged(values, "group", side, side_pairs, where)

    def columns(values, part):
        size = values.shape[-1] // 2
        return lax.dynamic_slice_in_dim(values, part * size, size, values.ndim - 1)

    def line_sum(values, where):
        return lax.psum_scatter(values, "dp", scatter_dimension=where, tiled=True)

    def products(pairs, part):
        out = [tn(left, columns(right, part)) for left, right in pairs]
        return out[0] if len(out) == 1 else jnp.stack(out)

    def to_core(pairs):
        return products(pairs, 1 - core).astype(BF)

    def of_chip(pairs, sent):
        got = lax.ppermute(sent, "group", core_pairs)
        return (products(pairs, core) + got.astype(F32)).astype(BF)

    dgu, mix_other = together((dgu, nt(dgu[tokens:], w_in).astype(BF)))
    in_pairs, down_pairs = [(mixed, dgu)], [(hidden, cots)]
    send_in, send_down = to_core(in_pairs), to_core(down_pairs)
    mix_got = [lax.ppermute(mix_other[:PATCHES], "section", swap)]
    dgu_own, send_in, send_down, mix_got[0], rest = together(
        (dgu[:tokens], send_in, send_down, mix_got[0], mix_other[PATCHES:])
    )
    mix_got.append(lax.ppermute(rest, "section", swap))

    half = D // sections
    parts = nn(hidden, w_down)
    parts = jnp.concatenate([residual + parts[:tokens], parts[tokens:]], axis=0)
    sent = lax.dynamic_slice_in_dim(parts, (1 - section) * half, half, 1).astype(BF)
    kept = lax.dynamic_slice_in_dim(parts, section * half, half, 1)
    dgu_own, sent = together((dgu_own, sent))
    got = lax.ppermute(sent, "section", swap)

    half_in, half_down = of_chip(in_pairs, send_in), of_chip(down_pairs, send_down)
    mix_got, half_in, half_down = together((mix_got, half_in, half_down))
    grad_mixed = nt(dgu_own, w_in) + jnp.concatenate(mix_got, axis=0).astype(F32)
    grad_mix, gain_mix = norm_backward(residual, second_scale, gains[1, 1], grad_mixed)
    grad_residual = grad_mix + cot.astype(F32)
    branch = grad_residual.astype(BF)
    dc2 = nt(branch, wo[1]).astype(BF)

    dq2, dk2, dv2 = attend_back(causal, q2, k2, v2, l2, c2, dc2, 8, CAUSAL_SPANS)
    two_pairs = [(normed_in, dq2), (normed_in, dk2), (normed_in, dv2), (c2, branch)]
    send_two = to_core(two_pairs)
    half_in = over_side(half_in.reshape(sections, line, 2, -1, units), 2)
    sum_down = line_sum(half_down, 0)
    dq2, dk2, dv2, send_two, half_in, sum_down = together((dq2, dk2, dv2, send_two, half_in, sum_down))
    sum_in = line_sum(half_in.reshape(sections, -1, units), 1)
    grad_normed = nt(dq2, wq[1]) + nt(dk2, wk[1]) + nt(dv2, wv[1])
    grad_carried, gain_normed = norm_backward(carried_wide, first_scale, gains[1, 0], grad_normed)
    d_carried = (grad_residual + grad_carried).astype(BF)
    dc1 = nt(d_carried, wo[0]).astype(BF)
    half_two = of_chip(two_pairs, send_two)
    dc1, half_two, got = together((dc1, half_two, got))
    got = got.astype(F32)
    latents = in_order(section, kept[:tokens] + got[tokens:], kept[tokens:] + got[:tokens])
    latents_out = latents.astype(BF).reshape(sections * rows, PATCHES, half)
    dq1, dk1, dv1 = attend_back(cross_back, q1, k1, v1, l1, c1, dc1, 4)
    half_two = over_section(half_two[:2], 2), over_side(half_two[2:], 2)
    dq1, half_two = together((dq1, half_two))
    half_two = jnp.concatenate([over_side(half_two[0], 2), over_section(half_two[1], 2)], axis=0)
    one_pairs = [(query_in, dq1), (key_in, dk1)], [(key_in, dv1), (c1, d_carried)]
    send_one = [to_core(pairs) for pairs in one_pairs]
    dq1, dk1, dv1, send_one, sum_down = together((dq1, dk1, dv1, send_one, sum_down))
    def gathered(part):
        return lax.all_gather(part, "group", axis=0, tiled=False)

    def laid_out(parts, order):
        return jnp.concatenate([parts[index] for index in order], axis=-1).astype(F32)

    half_one = [of_chip(pairs, sent) for pairs, sent in zip(one_pairs, send_one)]
    dq1, dk1, dv1, half_one, half_two, sum_in = together((dq1, dk1, dv1, half_one, half_two, sum_in))
    sum_two = line_sum(half_two, 1)
    sum_in = jnp.stack([lax.dynamic_index_in_dim(sum_in, section, 0, False),
                        lax.ppermute(lax.dynamic_index_in_dim(sum_in, 1 - section, 0, False), "section", swap)])
    sum_in = jnp.where(section == 0, sum_in, sum_in[::-1])
    sum_in = gathered(sum_in)
    grad_query_in = nt(dq1, wq[0])
    grad_key_in = nt(dk1, wk[0]) + nt(dv1, wv[0])
    half_one = over_section(half_one[0], 2), over_side(half_one[1], 2)
    grad_query_in, grad_key_in, half_one = together((grad_query_in, grad_key_in, half_one))
    half_one = jnp.concatenate([over_side(half_one[0], 2), over_section(half_one[1], 2)], axis=0)
    grad_query_in, grad_key_in, half_one, sum_two, sum_down, sum_in = together(
        (grad_query_in, grad_key_in, half_one, sum_two, sum_down, sum_in)
    )
    sum_down = over_side(sum_down, 1)
    sum_one = line_sum(half_one, 1)

    grad_pooled, gain_query = norm_backward(pooled, query_scale, gains[0, 0], grad_query_in)
    grad_wide, gain_key = norm_backward(wide, key_scale, gains[0, 1], grad_key_in)
    per_patch = (grad_pooled + d_carried.astype(F32)) / count
    spread_back = jnp.einsum(
        "rpb,rpd->rbd", member, per_patch.astype(BF).reshape(rows, PATCHES, D), preferred_element_type=F32
    )
    byte_grads = (grad_wide + spread_back.reshape(rows * ROW_BYTES, D)).astype(BF)
    byte_grads = byte_grads.reshape(rows, ROW_BYTES, D)
    other = lax.dynamic_slice_in_dim(byte_grads, (1 - section) * half, half, 2)
    own = lax.dynamic_slice_in_dim(byte_grads, section * half, half, 2)

    gain_grads = jnp.stack([gain_query, gain_key, gain_normed, gain_mix])
    gain_grads = gain_grads + lax.ppermute(gain_grads, "section", swap)
    ffn_gin = jnp.concatenate(
        [laid_out([sum_in[at, t] for at in (2 * y, 2 * y + 1) for t in range(sections)], range(4)) for y in (0, 1)],
        axis=0,
    )

    early, gain_grads = together(([other[row] for row in range(rows - 1)], gain_grads))
    bytes_got = [lax.ppermute(part, "section", swap) for part in early]
    for pairs in (core_pairs, side_pairs):
        gain_grads = gain_grads + lax.ppermute(gain_grads, "group", pairs)
    gain_grads = jnp.sum(lax.all_gather(gain_grads, "dp", axis=0, tiled=False), axis=0)
    ffn_gdown = laid_out(gathered(sum_down), (0, 2, 1, 3))
    late, gain_grads, sum_one, bytes_got, ffn_gdown = together(
        (other[rows - 1], gain_grads, sum_one, bytes_got, ffn_gdown)
    )
    bytes_got.append(lax.ppermute(late, "section", swap))
    kept = jnp.where(section == 0, sum_one, sum_two)
    sent = jnp.where(section == 0, sum_two, sum_one)
    got = lax.ppermute(sent, "section", swap)
    eighths = jnp.where(
        section == 0, jnp.concatenate([kept, got], axis=2), jnp.concatenate([got, kept], axis=2)
    )
    width = eighths.shape[2] // 2
    eighths, bytes_got = together((gathered(eighths), bytes_got))
    bytes_out = in_order(section, own, jnp.stack(bytes_got)).reshape(sections * rows, ROW_BYTES, half)
    parts = [piece for every in eighths for piece in (every[..., :width], every[..., width:])]
    section_first = laid_out([part[:2] for part in parts], (0, 4, 1, 5, 2, 6, 3, 7))
    side_first = laid_out([part[2:] for part in parts], (0, 1, 4, 5, 2, 3, 6, 7))
    grad_qkv = jnp.concatenate([section_first, side_first[:1]], axis=0)[None]

    gain_grads = lax.dynamic_slice_in_dim(gain_grads.reshape(2, 2, D), section, 1, 0)
    width = D // lax.axis_size("dp")
    gain_out = lax.dynamic_slice_in_dim(gain_grads, lax.axis_index("dp") * width, width, 2)
    return (latents_out, bytes_out, grad_qkv, side_first[1:], gain_out, ffn_gin, ffn_gdown)


def solution(mesh):
    in_specs = (
        P(("group", "dp"), None, None),
        P(("group", "dp"), None),
        P(("group", "dp"), None),
        P("section", None, "dp", None),
        P("section", "dp", None),
        P("section", None, None),
        P(("section", "dp"), None),
        P(("section", "dp"), None),
        P(("group", "dp"), None, None),
    )
    out_specs = (
        P(("group", "dp"), None, "section"),
        P(("group", "dp"), None, "section"),
        P("section", None, "dp", None),
        P("section", "dp", None),
        P("section", None, "dp"),
        P(("section", "dp"), None),
        P(("section", "dp"), None),
    )
    return jax.shard_map(shards, mesh=mesh, in_specs=in_specs, out_specs=out_specs, check_vma=False)
```

```python
import functools

import jax
import jax.numpy as jnp
from jax import lax
from jax.experimental import pallas as pl
from jax.experimental.pallas import tpu as pltpu
from jax.sharding import PartitionSpec as P

D = 1024
HEADS = 16
HEAD_DIM = 64
PAIR = 2 * HEAD_DIM
PAIRS = HEADS // 2
FF = 2816
ROW_BYTES = 1024
PATCHES = 256
QT = 128
TILES = PATCHES // QT
CAUSAL_SPANS = ((0, 1), (0, 2))

EPS = 1e-05
SCALE = HEAD_DIM ** (-0.5)
EXCLUDED = -1e30

BF = jnp.bfloat16
F32 = jnp.float32


def nn(left, right):
    return jnp.dot(left, right, preferred_element_type=F32)


def tn(left, right):
    return lax.dot_general(left, right, (((0,), (0,)), ((), ())), preferred_element_type=F32)


def nt(left, right):
    return lax.dot_general(left, right, (((1,), (1,)), ((), ())), preferred_element_type=F32)


def two_heads(block):
    lane = lax.broadcasted_iota(jnp.int32, block.shape, 1)
    zero = jnp.zeros_like(block)
    first = lane < HEAD_DIM
    return jnp.concatenate([jnp.where(first, block, zero), jnp.where(first, zero, block)], axis=0)


def own_lanes(both):
    picked = jnp.concatenate([both[:HEAD_DIM, :QT], both[HEAD_DIM:, QT:]], axis=0)
    return picked.T


def twice(row):
    return jnp.concatenate([row, row], axis=1)


def fill_bias(keys, lo_ref, hi_ref, bias_ref):
    at = lax.broadcasted_iota(jnp.int32, (keys, QT), 0)
    for tile in range(TILES):
        own = pl.ds(tile * QT, QT)
        inside = (at >= lo_ref[0, :, own]) & (at < hi_ref[0, :, own])
        bias_ref[tile] = jnp.where(inside, 0.0, EXCLUDED)


def over_chunks(spans, tile, bounds, body, init):
    if spans is None:
        return lax.fori_loop(*bounds, body, init)
    for j in range(*spans[tile]):
        init = body(j, init)
    return init


def chunk_at(spans, chunk, j):
    return pl.ds(j * chunk if spans is not None else pl.multiple_of(j * chunk, chunk), chunk)


def attend_kernel(
    chunk, spans, first_ref, stop_ref, lo_ref, hi_ref, q_ref, k_ref, v_ref, c_ref, l_ref, bias_ref, s_ref
):
    row = pl.program_id(0)
    pairs = range(q_ref.shape[1] // PAIR)
    lanes = [pl.ds(pair * PAIR, PAIR) for pair in pairs]
    pl.when(pl.program_id(1) == 0)(lambda: fill_bias(k_ref.shape[0], lo_ref, hi_ref, bias_ref))
    for tile in range(TILES):
        own = pl.ds(tile * QT, QT)
        queries = [two_heads(q_ref[own, at].astype(F32) * SCALE).astype(BF) for at in lanes]
        bounds = (first_ref[row, tile], stop_ref[row, tile])

        def scores(j, tops):
            here = chunk_at(spans, chunk, j)
            bias = twice(bias_ref[tile, here, :])
            out = []
            for pair in pairs:
                part = nt(k_ref[here, lanes[pair]], queries[pair]) + bias
                s_ref[pair, here, :] = part
                out.append(jnp.maximum(tops[pair], jnp.max(part, axis=0, keepdims=True)))
            return tuple(out)

        tops = (jnp.full((1, 2 * QT), EXCLUDED, F32),) * len(pairs)
        tops = over_chunks(spans, tile, bounds, scores, tops)

        def context(j, sums):
            here = chunk_at(spans, chunk, j)
            out = []
            for pair in pairs:
                total, acc = sums[pair]
                weight = jnp.exp(s_ref[pair, here, :] - tops[pair])
                total = total + jnp.sum(weight, axis=0, keepdims=True)
                out.append((total, acc + tn(v_ref[here, lanes[pair]], weight.astype(BF))))
            return tuple(out)

        sums = ((jnp.zeros((1, 2 * QT), F32), jnp.zeros((PAIR, 2 * QT), F32)),) * len(pairs)
        sums = over_chunks(spans, tile, bounds, context, sums)
        for pair in pairs:
            total, acc = sums[pair]
            c_ref[own, lanes[pair]] = own_lanes(acc / total).astype(BF)
            l_ref[0, pair, tile : tile + 1, :] = tops[pair] + jnp.log(total)


def attend_back_kernel(
    chunk, spans, first_ref, stop_ref, lo_ref, hi_ref, q_ref, k_ref, v_ref, l_ref, c_ref, dc_ref,
    dq_ref, dk_ref, dv_ref, bias_ref, dk_acc, dv_acc,
):
    row = pl.program_id(0)
    pairs = range(q_ref.shape[1] // PAIR)
    lanes = [pl.ds(pair * PAIR, PAIR) for pair in pairs]
    pl.when(pl.program_id(1) == 0)(lambda: fill_bias(k_ref.shape[0], lo_ref, hi_ref, bias_ref))
    dk_acc[...] = jnp.zeros_like(dk_acc)
    dv_acc[...] = jnp.zeros_like(dv_acc)
    for tile in range(TILES):
        own = pl.ds(tile * QT, QT)
        queries, grads, deltas, logs = [], [], [], []
        for pair in pairs:
            queries.append(two_heads(q_ref[own, lanes[pair]].astype(F32) * SCALE).astype(BF))
            grad = dc_ref[own, lanes[pair]].astype(F32)
            inner = (grad * c_ref[own, lanes[pair]].astype(F32)).T
            heads = [jnp.sum(part, axis=0, keepdims=True) for part in (inner[:HEAD_DIM], inner[HEAD_DIM:])]
            deltas.append(jnp.concatenate(heads, axis=1))
            grads.append(two_heads(grad).astype(BF))
            logs.append(l_ref[0, pair, tile : tile + 1, :])

        def step(j, accs):
            here = chunk_at(spans, chunk, j)
            bias = twice(bias_ref[tile, here, :])
            out = []
            for pair in pairs:
                keys = k_ref[here, lanes[pair]]
                prob = jnp.exp(nt(keys, queries[pair]) + bias - logs[pair])
                slope = prob * (nt(v_ref[here, lanes[pair]], grads[pair]) - deltas[pair])
                slope = slope.astype(BF)
                dv_acc[here, lanes[pair]] += nn(prob.astype(BF), grads[pair])
                dk_acc[here, lanes[pair]] += nn(slope, queries[pair])
                out.append(accs[pair] + tn(keys, slope))
            return tuple(out)

        bounds = (first_ref[row, tile], stop_ref[row, tile])
        accs = (jnp.zeros((PAIR, 2 * QT), F32),) * len(pairs)
        accs = over_chunks(spans, tile, bounds, step, accs)
        for pair in pairs:
            dq_ref[own, lanes[pair]] = (own_lanes(accs[pair]) * SCALE).astype(BF)
    dk_ref[...] = dk_acc[...].astype(BF)
    dv_ref[...] = dv_acc[...].astype(BF)


def attention_specs(keys, wide):
    per_query = pl.BlockSpec((PATCHES, wide * PAIR), lambda r, h, *_: (r, h))
    per_key = pl.BlockSpec((keys, wide * PAIR), lambda r, h, *_: (r, h))
    bound = pl.BlockSpec((1, 1, PATCHES), lambda r, h, *_: (r, 0, 0))
    logs = pl.BlockSpec((1, wide, TILES, 2 * QT), lambda r, h, *_: (r, h, 0, 0))
    return per_query, per_key, bound, logs


def kernel_cost(q, k, products):
    scores = q.shape[0] * k.shape[0] // (q.shape[0] // PATCHES) * HEADS
    return pl.CostEstimate(
        flops=products * 2 * scores * 256, bytes_accessed=2 * q.nbytes + 4 * k.nbytes, transcendentals=scores
    )


def attend(bounds, q, k, v, wide, spans=None):
    first, stop, lo, hi, chunk = bounds
    rows = lo.shape[0]
    keys = k.shape[0] // rows
    per_query, per_key, bound, logs = attention_specs(keys, wide)
    return pl.pallas_call(
        functools.partial(attend_kernel, chunk, spans),
        grid_spec=pltpu.PrefetchScalarGridSpec(
            num_scalar_prefetch=2,
            grid=(rows, PAIRS // wide),
            in_specs=[bound, bound, per_query, per_key, per_key],
            out_specs=[per_query, logs],
            scratch_shapes=[pltpu.VMEM((TILES, keys, QT), F32), pltpu.VMEM((wide, keys, 2 * QT), F32)],
        ),
        out_shape=[
            jax.ShapeDtypeStruct(q.shape, BF),
            jax.ShapeDtypeStruct((rows, PAIRS, TILES, 2 * QT), F32),
        ],
        compiler_params=pltpu.CompilerParams(vmem_limit_bytes=48 << 20),
        cost_estimate=kernel_cost(q, k, 2),
        name="attend",
    )(first, stop, lo, hi, q, k, v)


def attend_back(bounds, q, k, v, logsum, context, grads, wide, spans=None):
    first, stop, lo, hi, chunk = bounds
    rows = lo.shape[0]
    keys = k.shape[0] // rows
    per_query, per_key, bound, logs = attention_specs(keys, wide)
    return pl.pallas_call(
        functools.partial(attend_back_kernel, chunk, spans),
        grid_spec=pltpu.PrefetchScalarGridSpec(
            num_scalar_prefetch=2,
            grid=(rows, PAIRS // wide),
            in_specs=[bound, bound, per_query, per_key, per_key, logs, per_query, per_query],
            out_specs=[per_query, per_key, per_key],
            scratch_shapes=[pltpu.VMEM((TILES, keys, QT), F32)] + [pltpu.VMEM((keys, wide * PAIR), F32)] * 2,
        ),
        out_shape=[
            jax.ShapeDtypeStruct(q.shape, BF),
            jax.ShapeDtypeStruct(k.shape, BF),
            jax.ShapeDtypeStruct(k.shape, BF),
        ],
        compiler_params=pltpu.CompilerParams(vmem_limit_bytes=48 << 20),
        cost_estimate=kernel_cost(q, k, 5),
        name="attend_back",
    )(first, stop, lo, hi, q, k, v, logsum, context, grads)


def scale_of(values):
    return lax.rsqrt(jnp.mean(values * values, axis=-1, keepdims=True) + EPS)


def norm_backward(values, row_scale, gain_row, incoming):
    weighted = incoming * gain_row
    projection = jnp.mean(weighted * values, axis=-1, keepdims=True)
    grad_values = row_scale * weighted - values * (row_scale * row_scale * row_scale) * projection
    grad_gain = jnp.sum(incoming * values * row_scale, axis=0)
    return grad_values, grad_gain


def chunk_bounds(lo, hi, chunk):
    first = lo[:, ::QT] // chunk
    stop = (hi[:, QT - 1 :: QT] + chunk - 1) // chunk
    return first, stop, lo[:, None, :], hi[:, None, :], chunk


def shards(
    byte_states, patch_lengths, patch_docs, attn_qkv, attn_out, norm_gains, ffn_in, ffn_down, cotangent
):
    section = lax.axis_index("section")
    group = lax.axis_index("group")
    sections = lax.axis_size("section")
    groups = lax.axis_size("group")
    core, side = group % 2, group // 2

    core_pairs = [(0, 1), (1, 0), (2, 3), (3, 2)]
    side_pairs = [(0, 2), (1, 3), (2, 0), (3, 1)]
    swap = [(0, 1), (1, 0)]
    together = lax.optimization_barrier

    four = jnp.concatenate([attn_qkv[0], attn_out], axis=0)
    matrix = lax.dynamic_index_in_dim(four, group, 0, keepdims=False)
    matrices = lax.all_gather(matrix, ("section", "group", "dp"), axis=0, tiled=True)

    gains = lax.all_gather(norm_gains, "section", axis=0, tiled=True)

    def quarter_of(shard):
        height = shard.shape[0] // groups
        return lax.dynamic_slice_in_dim(shard, group * height, height, 0)

    def in_order(part, own, got):
        return jnp.where(part == 0, jnp.stack([own, got]), jnp.stack([got, own]))

    def both(values, part, axis, pairs):
        return in_order(part, values, lax.ppermute(values, axis, pairs))

    units = FF // sections

    def of_units(values, part):
        halves = [lax.dynamic_slice_in_dim(values, at + part * units, units, 1) for at in (0, FF)]
        return jnp.concatenate(halves, axis=1)

    quarter = quarter_of(ffn_in)
    got = lax.ppermute(of_units(quarter, 1 - section), "section", swap)
    w_in = in_order(section, of_units(quarter, section), got)
    w_in = lax.all_gather(w_in, ("dp", "group"), axis=1, tiled=True).reshape(D, 2 * units)

    line, place = lax.axis_size("dp"), lax.axis_index("dp")
    quarter = quarter_of(ffn_down)
    down = jnp.zeros((line,) + quarter.shape, BF)
    for step in range(line):
        moved = lax.ppermute(quarter, "dp", [(i, (i + step) % line) for i in range(line)]) if step else quarter
        down = lax.dynamic_update_slice_in_dim(down, moved[None], (place - step) % line, 0)

    rows = byte_states.shape[0] // sections
    mine = lambda a: lax.dynamic_slice_in_dim(a, section * rows, rows, 0)
    states, lengths, docs, cot = [mine(a) for a in (byte_states, patch_lengths, patch_docs, cotangent)]
    tokens = rows * PATCHES
    cot = cot.reshape(tokens, D)
    other_cot = lax.dynamic_slice_in_dim(cotangent, (1 - section) * rows, rows, 0).reshape(tokens, D)
    cots = jnp.concatenate([cot, other_cot], axis=0)

    ends = jnp.cumsum(lengths, axis=1)
    earlier = docs[:, None, :] < docs[:, :, None]
    doc_start = jnp.sum(jnp.where(earlier, lengths[:, None, :], 0), axis=2)
    doc_first = jnp.sum(earlier.astype(jnp.int32), axis=2)
    cross, cross_back = chunk_bounds(doc_start, ends, 256), chunk_bounds(doc_start, ends, 512)
    ids = jnp.broadcast_to(lax.iota(jnp.int32, PATCHES) + 1, doc_first.shape)
    causal = chunk_bounds(doc_first, ids, 128)
    positions = lax.iota(jnp.int32, ROW_BYTES)
    member = (positions < ends[:, :, None]) & (positions >= (ends - lengths)[:, :, None])
    member = member.astype(BF)
    count = lengths.astype(F32).reshape(rows * PATCHES, 1)

    pooled = jnp.einsum("rpb,rbd->rpd", member, states, preferred_element_type=F32)
    pooled = pooled.reshape(rows * PATCHES, D) / count
    wide = states.reshape(rows * ROW_BYTES, D).astype(F32)
    query_scale, key_scale = scale_of(pooled), scale_of(wide)
    query_in = (pooled * query_scale * gains[0, 0]).astype(BF)
    key_in = (wide * key_scale * gains[0, 1]).astype(BF)
    matrices, key_in, query_in = together((matrices, key_in, query_in))
    matrices = matrices.reshape(sections, groups, D, D)
    wq, wk, wv, wo = [matrices[:, index] for index in range(4)]
    q1 = nn(query_in, wq[0]).astype(BF)
    k1 = nn(key_in, wk[0]).astype(BF)
    v1 = nn(key_in, wv[0]).astype(BF)
    v1, down = together((v1, down))
    down = both(down, side, "group", side_pairs)
    c1, l1 = attend(cross, q1, k1, v1, 8)
    carried = (pooled + nn(c1, wo[0])).astype(BF)

    carried_wide = carried.astype(F32)
    first_scale = scale_of(carried_wide)
    normed_in = (carried_wide * first_scale * gains[1, 0]).astype(BF)
    q2 = nn(normed_in, wq[1]).astype(BF)
    k2 = nn(normed_in, wk[1]).astype(BF)
    v2 = nn(normed_in, wv[1]).astype(BF)
    c2, l2 = attend(causal, q2, k2, v2, 8, CAUSAL_SPANS)
    c2, down = together((c2, down))
    down = both(down, core, "group", core_pairs)
    w_down = down.transpose(2, 1, 0, 3, 4).reshape(units, D)
    residual = carried_wide + nn(c2, wo[1])
    second_scale = scale_of(residual)
    mix_in = (residual * second_scale * gains[1, 1]).astype(BF)
    mix_got = lax.ppermute(mix_in, "section", swap)
    grad_hidden = nt(cots, w_down).astype(BF)
    mix_got, grad_hidden = together((mix_got, grad_hidden))
    mixed = jnp.concatenate([mix_in, mix_got], axis=0)
    gate_up = nn(mixed, w_in)
    gate, up = gate_up[:, :units], gate_up[:, units:]
    sig = jax.nn.sigmoid(gate)
    hidden = (gate * sig * up).astype(BF)

    grad_hidden = grad_hidden.astype(F32)
    grad_gate = grad_hidden * up * sig * (1.0 + gate * (1.0 - sig))
    grad_up = grad_hidden * gate * sig
    dgu = together(jnp.concatenate([grad_gate, grad_up], axis=1).astype(BF))

    def exchanged(values, axis, part, pairs, where):
        size = values.shape[where] // 2
        other = lax.dynamic_slice_in_dim(values, (1 - part) * size, size, where)
        own = lax.dynamic_slice_in_dim(values, part * size, size, where)
        return (own.astype(F32) + lax.ppermute(other, axis, pairs).astype(F32)).astype(BF)

    def over_section(values, where):
        return exchanged(values, "section", section, swap, where)

    def over_side(values, where):
        return exchanged(values, "group", side, side_pairs, where)

    def columns(values, part):
        size = values.shape[-1] // 2
        return lax.dynamic_slice_in_dim(values, part * size, size, values.ndim - 1)

    def line_sum(values, where):
        return lax.psum_scatter(values, "dp", scatter_dimension=where, tiled=True)

    def products(pairs, part):
        out = [tn(left, columns(right, part)) for left, right in pairs]
        return out[0] if len(out) == 1 else jnp.stack(out)

    def to_core(pairs):
        return products(pairs, 1 - core).astype(BF)

    def of_chip(pairs, sent):
        got = lax.ppermute(sent, "group", core_pairs)
        return (products(pairs, core) + got.astype(F32)).astype(BF)

    dgu, mix_other = together((dgu, nt(dgu[tokens:], w_in).astype(BF)))
    in_pairs, down_pairs = [(mixed, dgu)], [(hidden, cots)]
    send_in, send_down = to_core(in_pairs), to_core(down_pairs)
    mix_got = [lax.ppermute(mix_other[:PATCHES], "section", swap)]
    dgu_own, send_in, send_down, mix_got[0], rest = together(
        (dgu[:tokens], send_in, send_down, mix_got[0], mix_other[PATCHES:])
    )
    mix_got.append(lax.ppermute(rest, "section", swap))

    half = D // sections
    parts = nn(hidden, w_down)
    parts = jnp.concatenate([residual + parts[:tokens], parts[tokens:]], axis=0)
    sent = lax.dynamic_slice_in_dim(parts, (1 - section) * half, half, 1).astype(BF)
    kept = lax.dynamic_slice_in_dim(parts, section * half, half, 1)
    dgu_own, sent = together((dgu_own, sent))
    got = lax.ppermute(sent, "section", swap)

    half_in, half_down = of_chip(in_pairs, send_in), of_chip(down_pairs, send_down)
    mix_got, half_in, half_down = together((mix_got, half_in, half_down))
    grad_mixed = nt(dgu_own, w_in) + jnp.concatenate(mix_got, axis=0).astype(F32)
    grad_mix, gain_mix = norm_backward(residual, second_scale, gains[1, 1], grad_mixed)
    grad_residual = grad_mix + cot.astype(F32)
    branch = grad_residual.astype(BF)
    dc2 = nt(branch, wo[1]).astype(BF)

    dq2, dk2, dv2 = attend_back(causal, q2, k2, v2, l2, c2, dc2, 8, CAUSAL_SPANS)
    two_pairs = [(normed_in, dq2), (normed_in, dk2), (normed_in, dv2), (c2, branch)]
    send_two = to_core(two_pairs)
    half_in = over_side(half_in.reshape(sections, line, 2, -1, units), 2)
    sum_down = line_sum(half_down, 0)
    dq2, dk2, dv2, send_two, half_in, sum_down = together((dq2, dk2, dv2, send_two, half_in, sum_down))
    sum_in = line_sum(half_in.reshape(sections, -1, units), 1)
    grad_normed = nt(dq2, wq[1]) + nt(dk2, wk[1]) + nt(dv2, wv[1])
    grad_carried, gain_normed = norm_backward(carried_wide, first_scale, gains[1, 0], grad_normed)
    d_carried = (grad_residual + grad_carried).astype(BF)
    dc1 = nt(d_carried, wo[0]).astype(BF)
    half_two = of_chip(two_pairs, send_two)
    dc1, half_two, got = together((dc1, half_two, got))
    got = got.astype(F32)
    latents = in_order(section, kept[:tokens] + got[tokens:], kept[tokens:] + got[:tokens])
    latents_out = latents.astype(BF).reshape(sections * rows, PATCHES, half)
    dq1, dk1, dv1 = attend_back(cross_back, q1, k1, v1, l1, c1, dc1, 4)
    half_two = over_section(half_two[:2], 2), over_side(half_two[2:], 2)
    dq1, half_two = together((dq1, half_two))
    half_two = jnp.concatenate([over_side(half_two[0], 2), over_section(half_two[1], 2)], axis=0)
    one_pairs = [(query_in, dq1), (key_in, dk1)], [(key_in, dv1), (c1, d_carried)]
    send_one = [to_core(pairs) for pairs in one_pairs]
    dq1, dk1, dv1, send_one, sum_down = together((dq1, dk1, dv1, send_one, sum_down))
    sum_down = over_side(sum_down, 1)
    def gathered(part):
        return lax.all_gather(part, "group", axis=0, tiled=False)

    def laid_out(parts, order):
        return jnp.concatenate([parts[index] for index in order], axis=-1).astype(F32)

    half_one = [of_chip(pairs, sent) for pairs, sent in zip(one_pairs, send_one)]
    dq1, dk1, dv1, half_one, half_two, sum_in = together((dq1, dk1, dv1, half_one, half_two, sum_in))
    sum_two = line_sum(half_two, 1)
    sum_in = jnp.stack([lax.dynamic_index_in_dim(sum_in, section, 0, False),
                        lax.ppermute(lax.dynamic_index_in_dim(sum_in, 1 - section, 0, False), "section", swap)])
    sum_in = jnp.where(section == 0, sum_in, sum_in[::-1])
    sum_in = gathered(sum_in)
    grad_query_in = nt(dq1, wq[0])
    grad_key_in = nt(dk1, wk[0]) + nt(dv1, wv[0])
    half_one = over_section(half_one[0], 2), over_side(half_one[1], 2)
    grad_query_in, grad_key_in, half_one = together((grad_query_in, grad_key_in, half_one))
    half_one = jnp.concatenate([over_side(half_one[0], 2), over_section(half_one[1], 2)], axis=0)
    ffn_gdown = laid_out(gathered(sum_down), (0, 2, 1, 3))
    grad_query_in, grad_key_in, half_one, sum_two, ffn_gdown, sum_in = together(
        (grad_query_in, grad_key_in, half_one, sum_two, ffn_gdown, sum_in)
    )
    sum_one = line_sum(half_one, 1)

    grad_pooled, gain_query = norm_backward(pooled, query_scale, gains[0, 0], grad_query_in)
    grad_wide, gain_key = norm_backward(wide, key_scale, gains[0, 1], grad_key_in)
    per_patch = (grad_pooled + d_carried.astype(F32)) / count
    spread_back = jnp.einsum(
        "rpb,rpd->rbd", member, per_patch.astype(BF).reshape(rows, PATCHES, D), preferred_element_type=F32
    )
    byte_grads = (grad_wide + spread_back.reshape(rows * ROW_BYTES, D)).astype(BF)
    byte_grads = byte_grads.reshape(rows, ROW_BYTES, D)
    other = lax.dynamic_slice_in_dim(byte_grads, (1 - section) * half, half, 2)
    own = lax.dynamic_slice_in_dim(byte_grads, section * half, half, 2)

    gain_grads = jnp.stack([gain_query, gain_key, gain_normed, gain_mix])
    gain_grads = gain_grads + lax.ppermute(gain_grads, "section", swap)
    ffn_gin = jnp.concatenate(
        [laid_out([sum_in[at, t] for at in (2 * y, 2 * y + 1) for t in range(sections)], range(4)) for y in (0, 1)],
        axis=0,
    )

    early, gain_grads = together(([other[row] for row in range(rows - 1)], gain_grads))
    bytes_got = [lax.ppermute(part, "section", swap) for part in early]
    for pairs in (core_pairs, side_pairs):
        gain_grads = gain_grads + lax.ppermute(gain_grads, "group", pairs)
    gain_grads = jnp.sum(lax.all_gather(gain_grads, "dp", axis=0, tiled=False), axis=0)
    late, gain_grads, sum_one, bytes_got = together((other[rows - 1], gain_grads, sum_one, bytes_got))
    bytes_got.append(lax.ppermute(late, "section", swap))
    kept = jnp.where(section == 0, sum_one, sum_two)
    sent = jnp.where(section == 0, sum_two, sum_one)
    got = lax.ppermute(sent, "section", swap)
    eighths = jnp.where(
        section == 0, jnp.concatenate([kept, got], axis=2), jnp.concatenate([got, kept], axis=2)
    )
    width = eighths.shape[2] // 2
    eighths, bytes_got = together((gathered(eighths), bytes_got))
    bytes_out = in_order(section, own, jnp.stack(bytes_got)).reshape(sections * rows, ROW_BYTES, half)
    parts = [piece for every in eighths for piece in (every[..., :width], every[..., width:])]
    section_first = laid_out([part[:2] for part in parts], (0, 4, 1, 5, 2, 6, 3, 7))
    side_first = laid_out([part[2:] for part in parts], (0, 1, 4, 5, 2, 3, 6, 7))
    grad_qkv = jnp.concatenate([section_first, side_first[:1]], axis=0)[None]

    gain_grads = lax.dynamic_slice_in_dim(gain_grads.reshape(2, 2, D), section, 1, 0)
    width = D // lax.axis_size("dp")
    gain_out = lax.dynamic_slice_in_dim(gain_grads, lax.axis_index("dp") * width, width, 2)
    return (latents_out, bytes_out, grad_qkv, side_first[1:], gain_out, ffn_gin, ffn_gdown)


def solution(mesh):
    in_specs = (
        P(("group", "dp"), None, None),
        P(("group", "dp"), None),
        P(("group", "dp"), None),
        P("section", None, "dp", None),
        P("section", "dp", None),
        P("section", None, None),
        P(("section", "dp"), None),
        P(("section", "dp"), None),
        P(("group", "dp"), None, None),
    )
    out_specs = (
        P(("group", "dp"), None, "section"),
        P(("group", "dp"), None, "section"),
        P("section", None, "dp", None),
        P("section", "dp", None),
        P("section", None, "dp"),
        P(("section", "dp"), None),
        P(("section", "dp"), None),
    )
    return jax.shard_map(shards, mesh=mesh, in_specs=in_specs, out_specs=out_specs, check_vma=False)
```

```python
import functools

import jax
import jax.numpy as jnp
from jax import lax
from jax.experimental import pallas as pl
from jax.experimental.pallas import tpu as pltpu
from jax.sharding import PartitionSpec as P

D = 1024
HEADS = 16
HEAD_DIM = 64
PAIR = 2 * HEAD_DIM
PAIRS = HEADS // 2
FF = 2816
ROW_BYTES = 1024
PATCHES = 256
QT = 128
TILES = PATCHES // QT
CAUSAL_SPANS = ((0, 1), (0, 2))

EPS = 1e-05
SCALE = HEAD_DIM ** (-0.5)
EXCLUDED = -1e30

BF = jnp.bfloat16
F32 = jnp.float32


def nn(left, right):
    return jnp.dot(left, right, preferred_element_type=F32)


def tn(left, right):
    return lax.dot_general(left, right, (((0,), (0,)), ((), ())), preferred_element_type=F32)


def nt(left, right):
    return lax.dot_general(left, right, (((1,), (1,)), ((), ())), preferred_element_type=F32)


def two_heads(block):
    lane = lax.broadcasted_iota(jnp.int32, block.shape, 1)
    zero = jnp.zeros_like(block)
    first = lane < HEAD_DIM
    return jnp.concatenate([jnp.where(first, block, zero), jnp.where(first, zero, block)], axis=0)


def own_lanes(both):
    picked = jnp.concatenate([both[:HEAD_DIM, :QT], both[HEAD_DIM:, QT:]], axis=0)
    return picked.T


def twice(row):
    return jnp.concatenate([row, row], axis=1)


def fill_bias(keys, lo_ref, hi_ref, bias_ref):
    at = lax.broadcasted_iota(jnp.int32, (keys, QT), 0)
    for tile in range(TILES):
        own = pl.ds(tile * QT, QT)
        inside = (at >= lo_ref[0, :, own]) & (at < hi_ref[0, :, own])
        bias_ref[tile] = jnp.where(inside, 0.0, EXCLUDED)


def over_chunks(spans, tile, bounds, body, init):
    if spans is None:
        return lax.fori_loop(*bounds, body, init)
    for j in range(*spans[tile]):
        init = body(j, init)
    return init


def chunk_at(spans, chunk, j):
    return pl.ds(j * chunk if spans is not None else pl.multiple_of(j * chunk, chunk), chunk)


def attend_kernel(
    chunk, spans, first_ref, stop_ref, lo_ref, hi_ref, q_ref, k_ref, v_ref, c_ref, l_ref, bias_ref, s_ref
):
    row = pl.program_id(0)
    pairs = range(q_ref.shape[1] // PAIR)
    lanes = [pl.ds(pair * PAIR, PAIR) for pair in pairs]
    pl.when(pl.program_id(1) == 0)(lambda: fill_bias(k_ref.shape[0], lo_ref, hi_ref, bias_ref))
    for tile in range(TILES):
        own = pl.ds(tile * QT, QT)
        queries = [two_heads(q_ref[own, at].astype(F32) * SCALE).astype(BF) for at in lanes]
        bounds = (first_ref[row, tile], stop_ref[row, tile])

        def scores(j, tops):
            here = chunk_at(spans, chunk, j)
            bias = twice(bias_ref[tile, here, :])
            out = []
            for pair in pairs:
                part = nt(k_ref[here, lanes[pair]], queries[pair]) + bias
                s_ref[pair, here, :] = part
                out.append(jnp.maximum(tops[pair], jnp.max(part, axis=0, keepdims=True)))
            return tuple(out)

        tops = (jnp.full((1, 2 * QT), EXCLUDED, F32),) * len(pairs)
        tops = over_chunks(spans, tile, bounds, scores, tops)

        def context(j, sums):
            here = chunk_at(spans, chunk, j)
            out = []
            for pair in pairs:
                total, acc = sums[pair]
                weight = jnp.exp(s_ref[pair, here, :] - tops[pair])
                total = total + jnp.sum(weight, axis=0, keepdims=True)
                out.append((total, acc + tn(v_ref[here, lanes[pair]], weight.astype(BF))))
            return tuple(out)

        sums = ((jnp.zeros((1, 2 * QT), F32), jnp.zeros((PAIR, 2 * QT), F32)),) * len(pairs)
        sums = over_chunks(spans, tile, bounds, context, sums)
        for pair in pairs:
            total, acc = sums[pair]
            c_ref[own, lanes[pair]] = own_lanes(acc / total).astype(BF)
            l_ref[0, pair, tile : tile + 1, :] = tops[pair] + jnp.log(total)


def attend_back_kernel(
    chunk, spans, first_ref, stop_ref, lo_ref, hi_ref, q_ref, k_ref, v_ref, l_ref, c_ref, dc_ref,
    dq_ref, dk_ref, dv_ref, bias_ref, dk_acc, dv_acc,
):
    row = pl.program_id(0)
    pairs = range(q_ref.shape[1] // PAIR)
    lanes = [pl.ds(pair * PAIR, PAIR) for pair in pairs]
    pl.when(pl.program_id(1) == 0)(lambda: fill_bias(k_ref.shape[0], lo_ref, hi_ref, bias_ref))
    dk_acc[...] = jnp.zeros_like(dk_acc)
    dv_acc[...] = jnp.zeros_like(dv_acc)
    for tile in range(TILES):
        own = pl.ds(tile * QT, QT)
        queries, grads, deltas, logs = [], [], [], []
        for pair in pairs:
            queries.append(two_heads(q_ref[own, lanes[pair]].astype(F32) * SCALE).astype(BF))
            grad = dc_ref[own, lanes[pair]].astype(F32)
            inner = (grad * c_ref[own, lanes[pair]].astype(F32)).T
            heads = [jnp.sum(part, axis=0, keepdims=True) for part in (inner[:HEAD_DIM], inner[HEAD_DIM:])]
            deltas.append(jnp.concatenate(heads, axis=1))
            grads.append(two_heads(grad).astype(BF))
            logs.append(l_ref[0, pair, tile : tile + 1, :])

        def step(j, accs):
            here = chunk_at(spans, chunk, j)
            bias = twice(bias_ref[tile, here, :])
            out = []
            for pair in pairs:
                keys = k_ref[here, lanes[pair]]
                prob = jnp.exp(nt(keys, queries[pair]) + bias - logs[pair])
                slope = prob * (nt(v_ref[here, lanes[pair]], grads[pair]) - deltas[pair])
                slope = slope.astype(BF)
                dv_acc[here, lanes[pair]] += nn(prob.astype(BF), grads[pair])
                dk_acc[here, lanes[pair]] += nn(slope, queries[pair])
                out.append(accs[pair] + tn(keys, slope))
            return tuple(out)

        bounds = (first_ref[row, tile], stop_ref[row, tile])
        accs = (jnp.zeros((PAIR, 2 * QT), F32),) * len(pairs)
        accs = over_chunks(spans, tile, bounds, step, accs)
        for pair in pairs:
            dq_ref[own, lanes[pair]] = (own_lanes(accs[pair]) * SCALE).astype(BF)
    dk_ref[...] = dk_acc[...].astype(BF)
    dv_ref[...] = dv_acc[...].astype(BF)


def attention_specs(keys, wide):
    per_query = pl.BlockSpec((PATCHES, wide * PAIR), lambda r, h, *_: (r, h))
    per_key = pl.BlockSpec((keys, wide * PAIR), lambda r, h, *_: (r, h))
    bound = pl.BlockSpec((1, 1, PATCHES), lambda r, h, *_: (r, 0, 0))
    logs = pl.BlockSpec((1, wide, TILES, 2 * QT), lambda r, h, *_: (r, h, 0, 0))
    return per_query, per_key, bound, logs


def kernel_cost(q, k, products):
    scores = q.shape[0] * k.shape[0] // (q.shape[0] // PATCHES) * HEADS
    return pl.CostEstimate(
        flops=products * 2 * scores * 256, bytes_accessed=2 * q.nbytes + 4 * k.nbytes, transcendentals=scores
    )


def attend(bounds, q, k, v, wide, spans=None):
    first, stop, lo, hi, chunk = bounds
    rows = lo.shape[0]
    keys = k.shape[0] // rows
    per_query, per_key, bound, logs = attention_specs(keys, wide)
    return pl.pallas_call(
        functools.partial(attend_kernel, chunk, spans),
        grid_spec=pltpu.PrefetchScalarGridSpec(
            num_scalar_prefetch=2,
            grid=(rows, PAIRS // wide),
            in_specs=[bound, bound, per_query, per_key, per_key],
            out_specs=[per_query, logs],
            scratch_shapes=[pltpu.VMEM((TILES, keys, QT), F32), pltpu.VMEM((wide, keys, 2 * QT), F32)],
        ),
        out_shape=[
            jax.ShapeDtypeStruct(q.shape, BF),
            jax.ShapeDtypeStruct((rows, PAIRS, TILES, 2 * QT), F32),
        ],
        compiler_params=pltpu.CompilerParams(vmem_limit_bytes=48 << 20),
        cost_estimate=kernel_cost(q, k, 2),
        name="attend",
    )(first, stop, lo, hi, q, k, v)


def attend_back(bounds, q, k, v, logsum, context, grads, wide, spans=None):
    first, stop, lo, hi, chunk = bounds
    rows = lo.shape[0]
    keys = k.shape[0] // rows
    per_query, per_key, bound, logs = attention_specs(keys, wide)
    return pl.pallas_call(
        functools.partial(attend_back_kernel, chunk, spans),
        grid_spec=pltpu.PrefetchScalarGridSpec(
            num_scalar_prefetch=2,
            grid=(rows, PAIRS // wide),
            in_specs=[bound, bound, per_query, per_key, per_key, logs, per_query, per_query],
            out_specs=[per_query, per_key, per_key],
            scratch_shapes=[pltpu.VMEM((TILES, keys, QT), F32)] + [pltpu.VMEM((keys, wide * PAIR), F32)] * 2,
        ),
        out_shape=[
            jax.ShapeDtypeStruct(q.shape, BF),
            jax.ShapeDtypeStruct(k.shape, BF),
            jax.ShapeDtypeStruct(k.shape, BF),
        ],
        compiler_params=pltpu.CompilerParams(vmem_limit_bytes=48 << 20),
        cost_estimate=kernel_cost(q, k, 5),
        name="attend_back",
    )(first, stop, lo, hi, q, k, v, logsum, context, grads)


def scale_of(values):
    return lax.rsqrt(jnp.mean(values * values, axis=-1, keepdims=True) + EPS)


def norm_backward(values, row_scale, gain_row, incoming):
    weighted = incoming * gain_row
    projection = jnp.mean(weighted * values, axis=-1, keepdims=True)
    grad_values = row_scale * weighted - values * (row_scale * row_scale * row_scale) * projection
    grad_gain = jnp.sum(incoming * values * row_scale, axis=0)
    return grad_values, grad_gain


def chunk_bounds(lo, hi, chunk):
    first = lo[:, ::QT] // chunk
    stop = (hi[:, QT - 1 :: QT] + chunk - 1) // chunk
    return first, stop, lo[:, None, :], hi[:, None, :], chunk


def shards(
    byte_states, patch_lengths, patch_docs, attn_qkv, attn_out, norm_gains, ffn_in, ffn_down, cotangent
):
    section = lax.axis_index("section")
    group = lax.axis_index("group")
    sections = lax.axis_size("section")
    groups = lax.axis_size("group")
    core, side = group % 2, group // 2

    core_pairs = [(0, 1), (1, 0), (2, 3), (3, 2)]
    side_pairs = [(0, 2), (1, 3), (2, 0), (3, 1)]
    swap = [(0, 1), (1, 0)]
    together = lax.optimization_barrier

    four = jnp.concatenate([attn_qkv[0], attn_out], axis=0)
    matrix = lax.dynamic_index_in_dim(four, group, 0, keepdims=False)
    matrices = lax.all_gather(matrix, ("section", "group", "dp"), axis=0, tiled=True)

    gains = lax.all_gather(norm_gains, "section", axis=0, tiled=True)

    def quarter_of(shard):
        height = shard.shape[0] // groups
        return lax.dynamic_slice_in_dim(shard, group * height, height, 0)

    def in_order(part, own, got):
        return jnp.where(part == 0, jnp.stack([own, got]), jnp.stack([got, own]))

    def both(values, part, axis, pairs):
        return in_order(part, values, lax.ppermute(values, axis, pairs))

    units = FF // sections

    def of_units(values, part):
        halves = [lax.dynamic_slice_in_dim(values, at + part * units, units, 1) for at in (0, FF)]
        return jnp.concatenate(halves, axis=1)

    quarter = quarter_of(ffn_in)
    got = lax.ppermute(of_units(quarter, 1 - section), "section", swap)
    w_in = in_order(section, of_units(quarter, section), got)
    w_in = lax.all_gather(w_in, ("dp", "group"), axis=1, tiled=True).reshape(D, 2 * units)

    line, place = lax.axis_size("dp"), lax.axis_index("dp")
    quarter = quarter_of(ffn_down)
    down = jnp.zeros((line,) + quarter.shape, BF)
    for step in range(line):
        moved = lax.ppermute(quarter, "dp", [(i, (i + step) % line) for i in range(line)]) if step else quarter
        down = lax.dynamic_update_slice_in_dim(down, moved[None], (place - step) % line, 0)
    matrices = matrices.reshape(sections, groups, D, D)
    wq, wk, wv, wo = [matrices[:, index] for index in range(4)]

    rows = byte_states.shape[0] // sections
    mine = lambda a: lax.dynamic_slice_in_dim(a, section * rows, rows, 0)
    states, lengths, docs, cot = [mine(a) for a in (byte_states, patch_lengths, patch_docs, cotangent)]
    tokens = rows * PATCHES
    cot = cot.reshape(tokens, D)
    other_cot = lax.dynamic_slice_in_dim(cotangent, (1 - section) * rows, rows, 0).reshape(tokens, D)
    cots = jnp.concatenate([cot, other_cot], axis=0)

    ends = jnp.cumsum(lengths, axis=1)
    earlier = docs[:, None, :] < docs[:, :, None]
    doc_start = jnp.sum(jnp.where(earlier, lengths[:, None, :], 0), axis=2)
    doc_first = jnp.sum(earlier.astype(jnp.int32), axis=2)
    cross, cross_back = chunk_bounds(doc_start, ends, 256), chunk_bounds(doc_start, ends, 512)
    ids = jnp.broadcast_to(lax.iota(jnp.int32, PATCHES) + 1, doc_first.shape)
    causal = chunk_bounds(doc_first, ids, 128)
    positions = lax.iota(jnp.int32, ROW_BYTES)
    member = (positions < ends[:, :, None]) & (positions >= (ends - lengths)[:, :, None])
    member = member.astype(BF)
    count = lengths.astype(F32).reshape(rows * PATCHES, 1)

    pooled = jnp.einsum("rpb,rbd->rpd", member, states, preferred_element_type=F32)
    pooled = pooled.reshape(rows * PATCHES, D) / count
    wide = states.reshape(rows * ROW_BYTES, D).astype(F32)
    query_scale, key_scale = scale_of(pooled), scale_of(wide)
    query_in = (pooled * query_scale * gains[0, 0]).astype(BF)
    key_in = (wide * key_scale * gains[0, 1]).astype(BF)
    q1 = nn(query_in, wq[0]).astype(BF)
    k1 = nn(key_in, wk[0]).astype(BF)
    v1 = nn(key_in, wv[0]).astype(BF)
    v1, down = together((v1, down))
    down = both(down, side, "group", side_pairs)
    c1, l1 = attend(cross, q1, k1, v1, 8)
    carried = (pooled + nn(c1, wo[0])).astype(BF)

    carried_wide = carried.astype(F32)
    first_scale = scale_of(carried_wide)
    normed_in = (carried_wide * first_scale * gains[1, 0]).astype(BF)
    q2 = nn(normed_in, wq[1]).astype(BF)
    k2 = nn(normed_in, wk[1]).astype(BF)
    v2 = nn(normed_in, wv[1]).astype(BF)
    c2, l2 = attend(causal, q2, k2, v2, 8, CAUSAL_SPANS)
    c2, down = together((c2, down))
    down = both(down, core, "group", core_pairs)
    w_down = down.transpose(2, 1, 0, 3, 4).reshape(units, D)
    residual = carried_wide + nn(c2, wo[1])
    second_scale = scale_of(residual)
    mix_in = (residual * second_scale * gains[1, 1]).astype(BF)
    mix_got = lax.ppermute(mix_in, "section", swap)
    grad_hidden = nt(cots, w_down).astype(BF)
    mix_got, grad_hidden = together((mix_got, grad_hidden))
    mixed = jnp.concatenate([mix_in, mix_got], axis=0)
    gate_up = nn(mixed, w_in)
    gate, up = gate_up[:, :units], gate_up[:, units:]
    sig = jax.nn.sigmoid(gate)
    hidden = (gate * sig * up).astype(BF)

    grad_hidden = grad_hidden.astype(F32)
    grad_gate = grad_hidden * up * sig * (1.0 + gate * (1.0 - sig))
    grad_up = grad_hidden * gate * sig
    dgu = together(jnp.concatenate([grad_gate, grad_up], axis=1).astype(BF))

    def exchanged(values, axis, part, pairs, where):
        size = values.shape[where] // 2
        other = lax.dynamic_slice_in_dim(values, (1 - part) * size, size, where)
        own = lax.dynamic_slice_in_dim(values, part * size, size, where)
        return (own.astype(F32) + lax.ppermute(other, axis, pairs).astype(F32)).astype(BF)

    def over_section(values, where):
        return exchanged(values, "section", section, swap, where)

    def over_side(values, where):
        return exchanged(values, "group", side, side_pairs, where)

    def columns(values, part):
        size = values.shape[-1] // 2
        return lax.dynamic_slice_in_dim(values, part * size, size, values.ndim - 1)

    def line_sum(values, where):
        return lax.psum_scatter(values, "dp", scatter_dimension=where, tiled=True)

    def products(pairs, part):
        out = [tn(left, columns(right, part)) for left, right in pairs]
        return out[0] if len(out) == 1 else jnp.stack(out)

    def to_core(pairs):
        return products(pairs, 1 - core).astype(BF)

    def of_chip(pairs, sent):
        got = lax.ppermute(sent, "group", core_pairs)
        return (products(pairs, core) + got.astype(F32)).astype(BF)

    dgu, mix_other = together((dgu, nt(dgu[tokens:], w_in).astype(BF)))
    in_pairs, down_pairs = [(mixed, dgu)], [(hidden, cots)]
    send_in, send_down = to_core(in_pairs), to_core(down_pairs)
    mix_got = [lax.ppermute(mix_other[:PATCHES], "section", swap)]
    dgu_own, send_in, send_down, mix_got[0], rest = together(
        (dgu[:tokens], send_in, send_down, mix_got[0], mix_other[PATCHES:])
    )
    mix_got.append(lax.ppermute(rest, "section", swap))

    half = D // sections
    parts = nn(hidden, w_down)
    parts = jnp.concatenate([residual + parts[:tokens], parts[tokens:]], axis=0)
    sent = lax.dynamic_slice_in_dim(parts, (1 - section) * half, half, 1).astype(BF)
    kept = lax.dynamic_slice_in_dim(parts, section * half, half, 1)
    dgu_own, sent = together((dgu_own, sent))
    got = lax.ppermute(sent, "section", swap)

    half_in, half_down = of_chip(in_pairs, send_in), of_chip(down_pairs, send_down)
    mix_got, half_in, half_down = together((mix_got, half_in, half_down))
    grad_mixed = nt(dgu_own, w_in) + jnp.concatenate(mix_got, axis=0).astype(F32)
    grad_mix, gain_mix = norm_backward(residual, second_scale, gains[1, 1], grad_mixed)
    grad_residual = grad_mix + cot.astype(F32)
    branch = grad_residual.astype(BF)
    dc2 = nt(branch, wo[1]).astype(BF)

    dq2, dk2, dv2 = attend_back(causal, q2, k2, v2, l2, c2, dc2, 8, CAUSAL_SPANS)
    two_pairs = [(normed_in, dq2), (normed_in, dk2), (normed_in, dv2), (c2, branch)]
    send_two = to_core(two_pairs)
    half_in = over_side(half_in.reshape(sections, line, 2, -1, units), 2)
    sum_down = line_sum(half_down, 0)
    dq2, dk2, dv2, send_two, half_in, sum_down = together((dq2, dk2, dv2, send_two, half_in, sum_down))
    sum_in = line_sum(half_in.reshape(sections, -1, units), 1)
    grad_normed = nt(dq2, wq[1]) + nt(dk2, wk[1]) + nt(dv2, wv[1])
    grad_carried, gain_normed = norm_backward(carried_wide, first_scale, gains[1, 0], grad_normed)
    d_carried = (grad_residual + grad_carried).astype(BF)
    dc1 = nt(d_carried, wo[0]).astype(BF)
    half_two = of_chip(two_pairs, send_two)
    dc1, half_two, got = together((dc1, half_two, got))
    got = got.astype(F32)
    latents = in_order(section, kept[:tokens] + got[tokens:], kept[tokens:] + got[:tokens])
    latents_out = latents.astype(BF).reshape(sections * rows, PATCHES, half)
    dq1, dk1, dv1 = attend_back(cross_back, q1, k1, v1, l1, c1, dc1, 4)
    half_two = over_section(half_two[:2], 2), over_side(half_two[2:], 2)
    dq1, half_two = together((dq1, half_two))
    half_two = jnp.concatenate([over_side(half_two[0], 2), over_section(half_two[1], 2)], axis=0)
    one_pairs = [(query_in, dq1), (key_in, dk1)], [(key_in, dv1), (c1, d_carried)]
    send_one = [to_core(pairs) for pairs in one_pairs]
    dq1, dk1, dv1, send_one, sum_down = together((dq1, dk1, dv1, send_one, sum_down))
    def gathered(part):
        return lax.all_gather(part, "group", axis=0, tiled=False)

    def laid_out(parts, order):
        return jnp.concatenate([parts[index] for index in order], axis=-1).astype(F32)

    half_one = [of_chip(pairs, sent) for pairs, sent in zip(one_pairs, send_one)]
    dq1, dk1, dv1, half_one, half_two, sum_in = together((dq1, dk1, dv1, half_one, half_two, sum_in))
    sum_two = line_sum(half_two, 1)
    sum_in = jnp.stack([lax.dynamic_index_in_dim(sum_in, section, 0, False),
                        lax.ppermute(lax.dynamic_index_in_dim(sum_in, 1 - section, 0, False), "section", swap)])
    sum_in = jnp.where(section == 0, sum_in, sum_in[::-1])
    sum_in = gathered(sum_in)
    grad_query_in = nt(dq1, wq[0])
    grad_key_in = nt(dk1, wk[0]) + nt(dv1, wv[0])
    half_one = over_section(half_one[0], 2), over_side(half_one[1], 2)
    grad_query_in, grad_key_in, half_one = together((grad_query_in, grad_key_in, half_one))
    half_one = jnp.concatenate([over_side(half_one[0], 2), over_section(half_one[1], 2)], axis=0)
    grad_query_in, grad_key_in, half_one, sum_two, sum_down, sum_in = together(
        (grad_query_in, grad_key_in, half_one, sum_two, sum_down, sum_in)
    )
    sum_down = over_side(sum_down, 1)
    sum_one = line_sum(half_one, 1)

    grad_pooled, gain_query = norm_backward(pooled, query_scale, gains[0, 0], grad_query_in)
    grad_wide, gain_key = norm_backward(wide, key_scale, gains[0, 1], grad_key_in)
    per_patch = (grad_pooled + d_carried.astype(F32)) / count
    spread_back = jnp.einsum(
        "rpb,rpd->rbd", member, per_patch.astype(BF).reshape(rows, PATCHES, D), preferred_element_type=F32
    )
    byte_grads = (grad_wide + spread_back.reshape(rows * ROW_BYTES, D)).astype(BF)
    byte_grads = byte_grads.reshape(rows, ROW_BYTES, D)
    other = lax.dynamic_slice_in_dim(byte_grads, (1 - section) * half, half, 2)
    own = lax.dynamic_slice_in_dim(byte_grads, section * half, half, 2)

    gain_grads = jnp.stack([gain_query, gain_key, gain_normed, gain_mix])
    gain_grads = gain_grads + lax.ppermute(gain_grads, "section", swap)
    ffn_gin = jnp.concatenate(
        [laid_out([sum_in[at, t] for at in (2 * y, 2 * y + 1) for t in range(sections)], range(4)) for y in (0, 1)],
        axis=0,
    )

    early, gain_grads = together(([other[row] for row in range(rows - 1)], gain_grads))
    bytes_got = [lax.ppermute(part, "section", swap) for part in early]
    for pairs in (core_pairs, side_pairs):
        gain_grads = gain_grads + lax.ppermute(gain_grads, "group", pairs)
    gain_grads = jnp.sum(lax.all_gather(gain_grads, "dp", axis=0, tiled=False), axis=0)
    late, gain_grads, sum_one, bytes_got, sum_down = together(
        (other[rows - 1], gain_grads, sum_one, bytes_got, sum_down)
    )
    bytes_got.append(lax.ppermute(late, "section", swap))
    kept = jnp.where(section == 0, sum_one, sum_two)
    sent = jnp.where(section == 0, sum_two, sum_one)
    got = lax.ppermute(sent, "section", swap)
    got, sum_down = together((got, sum_down))
    ffn_gdown = laid_out(gathered(sum_down), (0, 2, 1, 3))
    eighths = jnp.where(
        section == 0, jnp.concatenate([kept, got], axis=2), jnp.concatenate([got, kept], axis=2)
    )
    width = eighths.shape[2] // 2
    eighths, bytes_got = together((gathered(eighths), bytes_got))
    bytes_out = in_order(section, own, jnp.stack(bytes_got)).reshape(sections * rows, ROW_BYTES, half)
    parts = [piece for every in eighths for piece in (every[..., :width], every[..., width:])]
    section_first = laid_out([part[:2] for part in parts], (0, 4, 1, 5, 2, 6, 3, 7))
    side_first = laid_out([part[2:] for part in parts], (0, 1, 4, 5, 2, 3, 6, 7))
    grad_qkv = jnp.concatenate([section_first, side_first[:1]], axis=0)[None]

    gain_grads = lax.dynamic_slice_in_dim(gain_grads.reshape(2, 2, D), section, 1, 0)
    width = D // lax.axis_size("dp")
    gain_out = lax.dynamic_slice_in_dim(gain_grads, lax.axis_index("dp") * width, width, 2)
    return (latents_out, bytes_out, grad_qkv, side_first[1:], gain_out, ffn_gin, ffn_gdown)


def solution(mesh):
    in_specs = (
        P(("group", "dp"), None, None),
        P(("group", "dp"), None),
        P(("group", "dp"), None),
        P("section", None, "dp", None),
        P("section", "dp", None),
        P("section", None, None),
        P(("section", "dp"), None),
        P(("section", "dp"), None),
        P(("group", "dp"), None, None),
    )
    out_specs = (
        P(("group", "dp"), None, "section"),
        P(("group", "dp"), None, "section"),
        P("section", None, "dp", None),
        P("section", "dp", None),
        P("section", None, "dp"),
        P(("section", "dp"), None),
        P(("section", "dp"), None),
    )
    return jax.shard_map(shards, mesh=mesh, in_specs=in_specs, out_specs=out_specs, check_vma=False)
```

```python
import functools

import jax
import jax.numpy as jnp
from jax import lax
from jax.experimental import pallas as pl
from jax.experimental.pallas import tpu as pltpu
from jax.sharding import PartitionSpec as P

D = 1024
HEADS = 16
HEAD_DIM = 64
PAIR = 2 * HEAD_DIM
PAIRS = HEADS // 2
FF = 2816
ROW_BYTES = 1024
PATCHES = 256
QT = 128
TILES = PATCHES // QT
CAUSAL_SPANS = ((0, 1), (0, 2))

EPS = 1e-05
SCALE = HEAD_DIM ** (-0.5)
EXCLUDED = -1e30

BF = jnp.bfloat16
F32 = jnp.float32


def nn(left, right):
    return jnp.dot(left, right, preferred_element_type=F32)


def tn(left, right):
    return lax.dot_general(left, right, (((0,), (0,)), ((), ())), preferred_element_type=F32)


def nt(left, right):
    return lax.dot_general(left, right, (((1,), (1,)), ((), ())), preferred_element_type=F32)


def two_heads(block):
    lane = lax.broadcasted_iota(jnp.int32, block.shape, 1)
    zero = jnp.zeros_like(block)
    first = lane < HEAD_DIM
    return jnp.concatenate([jnp.where(first, block, zero), jnp.where(first, zero, block)], axis=0)


def own_lanes(both):
    picked = jnp.concatenate([both[:HEAD_DIM, :QT], both[HEAD_DIM:, QT:]], axis=0)
    return picked.T


def twice(row):
    return jnp.concatenate([row, row], axis=1)


def fill_bias(keys, lo_ref, hi_ref, bias_ref):
    at = lax.broadcasted_iota(jnp.int32, (keys, QT), 0)
    for tile in range(TILES):
        own = pl.ds(tile * QT, QT)
        inside = (at >= lo_ref[0, :, own]) & (at < hi_ref[0, :, own])
        bias_ref[tile] = jnp.where(inside, 0.0, EXCLUDED)


def over_chunks(spans, tile, bounds, body, init):
    if spans is None:
        return lax.fori_loop(*bounds, body, init)
    for j in range(*spans[tile]):
        init = body(j, init)
    return init


def chunk_at(spans, chunk, j):
    return pl.ds(j * chunk if spans is not None else pl.multiple_of(j * chunk, chunk), chunk)


def attend_kernel(
    chunk, spans, first_ref, stop_ref, lo_ref, hi_ref, q_ref, k_ref, v_ref, c_ref, l_ref, bias_ref, s_ref
):
    row = pl.program_id(0)
    pairs = range(q_ref.shape[1] // PAIR)
    lanes = [pl.ds(pair * PAIR, PAIR) for pair in pairs]
    pl.when(pl.program_id(1) == 0)(lambda: fill_bias(k_ref.shape[0], lo_ref, hi_ref, bias_ref))
    for tile in range(TILES):
        own = pl.ds(tile * QT, QT)
        queries = [two_heads(q_ref[own, at].astype(F32) * SCALE).astype(BF) for at in lanes]
        bounds = (first_ref[row, tile], stop_ref[row, tile])

        def scores(j, tops):
            here = chunk_at(spans, chunk, j)
            bias = twice(bias_ref[tile, here, :])
            out = []
            for pair in pairs:
                part = nt(k_ref[here, lanes[pair]], queries[pair]) + bias
                s_ref[pair, here, :] = part
                out.append(jnp.maximum(tops[pair], jnp.max(part, axis=0, keepdims=True)))
            return tuple(out)

        tops = (jnp.full((1, 2 * QT), EXCLUDED, F32),) * len(pairs)
        tops = over_chunks(spans, tile, bounds, scores, tops)

        def context(j, sums):
            here = chunk_at(spans, chunk, j)
            out = []
            for pair in pairs:
                total, acc = sums[pair]
                weight = jnp.exp(s_ref[pair, here, :] - tops[pair])
                total = total + jnp.sum(weight, axis=0, keepdims=True)
                out.append((total, acc + tn(v_ref[here, lanes[pair]], weight.astype(BF))))
            return tuple(out)

        sums = ((jnp.zeros((1, 2 * QT), F32), jnp.zeros((PAIR, 2 * QT), F32)),) * len(pairs)
        sums = over_chunks(spans, tile, bounds, context, sums)
        for pair in pairs:
            total, acc = sums[pair]
            c_ref[own, lanes[pair]] = own_lanes(acc / total).astype(BF)
            l_ref[0, pair, tile : tile + 1, :] = tops[pair] + jnp.log(total)


def attend_back_kernel(
    chunk, spans, first_ref, stop_ref, lo_ref, hi_ref, q_ref, k_ref, v_ref, l_ref, c_ref, dc_ref,
    dq_ref, dkv_ref, bias_ref, dk_acc, dv_acc,
):
    row = pl.program_id(0)
    pairs = range(q_ref.shape[1] // PAIR)
    lanes = [pl.ds(pair * PAIR, PAIR) for pair in pairs]
    pl.when(pl.program_id(1) == 0)(lambda: fill_bias(k_ref.shape[0], lo_ref, hi_ref, bias_ref))
    dk_acc[...] = jnp.zeros_like(dk_acc)
    dv_acc[...] = jnp.zeros_like(dv_acc)
    for tile in range(TILES):
        own = pl.ds(tile * QT, QT)
        queries, grads, deltas, logs = [], [], [], []
        for pair in pairs:
            queries.append(two_heads(q_ref[own, lanes[pair]].astype(F32) * SCALE).astype(BF))
            grad = dc_ref[own, lanes[pair]].astype(F32)
            inner = (grad * c_ref[own, lanes[pair]].astype(F32)).T
            heads = [jnp.sum(part, axis=0, keepdims=True) for part in (inner[:HEAD_DIM], inner[HEAD_DIM:])]
            deltas.append(jnp.concatenate(heads, axis=1))
            grads.append(two_heads(grad).astype(BF))
            logs.append(l_ref[0, pair, tile : tile + 1, :])

        def step(j, accs):
            here = chunk_at(spans, chunk, j)
            bias = twice(bias_ref[tile, here, :])
            out = []
            for pair in pairs:
                keys = k_ref[here, lanes[pair]]
                prob = jnp.exp(nt(keys, queries[pair]) + bias - logs[pair])
                slope = prob * (nt(v_ref[here, lanes[pair]], grads[pair]) - deltas[pair])
                slope = slope.astype(BF)
                dv_acc[here, lanes[pair]] += nn(prob.astype(BF), grads[pair])
                dk_acc[here, lanes[pair]] += nn(slope, queries[pair])
                out.append(accs[pair] + tn(keys, slope))
            return tuple(out)

        bounds = (first_ref[row, tile], stop_ref[row, tile])
        accs = (jnp.zeros((PAIR, 2 * QT), F32),) * len(pairs)
        accs = over_chunks(spans, tile, bounds, step, accs)
        for pair in pairs:
            dq_ref[own, lanes[pair]] = (own_lanes(accs[pair]) * SCALE).astype(BF)
    width = dk_acc.shape[1]
    dkv_ref[:, :width] = dk_acc[...].astype(BF)
    dkv_ref[:, width:] = dv_acc[...].astype(BF)


def attention_specs(keys, wide):
    per_query = pl.BlockSpec((PATCHES, wide * PAIR), lambda r, h, *_: (r, h))
    per_key = pl.BlockSpec((keys, wide * PAIR), lambda r, h, *_: (r, h))
    bound = pl.BlockSpec((1, 1, PATCHES), lambda r, h, *_: (r, 0, 0))
    logs = pl.BlockSpec((1, wide, TILES, 2 * QT), lambda r, h, *_: (r, h, 0, 0))
    return per_query, per_key, bound, logs


def kernel_cost(q, k, products):
    scores = q.shape[0] * k.shape[0] // (q.shape[0] // PATCHES) * HEADS
    return pl.CostEstimate(
        flops=products * 2 * scores * 256, bytes_accessed=2 * q.nbytes + 4 * k.nbytes, transcendentals=scores
    )


def attend(bounds, q, k, v, wide, spans=None):
    first, stop, lo, hi, chunk = bounds
    rows = lo.shape[0]
    keys = k.shape[0] // rows
    per_query, per_key, bound, logs = attention_specs(keys, wide)
    return pl.pallas_call(
        functools.partial(attend_kernel, chunk, spans),
        grid_spec=pltpu.PrefetchScalarGridSpec(
            num_scalar_prefetch=2,
            grid=(rows, PAIRS // wide),
            in_specs=[bound, bound, per_query, per_key, per_key],
            out_specs=[per_query, logs],
            scratch_shapes=[pltpu.VMEM((TILES, keys, QT), F32), pltpu.VMEM((wide, keys, 2 * QT), F32)],
        ),
        out_shape=[
            jax.ShapeDtypeStruct(q.shape, BF),
            jax.ShapeDtypeStruct((rows, PAIRS, TILES, 2 * QT), F32),
        ],
        compiler_params=pltpu.CompilerParams(vmem_limit_bytes=48 << 20),
        cost_estimate=kernel_cost(q, k, 2),
        name="attend",
    )(first, stop, lo, hi, q, k, v)


def attend_back(bounds, q, k, v, logsum, context, grads, wide, spans=None):
    first, stop, lo, hi, chunk = bounds
    rows = lo.shape[0]
    keys = k.shape[0] // rows
    per_query, per_key, bound, logs = attention_specs(keys, wide)
    return pl.pallas_call(
        functools.partial(attend_back_kernel, chunk, spans),
        grid_spec=pltpu.PrefetchScalarGridSpec(
            num_scalar_prefetch=2,
            grid=(rows, PAIRS // wide),
            in_specs=[bound, bound, per_query, per_key, per_key, logs, per_query, per_query],
            out_specs=[per_query, pl.BlockSpec((keys, 2 * wide * PAIR), lambda r, h, *_: (r, h))],
            scratch_shapes=[pltpu.VMEM((TILES, keys, QT), F32)] + [pltpu.VMEM((keys, wide * PAIR), F32)] * 2,
        ),
        out_shape=[
            jax.ShapeDtypeStruct(q.shape, BF),
            jax.ShapeDtypeStruct((k.shape[0], 2 * D), BF),
        ],
        compiler_params=pltpu.CompilerParams(vmem_limit_bytes=48 << 20),
        cost_estimate=kernel_cost(q, k, 5),
        name="attend_back",
    )(first, stop, lo, hi, q, k, v, logsum, context, grads)


def scale_of(values):
    return lax.rsqrt(jnp.mean(values * values, axis=-1, keepdims=True) + EPS)


def norm_backward(values, row_scale, gain_row, incoming):
    weighted = incoming * gain_row
    projection = jnp.mean(weighted * values, axis=-1, keepdims=True)
    grad_values = row_scale * weighted - values * (row_scale * row_scale * row_scale) * projection
    grad_gain = jnp.sum(incoming * values * row_scale, axis=0)
    return grad_values, grad_gain


def chunk_bounds(lo, hi, chunk):
    first = lo[:, ::QT] // chunk
    stop = (hi[:, QT - 1 :: QT] + chunk - 1) // chunk
    return first, stop, lo[:, None, :], hi[:, None, :], chunk


def shards(
    byte_states, patch_lengths, patch_docs, attn_qkv, attn_out, norm_gains, ffn_in, ffn_down, cotangent
):
    section = lax.axis_index("section")
    group = lax.axis_index("group")
    sections = lax.axis_size("section")
    groups = lax.axis_size("group")
    core, side = group % 2, group // 2

    core_pairs = [(0, 1), (1, 0), (2, 3), (3, 2)]
    side_pairs = [(0, 2), (1, 3), (2, 0), (3, 1)]
    swap = [(0, 1), (1, 0)]
    together = lax.optimization_barrier

    four = jnp.concatenate([attn_qkv[0], attn_out], axis=0)
    matrix = lax.dynamic_index_in_dim(four, group, 0, keepdims=False)
    matrices = lax.all_gather(matrix, ("section", "group", "dp"), axis=0, tiled=True)

    gains = lax.all_gather(norm_gains, "section", axis=0, tiled=True)

    def quarter_of(shard):
        height = shard.shape[0] // groups
        return lax.dynamic_slice_in_dim(shard, group * height, height, 0)

    def in_order(part, own, got):
        return jnp.where(part == 0, jnp.stack([own, got]), jnp.stack([got, own]))

    def both(values, part, axis, pairs):
        return in_order(part, values, lax.ppermute(values, axis, pairs))

    units = FF // sections

    def of_units(values, part):
        halves = [lax.dynamic_slice_in_dim(values, at + part * units, units, 1) for at in (0, FF)]
        return jnp.concatenate(halves, axis=1)

    quarter = quarter_of(ffn_in)
    got = lax.ppermute(of_units(quarter, 1 - section), "section", swap)
    w_in = in_order(section, of_units(quarter, section), got)
    w_in = lax.all_gather(w_in, ("dp", "group"), axis=1, tiled=True).reshape(D, 2 * units)

    line, place = lax.axis_size("dp"), lax.axis_index("dp")
    quarter = quarter_of(ffn_down)
    down = jnp.zeros((line,) + quarter.shape, BF)
    for step in range(line):
        moved = lax.ppermute(quarter, "dp", [(i, (i + step) % line) for i in range(line)]) if step else quarter
        down = lax.dynamic_update_slice_in_dim(down, moved[None], (place - step) % line, 0)
    matrices = matrices.reshape(sections, groups, D, D)
    wq, wk, wv, wo = [matrices[:, index] for index in range(4)]

    rows = byte_states.shape[0] // sections
    mine = lambda a: lax.dynamic_slice_in_dim(a, section * rows, rows, 0)
    states, lengths, docs, cot = [mine(a) for a in (byte_states, patch_lengths, patch_docs, cotangent)]
    tokens = rows * PATCHES
    cot = cot.reshape(tokens, D)
    other_cot = lax.dynamic_slice_in_dim(cotangent, (1 - section) * rows, rows, 0).reshape(tokens, D)
    cots = jnp.concatenate([cot, other_cot], axis=0)

    ends = jnp.cumsum(lengths, axis=1)
    earlier = docs[:, None, :] < docs[:, :, None]
    doc_start = jnp.sum(jnp.where(earlier, lengths[:, None, :], 0), axis=2)
    doc_first = jnp.sum(earlier.astype(jnp.int32), axis=2)
    cross, cross_back = chunk_bounds(doc_start, ends, 256), chunk_bounds(doc_start, ends, 512)
    ids = jnp.broadcast_to(lax.iota(jnp.int32, PATCHES) + 1, doc_first.shape)
    causal = chunk_bounds(doc_first, ids, 128)
    positions = lax.iota(jnp.int32, ROW_BYTES)
    member = (positions < ends[:, :, None]) & (positions >= (ends - lengths)[:, :, None])
    member = member.astype(BF)
    count = lengths.astype(F32).reshape(rows * PATCHES, 1)

    pooled = jnp.einsum("rpb,rbd->rpd", member, states, preferred_element_type=F32)
    pooled = pooled.reshape(rows * PATCHES, D) / count
    wide = states.reshape(rows * ROW_BYTES, D).astype(F32)
    query_scale, key_scale = scale_of(pooled), scale_of(wide)
    query_in = (pooled * query_scale * gains[0, 0]).astype(BF)
    key_in = (wide * key_scale * gains[0, 1]).astype(BF)
    q1 = nn(query_in, wq[0]).astype(BF)
    k1 = nn(key_in, wk[0]).astype(BF)
    v1 = nn(key_in, wv[0]).astype(BF)
    v1, down = together((v1, down))
    down = both(down, side, "group", side_pairs)
    c1, l1 = attend(cross, q1, k1, v1, 8)
    carried = (pooled + nn(c1, wo[0])).astype(BF)

    carried_wide = carried.astype(F32)
    first_scale = scale_of(carried_wide)
    normed_in = (carried_wide * first_scale * gains[1, 0]).astype(BF)
    q2 = nn(normed_in, wq[1]).astype(BF)
    k2 = nn(normed_in, wk[1]).astype(BF)
    v2 = nn(normed_in, wv[1]).astype(BF)
    c2, l2 = attend(causal, q2, k2, v2, 8, CAUSAL_SPANS)
    c2, down = together((c2, down))
    down = both(down, core, "group", core_pairs)
    w_down = down.transpose(2, 1, 0, 3, 4).reshape(units, D)
    residual = carried_wide + nn(c2, wo[1])
    second_scale = scale_of(residual)
    mix_in = (residual * second_scale * gains[1, 1]).astype(BF)
    mix_got = lax.ppermute(mix_in, "section", swap)
    grad_hidden = nt(cots, w_down).astype(BF)
    half_width = D // 2
    wkv = jnp.concatenate(
        [w[0][:, at : at + half_width] for at in (0, half_width) for w in (wk, wv)], axis=1
    )
    mix_got, grad_hidden, wkv = together((mix_got, grad_hidden, wkv))
    mixed = jnp.concatenate([mix_in, mix_got], axis=0)
    gate_up = nn(mixed, w_in)
    gate, up = gate_up[:, :units], gate_up[:, units:]
    sig = jax.nn.sigmoid(gate)
    hidden = (gate * sig * up).astype(BF)

    grad_hidden = grad_hidden.astype(F32)
    grad_gate = grad_hidden * up * sig * (1.0 + gate * (1.0 - sig))
    grad_up = grad_hidden * gate * sig
    dgu = together(jnp.concatenate([grad_gate, grad_up], axis=1).astype(BF))

    def exchanged(values, axis, part, pairs, where):
        size = values.shape[where] // 2
        other = lax.dynamic_slice_in_dim(values, (1 - part) * size, size, where)
        own = lax.dynamic_slice_in_dim(values, part * size, size, where)
        return (own.astype(F32) + lax.ppermute(other, axis, pairs).astype(F32)).astype(BF)

    def over_section(values, where):
        return exchanged(values, "section", section, swap, where)

    def over_side(values, where):
        return exchanged(values, "group", side, side_pairs, where)

    def columns(values, part):
        if callable(values):
            return values(part)
        size = values.shape[-1] // 2
        return lax.dynamic_slice_in_dim(values, part * size, size, values.ndim - 1)

    def line_sum(values, where):
        return lax.psum_scatter(values, "dp", scatter_dimension=where, tiled=True)

    def products(pairs, part):
        out = [tn(left, columns(right, part)) for left, right in pairs]
        return out[0] if len(out) == 1 else jnp.stack(out)

    def to_core(pairs):
        return products(pairs, 1 - core).astype(BF)

    def of_chip(pairs, sent):
        got = lax.ppermute(sent, "group", core_pairs)
        return (products(pairs, core) + got.astype(F32)).astype(BF)

    dgu, mix_other = together((dgu, nt(dgu[tokens:], w_in).astype(BF)))
    in_pairs, down_pairs = [(mixed, dgu)], [(hidden, cots)]
    send_in, send_down = to_core(in_pairs), to_core(down_pairs)
    mix_got = [lax.ppermute(mix_other[:PATCHES], "section", swap)]
    dgu_own, send_in, send_down, mix_got[0], rest = together(
        (dgu[:tokens], send_in, send_down, mix_got[0], mix_other[PATCHES:])
    )
    mix_got.append(lax.ppermute(rest, "section", swap))

    half = D // sections
    parts = nn(hidden, w_down)
    parts = jnp.concatenate([residual + parts[:tokens], parts[tokens:]], axis=0)
    sent = lax.dynamic_slice_in_dim(parts, (1 - section) * half, half, 1).astype(BF)
    kept = lax.dynamic_slice_in_dim(parts, section * half, half, 1)
    dgu_own, sent = together((dgu_own, sent))
    got = lax.ppermute(sent, "section", swap)

    half_in, half_down = of_chip(in_pairs, send_in), of_chip(down_pairs, send_down)
    mix_got, half_in, half_down = together((mix_got, half_in, half_down))
    grad_mixed = nt(dgu_own, w_in) + jnp.concatenate(mix_got, axis=0).astype(F32)
    grad_mix, gain_mix = norm_backward(residual, second_scale, gains[1, 1], grad_mixed)
    grad_residual = grad_mix + cot.astype(F32)
    branch = grad_residual.astype(BF)
    dc2 = nt(branch, wo[1]).astype(BF)

    dq2, dkv2 = attend_back(causal, q2, k2, v2, l2, c2, dc2, 8, CAUSAL_SPANS)
    dk2, dv2 = dkv2[:, :D], dkv2[:, D:]
    two_pairs = [(normed_in, dq2), (normed_in, dk2), (normed_in, dv2), (c2, branch)]
    send_two = to_core(two_pairs)
    half_in = over_side(half_in.reshape(sections, line, 2, -1, units), 2)
    sum_down = line_sum(half_down, 0)
    dq2, dk2, dv2, send_two, half_in, sum_down = together((dq2, dk2, dv2, send_two, half_in, sum_down))
    sum_in = line_sum(half_in.reshape(sections, -1, units), 1)
    grad_normed = nt(dq2, wq[1]) + nt(dk2, wk[1]) + nt(dv2, wv[1])
    grad_carried, gain_normed = norm_backward(carried_wide, first_scale, gains[1, 0], grad_normed)
    d_carried = (grad_residual + grad_carried).astype(BF)
    dc1 = nt(d_carried, wo[0]).astype(BF)
    half_two = of_chip(two_pairs, send_two)
    dc1, half_two, got = together((dc1, half_two, got))
    got = got.astype(F32)
    latents = in_order(section, kept[:tokens] + got[tokens:], kept[tokens:] + got[:tokens])
    latents_out = latents.astype(BF).reshape(sections * rows, PATCHES, half)
    def pairs_of(dq1, dkv1):
        def part_of(offset):
            return lambda part: lax.dynamic_slice_in_dim(dkv1, part * D + offset, D // 2, 1)

        return [(query_in, dq1), (key_in, part_of(0))], [(key_in, part_of(D // 2)), (c1, d_carried)]

    dq1, dkv1 = attend_back(cross_back, q1, k1, v1, l1, c1, dc1, 4)
    half_two = over_section(half_two[:2], 2), over_side(half_two[2:], 2)
    dq1, half_two = together((dq1, half_two))
    half_two = jnp.concatenate([over_side(half_two[0], 2), over_section(half_two[1], 2)], axis=0)
    one_pairs = pairs_of(dq1, dkv1)
    send_one = [to_core(pairs) for pairs in one_pairs]
    dq1, dkv1, send_one, sum_down = together((dq1, dkv1, send_one, sum_down))
    def gathered(part):
        return lax.all_gather(part, "group", axis=0, tiled=False)

    def laid_out(parts, order):
        return jnp.concatenate([parts[index] for index in order], axis=-1).astype(F32)

    half_one = [of_chip(pairs, sent) for pairs, sent in zip(one_pairs, send_one)]
    dq1, dkv1, half_one, half_two, sum_in = together((dq1, dkv1, half_one, half_two, sum_in))
    sum_two = line_sum(half_two, 1)
    sum_in = jnp.stack([lax.dynamic_index_in_dim(sum_in, section, 0, False),
                        lax.ppermute(lax.dynamic_index_in_dim(sum_in, 1 - section, 0, False), "section", swap)])
    sum_in = jnp.where(section == 0, sum_in, sum_in[::-1])
    sum_in = gathered(sum_in)
    grad_query_in = nt(dq1, wq[0])
    grad_key_in = nt(dkv1, wkv)
    half_one = over_section(half_one[0], 2), over_side(half_one[1], 2)
    grad_query_in, grad_key_in, half_one = together((grad_query_in, grad_key_in, half_one))
    half_one = jnp.concatenate([over_side(half_one[0], 2), over_section(half_one[1], 2)], axis=0)
    grad_query_in, grad_key_in, half_one, sum_two, sum_down, sum_in = together(
        (grad_query_in, grad_key_in, half_one, sum_two, sum_down, sum_in)
    )
    sum_down = over_side(sum_down, 1)
    sum_one = line_sum(half_one, 1)

    grad_pooled, gain_query = norm_backward(pooled, query_scale, gains[0, 0], grad_query_in)
    grad_wide, gain_key = norm_backward(wide, key_scale, gains[0, 1], grad_key_in)
    per_patch = (grad_pooled + d_carried.astype(F32)) / count
    spread_back = jnp.einsum(
        "rpb,rpd->rbd", member, per_patch.astype(BF).reshape(rows, PATCHES, D), preferred_element_type=F32
    )
    byte_grads = (grad_wide + spread_back.reshape(rows * ROW_BYTES, D)).astype(BF)
    byte_grads = byte_grads.reshape(rows, ROW_BYTES, D)
    other = lax.dynamic_slice_in_dim(byte_grads, (1 - section) * half, half, 2)
    own = lax.dynamic_slice_in_dim(byte_grads, section * half, half, 2)

    gain_grads = jnp.stack([gain_query, gain_key, gain_normed, gain_mix])
    gain_grads = gain_grads + lax.ppermute(gain_grads, "section", swap)
    ffn_gin = jnp.concatenate(
        [laid_out([sum_in[at, t] for at in (2 * y, 2 * y + 1) for t in range(sections)], range(4)) for y in (0, 1)],
        axis=0,
    )

    early, gain_grads = together(([other[row] for row in range(rows - 1)], gain_grads))
    bytes_got = [lax.ppermute(part, "section", swap) for part in early]
    for pairs in (core_pairs, side_pairs):
        gain_grads = gain_grads + lax.ppermute(gain_grads, "group", pairs)
    gain_grads = jnp.sum(lax.all_gather(gain_grads, "dp", axis=0, tiled=False), axis=0)
    late, gain_grads, sum_one, bytes_got, sum_down = together(
        (other[rows - 1], gain_grads, sum_one, bytes_got, sum_down)
    )
    bytes_got.append(lax.ppermute(late, "section", swap))
    kept = jnp.where(section == 0, sum_one, sum_two)
    sent = jnp.where(section == 0, sum_two, sum_one)
    got = lax.ppermute(sent, "section", swap)
    got, sum_down = together((got, sum_down))
    ffn_gdown = laid_out(gathered(sum_down), (0, 2, 1, 3))
    eighths = jnp.where(
        section == 0, jnp.concatenate([kept, got], axis=2), jnp.concatenate([got, kept], axis=2)
    )
    width = eighths.shape[2] // 2
    eighths, bytes_got = together((gathered(eighths), bytes_got))
    bytes_out = in_order(section, own, jnp.stack(bytes_got)).reshape(sections * rows, ROW_BYTES, half)
    parts = [piece for every in eighths for piece in (every[..., :width], every[..., width:])]
    section_first = laid_out([part[:2] for part in parts], (0, 4, 1, 5, 2, 6, 3, 7))
    side_first = laid_out([part[2:] for part in parts], (0, 1, 4, 5, 2, 3, 6, 7))
    grad_qkv = jnp.concatenate([section_first, side_first[:1]], axis=0)[None]

    gain_grads = lax.dynamic_slice_in_dim(gain_grads.reshape(2, 2, D), section, 1, 0)
    width = D // lax.axis_size("dp")
    gain_out = lax.dynamic_slice_in_dim(gain_grads, lax.axis_index("dp") * width, width, 2)
    return (latents_out, bytes_out, grad_qkv, side_first[1:], gain_out, ffn_gin, ffn_gdown)


def solution(mesh):
    in_specs = (
        P(("group", "dp"), None, None),
        P(("group", "dp"), None),
        P(("group", "dp"), None),
        P("section", None, "dp", None),
        P("section", "dp", None),
        P("section", None, None),
        P(("section", "dp"), None),
        P(("section", "dp"), None),
        P(("group", "dp"), None, None),
    )
    out_specs = (
        P(("group", "dp"), None, "section"),
        P(("group", "dp"), None, "section"),
        P("section", None, "dp", None),
        P("section", "dp", None),
        P("section", None, "dp"),
        P(("section", "dp"), None),
        P(("section", "dp"), None),
    )
    return jax.shard_map(shards, mesh=mesh, in_specs=in_specs, out_specs=out_specs, check_vma=False)
```

```python
import functools

import jax
import jax.numpy as jnp
from jax import lax
from jax.experimental import pallas as pl
from jax.experimental.pallas import tpu as pltpu
from jax.sharding import PartitionSpec as P

D = 1024
HEADS = 16
HEAD_DIM = 64
PAIR = 2 * HEAD_DIM
PAIRS = HEADS // 2
FF = 2816
ROW_BYTES = 1024
PATCHES = 256
QT = 128
TILES = PATCHES // QT
CAUSAL_SPANS = ((0, 1), (0, 2))

EPS = 1e-05
SCALE = HEAD_DIM ** (-0.5)
EXCLUDED = -1e30

BF = jnp.bfloat16
F32 = jnp.float32


def nn(left, right):
    return jnp.dot(left, right, preferred_element_type=F32)


def tn(left, right):
    return lax.dot_general(left, right, (((0,), (0,)), ((), ())), preferred_element_type=F32)


def nt(left, right):
    return lax.dot_general(left, right, (((1,), (1,)), ((), ())), preferred_element_type=F32)


def two_heads(block):
    lane = lax.broadcasted_iota(jnp.int32, block.shape, 1)
    zero = jnp.zeros_like(block)
    first = lane < HEAD_DIM
    return jnp.concatenate([jnp.where(first, block, zero), jnp.where(first, zero, block)], axis=0)


def own_lanes(both):
    picked = jnp.concatenate([both[:HEAD_DIM, :QT], both[HEAD_DIM:, QT:]], axis=0)
    return picked.T


def twice(row):
    return jnp.concatenate([row, row], axis=1)


def fill_bias(keys, lo_ref, hi_ref, bias_ref):
    at = lax.broadcasted_iota(jnp.int32, (keys, QT), 0)
    for tile in range(TILES):
        own = pl.ds(tile * QT, QT)
        inside = (at >= lo_ref[0, :, own]) & (at < hi_ref[0, :, own])
        bias_ref[tile] = jnp.where(inside, 0.0, EXCLUDED)


def over_chunks(spans, tile, bounds, body, init):
    if spans is None:
        return lax.fori_loop(*bounds, body, init)
    for j in range(*spans[tile]):
        init = body(j, init)
    return init


def chunk_at(spans, chunk, j):
    return pl.ds(j * chunk if spans is not None else pl.multiple_of(j * chunk, chunk), chunk)


def attend_kernel(
    chunk, spans, first_ref, stop_ref, lo_ref, hi_ref, q_ref, k_ref, v_ref, c_ref, l_ref, bias_ref, s_ref
):
    row = pl.program_id(0)
    pairs = range(q_ref.shape[1] // PAIR)
    lanes = [pl.ds(pair * PAIR, PAIR) for pair in pairs]
    pl.when(pl.program_id(1) == 0)(lambda: fill_bias(k_ref.shape[0], lo_ref, hi_ref, bias_ref))
    for tile in range(TILES):
        own = pl.ds(tile * QT, QT)
        queries = [two_heads(q_ref[own, at].astype(F32) * SCALE).astype(BF) for at in lanes]
        bounds = (first_ref[row, tile], stop_ref[row, tile])

        def scores(j, tops):
            here = chunk_at(spans, chunk, j)
            bias = twice(bias_ref[tile, here, :])
            out = []
            for pair in pairs:
                part = nt(k_ref[here, lanes[pair]], queries[pair]) + bias
                s_ref[pair, here, :] = part
                out.append(jnp.maximum(tops[pair], jnp.max(part, axis=0, keepdims=True)))
            return tuple(out)

        tops = (jnp.full((1, 2 * QT), EXCLUDED, F32),) * len(pairs)
        tops = over_chunks(spans, tile, bounds, scores, tops)

        def context(j, sums):
            here = chunk_at(spans, chunk, j)
            out = []
            for pair in pairs:
                total, acc = sums[pair]
                weight = jnp.exp(s_ref[pair, here, :] - tops[pair])
                total = total + jnp.sum(weight, axis=0, keepdims=True)
                out.append((total, acc + tn(v_ref[here, lanes[pair]], weight.astype(BF))))
            return tuple(out)

        sums = ((jnp.zeros((1, 2 * QT), F32), jnp.zeros((PAIR, 2 * QT), F32)),) * len(pairs)
        sums = over_chunks(spans, tile, bounds, context, sums)
        for pair in pairs:
            total, acc = sums[pair]
            c_ref[own, lanes[pair]] = own_lanes(acc / total).astype(BF)
            l_ref[0, pair, tile : tile + 1, :] = tops[pair] + jnp.log(total)


def attend_back_kernel(
    chunk, spans, first_ref, stop_ref, lo_ref, hi_ref, q_ref, k_ref, v_ref, l_ref, c_ref, dc_ref,
    dq_ref, dk_ref, dv_ref, bias_ref, dk_acc, dv_acc,
):
    row = pl.program_id(0)
    pairs = range(q_ref.shape[1] // PAIR)
    lanes = [pl.ds(pair * PAIR, PAIR) for pair in pairs]
    pl.when(pl.program_id(1) == 0)(lambda: fill_bias(k_ref.shape[0], lo_ref, hi_ref, bias_ref))
    dk_acc[...] = jnp.zeros_like(dk_acc)
    dv_acc[...] = jnp.zeros_like(dv_acc)
    for tile in range(TILES):
        own = pl.ds(tile * QT, QT)
        queries, grads, deltas, logs = [], [], [], []
        for pair in pairs:
            queries.append(two_heads(q_ref[own, lanes[pair]].astype(F32) * SCALE).astype(BF))
            grad = dc_ref[own, lanes[pair]].astype(F32)
            inner = (grad * c_ref[own, lanes[pair]].astype(F32)).T
            heads = [jnp.sum(part, axis=0, keepdims=True) for part in (inner[:HEAD_DIM], inner[HEAD_DIM:])]
            deltas.append(jnp.concatenate(heads, axis=1))
            grads.append(two_heads(grad).astype(BF))
            logs.append(l_ref[0, pair, tile : tile + 1, :])

        def step(j, accs):
            here = chunk_at(spans, chunk, j)
            bias = twice(bias_ref[tile, here, :])
            out = []
            for pair in pairs:
                keys = k_ref[here, lanes[pair]]
                prob = jnp.exp(nt(keys, queries[pair]) + bias - logs[pair])
                slope = prob * (nt(v_ref[here, lanes[pair]], grads[pair]) - deltas[pair])
                slope = slope.astype(BF)
                dv_acc[here, lanes[pair]] += nn(prob.astype(BF), grads[pair])
                dk_acc[here, lanes[pair]] += nn(slope, queries[pair])
                out.append(accs[pair] + tn(keys, slope))
            return tuple(out)

        bounds = (first_ref[row, tile], stop_ref[row, tile])
        accs = (jnp.zeros((PAIR, 2 * QT), F32),) * len(pairs)
        accs = over_chunks(spans, tile, bounds, step, accs)
        for pair in pairs:
            dq_ref[own, lanes[pair]] = (own_lanes(accs[pair]) * SCALE).astype(BF)
    dk_ref[...] = dk_acc[...].astype(BF)
    dv_ref[...] = dv_acc[...].astype(BF)


def attention_specs(keys, wide):
    per_query = pl.BlockSpec((PATCHES, wide * PAIR), lambda r, h, *_: (r, h))
    per_key = pl.BlockSpec((keys, wide * PAIR), lambda r, h, *_: (r, h))
    bound = pl.BlockSpec((1, 1, PATCHES), lambda r, h, *_: (r, 0, 0))
    logs = pl.BlockSpec((1, wide, TILES, 2 * QT), lambda r, h, *_: (r, h, 0, 0))
    return per_query, per_key, bound, logs


def kernel_cost(q, k, products):
    scores = q.shape[0] * k.shape[0] // (q.shape[0] // PATCHES) * HEADS
    return pl.CostEstimate(
        flops=products * 2 * scores * 256, bytes_accessed=2 * q.nbytes + 4 * k.nbytes, transcendentals=scores
    )


def attend(bounds, q, k, v, wide, spans=None):
    first, stop, lo, hi, chunk = bounds
    rows = lo.shape[0]
    keys = k.shape[0] // rows
    per_query, per_key, bound, logs = attention_specs(keys, wide)
    return pl.pallas_call(
        functools.partial(attend_kernel, chunk, spans),
        grid_spec=pltpu.PrefetchScalarGridSpec(
            num_scalar_prefetch=2,
            grid=(rows, PAIRS // wide),
            in_specs=[bound, bound, per_query, per_key, per_key],
            out_specs=[per_query, logs],
            scratch_shapes=[pltpu.VMEM((TILES, keys, QT), F32), pltpu.VMEM((wide, keys, 2 * QT), F32)],
        ),
        out_shape=[
            jax.ShapeDtypeStruct(q.shape, BF),
            jax.ShapeDtypeStruct((rows, PAIRS, TILES, 2 * QT), F32),
        ],
        compiler_params=pltpu.CompilerParams(vmem_limit_bytes=48 << 20),
        cost_estimate=kernel_cost(q, k, 2),
        name="attend",
    )(first, stop, lo, hi, q, k, v)


def attend_back(bounds, q, k, v, logsum, context, grads, wide, spans=None):
    first, stop, lo, hi, chunk = bounds
    rows = lo.shape[0]
    keys = k.shape[0] // rows
    per_query, per_key, bound, logs = attention_specs(keys, wide)
    return pl.pallas_call(
        functools.partial(attend_back_kernel, chunk, spans),
        grid_spec=pltpu.PrefetchScalarGridSpec(
            num_scalar_prefetch=2,
            grid=(rows, PAIRS // wide),
            in_specs=[bound, bound, per_query, per_key, per_key, logs, per_query, per_query],
            out_specs=[per_query, per_key, per_key],
            scratch_shapes=[pltpu.VMEM((TILES, keys, QT), F32)] + [pltpu.VMEM((keys, wide * PAIR), F32)] * 2,
        ),
        out_shape=[
            jax.ShapeDtypeStruct(q.shape, BF),
            jax.ShapeDtypeStruct(k.shape, BF),
            jax.ShapeDtypeStruct(k.shape, BF),
        ],
        compiler_params=pltpu.CompilerParams(vmem_limit_bytes=48 << 20),
        cost_estimate=kernel_cost(q, k, 5),
        name="attend_back",
    )(first, stop, lo, hi, q, k, v, logsum, context, grads)


def scale_of(values):
    return lax.rsqrt(jnp.mean(values * values, axis=-1, keepdims=True) + EPS)


def norm_backward(values, row_scale, gain_row, incoming):
    weighted = incoming * gain_row
    projection = jnp.mean(weighted * values, axis=-1, keepdims=True)
    grad_values = row_scale * weighted - values * (row_scale * row_scale * row_scale) * projection
    grad_gain = jnp.sum(incoming * values * row_scale, axis=0)
    return grad_values, grad_gain


def chunk_bounds(lo, hi, chunk):
    first = lo[:, ::QT] // chunk
    stop = (hi[:, QT - 1 :: QT] + chunk - 1) // chunk
    return first, stop, lo[:, None, :], hi[:, None, :], chunk


def shards(
    byte_states, patch_lengths, patch_docs, attn_qkv, attn_out, norm_gains, ffn_in, ffn_down, cotangent
):
    section = lax.axis_index("section")
    group = lax.axis_index("group")
    sections = lax.axis_size("section")
    groups = lax.axis_size("group")
    core, side = group % 2, group // 2

    core_pairs = [(0, 1), (1, 0), (2, 3), (3, 2)]
    side_pairs = [(0, 2), (1, 3), (2, 0), (3, 1)]
    swap = [(0, 1), (1, 0)]
    together = lax.optimization_barrier

    four = jnp.concatenate([attn_qkv[0], attn_out], axis=0)
    matrix = lax.dynamic_index_in_dim(four, group, 0, keepdims=False)
    matrices = lax.all_gather(matrix, ("section", "group", "dp"), axis=0, tiled=True)

    gains = lax.all_gather(norm_gains, "section", axis=0, tiled=True)

    def quarter_of(shard):
        height = shard.shape[0] // groups
        return lax.dynamic_slice_in_dim(shard, group * height, height, 0)

    def in_order(part, own, got):
        return jnp.where(part == 0, jnp.stack([own, got]), jnp.stack([got, own]))

    def both(values, part, axis, pairs):
        return in_order(part, values, lax.ppermute(values, axis, pairs))

    units = FF // sections

    def of_units(values, part):
        halves = [lax.dynamic_slice_in_dim(values, at + part * units, units, 1) for at in (0, FF)]
        return jnp.concatenate(halves, axis=1)

    quarter = quarter_of(ffn_in)
    got = lax.ppermute(of_units(quarter, 1 - section), "section", swap)
    w_in = in_order(section, of_units(quarter, section), got)
    w_in = lax.all_gather(w_in, ("dp", "group"), axis=1, tiled=True).reshape(D, 2 * units)

    line, place = lax.axis_size("dp"), lax.axis_index("dp")
    quarter = quarter_of(ffn_down)
    down = jnp.zeros((line,) + quarter.shape, BF)
    for step in range(line):
        moved = lax.ppermute(quarter, "dp", [(i, (i + step) % line) for i in range(line)]) if step else quarter
        down = lax.dynamic_update_slice_in_dim(down, moved[None], (place - step) % line, 0)
    matrices = matrices.reshape(sections, groups, D, D)
    wq, wk, wv, wo = [matrices[:, index] for index in range(4)]

    rows = byte_states.shape[0] // sections
    mine = lambda a: lax.dynamic_slice_in_dim(a, section * rows, rows, 0)
    states, lengths, docs, cot = [mine(a) for a in (byte_states, patch_lengths, patch_docs, cotangent)]
    tokens = rows * PATCHES
    cot = cot.reshape(tokens, D)
    other_cot = lax.dynamic_slice_in_dim(cotangent, (1 - section) * rows, rows, 0).reshape(tokens, D)
    cots = jnp.concatenate([cot, other_cot], axis=0)

    ends = jnp.cumsum(lengths, axis=1)
    earlier = docs[:, None, :] < docs[:, :, None]
    doc_start = jnp.sum(jnp.where(earlier, lengths[:, None, :], 0), axis=2)
    doc_first = jnp.sum(earlier.astype(jnp.int32), axis=2)
    cross, cross_back = chunk_bounds(doc_start, ends, 256), chunk_bounds(doc_start, ends, 512)
    ids = jnp.broadcast_to(lax.iota(jnp.int32, PATCHES) + 1, doc_first.shape)
    causal = chunk_bounds(doc_first, ids, 128)
    positions = lax.iota(jnp.int32, ROW_BYTES)
    member = (positions < ends[:, :, None]) & (positions >= (ends - lengths)[:, :, None])
    member = member.astype(BF)
    count = lengths.astype(F32).reshape(rows * PATCHES, 1)

    pooled = jnp.einsum("rpb,rbd->rpd", member, states, preferred_element_type=F32)
    pooled = pooled.reshape(rows * PATCHES, D) / count
    wide = states.reshape(rows * ROW_BYTES, D).astype(F32)
    query_scale, key_scale = scale_of(pooled), scale_of(wide)
    query_in = (pooled * query_scale * gains[0, 0]).astype(BF)
    key_in = (wide * key_scale * gains[0, 1]).astype(BF)
    q1 = nn(query_in, wq[0]).astype(BF)
    k1 = nn(key_in, wk[0]).astype(BF)
    v1 = nn(key_in, wv[0]).astype(BF)
    v1, down = together((v1, down))
    down = both(down, side, "group", side_pairs)
    c1, l1 = attend(cross, q1, k1, v1, 8)
    carried = (pooled + nn(c1, wo[0])).astype(BF)

    carried_wide = carried.astype(F32)
    first_scale = scale_of(carried_wide)
    normed_in = (carried_wide * first_scale * gains[1, 0]).astype(BF)
    q2 = nn(normed_in, wq[1]).astype(BF)
    k2 = nn(normed_in, wk[1]).astype(BF)
    v2 = nn(normed_in, wv[1]).astype(BF)
    c2, l2 = attend(causal, q2, k2, v2, 8, CAUSAL_SPANS)
    c2, down = together((c2, down))
    down = both(down, core, "group", core_pairs)
    w_down = down.transpose(2, 1, 0, 3, 4).reshape(units, D)
    residual = carried_wide + nn(c2, wo[1])
    second_scale = scale_of(residual)
    mix_in = (residual * second_scale * gains[1, 1]).astype(BF)
    mix_got = lax.ppermute(mix_in, "section", swap)
    grad_hidden = nt(cots, w_down).astype(BF)
    mix_got, grad_hidden = together((mix_got, grad_hidden))
    mixed = jnp.concatenate([mix_in, mix_got], axis=0)
    gate_up = nn(mixed, w_in)
    gate, up = gate_up[:, :units], gate_up[:, units:]
    sig = jax.nn.sigmoid(gate)
    hidden = (gate * sig * up).astype(BF)

    grad_hidden = grad_hidden.astype(F32)
    grad_gate = grad_hidden * up * sig * (1.0 + gate * (1.0 - sig))
    grad_up = grad_hidden * gate * sig
    dgu = together(jnp.concatenate([grad_gate, grad_up], axis=1).astype(BF))

    def exchanged(values, axis, part, pairs, where):
        size = values.shape[where] // 2
        other = lax.dynamic_slice_in_dim(values, (1 - part) * size, size, where)
        own = lax.dynamic_slice_in_dim(values, part * size, size, where)
        return (own.astype(F32) + lax.ppermute(other, axis, pairs).astype(F32)).astype(BF)

    def over_section(values, where):
        return exchanged(values, "section", section, swap, where)

    def over_side(values, where):
        return exchanged(values, "group", side, side_pairs, where)

    def columns(values, part):
        size = values.shape[-1] // 2
        return lax.dynamic_slice_in_dim(values, part * size, size, values.ndim - 1)

    def line_sum(values, where):
        return lax.psum_scatter(values, "dp", scatter_dimension=where, tiled=True)

    def products(pairs, part):
        out = [tn(left, columns(right, part)) for left, right in pairs]
        return out[0] if len(out) == 1 else jnp.stack(out)

    def to_core(pairs):
        return products(pairs, 1 - core).astype(BF)

    def of_chip(pairs, sent):
        got = lax.ppermute(sent, "group", core_pairs)
        return (products(pairs, core) + got.astype(F32)).astype(BF)

    dgu, mix_other = together((dgu, nt(dgu[tokens:], w_in).astype(BF)))
    in_pairs, down_pairs = [(mixed, dgu)], [(hidden, cots)]
    send_in, send_down = to_core(in_pairs), to_core(down_pairs)
    mix_got = [lax.ppermute(mix_other[:PATCHES], "section", swap)]
    dgu_own, send_in, send_down, mix_got[0], rest = together(
        (dgu[:tokens], send_in, send_down, mix_got[0], mix_other[PATCHES:])
    )
    mix_got.append(lax.ppermute(rest, "section", swap))

    half = D // sections
    parts = nn(hidden, w_down)
    parts = jnp.concatenate([residual + parts[:tokens], parts[tokens:]], axis=0)
    sent = lax.dynamic_slice_in_dim(parts, (1 - section) * half, half, 1).astype(BF)
    kept = lax.dynamic_slice_in_dim(parts, section * half, half, 1)
    dgu_own, sent = together((dgu_own, sent))
    got = lax.ppermute(sent, "section", swap)

    half_in, half_down = of_chip(in_pairs, send_in), of_chip(down_pairs, send_down)
    mix_got, half_in, half_down = together((mix_got, half_in, half_down))
    grad_mixed = nt(dgu_own, w_in) + jnp.concatenate(mix_got, axis=0).astype(F32)
    grad_mix, gain_mix = norm_backward(residual, second_scale, gains[1, 1], grad_mixed)
    grad_residual = grad_mix + cot.astype(F32)
    branch = grad_residual.astype(BF)
    dc2 = nt(branch, wo[1]).astype(BF)

    dq2, dk2, dv2 = attend_back(causal, q2, k2, v2, l2, c2, dc2, 8, CAUSAL_SPANS)
    two_pairs = [(normed_in, dq2), (normed_in, dk2), (normed_in, dv2), (c2, branch)]
    send_two = to_core(two_pairs)
    half_in = over_side(half_in.reshape(sections, line, 2, -1, units), 2)
    sum_down = line_sum(half_down, 0)
    dq2, dk2, dv2, send_two, half_in, sum_down = together((dq2, dk2, dv2, send_two, half_in, sum_down))
    sum_in = line_sum(half_in.reshape(sections, -1, units), 1)
    grad_normed = nt(dq2, wq[1]) + nt(dk2, wk[1]) + nt(dv2, wv[1])
    grad_carried, gain_normed = norm_backward(carried_wide, first_scale, gains[1, 0], grad_normed)
    d_carried = (grad_residual + grad_carried).astype(BF)
    dc1 = nt(d_carried, wo[0]).astype(BF)
    half_two = of_chip(two_pairs, send_two)
    dc1, half_two, got = together((dc1, half_two, got))
    got = got.astype(F32)
    latents = in_order(section, kept[:tokens] + got[tokens:], kept[tokens:] + got[:tokens])
    latents_out = latents.astype(BF).reshape(sections * rows, PATCHES, half)
    dq1, dk1, dv1 = attend_back(cross_back, q1, k1, v1, l1, c1, dc1, 4)
    half_two = over_section(half_two[:2], 2), over_side(half_two[2:], 2)
    dq1, half_two = together((dq1, half_two))
    half_two = jnp.concatenate([over_side(half_two[0], 2), over_section(half_two[1], 2)], axis=0)
    one_pairs = [(query_in, dq1), (key_in, dk1)], [(key_in, dv1), (c1, d_carried)]
    send_one = [to_core(pairs) for pairs in one_pairs]
    dq1, dk1, dv1, send_one, sum_down = together((dq1, dk1, dv1, send_one, sum_down))
    def gathered(part):
        return lax.all_gather(part, "group", axis=0, tiled=False)

    def laid_out(parts, order):
        return jnp.concatenate([parts[index] for index in order], axis=-1).astype(F32)

    half_one = [of_chip(pairs, sent) for pairs, sent in zip(one_pairs, send_one)]
    dq1, dk1, dv1, half_one, half_two, sum_in = together((dq1, dk1, dv1, half_one, half_two, sum_in))
    sum_two = line_sum(half_two, 1)
    sum_in = jnp.stack([lax.dynamic_index_in_dim(sum_in, section, 0, False),
                        lax.ppermute(lax.dynamic_index_in_dim(sum_in, 1 - section, 0, False), "section", swap)])
    sum_in = jnp.where(section == 0, sum_in, sum_in[::-1])
    sum_in = gathered(sum_in)
    grad_query_in = nt(dq1, wq[0])
    grad_key_in = nt(dk1, wk[0]) + nt(dv1, wv[0])
    half_one = over_section(half_one[0], 2), over_side(half_one[1], 2)
    grad_query_in, grad_key_in, half_one = together((grad_query_in, grad_key_in, half_one))
    half_one = jnp.concatenate([over_side(half_one[0], 2), over_section(half_one[1], 2)], axis=0)
    grad_query_in, grad_key_in, half_one, sum_two, sum_down = together(
        (grad_query_in, grad_key_in, half_one, sum_two, sum_down)
    )
    sum_down = over_side(sum_down, 1)
    sum_one = line_sum(half_one, 1)

    grad_pooled, gain_query = norm_backward(pooled, query_scale, gains[0, 0], grad_query_in)
    grad_wide, gain_key = norm_backward(wide, key_scale, gains[0, 1], grad_key_in)
    per_patch = (grad_pooled + d_carried.astype(F32)) / count
    spread_back = jnp.einsum(
        "rpb,rpd->rbd", member, per_patch.astype(BF).reshape(rows, PATCHES, D), preferred_element_type=F32
    )
    byte_grads = (grad_wide + spread_back.reshape(rows * ROW_BYTES, D)).astype(BF)
    byte_grads = byte_grads.reshape(rows, ROW_BYTES, D)
    other = lax.dynamic_slice_in_dim(byte_grads, (1 - section) * half, half, 2)
    own = lax.dynamic_slice_in_dim(byte_grads, section * half, half, 2)

    gain_grads = jnp.stack([gain_query, gain_key, gain_normed, gain_mix])
    gain_grads = gain_grads + lax.ppermute(gain_grads, "section", swap)
    ffn_gin = jnp.concatenate(
        [laid_out([sum_in[at, t] for at in (2 * y, 2 * y + 1) for t in range(sections)], range(4)) for y in (0, 1)],
        axis=0,
    )

    early, gain_grads = together(([other[row] for row in range(rows - 1)], gain_grads))
    bytes_got = [lax.ppermute(part, "section", swap) for part in early]
    for pairs in (core_pairs, side_pairs):
        gain_grads = gain_grads + lax.ppermute(gain_grads, "group", pairs)
    gain_grads = jnp.sum(lax.all_gather(gain_grads, "dp", axis=0, tiled=False), axis=0)
    late, gain_grads, sum_one, bytes_got, sum_down = together(
        (other[rows - 1], gain_grads, sum_one, bytes_got, sum_down)
    )
    bytes_got.append(lax.ppermute(late, "section", swap))
    kept = jnp.where(section == 0, sum_one, sum_two)
    sent = jnp.where(section == 0, sum_two, sum_one)
    got = lax.ppermute(sent, "section", swap)
    got, sum_down = together((got, sum_down))
    ffn_gdown = laid_out(gathered(sum_down), (0, 2, 1, 3))
    eighths = jnp.where(
        section == 0, jnp.concatenate([kept, got], axis=2), jnp.concatenate([got, kept], axis=2)
    )
    width = eighths.shape[2] // 2
    eighths, bytes_got = together((gathered(eighths), bytes_got))
    bytes_out = in_order(section, own, jnp.stack(bytes_got)).reshape(sections * rows, ROW_BYTES, half)
    parts = [piece for every in eighths for piece in (every[..., :width], every[..., width:])]
    section_first = laid_out([part[:2] for part in parts], (0, 4, 1, 5, 2, 6, 3, 7))
    side_first = laid_out([part[2:] for part in parts], (0, 1, 4, 5, 2, 3, 6, 7))
    grad_qkv = jnp.concatenate([section_first, side_first[:1]], axis=0)[None]

    gain_grads = lax.dynamic_slice_in_dim(gain_grads.reshape(2, 2, D), section, 1, 0)
    width = D // lax.axis_size("dp")
    gain_out = lax.dynamic_slice_in_dim(gain_grads, lax.axis_index("dp") * width, width, 2)
    return (latents_out, bytes_out, grad_qkv, side_first[1:], gain_out, ffn_gin, ffn_gdown)


def solution(mesh):
    in_specs = (
        P(("group", "dp"), None, None),
        P(("group", "dp"), None),
        P(("group", "dp"), None),
        P("section", None, "dp", None),
        P("section", "dp", None),
        P("section", None, None),
        P(("section", "dp"), None),
        P(("section", "dp"), None),
        P(("group", "dp"), None, None),
    )
    out_specs = (
        P(("group", "dp"), None, "section"),
        P(("group", "dp"), None, "section"),
        P("section", None, "dp", None),
        P("section", "dp", None),
        P("section", None, "dp"),
        P(("section", "dp"), None),
        P(("section", "dp"), None),
    )
    return jax.shard_map(shards, mesh=mesh, in_specs=in_specs, out_specs=out_specs, check_vma=False)
```

```python
import functools

import jax
import jax.numpy as jnp
from jax import lax
from jax.experimental import pallas as pl
from jax.experimental.pallas import tpu as pltpu
from jax.sharding import PartitionSpec as P

D = 1024
HEADS = 16
HEAD_DIM = 64
PAIR = 2 * HEAD_DIM
PAIRS = HEADS // 2
FF = 2816
ROW_BYTES = 1024
PATCHES = 256
QT = 128
TILES = PATCHES // QT
CAUSAL_SPANS = ((0, 1), (0, 2))

EPS = 1e-05
SCALE = HEAD_DIM ** (-0.5)
EXCLUDED = -1e30

BF = jnp.bfloat16
F32 = jnp.float32


def nn(left, right):
    return jnp.dot(left, right, preferred_element_type=F32)


def tn(left, right):
    return lax.dot_general(left, right, (((0,), (0,)), ((), ())), preferred_element_type=F32)


def nt(left, right):
    return lax.dot_general(left, right, (((1,), (1,)), ((), ())), preferred_element_type=F32)


def two_heads(block):
    lane = lax.broadcasted_iota(jnp.int32, block.shape, 1)
    zero = jnp.zeros_like(block)
    first = lane < HEAD_DIM
    return jnp.concatenate([jnp.where(first, block, zero), jnp.where(first, zero, block)], axis=0)


def own_lanes(both):
    picked = jnp.concatenate([both[:HEAD_DIM, :QT], both[HEAD_DIM:, QT:]], axis=0)
    return picked.T


def twice(row):
    return jnp.concatenate([row, row], axis=1)


def fill_bias(keys, lo_ref, hi_ref, bias_ref):
    at = lax.broadcasted_iota(jnp.int32, (keys, QT), 0)
    for tile in range(TILES):
        own = pl.ds(tile * QT, QT)
        inside = (at >= lo_ref[0, :, own]) & (at < hi_ref[0, :, own])
        bias_ref[tile] = jnp.where(inside, 0.0, EXCLUDED)


def over_chunks(spans, tile, bounds, body, init):
    if spans is None:
        return lax.fori_loop(*bounds, body, init)
    for j in range(*spans[tile]):
        init = body(j, init)
    return init


def chunk_at(spans, chunk, j):
    return pl.ds(j * chunk if spans is not None else pl.multiple_of(j * chunk, chunk), chunk)


def attend_kernel(
    chunk, spans, first_ref, stop_ref, lo_ref, hi_ref, q_ref, k_ref, v_ref, c_ref, l_ref, bias_ref, s_ref
):
    row = pl.program_id(0)
    pairs = range(q_ref.shape[1] // PAIR)
    lanes = [pl.ds(pair * PAIR, PAIR) for pair in pairs]
    pl.when(pl.program_id(1) == 0)(lambda: fill_bias(k_ref.shape[0], lo_ref, hi_ref, bias_ref))
    for tile in range(TILES):
        own = pl.ds(tile * QT, QT)
        queries = [two_heads(q_ref[own, at].astype(F32) * SCALE).astype(BF) for at in lanes]
        bounds = (first_ref[row, tile], stop_ref[row, tile])

        def scores(j, tops):
            here = chunk_at(spans, chunk, j)
            bias = twice(bias_ref[tile, here, :])
            out = []
            for pair in pairs:
                part = nt(k_ref[here, lanes[pair]], queries[pair]) + bias
                s_ref[pair, here, :] = part
                out.append(jnp.maximum(tops[pair], jnp.max(part, axis=0, keepdims=True)))
            return tuple(out)

        tops = (jnp.full((1, 2 * QT), EXCLUDED, F32),) * len(pairs)
        tops = over_chunks(spans, tile, bounds, scores, tops)

        def context(j, sums):
            here = chunk_at(spans, chunk, j)
            out = []
            for pair in pairs:
                total, acc = sums[pair]
                weight = jnp.exp(s_ref[pair, here, :] - tops[pair])
                total = total + jnp.sum(weight, axis=0, keepdims=True)
                out.append((total, acc + tn(v_ref[here, lanes[pair]], weight.astype(BF))))
            return tuple(out)

        sums = ((jnp.zeros((1, 2 * QT), F32), jnp.zeros((PAIR, 2 * QT), F32)),) * len(pairs)
        sums = over_chunks(spans, tile, bounds, context, sums)
        for pair in pairs:
            total, acc = sums[pair]
            c_ref[own, lanes[pair]] = own_lanes(acc / total).astype(BF)
            l_ref[0, pair, tile : tile + 1, :] = tops[pair] + jnp.log(total)


def attend_back_kernel(
    chunk, spans, first_ref, stop_ref, lo_ref, hi_ref, q_ref, k_ref, v_ref, l_ref, c_ref, dc_ref,
    dq_ref, dk_ref, dv_ref, bias_ref, dk_acc, dv_acc,
):
    row = pl.program_id(0)
    pairs = range(q_ref.shape[1] // PAIR)
    lanes = [pl.ds(pair * PAIR, PAIR) for pair in pairs]
    pl.when(pl.program_id(1) == 0)(lambda: fill_bias(k_ref.shape[0], lo_ref, hi_ref, bias_ref))
    dk_acc[...] = jnp.zeros_like(dk_acc)
    dv_acc[...] = jnp.zeros_like(dv_acc)
    for tile in range(TILES):
        own = pl.ds(tile * QT, QT)
        queries, grads, deltas, logs = [], [], [], []
        for pair in pairs:
            queries.append(two_heads(q_ref[own, lanes[pair]].astype(F32) * SCALE).astype(BF))
            grad = dc_ref[own, lanes[pair]].astype(F32)
            inner = (grad * c_ref[own, lanes[pair]].astype(F32)).T
            heads = [jnp.sum(part, axis=0, keepdims=True) for part in (inner[:HEAD_DIM], inner[HEAD_DIM:])]
            deltas.append(jnp.concatenate(heads, axis=1))
            grads.append(two_heads(grad).astype(BF))
            logs.append(l_ref[0, pair, tile : tile + 1, :])

        def step(j, accs):
            here = chunk_at(spans, chunk, j)
            bias = twice(bias_ref[tile, here, :])
            out = []
            for pair in pairs:
                keys = k_ref[here, lanes[pair]]
                prob = jnp.exp(nt(keys, queries[pair]) + bias - logs[pair])
                slope = prob * (nt(v_ref[here, lanes[pair]], grads[pair]) - deltas[pair])
                slope = slope.astype(BF)
                dv_acc[here, lanes[pair]] += nn(prob.astype(BF), grads[pair])
                dk_acc[here, lanes[pair]] += nn(slope, queries[pair])
                out.append(accs[pair] + tn(keys, slope))
            return tuple(out)

        bounds = (first_ref[row, tile], stop_ref[row, tile])
        accs = (jnp.zeros((PAIR, 2 * QT), F32),) * len(pairs)
        accs = over_chunks(spans, tile, bounds, step, accs)
        for pair in pairs:
            dq_ref[own, lanes[pair]] = (own_lanes(accs[pair]) * SCALE).astype(BF)
    dk_ref[...] = dk_acc[...].astype(BF)
    dv_ref[...] = dv_acc[...].astype(BF)


def attention_specs(keys, wide):
    per_query = pl.BlockSpec((PATCHES, wide * PAIR), lambda r, h, *_: (r, h))
    per_key = pl.BlockSpec((keys, wide * PAIR), lambda r, h, *_: (r, h))
    bound = pl.BlockSpec((1, 1, PATCHES), lambda r, h, *_: (r, 0, 0))
    logs = pl.BlockSpec((1, wide, TILES, 2 * QT), lambda r, h, *_: (r, h, 0, 0))
    return per_query, per_key, bound, logs


def kernel_cost(q, k, products):
    scores = q.shape[0] * k.shape[0] // (q.shape[0] // PATCHES) * HEADS
    return pl.CostEstimate(
        flops=products * 2 * scores * 256, bytes_accessed=2 * q.nbytes + 4 * k.nbytes, transcendentals=scores
    )


def attend(bounds, q, k, v, wide, spans=None):
    first, stop, lo, hi, chunk = bounds
    rows = lo.shape[0]
    keys = k.shape[0] // rows
    per_query, per_key, bound, logs = attention_specs(keys, wide)
    return pl.pallas_call(
        functools.partial(attend_kernel, chunk, spans),
        grid_spec=pltpu.PrefetchScalarGridSpec(
            num_scalar_prefetch=2,
            grid=(rows, PAIRS // wide),
            in_specs=[bound, bound, per_query, per_key, per_key],
            out_specs=[per_query, logs],
            scratch_shapes=[pltpu.VMEM((TILES, keys, QT), F32), pltpu.VMEM((wide, keys, 2 * QT), F32)],
        ),
        out_shape=[
            jax.ShapeDtypeStruct(q.shape, BF),
            jax.ShapeDtypeStruct((rows, PAIRS, TILES, 2 * QT), F32),
        ],
        compiler_params=pltpu.CompilerParams(vmem_limit_bytes=48 << 20),
        cost_estimate=kernel_cost(q, k, 2),
        name="attend",
    )(first, stop, lo, hi, q, k, v)


def attend_back(bounds, q, k, v, logsum, context, grads, wide, spans=None):
    first, stop, lo, hi, chunk = bounds
    rows = lo.shape[0]
    keys = k.shape[0] // rows
    per_query, per_key, bound, logs = attention_specs(keys, wide)
    return pl.pallas_call(
        functools.partial(attend_back_kernel, chunk, spans),
        grid_spec=pltpu.PrefetchScalarGridSpec(
            num_scalar_prefetch=2,
            grid=(rows, PAIRS // wide),
            in_specs=[bound, bound, per_query, per_key, per_key, logs, per_query, per_query],
            out_specs=[per_query, per_key, per_key],
            scratch_shapes=[pltpu.VMEM((TILES, keys, QT), F32)] + [pltpu.VMEM((keys, wide * PAIR), F32)] * 2,
        ),
        out_shape=[
            jax.ShapeDtypeStruct(q.shape, BF),
            jax.ShapeDtypeStruct(k.shape, BF),
            jax.ShapeDtypeStruct(k.shape, BF),
        ],
        compiler_params=pltpu.CompilerParams(vmem_limit_bytes=48 << 20),
        cost_estimate=kernel_cost(q, k, 5),
        name="attend_back",
    )(first, stop, lo, hi, q, k, v, logsum, context, grads)


def scale_of(values):
    return lax.rsqrt(jnp.mean(values * values, axis=-1, keepdims=True) + EPS)


def norm_backward(values, row_scale, gain_row, incoming):
    weighted = incoming * gain_row
    projection = jnp.mean(weighted * values, axis=-1, keepdims=True)
    grad_values = row_scale * weighted - values * (row_scale * row_scale * row_scale) * projection
    grad_gain = jnp.sum(incoming * values * row_scale, axis=0)
    return grad_values, grad_gain


def chunk_bounds(lo, hi, chunk):
    first = lo[:, ::QT] // chunk
    stop = (hi[:, QT - 1 :: QT] + chunk - 1) // chunk
    return first, stop, lo[:, None, :], hi[:, None, :], chunk


def shards(
    byte_states, patch_lengths, patch_docs, attn_qkv, attn_out, norm_gains, ffn_in, ffn_down, cotangent
):
    section = lax.axis_index("section")
    group = lax.axis_index("group")
    sections = lax.axis_size("section")
    groups = lax.axis_size("group")
    core, side = group % 2, group // 2

    core_pairs = [(0, 1), (1, 0), (2, 3), (3, 2)]
    side_pairs = [(0, 2), (1, 3), (2, 0), (3, 1)]
    swap = [(0, 1), (1, 0)]
    together = lax.optimization_barrier

    four = jnp.concatenate([attn_qkv[0], attn_out], axis=0)
    matrix = lax.dynamic_index_in_dim(four, group, 0, keepdims=False)
    matrices = lax.all_gather(matrix, ("section", "group", "dp"), axis=0, tiled=True)

    gains = lax.all_gather(norm_gains, "section", axis=0, tiled=True)

    def quarter_of(shard):
        height = shard.shape[0] // groups
        return lax.dynamic_slice_in_dim(shard, group * height, height, 0)

    def in_order(part, own, got):
        return jnp.where(part == 0, jnp.stack([own, got]), jnp.stack([got, own]))

    def both(values, part, axis, pairs):
        return in_order(part, values, lax.ppermute(values, axis, pairs))

    units = FF // sections

    def of_units(values, part):
        halves = [lax.dynamic_slice_in_dim(values, at + part * units, units, 1) for at in (0, FF)]
        return jnp.concatenate(halves, axis=1)

    quarter = quarter_of(ffn_in)
    got = lax.ppermute(of_units(quarter, 1 - section), "section", swap)
    w_in = in_order(section, of_units(quarter, section), got)
    w_in = lax.all_gather(w_in, ("dp", "group"), axis=1, tiled=True).reshape(D, 2 * units)

    line, place = lax.axis_size("dp"), lax.axis_index("dp")
    quarter = quarter_of(ffn_down)
    down = jnp.zeros((line,) + quarter.shape, BF)
    for step in range(line):
        moved = lax.ppermute(quarter, "dp", [(i, (i + step) % line) for i in range(line)]) if step else quarter
        down = lax.dynamic_update_slice_in_dim(down, moved[None], (place - step) % line, 0)
    matrices = matrices.reshape(sections, groups, D, D)
    wq, wk, wv, wo = [matrices[:, index] for index in range(4)]

    rows = byte_states.shape[0] // sections
    mine = lambda a: lax.dynamic_slice_in_dim(a, section * rows, rows, 0)
    states, lengths, docs, cot = [mine(a) for a in (byte_states, patch_lengths, patch_docs, cotangent)]
    tokens = rows * PATCHES
    cot = cot.reshape(tokens, D)
    other_cot = lax.dynamic_slice_in_dim(cotangent, (1 - section) * rows, rows, 0).reshape(tokens, D)
    cots = jnp.concatenate([cot, other_cot], axis=0)

    ends = jnp.cumsum(lengths, axis=1)
    earlier = docs[:, None, :] < docs[:, :, None]
    doc_start = jnp.sum(jnp.where(earlier, lengths[:, None, :], 0), axis=2)
    doc_first = jnp.sum(earlier.astype(jnp.int32), axis=2)
    cross, cross_back = chunk_bounds(doc_start, ends, 256), chunk_bounds(doc_start, ends, 512)
    ids = jnp.broadcast_to(lax.iota(jnp.int32, PATCHES) + 1, doc_first.shape)
    causal = chunk_bounds(doc_first, ids, 128)
    positions = lax.iota(jnp.int32, ROW_BYTES)
    member = (positions < ends[:, :, None]) & (positions >= (ends - lengths)[:, :, None])
    member = member.astype(BF)
    count = lengths.astype(F32).reshape(rows * PATCHES, 1)

    pooled = jnp.einsum("rpb,rbd->rpd", member, states, preferred_element_type=F32)
    pooled = pooled.reshape(rows * PATCHES, D) / count
    wide = states.reshape(rows * ROW_BYTES, D).astype(F32)
    query_scale, key_scale = scale_of(pooled), scale_of(wide)
    query_in = (pooled * query_scale * gains[0, 0]).astype(BF)
    key_in = (wide * key_scale * gains[0, 1]).astype(BF)
    q1 = nn(query_in, wq[0]).astype(BF)
    k1 = nn(key_in, wk[0]).astype(BF)
    v1 = nn(key_in, wv[0]).astype(BF)
    v1, down = together((v1, down))
    down = both(down, side, "group", side_pairs)
    c1, l1 = attend(cross, q1, k1, v1, 8)
    carried = (pooled + nn(c1, wo[0])).astype(BF)

    carried_wide = carried.astype(F32)
    first_scale = scale_of(carried_wide)
    normed_in = (carried_wide * first_scale * gains[1, 0]).astype(BF)
    q2 = nn(normed_in, wq[1]).astype(BF)
    k2 = nn(normed_in, wk[1]).astype(BF)
    v2 = nn(normed_in, wv[1]).astype(BF)
    c2, l2 = attend(causal, q2, k2, v2, 8, CAUSAL_SPANS)
    c2, down = together((c2, down))
    down = both(down, core, "group", core_pairs)
    w_down = down.transpose(2, 1, 0, 3, 4).reshape(units, D)
    residual = carried_wide + nn(c2, wo[1])
    second_scale = scale_of(residual)
    mix_in = (residual * second_scale * gains[1, 1]).astype(BF)
    mix_got = lax.ppermute(mix_in, "section", swap)
    grad_hidden = nt(cots, w_down).astype(BF)
    mix_got, grad_hidden = together((mix_got, grad_hidden))
    mixed = jnp.concatenate([mix_in, mix_got], axis=0)
    gate_up = nn(mixed, w_in)
    gate, up = gate_up[:, :units], gate_up[:, units:]
    sig = jax.nn.sigmoid(gate)
    hidden = (gate * sig * up).astype(BF)

    grad_hidden = grad_hidden.astype(F32)
    grad_gate = grad_hidden * up * sig * (1.0 + gate * (1.0 - sig))
    grad_up = grad_hidden * gate * sig
    dgu = together(jnp.concatenate([grad_gate, grad_up], axis=1).astype(BF))

    def exchanged(values, axis, part, pairs, where):
        size = values.shape[where] // 2
        other = lax.dynamic_slice_in_dim(values, (1 - part) * size, size, where)
        own = lax.dynamic_slice_in_dim(values, part * size, size, where)
        return (own.astype(F32) + lax.ppermute(other, axis, pairs).astype(F32)).astype(BF)

    def over_section(values, where):
        return exchanged(values, "section", section, swap, where)

    def over_side(values, where):
        return exchanged(values, "group", side, side_pairs, where)

    def columns(values, part):
        size = values.shape[-1] // 2
        return lax.dynamic_slice_in_dim(values, part * size, size, values.ndim - 1)

    def line_sum(values, where):
        return lax.psum_scatter(values, "dp", scatter_dimension=where, tiled=True)

    def products(pairs, part):
        out = [tn(left, columns(right, part)) for left, right in pairs]
        return out[0] if len(out) == 1 else jnp.stack(out)

    def to_core(pairs):
        return products(pairs, 1 - core).astype(BF)

    def of_chip(pairs, sent):
        got = lax.ppermute(sent, "group", core_pairs)
        return (products(pairs, core) + got.astype(F32)).astype(BF)

    dgu, mix_other = together((dgu, nt(dgu[tokens:], w_in).astype(BF)))
    in_pairs, down_pairs = [(mixed, dgu)], [(hidden, cots)]
    send_in, send_down = to_core(in_pairs), to_core(down_pairs)
    mix_got = [lax.ppermute(mix_other[:PATCHES], "section", swap)]
    dgu_own, send_in, send_down, mix_got[0], rest = together(
        (dgu[:tokens], send_in, send_down, mix_got[0], mix_other[PATCHES:])
    )
    mix_got.append(lax.ppermute(rest, "section", swap))

    half = D // sections
    parts = nn(hidden, w_down)
    parts = jnp.concatenate([residual + parts[:tokens], parts[tokens:]], axis=0)
    sent = lax.dynamic_slice_in_dim(parts, (1 - section) * half, half, 1).astype(BF)
    kept = lax.dynamic_slice_in_dim(parts, section * half, half, 1)
    dgu_own, sent = together((dgu_own, sent))
    got = lax.ppermute(sent, "section", swap)

    half_in, half_down = of_chip(in_pairs, send_in), of_chip(down_pairs, send_down)
    mix_got, half_in, half_down = together((mix_got, half_in, half_down))
    grad_mixed = nt(dgu_own, w_in) + jnp.concatenate(mix_got, axis=0).astype(F32)
    grad_mix, gain_mix = norm_backward(residual, second_scale, gains[1, 1], grad_mixed)
    grad_residual = grad_mix + cot.astype(F32)
    branch = grad_residual.astype(BF)
    dc2 = nt(branch, wo[1]).astype(BF)

    dq2, dk2, dv2 = attend_back(causal, q2, k2, v2, l2, c2, dc2, 8, CAUSAL_SPANS)
    two_pairs = [(normed_in, dq2), (normed_in, dk2), (normed_in, dv2), (c2, branch)]
    send_two = to_core(two_pairs)
    half_in = over_side(half_in.reshape(sections, line, 2, -1, units), 2)
    sum_down = line_sum(half_down, 0)
    dq2, dk2, dv2, send_two, half_in, sum_down = together((dq2, dk2, dv2, send_two, half_in, sum_down))
    sum_in = line_sum(half_in.reshape(sections, -1, units), 1)
    grad_normed = nt(dq2, wq[1]) + nt(dk2, wk[1]) + nt(dv2, wv[1])
    grad_carried, gain_normed = norm_backward(carried_wide, first_scale, gains[1, 0], grad_normed)
    d_carried = (grad_residual + grad_carried).astype(BF)
    dc1 = nt(d_carried, wo[0]).astype(BF)
    half_two = of_chip(two_pairs, send_two)
    dc1, half_two, got = together((dc1, half_two, got))
    got = got.astype(F32)
    latents = in_order(section, kept[:tokens] + got[tokens:], kept[tokens:] + got[:tokens])
    latents_out = latents.astype(BF).reshape(sections * rows, PATCHES, half)
    dq1, dk1, dv1 = attend_back(cross_back, q1, k1, v1, l1, c1, dc1, 4)
    half_two = over_section(half_two[:2], 2), over_side(half_two[2:], 2)
    dq1, half_two = together((dq1, half_two))
    half_two = jnp.concatenate([over_side(half_two[0], 2), over_section(half_two[1], 2)], axis=0)
    one_pairs = [(query_in, dq1), (key_in, dk1)], [(key_in, dv1), (c1, d_carried)]
    send_one = [to_core(pairs) for pairs in one_pairs]
    dq1, dk1, dv1, send_one, sum_down = together((dq1, dk1, dv1, send_one, sum_down))
    def gathered(part):
        return lax.all_gather(part, "group", axis=0, tiled=False)

    def laid_out(parts, order):
        return jnp.concatenate([parts[index] for index in order], axis=-1).astype(F32)

    half_one = [of_chip(pairs, sent) for pairs, sent in zip(one_pairs, send_one)]
    dq1, dk1, dv1, half_one, half_two, sum_in = together((dq1, dk1, dv1, half_one, half_two, sum_in))
    sum_two = line_sum(half_two, 1)
    sum_in = jnp.stack([lax.dynamic_index_in_dim(sum_in, section, 0, False),
                        lax.ppermute(lax.dynamic_index_in_dim(sum_in, 1 - section, 0, False), "section", swap)])
    sum_in = jnp.where(section == 0, sum_in, sum_in[::-1])
    sum_in = gathered(sum_in)
    grad_query_in = nt(dq1, wq[0])
    grad_key_in = (nt(dk1, wk[0]) + nt(dv1, wv[0])).astype(BF)
    half_one = over_section(half_one[0], 2), over_side(half_one[1], 2)
    grad_query_in, grad_key_in, half_one = together((grad_query_in, grad_key_in, half_one))
    half_one = jnp.concatenate([over_side(half_one[0], 2), over_section(half_one[1], 2)], axis=0)
    grad_query_in, grad_key_in, half_one, sum_two, sum_down = together(
        (grad_query_in, grad_key_in, half_one, sum_two, sum_down)
    )
    sum_down = over_side(sum_down, 1)
    sum_one = line_sum(half_one, 1)

    grad_pooled, gain_query = norm_backward(pooled, query_scale, gains[0, 0], grad_query_in)
    grad_wide, gain_key = norm_backward(wide, key_scale, gains[0, 1], grad_key_in.astype(F32))
    per_patch = (grad_pooled + d_carried.astype(F32)) / count
    spread_back = jnp.einsum(
        "rpb,rpd->rbd", member, per_patch.astype(BF).reshape(rows, PATCHES, D), preferred_element_type=F32
    )
    byte_grads = (grad_wide + spread_back.reshape(rows * ROW_BYTES, D)).astype(BF)
    byte_grads = byte_grads.reshape(rows, ROW_BYTES, D)
    other = lax.dynamic_slice_in_dim(byte_grads, (1 - section) * half, half, 2)
    own = lax.dynamic_slice_in_dim(byte_grads, section * half, half, 2)

    gain_grads = jnp.stack([gain_query, gain_key, gain_normed, gain_mix])
    gain_grads = gain_grads + lax.ppermute(gain_grads, "section", swap)
    ffn_gin = jnp.concatenate(
        [laid_out([sum_in[at, t] for at in (2 * y, 2 * y + 1) for t in range(sections)], range(4)) for y in (0, 1)],
        axis=0,
    )

    early, gain_grads = together(([other[row] for row in range(rows - 1)], gain_grads))
    bytes_got = [lax.ppermute(part, "section", swap) for part in early]
    for pairs in (core_pairs, side_pairs):
        gain_grads = gain_grads + lax.ppermute(gain_grads, "group", pairs)
    gain_grads = jnp.sum(lax.all_gather(gain_grads, "dp", axis=0, tiled=False), axis=0)
    late, gain_grads, sum_one, bytes_got, sum_down = together(
        (other[rows - 1], gain_grads, sum_one, bytes_got, sum_down)
    )
    bytes_got.append(lax.ppermute(late, "section", swap))
    kept = jnp.where(section == 0, sum_one, sum_two)
    sent = jnp.where(section == 0, sum_two, sum_one)
    got = lax.ppermute(sent, "section", swap)
    got, sum_down = together((got, sum_down))
    ffn_gdown = laid_out(gathered(sum_down), (0, 2, 1, 3))
    eighths = jnp.where(
        section == 0, jnp.concatenate([kept, got], axis=2), jnp.concatenate([got, kept], axis=2)
    )
    width = eighths.shape[2] // 2
    eighths, bytes_got = together((gathered(eighths), bytes_got))
    bytes_out = in_order(section, own, jnp.stack(bytes_got)).reshape(sections * rows, ROW_BYTES, half)
    parts = [piece for every in eighths for piece in (every[..., :width], every[..., width:])]
    section_first = laid_out([part[:2] for part in parts], (0, 4, 1, 5, 2, 6, 3, 7))
    side_first = laid_out([part[2:] for part in parts], (0, 1, 4, 5, 2, 3, 6, 7))
    grad_qkv = jnp.concatenate([section_first, side_first[:1]], axis=0)[None]

    gain_grads = lax.dynamic_slice_in_dim(gain_grads.reshape(2, 2, D), section, 1, 0)
    width = D // lax.axis_size("dp")
    gain_out = lax.dynamic_slice_in_dim(gain_grads, lax.axis_index("dp") * width, width, 2)
    return (latents_out, bytes_out, grad_qkv, side_first[1:], gain_out, ffn_gin, ffn_gdown)


def solution(mesh):
    in_specs = (
        P(("group", "dp"), None, None),
        P(("group", "dp"), None),
        P(("group", "dp"), None),
        P("section", None, "dp", None),
        P("section", "dp", None),
        P("section", None, None),
        P(("section", "dp"), None),
        P(("section", "dp"), None),
        P(("group", "dp"), None, None),
    )
    out_specs = (
        P(("group", "dp"), None, "section"),
        P(("group", "dp"), None, "section"),
        P("section", None, "dp", None),
        P("section", "dp", None),
        P("section", None, "dp"),
        P(("section", "dp"), None),
        P(("section", "dp"), None),
    )
    return jax.shard_map(shards, mesh=mesh, in_specs=in_specs, out_specs=out_specs, check_vma=False)
```

```python
import functools

import jax
import jax.numpy as jnp
from jax import lax
from jax.experimental import pallas as pl
from jax.experimental.pallas import tpu as pltpu
from jax.sharding import PartitionSpec as P

D = 1024
HEADS = 16
HEAD_DIM = 64
PAIR = 2 * HEAD_DIM
PAIRS = HEADS // 2
FF = 2816
ROW_BYTES = 1024
PATCHES = 256
QT = 128
TILES = PATCHES // QT
CAUSAL_SPANS = ((0, 1), (0, 2))

EPS = 1e-05
SCALE = HEAD_DIM ** (-0.5)
EXCLUDED = -1e30

BF = jnp.bfloat16
F32 = jnp.float32


def nn(left, right):
    return jnp.dot(left, right, preferred_element_type=F32)


def tn(left, right):
    return lax.dot_general(left, right, (((0,), (0,)), ((), ())), preferred_element_type=F32)


def nt(left, right):
    return lax.dot_general(left, right, (((1,), (1,)), ((), ())), preferred_element_type=F32)


def two_heads(block):
    lane = lax.broadcasted_iota(jnp.int32, block.shape, 1)
    zero = jnp.zeros_like(block)
    first = lane < HEAD_DIM
    return jnp.concatenate([jnp.where(first, block, zero), jnp.where(first, zero, block)], axis=0)


def own_lanes(both):
    picked = jnp.concatenate([both[:HEAD_DIM, :QT], both[HEAD_DIM:, QT:]], axis=0)
    return picked.T


def twice(row):
    return jnp.concatenate([row, row], axis=1)


def fill_bias(keys, lo_ref, hi_ref, bias_ref):
    at = lax.broadcasted_iota(jnp.int32, (keys, QT), 0)
    for tile in range(TILES):
        own = pl.ds(tile * QT, QT)
        inside = (at >= lo_ref[0, :, own]) & (at < hi_ref[0, :, own])
        bias_ref[tile] = jnp.where(inside, 0.0, EXCLUDED)


def over_chunks(spans, tile, bounds, body, init):
    if spans is None:
        return lax.fori_loop(*bounds, body, init)
    for j in range(*spans[tile]):
        init = body(j, init)
    return init


def chunk_at(spans, chunk, j):
    return pl.ds(j * chunk if spans is not None else pl.multiple_of(j * chunk, chunk), chunk)


def attend_kernel(
    chunk, spans, first_ref, stop_ref, lo_ref, hi_ref, q_ref, k_ref, v_ref, c_ref, l_ref, bias_ref, s_ref
):
    row = pl.program_id(0)
    pairs = range(q_ref.shape[1] // PAIR)
    lanes = [pl.ds(pair * PAIR, PAIR) for pair in pairs]
    pl.when(pl.program_id(1) == 0)(lambda: fill_bias(k_ref.shape[0], lo_ref, hi_ref, bias_ref))
    for tile in range(TILES):
        own = pl.ds(tile * QT, QT)
        queries = [two_heads(q_ref[own, at].astype(F32) * SCALE).astype(BF) for at in lanes]
        bounds = (first_ref[row, tile], stop_ref[row, tile])

        def scores(j, tops):
            here = chunk_at(spans, chunk, j)
            bias = twice(bias_ref[tile, here, :])
            out = []
            for pair in pairs:
                part = nt(k_ref[here, lanes[pair]], queries[pair]) + bias
                s_ref[pair, here, :] = part
                out.append(jnp.maximum(tops[pair], jnp.max(part, axis=0, keepdims=True)))
            return tuple(out)

        tops = (jnp.full((1, 2 * QT), EXCLUDED, F32),) * len(pairs)
        tops = over_chunks(spans, tile, bounds, scores, tops)

        def context(j, sums):
            here = chunk_at(spans, chunk, j)
            out = []
            for pair in pairs:
                total, acc = sums[pair]
                weight = jnp.exp(s_ref[pair, here, :] - tops[pair])
                total = total + jnp.sum(weight, axis=0, keepdims=True)
                out.append((total, acc + tn(v_ref[here, lanes[pair]], weight.astype(BF))))
            return tuple(out)

        sums = ((jnp.zeros((1, 2 * QT), F32), jnp.zeros((PAIR, 2 * QT), F32)),) * len(pairs)
        sums = over_chunks(spans, tile, bounds, context, sums)
        for pair in pairs:
            total, acc = sums[pair]
            c_ref[own, lanes[pair]] = own_lanes(acc / total).astype(BF)
            l_ref[0, pair, tile : tile + 1, :] = tops[pair] + jnp.log(total)


def attend_back_kernel(
    chunk, spans, first_ref, stop_ref, lo_ref, hi_ref, q_ref, k_ref, v_ref, l_ref, c_ref, dc_ref,
    dq_ref, dk_ref, dv_ref, bias_ref, dk_acc, dv_acc,
):
    row = pl.program_id(0)
    pairs = range(q_ref.shape[1] // PAIR)
    lanes = [pl.ds(pair * PAIR, PAIR) for pair in pairs]
    pl.when(pl.program_id(1) == 0)(lambda: fill_bias(k_ref.shape[0], lo_ref, hi_ref, bias_ref))
    dk_acc[...] = jnp.zeros_like(dk_acc)
    dv_acc[...] = jnp.zeros_like(dv_acc)
    for tile in range(TILES):
        own = pl.ds(tile * QT, QT)
        queries, grads, deltas, logs = [], [], [], []
        for pair in pairs:
            queries.append(two_heads(q_ref[own, lanes[pair]].astype(F32) * SCALE).astype(BF))
            grad = dc_ref[own, lanes[pair]].astype(F32)
            inner = (grad * c_ref[own, lanes[pair]].astype(F32)).T
            heads = [jnp.sum(part, axis=0, keepdims=True) for part in (inner[:HEAD_DIM], inner[HEAD_DIM:])]
            deltas.append(jnp.concatenate(heads, axis=1))
            grads.append(two_heads(grad).astype(BF))
            logs.append(l_ref[0, pair, tile : tile + 1, :])

        def step(j, accs):
            here = chunk_at(spans, chunk, j)
            bias = twice(bias_ref[tile, here, :])
            out = []
            for pair in pairs:
                keys = k_ref[here, lanes[pair]]
                prob = jnp.exp(nt(keys, queries[pair]) + bias - logs[pair])
                slope = prob * (nt(v_ref[here, lanes[pair]], grads[pair]) - deltas[pair])
                slope = slope.astype(BF)
                dv_acc[here, lanes[pair]] += nn(prob.astype(BF), grads[pair])
                dk_acc[here, lanes[pair]] += nn(slope, queries[pair])
                out.append(accs[pair] + tn(keys, slope))
            return tuple(out)

        bounds = (first_ref[row, tile], stop_ref[row, tile])
        accs = (jnp.zeros((PAIR, 2 * QT), F32),) * len(pairs)
        accs = over_chunks(spans, tile, bounds, step, accs)
        for pair in pairs:
            dq_ref[own, lanes[pair]] = (own_lanes(accs[pair]) * SCALE).astype(BF)
    dk_ref[...] = dk_acc[...].astype(BF)
    dv_ref[...] = dv_acc[...].astype(BF)


def attention_specs(keys, wide):
    per_query = pl.BlockSpec((PATCHES, wide * PAIR), lambda r, h, *_: (r, h))
    per_key = pl.BlockSpec((keys, wide * PAIR), lambda r, h, *_: (r, h))
    bound = pl.BlockSpec((1, 1, PATCHES), lambda r, h, *_: (r, 0, 0))
    logs = pl.BlockSpec((1, wide, TILES, 2 * QT), lambda r, h, *_: (r, h, 0, 0))
    return per_query, per_key, bound, logs


def kernel_cost(q, k, products):
    scores = q.shape[0] * k.shape[0] // (q.shape[0] // PATCHES) * HEADS
    return pl.CostEstimate(
        flops=products * 2 * scores * 256, bytes_accessed=2 * q.nbytes + 4 * k.nbytes, transcendentals=scores
    )


def attend(bounds, q, k, v, wide, spans=None):
    first, stop, lo, hi, chunk = bounds
    rows = lo.shape[0]
    keys = k.shape[0] // rows
    per_query, per_key, bound, logs = attention_specs(keys, wide)
    return pl.pallas_call(
        functools.partial(attend_kernel, chunk, spans),
        grid_spec=pltpu.PrefetchScalarGridSpec(
            num_scalar_prefetch=2,
            grid=(rows, PAIRS // wide),
            in_specs=[bound, bound, per_query, per_key, per_key],
            out_specs=[per_query, logs],
            scratch_shapes=[pltpu.VMEM((TILES, keys, QT), F32), pltpu.VMEM((wide, keys, 2 * QT), F32)],
        ),
        out_shape=[
            jax.ShapeDtypeStruct(q.shape, BF),
            jax.ShapeDtypeStruct((rows, PAIRS, TILES, 2 * QT), F32),
        ],
        compiler_params=pltpu.CompilerParams(vmem_limit_bytes=48 << 20),
        cost_estimate=kernel_cost(q, k, 2),
        name="attend",
    )(first, stop, lo, hi, q, k, v)


def attend_back(bounds, q, k, v, logsum, context, grads, wide, spans=None):
    first, stop, lo, hi, chunk = bounds
    rows = lo.shape[0]
    keys = k.shape[0] // rows
    per_query, per_key, bound, logs = attention_specs(keys, wide)
    return pl.pallas_call(
        functools.partial(attend_back_kernel, chunk, spans),
        grid_spec=pltpu.PrefetchScalarGridSpec(
            num_scalar_prefetch=2,
            grid=(rows, PAIRS // wide),
            in_specs=[bound, bound, per_query, per_key, per_key, logs, per_query, per_query],
            out_specs=[per_query, per_key, per_key],
            scratch_shapes=[pltpu.VMEM((TILES, keys, QT), F32)] + [pltpu.VMEM((keys, wide * PAIR), F32)] * 2,
        ),
        out_shape=[
            jax.ShapeDtypeStruct(q.shape, BF),
            jax.ShapeDtypeStruct(k.shape, BF),
            jax.ShapeDtypeStruct(k.shape, BF),
        ],
        compiler_params=pltpu.CompilerParams(vmem_limit_bytes=48 << 20),
        cost_estimate=kernel_cost(q, k, 5),
        name="attend_back",
    )(first, stop, lo, hi, q, k, v, logsum, context, grads)


def scale_of(values):
    return lax.rsqrt(jnp.mean(values * values, axis=-1, keepdims=True) + EPS)


def norm_backward(values, row_scale, gain_row, incoming):
    weighted = incoming * gain_row
    projection = jnp.mean(weighted * values, axis=-1, keepdims=True)
    grad_values = row_scale * weighted - values * (row_scale * row_scale * row_scale) * projection
    grad_gain = jnp.sum(incoming * values * row_scale, axis=0)
    return grad_values, grad_gain


def chunk_bounds(lo, hi, chunk):
    first = lo[:, ::QT] // chunk
    stop = (hi[:, QT - 1 :: QT] + chunk - 1) // chunk
    return first, stop, lo[:, None, :], hi[:, None, :], chunk


def shards(
    byte_states, patch_lengths, patch_docs, attn_qkv, attn_out, norm_gains, ffn_in, ffn_down, cotangent
):
    section = lax.axis_index("section")
    group = lax.axis_index("group")
    sections = lax.axis_size("section")
    groups = lax.axis_size("group")
    core, side = group % 2, group // 2

    core_pairs = [(0, 1), (1, 0), (2, 3), (3, 2)]
    side_pairs = [(0, 2), (1, 3), (2, 0), (3, 1)]
    swap = [(0, 1), (1, 0)]
    together = lax.optimization_barrier

    four = jnp.concatenate([attn_qkv[0], attn_out], axis=0)
    matrix = lax.dynamic_index_in_dim(four, group, 0, keepdims=False)
    matrices = lax.all_gather(matrix, ("section", "group", "dp"), axis=0, tiled=True)

    gains = lax.all_gather(norm_gains, "section", axis=0, tiled=True)

    def quarter_of(shard):
        height = shard.shape[0] // groups
        return lax.dynamic_slice_in_dim(shard, group * height, height, 0)

    def in_order(part, own, got):
        return jnp.where(part == 0, jnp.stack([own, got]), jnp.stack([got, own]))

    def both(values, part, axis, pairs):
        return in_order(part, values, lax.ppermute(values, axis, pairs))

    units = FF // sections

    def of_units(values, part):
        halves = [lax.dynamic_slice_in_dim(values, at + part * units, units, 1) for at in (0, FF)]
        return jnp.concatenate(halves, axis=1)

    quarter = quarter_of(ffn_in)
    got = lax.ppermute(of_units(quarter, 1 - section), "section", swap)
    w_in = in_order(section, of_units(quarter, section), got)
    w_in = lax.all_gather(w_in, ("dp", "group"), axis=1, tiled=True).reshape(D, 2 * units)

    line, place = lax.axis_size("dp"), lax.axis_index("dp")
    quarter = quarter_of(ffn_down)
    down = jnp.zeros((line,) + quarter.shape, BF)
    for step in range(line):
        moved = lax.ppermute(quarter, "dp", [(i, (i + step) % line) for i in range(line)]) if step else quarter
        down = lax.dynamic_update_slice_in_dim(down, moved[None], (place - step) % line, 0)
    matrices = matrices.reshape(sections, groups, D, D)
    wq, wk, wv, wo = [matrices[:, index] for index in range(4)]

    rows = byte_states.shape[0] // sections
    mine = lambda a: lax.dynamic_slice_in_dim(a, section * rows, rows, 0)
    states, lengths, docs, cot = [mine(a) for a in (byte_states, patch_lengths, patch_docs, cotangent)]
    tokens = rows * PATCHES
    cot = cot.reshape(tokens, D)
    other_cot = lax.dynamic_slice_in_dim(cotangent, (1 - section) * rows, rows, 0).reshape(tokens, D)
    cots = jnp.concatenate([cot, other_cot], axis=0)

    ends = jnp.cumsum(lengths, axis=1)
    earlier = docs[:, None, :] < docs[:, :, None]
    doc_start = jnp.sum(jnp.where(earlier, lengths[:, None, :], 0), axis=2)
    doc_first = jnp.sum(earlier.astype(jnp.int32), axis=2)
    cross, cross_back = chunk_bounds(doc_start, ends, 256), chunk_bounds(doc_start, ends, 512)
    ids = jnp.broadcast_to(lax.iota(jnp.int32, PATCHES) + 1, doc_first.shape)
    causal = chunk_bounds(doc_first, ids, 128)
    positions = lax.iota(jnp.int32, ROW_BYTES)
    member = (positions < ends[:, :, None]) & (positions >= (ends - lengths)[:, :, None])
    member = member.astype(BF)
    count = lengths.astype(F32).reshape(rows * PATCHES, 1)

    pooled = jnp.einsum("rpb,rbd->rpd", member, states, preferred_element_type=F32)
    pooled = pooled.reshape(rows * PATCHES, D) / count
    wide = states.reshape(rows * ROW_BYTES, D).astype(F32)
    query_scale, key_scale = scale_of(pooled), scale_of(wide)
    query_in = (pooled * query_scale * gains[0, 0]).astype(BF)
    key_in = (wide * key_scale * gains[0, 1]).astype(BF)
    q1 = nn(query_in, wq[0]).astype(BF)
    k1 = nn(key_in, wk[0]).astype(BF)
    v1 = nn(key_in, wv[0]).astype(BF)
    v1, down = together((v1, down))
    down = both(down, side, "group", side_pairs)
    c1, l1 = attend(cross, q1, k1, v1, 8)
    carried = (pooled + nn(c1, wo[0])).astype(BF)

    carried_wide = carried.astype(F32)
    first_scale = scale_of(carried_wide)
    normed_in = (carried_wide * first_scale * gains[1, 0]).astype(BF)
    q2 = nn(normed_in, wq[1]).astype(BF)
    k2 = nn(normed_in, wk[1]).astype(BF)
    v2 = nn(normed_in, wv[1]).astype(BF)
    c2, l2 = attend(causal, q2, k2, v2, 8, CAUSAL_SPANS)
    c2, down = together((c2, down))
    down = both(down, core, "group", core_pairs)
    w_down = down.transpose(2, 1, 0, 3, 4).reshape(units, D)
    residual = carried_wide + nn(c2, wo[1])
    second_scale = scale_of(residual)
    mix_in = (residual * second_scale * gains[1, 1]).astype(BF)
    mix_got = lax.ppermute(mix_in, "section", swap)
    grad_hidden = nt(cots, w_down).astype(BF)
    mix_got, grad_hidden = together((mix_got, grad_hidden))
    mixed = jnp.concatenate([mix_in, mix_got], axis=0)
    gate_up = nn(mixed, w_in)
    gate, up = gate_up[:, :units], gate_up[:, units:]
    sig = jax.nn.sigmoid(gate)
    hidden = (gate * sig * up).astype(BF)

    grad_hidden = grad_hidden.astype(F32)
    grad_gate = grad_hidden * up * sig * (1.0 + gate * (1.0 - sig))
    grad_up = grad_hidden * gate * sig
    dgu = together(jnp.concatenate([grad_gate, grad_up], axis=1).astype(BF))

    def exchanged(values, axis, part, pairs, where):
        size = values.shape[where] // 2
        other = lax.dynamic_slice_in_dim(values, (1 - part) * size, size, where)
        own = lax.dynamic_slice_in_dim(values, part * size, size, where)
        return (own.astype(F32) + lax.ppermute(other, axis, pairs).astype(F32)).astype(BF)

    def over_section(values, where):
        return exchanged(values, "section", section, swap, where)

    def over_side(values, where):
        return exchanged(values, "group", side, side_pairs, where)

    def columns(values, part):
        size = values.shape[-1] // 2
        return lax.dynamic_slice_in_dim(values, part * size, size, values.ndim - 1)

    def line_sum(values, where):
        return lax.psum_scatter(values, "dp", scatter_dimension=where, tiled=True)

    def products(pairs, part):
        out = [tn(left, columns(right, part)) for left, right in pairs]
        return out[0] if len(out) == 1 else jnp.stack(out)

    def to_core(pairs):
        return products(pairs, 1 - core).astype(BF)

    def of_chip(pairs, sent):
        got = lax.ppermute(sent, "group", core_pairs)
        return (products(pairs, core) + got.astype(F32)).astype(BF)

    dgu, mix_other = together((dgu, nt(dgu[tokens:], w_in).astype(BF)))
    in_pairs, down_pairs = [(mixed, dgu)], [(hidden, cots)]
    send_in, send_down = to_core(in_pairs), to_core(down_pairs)
    mix_got = [lax.ppermute(mix_other[:PATCHES], "section", swap)]
    dgu_own, send_in, send_down, mix_got[0], rest = together(
        (dgu[:tokens], send_in, send_down, mix_got[0], mix_other[PATCHES:])
    )
    mix_got.append(lax.ppermute(rest, "section", swap))

    half = D // sections
    parts = nn(hidden, w_down)
    parts = jnp.concatenate([residual + parts[:tokens], parts[tokens:]], axis=0)
    sent = lax.dynamic_slice_in_dim(parts, (1 - section) * half, half, 1).astype(BF)
    kept = lax.dynamic_slice_in_dim(parts, section * half, half, 1)
    dgu_own, sent = together((dgu_own, sent))
    got = lax.ppermute(sent, "section", swap)

    half_in, half_down = of_chip(in_pairs, send_in), of_chip(down_pairs, send_down)
    mix_got, half_in, half_down = together((mix_got, half_in, half_down))
    grad_mixed = nt(dgu_own, w_in) + jnp.concatenate(mix_got, axis=0).astype(F32)
    grad_mix, gain_mix = norm_backward(residual, second_scale, gains[1, 1], grad_mixed)
    grad_residual = grad_mix + cot.astype(F32)
    branch = grad_residual.astype(BF)
    dc2 = nt(branch, wo[1]).astype(BF)

    dq2, dk2, dv2 = attend_back(causal, q2, k2, v2, l2, c2, dc2, 8, CAUSAL_SPANS)
    two_pairs = [(normed_in, dq2), (normed_in, dk2), (normed_in, dv2), (c2, branch)]
    send_two = to_core(two_pairs)
    half_in = over_side(half_in.reshape(sections, line, 2, -1, units), 2)
    sum_down = line_sum(half_down, 0)
    dq2, dk2, dv2, send_two, half_in, sum_down = together((dq2, dk2, dv2, send_two, half_in, sum_down))
    sum_in = line_sum(half_in.reshape(sections, -1, units), 1)
    grad_normed = nt(dq2, wq[1]) + nt(dk2, wk[1]) + nt(dv2, wv[1])
    grad_carried, gain_normed = norm_backward(carried_wide, first_scale, gains[1, 0], grad_normed)
    d_carried = (grad_residual + grad_carried).astype(BF)
    dc1 = nt(d_carried, wo[0]).astype(BF)
    half_two = of_chip(two_pairs, send_two)
    dc1, half_two, got = together((dc1, half_two, got))
    got = got.astype(F32)
    latents = in_order(section, kept[:tokens] + got[tokens:], kept[tokens:] + got[:tokens])
    latents_out = latents.astype(BF).reshape(sections * rows, PATCHES, half)
    dq1, dk1, dv1 = attend_back(cross_back, q1, k1, v1, l1, c1, dc1, 4)
    half_two = over_section(half_two[:2], 2), over_side(half_two[2:], 2)
    dq1, half_two = together((dq1, half_two))
    half_two = jnp.concatenate([over_side(half_two[0], 2), over_section(half_two[1], 2)], axis=0)
    one_pairs = [(query_in, dq1), (key_in, dk1)], [(key_in, dv1), (c1, d_carried)]
    send_one = [to_core(pairs) for pairs in one_pairs]
    dq1, dk1, dv1, send_one, sum_down = together((dq1, dk1, dv1, send_one, sum_down))
    def gathered(part):
        return lax.all_gather(part, "group", axis=0, tiled=False)

    def laid_out(parts, order):
        return jnp.concatenate([parts[index] for index in order], axis=-1).astype(F32)

    half_one = [of_chip(pairs, sent) for pairs, sent in zip(one_pairs, send_one)]
    dq1, dk1, dv1, half_one, half_two, sum_in = together((dq1, dk1, dv1, half_one, half_two, sum_in))
    sum_two = line_sum(half_two, 1)
    sum_in = jnp.stack([lax.dynamic_index_in_dim(sum_in, section, 0, False),
                        lax.ppermute(lax.dynamic_index_in_dim(sum_in, 1 - section, 0, False), "section", swap)])
    sum_in = jnp.where(section == 0, sum_in, sum_in[::-1])
    sum_in = gathered(sum_in)
    grad_query_in = nt(dq1, wq[0])
    of_keys = together(nt(dk1, wk[0]).astype(BF))
    grad_key_in = (of_keys.astype(F32) + nt(dv1, wv[0])).astype(BF)
    half_one = over_section(half_one[0], 2), over_side(half_one[1], 2)
    grad_query_in, grad_key_in, half_one = together((grad_query_in, grad_key_in, half_one))
    half_one = jnp.concatenate([over_side(half_one[0], 2), over_section(half_one[1], 2)], axis=0)
    grad_query_in, grad_key_in, half_one, sum_two, sum_down = together(
        (grad_query_in, grad_key_in, half_one, sum_two, sum_down)
    )
    sum_down = over_side(sum_down, 1)
    sum_one = line_sum(half_one, 1)

    grad_pooled, gain_query = norm_backward(pooled, query_scale, gains[0, 0], grad_query_in)
    grad_wide, gain_key = norm_backward(wide, key_scale, gains[0, 1], grad_key_in.astype(F32))
    per_patch = (grad_pooled + d_carried.astype(F32)) / count
    spread_back = jnp.einsum(
        "rpb,rpd->rbd", member, per_patch.astype(BF).reshape(rows, PATCHES, D), preferred_element_type=F32
    )
    byte_grads = (grad_wide + spread_back.reshape(rows * ROW_BYTES, D)).astype(BF)
    byte_grads = byte_grads.reshape(rows, ROW_BYTES, D)
    other = lax.dynamic_slice_in_dim(byte_grads, (1 - section) * half, half, 2)
    own = lax.dynamic_slice_in_dim(byte_grads, section * half, half, 2)

    gain_grads = jnp.stack([gain_query, gain_key, gain_normed, gain_mix])
    gain_grads = gain_grads + lax.ppermute(gain_grads, "section", swap)
    ffn_gin = jnp.concatenate(
        [laid_out([sum_in[at, t] for at in (2 * y, 2 * y + 1) for t in range(sections)], range(4)) for y in (0, 1)],
        axis=0,
    )

    early, gain_grads = together(([other[row] for row in range(rows - 1)], gain_grads))
    bytes_got = [lax.ppermute(part, "section", swap) for part in early]
    for pairs in (core_pairs, side_pairs):
        gain_grads = gain_grads + lax.ppermute(gain_grads, "group", pairs)
    gain_grads = jnp.sum(lax.all_gather(gain_grads, "dp", axis=0, tiled=False), axis=0)
    late, gain_grads, sum_one, bytes_got, sum_down = together(
        (other[rows - 1], gain_grads, sum_one, bytes_got, sum_down)
    )
    bytes_got.append(lax.ppermute(late, "section", swap))
    kept = jnp.where(section == 0, sum_one, sum_two)
    sent = jnp.where(section == 0, sum_two, sum_one)
    got = lax.ppermute(sent, "section", swap)
    got, sum_down = together((got, sum_down))
    ffn_gdown = laid_out(gathered(sum_down), (0, 2, 1, 3))
    eighths = jnp.where(
        section == 0, jnp.concatenate([kept, got], axis=2), jnp.concatenate([got, kept], axis=2)
    )
    width = eighths.shape[2] // 2
    eighths, bytes_got = together((gathered(eighths), bytes_got))
    bytes_out = in_order(section, own, jnp.stack(bytes_got)).reshape(sections * rows, ROW_BYTES, half)
    parts = [piece for every in eighths for piece in (every[..., :width], every[..., width:])]
    section_first = laid_out([part[:2] for part in parts], (0, 4, 1, 5, 2, 6, 3, 7))
    side_first = laid_out([part[2:] for part in parts], (0, 1, 4, 5, 2, 3, 6, 7))
    grad_qkv = jnp.concatenate([section_first, side_first[:1]], axis=0)[None]

    gain_grads = lax.dynamic_slice_in_dim(gain_grads.reshape(2, 2, D), section, 1, 0)
    width = D // lax.axis_size("dp")
    gain_out = lax.dynamic_slice_in_dim(gain_grads, lax.axis_index("dp") * width, width, 2)
    return (latents_out, bytes_out, grad_qkv, side_first[1:], gain_out, ffn_gin, ffn_gdown)


def solution(mesh):
    in_specs = (
        P(("group", "dp"), None, None),
        P(("group", "dp"), None),
        P(("group", "dp"), None),
        P("section", None, "dp", None),
        P("section", "dp", None),
        P("section", None, None),
        P(("section", "dp"), None),
        P(("section", "dp"), None),
        P(("group", "dp"), None, None),
    )
    out_specs = (
        P(("group", "dp"), None, "section"),
        P(("group", "dp"), None, "section"),
        P("section", None, "dp", None),
        P("section", "dp", None),
        P("section", None, "dp"),
        P(("section", "dp"), None),
        P(("section", "dp"), None),
    )
    return jax.shard_map(shards, mesh=mesh, in_specs=in_specs, out_specs=out_specs, check_vma=False)
```
